32 devices in a mesh: dp: 2 (over x), ctx: 4 (over z), wa: 4 (over y, core).
Axes of the slice: x: 2, y: 2, z: 4, core: 2. Of those that a mesh axis runs over, the one named last changes fastest.
Arguments:
- tokens: bfloat16 [2, 2048, 2048], P('dp', ('ctx', 'wa')), may hold values from -6 to 6
- doc_starts: int32 [2, 8], P('dp'), may hold values from 0 to 2047, as said below
- out_grad: bfloat16 [2, 2048, 2048], P('dp', ('ctx', 'wa')), may hold values from -6 to 6
- attn_gain: bfloat16 [2048], P(('ctx', 'wa')), may hold values from 0.25 to 1.75
- w_query: bfloat16 [2048, 2048], P(('ctx', 'wa')), may hold values from -0.125 to 0.125
- w_key: bfloat16 [2048, 512], P(('ctx', 'wa')), may hold values from -0.125 to 0.125
- w_value: bfloat16 [2048, 512], P(('ctx', 'wa')), may hold values from -0.125 to 0.125
- q_gain: bfloat16 [64], P(('ctx', 'wa')), may hold values from 0.25 to 1.75
- k_gain: bfloat16 [64], P(('ctx', 'wa')), may hold values from 0.25 to 1.75
- w_out: bfloat16 [2048, 2048], P(('ctx', 'wa')), may hold values from -0.75 to 0.75
- ffn_gain: bfloat16 [2048], P(('ctx', 'wa')), may hold values from 0.25 to 1.75
- w_gate: bfloat16 [2048, 8192], P(('ctx', 'wa')), may hold values from -0.125 to 0.125
- w_up: bfloat16 [2048, 8192], P(('ctx', 'wa')), may hold values from -0.125 to 0.125
- w_down: bfloat16 [8192, 2048], P(('ctx', 'wa')), may hold values from -0.0625 to 0.0625
Outputs:
- layer_out: bfloat16 [2, 2048, 2048], P('dp', ('ctx', 'wa'))
- input_grad: bfloat16 [2, 2048, 2048], P('dp', ('ctx', 'wa'))
- attn_gain_grad: float32 [2048], P(('ctx', 'wa'))
- w_query_grad: float32 [2048, 2048], P(('ctx', 'wa'))
- w_key_grad: float32 [2048, 512], P(('ctx', 'wa'))
- w_value_grad: float32 [2048, 512], P(('ctx', 'wa'))
- q_gain_grad: float32 [64], P(('ctx', 'wa'))
- k_gain_grad: float32 [64], P(('ctx', 'wa'))
- w_out_grad: float32 [2048, 2048], P(('ctx', 'wa'))
- ffn_gain_grad: float32 [2048], P(('ctx', 'wa'))
- w_gate_grad: float32 [2048, 8192], P(('ctx', 'wa'))
- w_up_grad: float32 [2048, 8192], P(('ctx', 'wa'))
- w_down_grad: float32 [8192, 2048], P(('ctx', 'wa'))
The draws below stay inside these ranges and needn't reach their ends.
Inputs may be any that keep to these rules, and one draw needn't show every extreme that they name: `doc_starts`: for each stream the 8 document starts rise strictly from 0; every document has at most 1024 tokens and one document of each stream has exactly 1024.
All inputs are finite; a program needn't handle non-finite values.
Results may differ from the reference program's by a relative error of at most 0.019.
Values may be sent and summed in bfloat16 or wider, within the bound.
A program may use at most 576 MiB of HBM per device.

```python
import jax
import jax.numpy as jnp
from jax import lax

D = 2048
H = 32
KV = 8
HD = 64
FF = 8192
TOK_DEV = 128
NDOC = 8
STREAMS = 2
STREAM = 2048
QUERY_BLOCK = 256
N_CTX = 4
N_WA = 4


def draw_doc_starts(key, part):
    key = jax.random.fold_in(key, 11)
    half_stream = STREAM // 2

    def draw_stream(stream_key):
        key_cuts, key_side = jax.random.split(stream_key)
        cut_points = jnp.sort(jax.random.permutation(key_cuts, half_stream - 1)[:NDOC - 2] + 1).astype(jnp.int32)
        long_first = jax.random.randint(key_side, (), 0, 2)
        leading = jnp.concatenate([jnp.array([0, half_stream], jnp.int32), half_stream + cut_points])
        trailing = jnp.concatenate([jnp.array([0], jnp.int32), cut_points, jnp.array([half_stream], jnp.int32)])
        return jnp.where(long_first == 1, leading, trailing)
    return jax.vmap(draw_stream)(jax.random.split(key, STREAMS)).astype(jnp.int32)


def levels(key, dims, cuts, low, high):
    loudness, own = 1.0, jax.random.fold_in(key, 6)
    for axis_at, shards_of in cuts:
        draws = jnp.exp(jax.random.uniform(jax.random.fold_in(own, axis_at), (shards_of,), jnp.float32, low / len(cuts), high / len(cuts)))
        loudness = loudness * jnp.repeat(draws, dims[axis_at] // shards_of).reshape([-1 if axis == axis_at else 1 for axis in range(len(dims))])
    return loudness


def normal_values(rng, dims, scale, limit, pieces=(), held_as=jnp.bfloat16):
    entries = scale * jax.random.normal(rng, dims, jnp.float32)
    if pieces:
        entries = entries * levels(rng, dims, pieces, -0.22, 0.18)
    return jnp.clip(entries, -limit, limit).astype(held_as)


def setup_inputs(seed: int = 0) -> dict:
    seeds = jax.random.split(jax.random.key(seed), 15)
    return {
        "tokens": normal_values(seeds[0], (STREAMS, STREAM, D), 1.0, 6.0, ((0, 2), (1, 16))),
        "doc_starts": draw_doc_starts(jax.random.fold_in(seeds[14], 71), 0),
        "out_grad": normal_values(seeds[2], (STREAMS, STREAM, D), 1.0, 6.0, ((0, 2), (1, 16))),
        "attn_gain": jnp.clip(1.0 + 0.15 * jax.random.normal(seeds[3], (D,), jnp.float32), 0.25, 1.75).astype(jnp.bfloat16),
        "w_query": normal_values(seeds[4], (D, H * HD), D ** -0.5, 0.125, ((0, 16),)),
        "w_key": normal_values(seeds[5], (D, KV * HD), D ** -0.5, 0.125, ((0, 16),)),
        "w_value": normal_values(seeds[6], (D, KV * HD), D ** -0.5, 0.125, ((0, 16),)),
        "q_gain": jnp.clip(1.0 + 0.15 * jax.random.normal(seeds[7], (HD,), jnp.float32), 0.25, 1.75).astype(jnp.bfloat16),
        "k_gain": jnp.clip(1.0 + 0.15 * jax.random.normal(seeds[8], (HD,), jnp.float32), 0.25, 1.75).astype(jnp.bfloat16),
        "w_out": normal_values(seeds[9], (H * HD, D), (H * HD // 32) ** -0.5, 0.75, ((0, 16),)),
        "ffn_gain": jnp.clip(1.0 + 0.15 * jax.random.normal(seeds[10], (D,), jnp.float32), 0.25, 1.75).astype(jnp.bfloat16),
        "w_gate": normal_values(seeds[11], (D, FF), D ** -0.5, 0.125, ((0, 16),)),
        "w_up": normal_values(seeds[12], (D, FF), D ** -0.5, 0.125, ((0, 16),)),
        "w_down": normal_values(seeds[13], (FF, D), FF ** -0.5, 0.0625, ((0, 16),)),
    }


EPS = 1e-05
THETA = 1000000.0
precise = lax.Precision.HIGHEST

@jax.custom_vjp
def low(v):
    return lax.optimization_barrier(v.astype(jnp.bfloat16)).astype(jnp.float32)

@jax.custom_vjp
def low_back(v):
    return v

def low_keep(v):
    return (low(v), None)

def low_pass(kept, grad):
    return (grad,)

def back_keep(v):
    return (v, None)

def back_low(kept, grad):
    return (low(grad),)
low.defvjp(low_keep, low_pass)
low_back.defvjp(back_keep, back_low)

def stored_positions(index):
    device = index // TOK_DEV
    local = index % TOK_DEV
    half_rows = TOK_DEV // 2
    ctx_part = device // N_WA
    wa_part = device % N_WA
    span_idx = jnp.where(local < half_rows, ctx_part, 2 * N_CTX - 1 - ctx_part)
    return (span_idx * (half_rows * N_WA) + wa_part * half_rows + local % half_rows).astype(jnp.int32)

def segments(position, starts):
    return lax.optimization_barrier(jnp.sum((starts[None, :] <= position[:, None]).astype(jnp.int32), axis=1)) - 1

def rms_norm(values, gain):
    return values * lax.rsqrt(lax.optimization_barrier(jnp.mean(values * values, axis=-1, keepdims=True)) + EPS) * gain

def rotate(values, position):
    half_dim = HD // 2
    frequency = THETA ** (-2.0 * jnp.arange(half_dim, dtype=jnp.float32) / HD)
    angles = position.astype(jnp.float32)[:, None] * frequency[None, :]
    cosine = jnp.cos(angles)[:, None, :]
    sine_part = jnp.sin(angles)[:, None, :]
    first_half = values[..., :half_dim]
    second_half = values[..., half_dim:]
    return jnp.concatenate([first_half * cosine - second_half * sine_part, second_half * cosine + first_half * sine_part], axis=-1)

def attention(queries, keys, values, position, segment):
    grouped = queries.reshape(STREAM // QUERY_BLOCK, QUERY_BLOCK, KV, H // KV, HD)

    def one_block(block_args):
        query_blk, pos_blk, seg_blk = block_args
        scores = jnp.einsum('bkgd,tkd->kgbt', query_blk, keys, precision=precise) * HD ** (-0.5)
        scores = low_back(scores)
        allowed = (segment[None, :] == seg_blk[:, None]) & (position[None, :] <= pos_blk[:, None])
        scores = jnp.where(allowed[None, None], scores, -1e+30)
        shifted = jnp.exp(scores - lax.optimization_barrier(jnp.max(scores, axis=-1, keepdims=True)))
        probability = low(shifted / lax.optimization_barrier(jnp.sum(shifted, axis=-1, keepdims=True)))
        return jnp.einsum('kgbt,tkd->bkgd', probability, values, precision=precise)
    attended = lax.map(jax.checkpoint(one_block), (grouped, position.reshape(-1, QUERY_BLOCK), segment.reshape(-1, QUERY_BLOCK)))
    return attended.reshape(STREAM, H * HD)

def layer(inputs, position, segment, params):
    attn_gain, w_query, w_key, w_value, q_gain, k_gain, w_out, ffn_gain, w_gate, w_up, w_down = params
    normed = low(rms_norm(inputs, attn_gain))
    query_raw = low_back(jnp.dot(normed, w_query, precision=precise)).reshape(STREAM, H, HD)
    key_raw = low_back(jnp.dot(normed, w_key, precision=precise)).reshape(STREAM, KV, HD)
    value_raw = low(low_back(jnp.dot(normed, w_value, precision=precise))).reshape(STREAM, KV, HD)
    queries = low(rotate(rms_norm(query_raw, q_gain), position))
    keys = low(rotate(rms_norm(key_raw, k_gain), position))
    attended = low(low_back(attention(queries, keys, value_raw, position, segment)))
    middle = inputs + low_back(jnp.dot(attended, w_out, precision=precise))
    normed_two = low(rms_norm(middle, ffn_gain))
    gate_act = low_back(jnp.dot(normed_two, w_gate, precision=precise))
    up_act = low_back(jnp.dot(normed_two, w_up, precision=precise))
    hidden = low(jax.nn.silu(gate_act) * up_act)
    return middle + low_back(jnp.dot(hidden, w_down, precision=precise))

def reference(tokens, doc_starts, out_grad, attn_gain, w_query, w_key, w_value, q_gain, k_gain, w_out, ffn_gain, w_gate, w_up, w_down):
    position = stored_positions(jnp.arange(STREAM, dtype=jnp.int32))
    params = (attn_gain.astype(jnp.float32), w_query.astype(jnp.float32), w_key.astype(jnp.float32), w_value.astype(jnp.float32), q_gain.astype(jnp.float32), k_gain.astype(jnp.float32), w_out.astype(jnp.float32), ffn_gain.astype(jnp.float32), w_gate.astype(jnp.float32), w_up.astype(jnp.float32), w_down.astype(jnp.float32))
    inputs = tokens.astype(jnp.float32)

    def whole(inputs, params):
        return jnp.stack([layer(inputs[stream], position, segments(position, doc_starts[stream]), params) for stream in range(STREAMS)])
    result, pullback = jax.vjp(whole, inputs, params)
    d_inputs, d_params = pullback(out_grad.astype(jnp.float32))
    return (result.astype(jnp.bfloat16), d_inputs.astype(jnp.bfloat16), d_params[0], d_params[1], d_params[2], d_params[3], d_params[4], d_params[5], d_params[6], d_params[7], d_params[8], d_params[9], d_params[10])
```

```python
from functools import partial

import jax
import jax.numpy as jnp
from jax import lax
from jax.experimental import pallas as pl
from jax.experimental.pallas import tpu as pltpu
from jax.sharding import PartitionSpec as P

H = 32
KV = 8
HD = 64
FF = 8192


EPS = 1e-05
THETA = 1000000.0


def stored_positions(index, tok_rows, n_ctx, n_wa):
    device = index // tok_rows
    local = index % tok_rows
    half_rows = tok_rows // 2
    ctx_part = device // n_wa
    wa_part = device % n_wa
    span_idx = jnp.where(local < half_rows, ctx_part, 2 * n_ctx - 1 - ctx_part)
    return span_idx * (half_rows * n_wa) + wa_part * half_rows + local % half_rows


def segments(position, starts):
    return jnp.sum((starts[None, :] <= position[:, None]).astype(jnp.int32), axis=1) - 1


def rms_norm(values, gain):
    return values * lax.rsqrt(jnp.mean(values * values, axis=-1, keepdims=True) + EPS) * gain


def rotate(values, position):
    half_dim = HD // 2
    frequency = THETA ** (-2.0 * jnp.arange(half_dim, dtype=jnp.float32) / HD)
    angles = position.astype(jnp.float32)[:, None] * frequency[None, :]
    cosine = jnp.cos(angles)[:, None, :]
    sine_part = jnp.sin(angles)[:, None, :]
    first_half = values[..., :half_dim]
    second_half = values[..., half_dim:]
    return jnp.concatenate(
        [
            first_half * cosine - second_half * sine_part,
            second_half * cosine + first_half * sine_part,
        ],
        axis=-1,
    )


def prepare(query_raw, key_raw, query_gain, key_gain, position):
    return (
        rotate(rms_norm(query_raw, query_gain), position),
        rotate(rms_norm(key_raw, key_gain), position),
    )


def per_device(
    tokens,
    doc_starts,
    out_grad,
    attn_gain,
    w_query,
    w_key,
    w_value,
    q_gain,
    k_gain,
    w_out,
    ffn_gain,
    w_gate,
    w_up,
    w_down,
):
    n_ctx = lax.axis_size("ctx")
    n_wa = lax.axis_size("wa")
    tok_rows = tokens.shape[1]
    stream_len = tok_rows * n_ctx * n_wa
    key_width = min(1024, stream_len)
    key_blocks = stream_len // key_width
    groups = H // KV
    scale = HD ** (-0.5)
    first_row = (lax.axis_index("ctx") * n_wa + lax.axis_index("wa")) * tok_rows
    own_pos = stored_positions(
        first_row + jnp.arange(tok_rows, dtype=jnp.int32), tok_rows, n_ctx, n_wa
    )
    starts = doc_starts[0]
    own_seg = segments(own_pos, starts)
    key_pos = stored_positions(jnp.arange(stream_len, dtype=jnp.int32), tok_rows, n_ctx, n_wa)
    key_seg = segments(key_pos, starts)
    residual = tokens[0].astype(jnp.float32)
    attn_set = (
        lax.all_gather(attn_gain, ("ctx", "wa"), axis=0, tiled=True),
        lax.all_gather(w_query, ("ctx", "wa"), axis=0, tiled=True),
        lax.all_gather(w_key, ("ctx", "wa"), axis=0, tiled=True),
        lax.all_gather(w_value, ("ctx", "wa"), axis=0, tiled=True),
        lax.all_gather(q_gain, ("ctx", "wa"), axis=0, tiled=True),
        lax.all_gather(k_gain, ("ctx", "wa"), axis=0, tiled=True),
        lax.all_gather(w_out, ("ctx", "wa"), axis=0, tiled=True),
    )
    g_attn, wq_full, wk_full, wv_full, gq_full, gk_full, wo_full = attn_set
    attn_gain32 = g_attn.astype(jnp.float32)
    qgain32 = gq_full.astype(jnp.float32)
    kgain32 = gk_full.astype(jnp.float32)
    normed_one = rms_norm(residual, attn_gain32).astype(jnp.bfloat16)
    query_raw = jnp.dot(normed_one, wq_full, preferred_element_type=jnp.float32).reshape(
        tok_rows, H, HD
    )
    key_raw = jnp.dot(normed_one, wk_full, preferred_element_type=jnp.float32).reshape(
        tok_rows, KV, HD
    )
    value_b = jnp.dot(normed_one, wv_full, preferred_element_type=jnp.float32).astype(jnp.bfloat16)
    query_rot, key_rot = prepare(query_raw, key_raw, qgain32, kgain32, own_pos)
    query_b = query_rot.astype(jnp.bfloat16).reshape(tok_rows, KV, groups, HD)
    key_b = key_rot.astype(jnp.bfloat16).reshape(tok_rows, KV * HD)
    all_keys, all_values = (
        lax.all_gather(key_b, ("ctx", "wa"), axis=0, tiled=True),
        lax.all_gather(value_b, ("ctx", "wa"), axis=0, tiled=True),
    )

    def key_block(keys_in, values_in, block_idx):
        begin = block_idx * key_width
        key_part = lax.dynamic_slice_in_dim(keys_in, begin, key_width, 0).reshape(key_width, KV, HD)
        value_part = lax.dynamic_slice_in_dim(values_in, begin, key_width, 0).reshape(
            key_width, KV, HD
        )
        pos_part = lax.dynamic_slice_in_dim(key_pos, begin, key_width, 0)
        seg_part = lax.dynamic_slice_in_dim(key_seg, begin, key_width, 0)
        scores = (
            jnp.einsum("rkgd,tkd->kgrt", query_b, key_part, preferred_element_type=jnp.float32)
            * scale
        )
        allowed = (
            (seg_part[None, :] == own_seg[:, None]) & (pos_part[None, :] <= own_pos[:, None])
        )[None, None]
        return (scores, allowed, key_part, value_part)

    def stat_step(block_idx, carry):
        row_max, row_total = carry
        scores, allowed, key_part, value_part = key_block(all_keys, all_values, block_idx)
        masked = jnp.where(allowed, scores, -1e30)
        new_max = jnp.maximum(row_max, jnp.max(masked, axis=-1))
        fresh = jnp.sum(jnp.where(allowed, jnp.exp(masked - new_max[..., None]), 0.0), axis=-1)
        return (new_max, row_total * jnp.exp(row_max - new_max) + fresh)

    stat_init = (
        jnp.full((KV, groups, tok_rows), -1e30, jnp.float32),
        jnp.zeros((KV, groups, tok_rows), jnp.float32),
    )
    row_max, row_total = lax.fori_loop(0, key_blocks, stat_step, stat_init)

    def out_step(block_idx, summed):
        scores, allowed, key_part, value_part = key_block(all_keys, all_values, block_idx)
        probability = (
            jnp.where(allowed, jnp.exp(scores - row_max[..., None]), 0.0) / row_total[..., None]
        )
        return summed + jnp.einsum(
            "kgrt,tkd->rkgd",
            probability.astype(jnp.bfloat16),
            value_part,
            preferred_element_type=jnp.float32,
        )

    attended = lax.fori_loop(
        0, key_blocks, out_step, jnp.zeros((tok_rows, KV, groups, HD), jnp.float32)
    )
    attended_b = attended.reshape(tok_rows, H * HD).astype(jnp.bfloat16)
    middle = residual + jnp.dot(attended_b, wo_full, preferred_element_type=jnp.float32)
    ffn_set = (
        lax.all_gather(ffn_gain, ("ctx", "wa"), axis=0, tiled=True),
        lax.all_gather(w_gate, ("ctx", "wa"), axis=0, tiled=True),
        lax.all_gather(w_up, ("ctx", "wa"), axis=0, tiled=True),
        lax.all_gather(w_down, ("ctx", "wa"), axis=0, tiled=True),
    )
    g_ffn, wg_full, wu_full, wd_full = ffn_set
    ffn_gain32 = g_ffn.astype(jnp.float32)
    normed_two = rms_norm(middle, ffn_gain32).astype(jnp.bfloat16)
    gate_act = jnp.dot(normed_two, wg_full, preferred_element_type=jnp.float32)
    up_act = jnp.dot(normed_two, wu_full, preferred_element_type=jnp.float32)
    sigmoid_gate = jax.nn.sigmoid(gate_act)
    silu_gate = gate_act * sigmoid_gate
    hidden = (silu_gate * up_act).astype(jnp.bfloat16)
    layer_out = (middle + jnp.dot(hidden, wd_full, preferred_element_type=jnp.float32)).astype(
        jnp.bfloat16
    )
    g_ffn, wg_full, wu_full, wd_full = (
        lax.all_gather(ffn_gain, ("ctx", "wa"), axis=0, tiled=True),
        lax.all_gather(w_gate, ("ctx", "wa"), axis=0, tiled=True),
        lax.all_gather(w_up, ("ctx", "wa"), axis=0, tiled=True),
        lax.all_gather(w_down, ("ctx", "wa"), axis=0, tiled=True),
    )
    d_out = out_grad[0].astype(jnp.float32)
    d_out_b = d_out.astype(jnp.bfloat16)
    d_hidden = jnp.einsum("rd,fd->rf", d_out_b, wd_full, preferred_element_type=jnp.float32)
    d_gate = (d_hidden * up_act * (sigmoid_gate * (1.0 + gate_act * (1.0 - sigmoid_gate)))).astype(
        jnp.bfloat16
    )
    d_up = (d_hidden * silu_gate).astype(jnp.bfloat16)
    d_normed_two = jnp.einsum(
        "rf,df->rd", d_gate, wg_full, preferred_element_type=jnp.float32
    ) + jnp.einsum("rf,df->rd", d_up, wu_full, preferred_element_type=jnp.float32)
    norm_out, norm_back = jax.vjp(rms_norm, middle, ffn_gain32)
    d_middle_part, d_ffn_gain = norm_back(d_normed_two)
    d_middle = d_out + d_middle_part
    gate_up = jnp.concatenate([d_gate, d_up], axis=1)
    part_rows = normed_two
    in_grad = lax.psum_scatter(
        jnp.einsum("rc,rf->cf", part_rows, gate_up, preferred_element_type=jnp.float32),
        ("ctx", "wa"),
        scatter_dimension=0,
        tiled=True,
    )
    part_rows = hidden
    down_grad = lax.psum_scatter(
        jnp.einsum("rc,rd->cd", part_rows, d_out_b, preferred_element_type=jnp.float32),
        ("ctx", "wa"),
        scatter_dimension=0,
        tiled=True,
    )
    g_attn, wq_full, wk_full, wv_full, gq_full, gk_full, wo_full = (
        lax.all_gather(attn_gain, ("ctx", "wa"), axis=0, tiled=True),
        lax.all_gather(w_query, ("ctx", "wa"), axis=0, tiled=True),
        lax.all_gather(w_key, ("ctx", "wa"), axis=0, tiled=True),
        lax.all_gather(w_value, ("ctx", "wa"), axis=0, tiled=True),
        lax.all_gather(q_gain, ("ctx", "wa"), axis=0, tiled=True),
        lax.all_gather(k_gain, ("ctx", "wa"), axis=0, tiled=True),
        lax.all_gather(w_out, ("ctx", "wa"), axis=0, tiled=True),
    )
    d_branch = d_middle.astype(jnp.bfloat16)
    wo_grad = jnp.einsum("re,rd->ed", attended_b, d_branch, preferred_element_type=jnp.float32)
    d_attended = jnp.einsum(
        "rd,ed->re", d_branch, wo_full, preferred_element_type=jnp.float32
    ).astype(jnp.bfloat16)
    d_att4 = d_attended.reshape(tok_rows, KV, groups, HD)
    delta = jnp.einsum("rkgd,rkgd->kgr", d_att4.astype(jnp.float32), attended)

    def back_step(d_query, block_idx):
        scores, allowed, key_part, value_part = key_block(all_keys, all_values, block_idx)
        probability = (
            jnp.where(allowed, jnp.exp(scores - row_max[..., None]), 0.0) / row_total[..., None]
        )
        d_prob = jnp.einsum(
            "rkgd,tkd->kgrt", d_att4, value_part, preferred_element_type=jnp.float32
        )
        d_scores = (probability * (d_prob - delta[..., None])).astype(jnp.bfloat16)
        d_query = (
            d_query
            + jnp.einsum("kgrt,tkd->rkgd", d_scores, key_part, preferred_element_type=jnp.float32)
            * scale
        )
        d_key_part = (
            jnp.einsum("kgrt,rkgd->tkd", d_scores, query_b, preferred_element_type=jnp.float32)
            * scale
        )
        d_value_part = jnp.einsum(
            "kgrt,rkgd->tkd",
            probability.astype(jnp.bfloat16),
            d_att4,
            preferred_element_type=jnp.float32,
        )
        return (
            d_query,
            (d_key_part.reshape(key_width, KV * HD), d_value_part.reshape(key_width, KV * HD)),
        )

    d_query, (d_keys, d_values) = lax.scan(
        back_step, jnp.zeros((tok_rows, KV, groups, HD), jnp.float32), jnp.arange(key_blocks)
    )
    d_key_own, d_value_own = (
        lax.psum_scatter(
            d_keys.reshape(stream_len, KV * HD), ("ctx", "wa"), scatter_dimension=0, tiled=True
        ),
        lax.psum_scatter(
            d_values.reshape(stream_len, KV * HD), ("ctx", "wa"), scatter_dimension=0, tiled=True
        ),
    )
    prep_out, prep_back = jax.vjp(
        partial(prepare, position=own_pos), query_raw, key_raw, qgain32, kgain32
    )
    d_query_raw, d_key_raw, d_qgain, d_kgain = prep_back(
        (d_query.reshape(tok_rows, H, HD), d_key_own.reshape(tok_rows, KV, HD))
    )
    dq_b = d_query_raw.reshape(tok_rows, H * HD).astype(jnp.bfloat16)
    dk_b = d_key_raw.reshape(tok_rows, KV * HD).astype(jnp.bfloat16)
    dv_b = d_value_own.astype(jnp.bfloat16)
    d_normed_one = (
        jnp.einsum("re,de->rd", dq_b, wq_full, preferred_element_type=jnp.float32)
        + jnp.einsum("re,de->rd", dk_b, wk_full, preferred_element_type=jnp.float32)
        + jnp.einsum("re,de->rd", dv_b, wv_full, preferred_element_type=jnp.float32)
    )
    first_out, first_back = jax.vjp(rms_norm, residual, attn_gain32)
    d_res_part, d_attn_gain = first_back(d_normed_one)
    input_grad = (d_middle + d_res_part).astype(jnp.bfloat16)
    wq_grad = jnp.einsum("rc,re->ce", normed_one, dq_b, preferred_element_type=jnp.float32)
    wk_grad = jnp.einsum("rc,re->ce", normed_one, dk_b, preferred_element_type=jnp.float32)
    wv_grad = jnp.einsum("rc,re->ce", normed_one, dv_b, preferred_element_type=jnp.float32)
    attn_terms = (d_attn_gain, wq_grad, wk_grad, wv_grad, d_qgain, d_kgain, d_ffn_gain, wo_grad)
    attn_shards = (
        lax.psum_scatter(attn_terms[0], ("ctx", "wa"), scatter_dimension=0, tiled=True),
        lax.psum_scatter(attn_terms[1], ("ctx", "wa"), scatter_dimension=0, tiled=True),
        lax.psum_scatter(attn_terms[2], ("ctx", "wa"), scatter_dimension=0, tiled=True),
        lax.psum_scatter(attn_terms[3], ("ctx", "wa"), scatter_dimension=0, tiled=True),
        lax.psum_scatter(attn_terms[4], ("ctx", "wa"), scatter_dimension=0, tiled=True),
        lax.psum_scatter(attn_terms[5], ("ctx", "wa"), scatter_dimension=0, tiled=True),
        lax.psum_scatter(attn_terms[6], ("ctx", "wa"), scatter_dimension=0, tiled=True),
        lax.psum_scatter(attn_terms[7], ("ctx", "wa"), scatter_dimension=0, tiled=True),
    )
    wo_shard = attn_shards[7]
    summed = (
        lax.psum(attn_shards[0].astype(jnp.bfloat16), "dp").astype(jnp.float32),
        lax.psum(attn_shards[1].astype(jnp.bfloat16), "dp").astype(jnp.float32),
        lax.psum(attn_shards[2].astype(jnp.bfloat16), "dp").astype(jnp.float32),
        lax.psum(attn_shards[3].astype(jnp.bfloat16), "dp").astype(jnp.float32),
        lax.psum(attn_shards[4].astype(jnp.bfloat16), "dp").astype(jnp.float32),
        lax.psum(attn_shards[5].astype(jnp.bfloat16), "dp").astype(jnp.float32),
        lax.psum(wo_shard.astype(jnp.bfloat16), "dp").astype(jnp.float32),
        lax.psum(attn_shards[6].astype(jnp.bfloat16), "dp").astype(jnp.float32),
        lax.psum(in_grad[:, :FF].astype(jnp.bfloat16), "dp").astype(jnp.float32),
        lax.psum(in_grad[:, FF:].astype(jnp.bfloat16), "dp").astype(jnp.float32),
        lax.psum(down_grad.astype(jnp.bfloat16), "dp").astype(jnp.float32),
    )
    return (layer_out[None], input_grad[None]) + tuple(summed)


AXES = ("ctx", "wa")
LANES = 2 * HD
ROWS_BLOCK = 256
LOG2E = 1.4426950408889634
F32 = jnp.float32
BF16 = jnp.bfloat16


def to_position(rows, n_ctx, n_wa):
    half = rows.shape[0] // (2 * n_ctx * n_wa)
    parts = rows.reshape(n_ctx, n_wa, 2, half, -1)
    ordered = jnp.concatenate([parts[:, :, 0], jnp.flip(parts[:, :, 1], axis=0)], axis=0)
    return ordered.reshape(rows.shape)


def to_stored(rows, n_ctx, n_wa):
    half = rows.shape[0] // (2 * n_ctx * n_wa)
    parts = rows.reshape(2 * n_ctx, n_wa, half, -1)
    paired = jnp.stack([parts[:n_ctx], jnp.flip(parts[n_ctx:], axis=0)], axis=2)
    return paired.reshape(rows.shape)


def low_key(starts, row):
    first = jnp.int32(0)
    for doc in range(starts.shape[1]):
        begin = starts[0, doc]
        first = jnp.where(begin <= row, begin, first)
    return first


def block_mask(starts, q_begin, k_begin, bq, bk):
    row = q_begin + lax.broadcasted_iota(jnp.int32, (bq, 1), 0)
    first = low_key(starts, row)
    col = k_begin + lax.broadcasted_iota(jnp.int32, (1, bk), 1)
    return (col >= first) & (col <= row)


def attend_kernel(starts, q_ref, kv_ref, ov_ref, att_ref, inv_ref):
    block = pl.program_id(0)
    bq = q_ref.shape[0]
    q_begin = block * bq
    q = q_ref[...]
    zero = jnp.zeros((bq, HD), BF16)
    q2 = jnp.concatenate(
        [
            jnp.concatenate([q[:, :HD], zero], axis=1),
            jnp.concatenate([q[:, HD:], zero], axis=1),
        ],
        axis=0,
    )

    def step(j, acc):
        k_begin = pl.multiple_of(j * bq, bq)
        keys = kv_ref[pl.ds(k_begin, bq), :]
        s = lax.dot_general(q2, keys, (((1,), (1,)), ((), ())), preferred_element_type=F32)
        mask = block_mask(starts, q_begin, k_begin, bq, bq)
        p = jnp.exp2(s * (LOG2E * HD**-0.5))
        p = jnp.where(jnp.concatenate([mask, mask], axis=0), p, 0.0).astype(BF16)
        return acc + jnp.dot(p, ov_ref[pl.ds(k_begin, bq), :], preferred_element_type=F32)

    low = low_key(starts, q_begin) // bq
    acc = lax.fori_loop(low, block + 1, step, jnp.zeros((2 * bq, LANES), F32))
    inv = 1.0 / acc[:, :1]
    out = acc[:, HD:] * inv
    att_ref[...] = jnp.concatenate([out[:bq], out[bq:]], axis=1).astype(BF16)
    inv_ref[...] = jnp.concatenate(
        [jnp.broadcast_to(inv[:bq], (bq, HD)), jnp.broadcast_to(inv[bq:], (bq, HD))], axis=1
    )


def attend_back_kernel(starts, q_ref, kv_ref, att_ref, inv_ref, da_ref, dq_ref, dkv_ref):
    block = pl.program_id(0)
    bq = q_ref.shape[0]
    q_begin = block * bq

    @pl.when(block == 0)
    def _():
        dkv_ref[...] = jnp.zeros_like(dkv_ref)

    q = q_ref[...]
    da = da_ref[...]
    zero = jnp.zeros((bq, HD), BF16)
    q2 = jnp.concatenate(
        [
            jnp.concatenate([q[:, :HD], zero], axis=1),
            jnp.concatenate([q[:, HD:], zero], axis=1),
        ],
        axis=0,
    )
    da2 = jnp.concatenate(
        [
            jnp.concatenate([zero, da[:, :HD]], axis=1),
            jnp.concatenate([zero, da[:, HD:]], axis=1),
        ],
        axis=0,
    )
    prod = da.astype(F32) * att_ref[...].astype(F32)
    delta = jnp.concatenate(
        [
            jnp.sum(prod[:, :HD], axis=1, keepdims=True),
            jnp.sum(prod[:, HD:], axis=1, keepdims=True),
        ],
        axis=0,
    )
    inv_all = inv_ref[...]
    inv = jnp.concatenate([inv_all[:, :1], inv_all[:, HD : HD + 1]], axis=0)

    def step(j, dq):
        k_begin = pl.multiple_of(j * bq, bq)
        keys = kv_ref[pl.ds(k_begin, bq), :]
        s = lax.dot_general(q2, keys, (((1,), (1,)), ((), ())), preferred_element_type=F32)
        mask = block_mask(starts, q_begin, k_begin, bq, bq)
        p = jnp.exp2(s * (LOG2E * HD**-0.5)) * inv
        p = jnp.where(jnp.concatenate([mask, mask], axis=0), p, 0.0)
        dp = lax.dot_general(da2, keys, (((1,), (1,)), ((), ())), preferred_element_type=F32)
        ds = (p * (dp - delta)).astype(BF16)
        back = (((0,), (0,)), ((), ()))
        dkv_ref[pl.ds(k_begin, bq), :] += lax.dot_general(
            ds, q2, back, preferred_element_type=F32
        ) + lax.dot_general(p.astype(BF16), da2, back, preferred_element_type=F32)
        return dq + jnp.dot(ds, keys, preferred_element_type=F32)

    low = low_key(starts, q_begin) // bq
    dq = lax.fori_loop(low, block + 1, step, jnp.zeros((2 * bq, LANES), F32))
    dq_ref[...] = jnp.concatenate([dq[:bq, :HD], dq[bq:, :HD]], axis=1)


def attend(starts, q, kv, ov):
    stream = q.shape[0]
    bq = ROWS_BLOCK
    rows = pl.BlockSpec((bq, LANES), lambda i: (i, 0))
    whole = pl.BlockSpec((stream, LANES), lambda i: (0, 0))
    return pl.pallas_call(
        attend_kernel,
        grid=(stream // bq,),
        in_specs=[pl.BlockSpec(memory_space=pltpu.SMEM), rows, whole, whole],
        out_specs=[rows, rows],
        out_shape=[
            jax.ShapeDtypeStruct((stream, LANES), BF16),
            jax.ShapeDtypeStruct((stream, LANES), F32),
        ],
        compiler_params=pltpu.CompilerParams(vmem_limit_bytes=32 * 2**20),
        cost_estimate=pl.CostEstimate(
            flops=4 * stream * 1024 * LANES, bytes_accessed=6 * stream * LANES * 2, transcendentals=0
        ),
    )(starts, q, kv, ov)


def attend_back(starts, q, kv, att, inv, da):
    stream = q.shape[0]
    bq = ROWS_BLOCK
    rows = pl.BlockSpec((bq, LANES), lambda i: (i, 0))
    whole = pl.BlockSpec((stream, LANES), lambda i: (0, 0))
    return pl.pallas_call(
        attend_back_kernel,
        grid=(stream // bq,),
        in_specs=[pl.BlockSpec(memory_space=pltpu.SMEM), rows, whole, rows, rows, rows],
        out_specs=[rows, whole],
        out_shape=[
            jax.ShapeDtypeStruct((stream, LANES), F32),
            jax.ShapeDtypeStruct((stream, LANES), F32),
        ],
        compiler_params=pltpu.CompilerParams(vmem_limit_bytes=32 * 2**20),
        cost_estimate=pl.CostEstimate(
            flops=10 * stream * 1024 * LANES, bytes_accessed=8 * stream * LANES * 2, transcendentals=0
        ),
    )(starts, q, kv, att, inv, da)


def head_prepare(q_raw, k_raw, q_gain, k_gain, position):
    stream = q_raw.shape[0]
    q, k = prepare(
        q_raw.reshape(stream, 2, HD), k_raw.reshape(stream, 1, HD), q_gain, k_gain, position
    )
    return q.reshape(stream, LANES), k.reshape(stream, HD)


def per_device_heads(
    tokens,
    doc_starts,
    out_grad,
    attn_gain,
    w_query,
    w_key,
    w_value,
    q_gain,
    k_gain,
    w_out,
    ffn_gain,
    w_gate,
    w_up,
    w_down,
):
    n_ctx = lax.axis_size("ctx")
    n_wa = lax.axis_size("wa")
    n = n_ctx * n_wa
    me = lax.axis_index("ctx") * n_wa + lax.axis_index("wa")
    even = lax.axis_index("wa") % 2 == 0
    tok_rows, width = tokens.shape[1:]
    d_rows = w_query.shape[0]
    stream = tok_rows * n
    ff_cols = FF // n
    position = jnp.arange(stream, dtype=jnp.int32)

    def gather_rows(own):
        return to_position(lax.all_gather(own, AXES, axis=0, tiled=True), n_ctx, n_wa)

    def scatter_rows(part):
        return lax.psum_scatter(
            to_stored(part, n_ctx, n_wa), AXES, scatter_dimension=0, tiled=True
        ).astype(F32)

    def mm(a, b):
        return jnp.dot(a, b, preferred_element_type=F32)

    def mm_t(a, b):
        return lax.dot_general(a, b, (((1,), (1,)), ((), ())), preferred_element_type=F32)

    def t_mm(a, b):
        return lax.dot_general(a, b, (((0,), (0,)), ((), ())), preferred_element_type=F32)

    gains = lax.all_gather(
        jnp.concatenate([attn_gain, ffn_gain, q_gain, k_gain]), AXES, axis=0
    ).astype(F32)
    attn_gain32 = gains[:, :d_rows].reshape(-1)
    ffn_gain32 = gains[:, d_rows : 2 * d_rows].reshape(-1)
    per = HD // n
    qgain32 = gains[:, 2 * d_rows : 2 * d_rows + per].reshape(-1)
    kgain32 = gains[:, 2 * d_rows + per :].reshape(-1)

    def pair(w):
        return jnp.repeat(w.reshape(d_rows, KV, 1, HD), n // KV, axis=2).reshape(d_rows, n, HD)

    columns = jnp.concatenate(
        [
            w_query.reshape(d_rows, n, LANES),
            pair(w_key),
            pair(w_value),
            w_gate.reshape(d_rows, n, ff_cols),
            w_up.reshape(d_rows, n, ff_cols),
        ],
        axis=2,
    ).transpose(1, 0, 2)
    columns = lax.all_to_all(columns, AXES, 0, 0, tiled=True).reshape(width, -1)
    w_qkv = columns[:, : 2 * LANES]
    w_gu = columns[:, 2 * LANES :]

    x_all = gather_rows(tokens[0])
    dy_all = gather_rows(out_grad[0])
    x_own = tokens[0].astype(F32)
    n1_all = rms_norm(x_all.astype(F32), attn_gain32).astype(BF16)
    qkv = mm(n1_all, w_qkv)
    q_raw, k_raw, v_raw = qkv[:, :LANES], qkv[:, LANES : LANES + HD], qkv[:, LANES + HD :]
    v_b = v_raw.astype(BF16)
    (q_rot, k_rot), prep_back = jax.vjp(
        partial(head_prepare, position=position), q_raw, k_raw, qgain32, kgain32
    )
    q_b = q_rot.astype(BF16)
    kv_b = jnp.concatenate([k_rot.astype(BF16), v_b], axis=1)
    ov_b = jnp.concatenate([jnp.ones_like(v_b), v_b], axis=1)
    att, inv = attend(doc_starts, q_b, kv_b, ov_b)
    middle = x_own + scatter_rows(mm(att, w_out).astype(BF16))
    n2_own, n2_back = jax.vjp(rms_norm, middle, ffn_gain32)
    n2_all = gather_rows(n2_own.astype(BF16))
    gate_up = mm(n2_all, w_gu)
    gate, up = gate_up[:, :ff_cols], gate_up[:, ff_cols:]
    sig = jax.nn.sigmoid(gate)
    silu = gate * sig
    hidden = (silu * up).astype(BF16)
    layer_out = middle + scatter_rows(mm(hidden, w_down).astype(BF16))

    d_hidden = mm_t(dy_all, w_down)
    d_gu = jnp.concatenate(
        [d_hidden * up * (sig * (1.0 + gate * (1.0 - sig))), d_hidden * silu], axis=1
    ).astype(BF16)
    d_n2 = scatter_rows(mm_t(d_gu, w_gu).astype(BF16))
    down_grad = t_mm(hidden, dy_all)
    gu_grad = t_mm(n2_all, d_gu)
    d_mid_part, d_ffn_gain = n2_back(d_n2)
    d_middle = out_grad[0].astype(F32) + d_mid_part
    db_all = gather_rows(d_middle.astype(BF16))
    out_w_grad = t_mm(att, db_all)
    d_att = mm_t(db_all, w_out).astype(BF16)
    dq, dkv = attend_back(doc_starts, q_b, kv_b, att, inv, d_att)
    swap = [(i, i ^ 1) for i in range(n_wa)]
    dkv = dkv + lax.ppermute(dkv, "wa", swap)
    dq_raw, dk_raw, d_qgain, d_kgain = prep_back((dq * HD**-0.5, dkv[:, :HD] * HD**-0.5))
    d_kgain = jnp.where(even, d_kgain, 0.0)
    d_kv_own = jnp.where(even, dk_raw, dkv[:, HD:])
    w_kv_own = jnp.where(even, w_qkv[:, LANES : LANES + HD], w_qkv[:, LANES + HD :])
    d_qkv = jnp.concatenate([dq_raw, d_kv_own], axis=1).astype(BF16)
    d_n1 = scatter_rows(mm_t(d_qkv, jnp.concatenate([w_qkv[:, :LANES], w_kv_own], axis=1)).astype(BF16))
    qkv_grad = t_mm(n1_all, d_qkv)
    _, n1_back = jax.vjp(rms_norm, x_own, attn_gain32)
    d_x_part, d_attn_gain = n1_back(d_n1)
    input_grad = d_middle + d_x_part

    col_grads = jnp.concatenate([gu_grad, qkv_grad], axis=1).astype(BF16)
    row_grads = lax.all_to_all(col_grads, AXES, 0, 0, tiled=True).reshape(n, d_rows, -1)
    swap_dp = [(0, 1), (1, 0)]
    row_other = lax.ppermute(row_grads, "dp", swap_dp)
    row_grads = (row_grads.astype(F32) + row_other.astype(F32)).transpose(1, 0, 2)

    def both(part):
        return part + lax.ppermute(part.astype(BF16), "dp", swap_dp).astype(F32)

    def flat(part):
        return part.reshape(d_rows, -1)

    kv_grads = row_grads[:, :, 2 * ff_cols + LANES :].reshape(d_rows, KV, 2, HD)
    small = jnp.concatenate([d_attn_gain, d_ffn_gain, d_qgain, d_kgain])
    small = lax.psum(small, ("dp",) + AXES)

    def mine(total, begin, size):
        return lax.dynamic_slice_in_dim(total, begin + me * size, size)

    return (
        layer_out.astype(BF16)[None],
        input_grad.astype(BF16)[None],
        mine(small, 0, d_rows),
        flat(row_grads[:, :, 2 * ff_cols : 2 * ff_cols + LANES]),
        flat(kv_grads[:, :, 0]),
        flat(kv_grads[:, :, 1]),
        mine(small, 2 * width, per),
        mine(small, 2 * width + HD, per),
        both(out_w_grad),
        mine(small, width, d_rows),
        flat(row_grads[:, :, :ff_cols]),
        flat(row_grads[:, :, ff_cols : 2 * ff_cols]),
        both(down_grad),
    )


def solution(mesh):
    split = mesh.shape["ctx"] * mesh.shape["wa"]
    by_heads = 2 * split == H
    placed = (
        P("dp", ("ctx", "wa"), None),
        P("dp", None),
        P("dp", ("ctx", "wa"), None),
        P(("ctx", "wa")),
        P(("ctx", "wa"), None),
        P(("ctx", "wa"), None),
        P(("ctx", "wa"), None),
        P(("ctx", "wa")),
        P(("ctx", "wa")),
        P(("ctx", "wa"), None),
        P(("ctx", "wa")),
        P(("ctx", "wa"), None),
        P(("ctx", "wa"), None),
        P(("ctx", "wa"), None),
    )
    return jax.shard_map(
        per_device_heads if by_heads else per_device,
        mesh=mesh,
        in_specs=placed,
        out_specs=(
            P("dp", ("ctx", "wa"), None),
            P("dp", ("ctx", "wa"), None),
            P(("ctx", "wa")),
            P(("ctx", "wa"), None),
            P(("ctx", "wa"), None),
            P(("ctx", "wa"), None),
            P(("ctx", "wa")),
            P(("ctx", "wa")),
            P(("ctx", "wa"), None),
            P(("ctx", "wa")),
            P(("ctx", "wa"), None),
            P(("ctx", "wa"), None),
            P(("ctx", "wa"), None),
        ),
        check_vma=False,
    )
```

```python
from functools import partial

import jax
import jax.numpy as jnp
from jax import lax
from jax.experimental import pallas as pl
from jax.experimental.pallas import tpu as pltpu
from jax.sharding import PartitionSpec as P

H = 32
KV = 8
HD = 64
FF = 8192


EPS = 1e-05
THETA = 1000000.0


def stored_positions(index, tok_rows, n_ctx, n_wa):
    device = index // tok_rows
    local = index % tok_rows
    half_rows = tok_rows // 2
    ctx_part = device // n_wa
    wa_part = device % n_wa
    span_idx = jnp.where(local < half_rows, ctx_part, 2 * n_ctx - 1 - ctx_part)
    return span_idx * (half_rows * n_wa) + wa_part * half_rows + local % half_rows


def segments(position, starts):
    return jnp.sum((starts[None, :] <= position[:, None]).astype(jnp.int32), axis=1) - 1


def rms_norm(values, gain):
    return values * lax.rsqrt(jnp.mean(values * values, axis=-1, keepdims=True) + EPS) * gain


def rotate(values, position):
    half_dim = HD // 2
    frequency = THETA ** (-2.0 * jnp.arange(half_dim, dtype=jnp.float32) / HD)
    angles = position.astype(jnp.float32)[:, None] * frequency[None, :]
    cosine = jnp.cos(angles)[:, None, :]
    sine_part = jnp.sin(angles)[:, None, :]
    first_half = values[..., :half_dim]
    second_half = values[..., half_dim:]
    return jnp.concatenate(
        [
            first_half * cosine - second_half * sine_part,
            second_half * cosine + first_half * sine_part,
        ],
        axis=-1,
    )


def prepare(query_raw, key_raw, query_gain, key_gain, position):
    return (
        rotate(rms_norm(query_raw, query_gain), position),
        rotate(rms_norm(key_raw, key_gain), position),
    )


def per_device(
    tokens,
    doc_starts,
    out_grad,
    attn_gain,
    w_query,
    w_key,
    w_value,
    q_gain,
    k_gain,
    w_out,
    ffn_gain,
    w_gate,
    w_up,
    w_down,
):
    n_ctx = lax.axis_size("ctx")
    n_wa = lax.axis_size("wa")
    tok_rows = tokens.shape[1]
    stream_len = tok_rows * n_ctx * n_wa
    key_width = min(1024, stream_len)
    key_blocks = stream_len // key_width
    groups = H // KV
    scale = HD ** (-0.5)
    first_row = (lax.axis_index("ctx") * n_wa + lax.axis_index("wa")) * tok_rows
    own_pos = stored_positions(
        first_row + jnp.arange(tok_rows, dtype=jnp.int32), tok_rows, n_ctx, n_wa
    )
    starts = doc_starts[0]
    own_seg = segments(own_pos, starts)
    key_pos = stored_positions(jnp.arange(stream_len, dtype=jnp.int32), tok_rows, n_ctx, n_wa)
    key_seg = segments(key_pos, starts)
    residual = tokens[0].astype(jnp.float32)
    attn_set = (
        lax.all_gather(attn_gain, ("ctx", "wa"), axis=0, tiled=True),
        lax.all_gather(w_query, ("ctx", "wa"), axis=0, tiled=True),
        lax.all_gather(w_key, ("ctx", "wa"), axis=0, tiled=True),
        lax.all_gather(w_value, ("ctx", "wa"), axis=0, tiled=True),
        lax.all_gather(q_gain, ("ctx", "wa"), axis=0, tiled=True),
        lax.all_gather(k_gain, ("ctx", "wa"), axis=0, tiled=True),
        lax.all_gather(w_out, ("ctx", "wa"), axis=0, tiled=True),
    )
    g_attn, wq_full, wk_full, wv_full, gq_full, gk_full, wo_full = attn_set
    attn_gain32 = g_attn.astype(jnp.float32)
    qgain32 = gq_full.astype(jnp.float32)
    kgain32 = gk_full.astype(jnp.float32)
    normed_one = rms_norm(residual, attn_gain32).astype(jnp.bfloat16)
    query_raw = jnp.dot(normed_one, wq_full, preferred_element_type=jnp.float32).reshape(
        tok_rows, H, HD
    )
    key_raw = jnp.dot(normed_one, wk_full, preferred_element_type=jnp.float32).reshape(
        tok_rows, KV, HD
    )
    value_b = jnp.dot(normed_one, wv_full, preferred_element_type=jnp.float32).astype(jnp.bfloat16)
    query_rot, key_rot = prepare(query_raw, key_raw, qgain32, kgain32, own_pos)
    query_b = query_rot.astype(jnp.bfloat16).reshape(tok_rows, KV, groups, HD)
    key_b = key_rot.astype(jnp.bfloat16).reshape(tok_rows, KV * HD)
    all_keys, all_values = (
        lax.all_gather(key_b, ("ctx", "wa"), axis=0, tiled=True),
        lax.all_gather(value_b, ("ctx", "wa"), axis=0, tiled=True),
    )

    def key_block(keys_in, values_in, block_idx):
        begin = block_idx * key_width
        key_part = lax.dynamic_slice_in_dim(keys_in, begin, key_width, 0).reshape(key_width, KV, HD)
        value_part = lax.dynamic_slice_in_dim(values_in, begin, key_width, 0).reshape(
            key_width, KV, HD
        )
        pos_part = lax.dynamic_slice_in_dim(key_pos, begin, key_width, 0)
        seg_part = lax.dynamic_slice_in_dim(key_seg, begin, key_width, 0)
        scores = (
            jnp.einsum("rkgd,tkd->kgrt", query_b, key_part, preferred_element_type=jnp.float32)
            * scale
        )
        allowed = (
            (seg_part[None, :] == own_seg[:, None]) & (pos_part[None, :] <= own_pos[:, None])
        )[None, None]
        return (scores, allowed, key_part, value_part)

    def stat_step(block_idx, carry):
        row_max, row_total = carry
        scores, allowed, key_part, value_part = key_block(all_keys, all_values, block_idx)
        masked = jnp.where(allowed, scores, -1e30)
        new_max = jnp.maximum(row_max, jnp.max(masked, axis=-1))
        fresh = jnp.sum(jnp.where(allowed, jnp.exp(masked - new_max[..., None]), 0.0), axis=-1)
        return (new_max, row_total * jnp.exp(row_max - new_max) + fresh)

    stat_init = (
        jnp.full((KV, groups, tok_rows), -1e30, jnp.float32),
        jnp.zeros((KV, groups, tok_rows), jnp.float32),
    )
    row_max, row_total = lax.fori_loop(0, key_blocks, stat_step, stat_init)

    def out_step(block_idx, summed):
        scores, allowed, key_part, value_part = key_block(all_keys, all_values, block_idx)
        probability = (
            jnp.where(allowed, jnp.exp(scores - row_max[..., None]), 0.0) / row_total[..., None]
        )
        return summed + jnp.einsum(
            "kgrt,tkd->rkgd",
            probability.astype(jnp.bfloat16),
            value_part,
            preferred_element_type=jnp.float32,
        )

    attended = lax.fori_loop(
        0, key_blocks, out_step, jnp.zeros((tok_rows, KV, groups, HD), jnp.float32)
    )
    attended_b = attended.reshape(tok_rows, H * HD).astype(jnp.bfloat16)
    middle = residual + jnp.dot(attended_b, wo_full, preferred_element_type=jnp.float32)
    ffn_set = (
        lax.all_gather(ffn_gain, ("ctx", "wa"), axis=0, tiled=True),
        lax.all_gather(w_gate, ("ctx", "wa"), axis=0, tiled=True),
        lax.all_gather(w_up, ("ctx", "wa"), axis=0, tiled=True),
        lax.all_gather(w_down, ("ctx", "wa"), axis=0, tiled=True),
    )
    g_ffn, wg_full, wu_full, wd_full = ffn_set
    ffn_gain32 = g_ffn.astype(jnp.float32)
    normed_two = rms_norm(middle, ffn_gain32).astype(jnp.bfloat16)
    gate_act = jnp.dot(normed_two, wg_full, preferred_element_type=jnp.float32)
    up_act = jnp.dot(normed_two, wu_full, preferred_element_type=jnp.float32)
    sigmoid_gate = jax.nn.sigmoid(gate_act)
    silu_gate = gate_act * sigmoid_gate
    hidden = (silu_gate * up_act).astype(jnp.bfloat16)
    layer_out = (middle + jnp.dot(hidden, wd_full, preferred_element_type=jnp.float32)).astype(
        jnp.bfloat16
    )
    g_ffn, wg_full, wu_full, wd_full = (
        lax.all_gather(ffn_gain, ("ctx", "wa"), axis=0, tiled=True),
        lax.all_gather(w_gate, ("ctx", "wa"), axis=0, tiled=True),
        lax.all_gather(w_up, ("ctx", "wa"), axis=0, tiled=True),
        lax.all_gather(w_down, ("ctx", "wa"), axis=0, tiled=True),
    )
    d_out = out_grad[0].astype(jnp.float32)
    d_out_b = d_out.astype(jnp.bfloat16)
    d_hidden = jnp.einsum("rd,fd->rf", d_out_b, wd_full, preferred_element_type=jnp.float32)
    d_gate = (d_hidden * up_act * (sigmoid_gate * (1.0 + gate_act * (1.0 - sigmoid_gate)))).astype(
        jnp.bfloat16
    )
    d_up = (d_hidden * silu_gate).astype(jnp.bfloat16)
    d_normed_two = jnp.einsum(
        "rf,df->rd", d_gate, wg_full, preferred_element_type=jnp.float32
    ) + jnp.einsum("rf,df->rd", d_up, wu_full, preferred_element_type=jnp.float32)
    norm_out, norm_back = jax.vjp(rms_norm, middle, ffn_gain32)
    d_middle_part, d_ffn_gain = norm_back(d_normed_two)
    d_middle = d_out + d_middle_part
    gate_up = jnp.concatenate([d_gate, d_up], axis=1)
    part_rows = normed_two
    in_grad = lax.psum_scatter(
        jnp.einsum("rc,rf->cf", part_rows, gate_up, preferred_element_type=jnp.float32),
        ("ctx", "wa"),
        scatter_dimension=0,
        tiled=True,
    )
    part_rows = hidden
    down_grad = lax.psum_scatter(
        jnp.einsum("rc,rd->cd", part_rows, d_out_b, preferred_element_type=jnp.float32),
        ("ctx", "wa"),
        scatter_dimension=0,
        tiled=True,
    )
    g_attn, wq_full, wk_full, wv_full, gq_full, gk_full, wo_full = (
        lax.all_gather(attn_gain, ("ctx", "wa"), axis=0, tiled=True),
        lax.all_gather(w_query, ("ctx", "wa"), axis=0, tiled=True),
        lax.all_gather(w_key, ("ctx", "wa"), axis=0, tiled=True),
        lax.all_gather(w_value, ("ctx", "wa"), axis=0, tiled=True),
        lax.all_gather(q_gain, ("ctx", "wa"), axis=0, tiled=True),
        lax.all_gather(k_gain, ("ctx", "wa"), axis=0, tiled=True),
        lax.all_gather(w_out, ("ctx", "wa"), axis=0, tiled=True),
    )
    d_branch = d_middle.astype(jnp.bfloat16)
    wo_grad = jnp.einsum("re,rd->ed", attended_b, d_branch, preferred_element_type=jnp.float32)
    d_attended = jnp.einsum(
        "rd,ed->re", d_branch, wo_full, preferred_element_type=jnp.float32
    ).astype(jnp.bfloat16)
    d_att4 = d_attended.reshape(tok_rows, KV, groups, HD)
    delta = jnp.einsum("rkgd,rkgd->kgr", d_att4.astype(jnp.float32), attended)

    def back_step(d_query, block_idx):
        scores, allowed, key_part, value_part = key_block(all_keys, all_values, block_idx)
        probability = (
            jnp.where(allowed, jnp.exp(scores - row_max[..., None]), 0.0) / row_total[..., None]
        )
        d_prob = jnp.einsum(
            "rkgd,tkd->kgrt", d_att4, value_part, preferred_element_type=jnp.float32
        )
        d_scores = (probability * (d_prob - delta[..., None])).astype(jnp.bfloat16)
        d_query = (
            d_query
            + jnp.einsum("kgrt,tkd->rkgd", d_scores, key_part, preferred_element_type=jnp.float32)
            * scale
        )
        d_key_part = (
            jnp.einsum("kgrt,rkgd->tkd", d_scores, query_b, preferred_element_type=jnp.float32)
            * scale
        )
        d_value_part = jnp.einsum(
            "kgrt,rkgd->tkd",
            probability.astype(jnp.bfloat16),
            d_att4,
            preferred_element_type=jnp.float32,
        )
        return (
            d_query,
            (d_key_part.reshape(key_width, KV * HD), d_value_part.reshape(key_width, KV * HD)),
        )

    d_query, (d_keys, d_values) = lax.scan(
        back_step, jnp.zeros((tok_rows, KV, groups, HD), jnp.float32), jnp.arange(key_blocks)
    )
    d_key_own, d_value_own = (
        lax.psum_scatter(
            d_keys.reshape(stream_len, KV * HD), ("ctx", "wa"), scatter_dimension=0, tiled=True
        ),
        lax.psum_scatter(
            d_values.reshape(stream_len, KV * HD), ("ctx", "wa"), scatter_dimension=0, tiled=True
        ),
    )
    prep_out, prep_back = jax.vjp(
        partial(prepare, position=own_pos), query_raw, key_raw, qgain32, kgain32
    )
    d_query_raw, d_key_raw, d_qgain, d_kgain = prep_back(
        (d_query.reshape(tok_rows, H, HD), d_key_own.reshape(tok_rows, KV, HD))
    )
    dq_b = d_query_raw.reshape(tok_rows, H * HD).astype(jnp.bfloat16)
    dk_b = d_key_raw.reshape(tok_rows, KV * HD).astype(jnp.bfloat16)
    dv_b = d_value_own.astype(jnp.bfloat16)
    d_normed_one = (
        jnp.einsum("re,de->rd", dq_b, wq_full, preferred_element_type=jnp.float32)
        + jnp.einsum("re,de->rd", dk_b, wk_full, preferred_element_type=jnp.float32)
        + jnp.einsum("re,de->rd", dv_b, wv_full, preferred_element_type=jnp.float32)
    )
    first_out, first_back = jax.vjp(rms_norm, residual, attn_gain32)
    d_res_part, d_attn_gain = first_back(d_normed_one)
    input_grad = (d_middle + d_res_part).astype(jnp.bfloat16)
    wq_grad = jnp.einsum("rc,re->ce", normed_one, dq_b, preferred_element_type=jnp.float32)
    wk_grad = jnp.einsum("rc,re->ce", normed_one, dk_b, preferred_element_type=jnp.float32)
    wv_grad = jnp.einsum("rc,re->ce", normed_one, dv_b, preferred_element_type=jnp.float32)
    attn_terms = (d_attn_gain, wq_grad, wk_grad, wv_grad, d_qgain, d_kgain, d_ffn_gain, wo_grad)
    attn_shards = (
        lax.psum_scatter(attn_terms[0], ("ctx", "wa"), scatter_dimension=0, tiled=True),
        lax.psum_scatter(attn_terms[1], ("ctx", "wa"), scatter_dimension=0, tiled=True),
        lax.psum_scatter(attn_terms[2], ("ctx", "wa"), scatter_dimension=0, tiled=True),
        lax.psum_scatter(attn_terms[3], ("ctx", "wa"), scatter_dimension=0, tiled=True),
        lax.psum_scatter(attn_terms[4], ("ctx", "wa"), scatter_dimension=0, tiled=True),
        lax.psum_scatter(attn_terms[5], ("ctx", "wa"), scatter_dimension=0, tiled=True),
        lax.psum_scatter(attn_terms[6], ("ctx", "wa"), scatter_dimension=0, tiled=True),
        lax.psum_scatter(attn_terms[7], ("ctx", "wa"), scatter_dimension=0, tiled=True),
    )
    wo_shard = attn_shards[7]
    summed = (
        lax.psum(attn_shards[0].astype(jnp.bfloat16), "dp").astype(jnp.float32),
        lax.psum(attn_shards[1].astype(jnp.bfloat16), "dp").astype(jnp.float32),
        lax.psum(attn_shards[2].astype(jnp.bfloat16), "dp").astype(jnp.float32),
        lax.psum(attn_shards[3].astype(jnp.bfloat16), "dp").astype(jnp.float32),
        lax.psum(attn_shards[4].astype(jnp.bfloat16), "dp").astype(jnp.float32),
        lax.psum(attn_shards[5].astype(jnp.bfloat16), "dp").astype(jnp.float32),
        lax.psum(wo_shard.astype(jnp.bfloat16), "dp").astype(jnp.float32),
        lax.psum(attn_shards[6].astype(jnp.bfloat16), "dp").astype(jnp.float32),
        lax.psum(in_grad[:, :FF].astype(jnp.bfloat16), "dp").astype(jnp.float32),
        lax.psum(in_grad[:, FF:].astype(jnp.bfloat16), "dp").astype(jnp.float32),
        lax.psum(down_grad.astype(jnp.bfloat16), "dp").astype(jnp.float32),
    )
    return (layer_out[None], input_grad[None]) + tuple(summed)


AXES = ("ctx", "wa")
LANES = 2 * HD
ROWS_BLOCK = 256
LOG2E = 1.4426950408889634
F32 = jnp.float32
BF16 = jnp.bfloat16


def low_key(starts, row):
    first = jnp.int32(0)
    for doc in range(starts.shape[1]):
        begin = starts[0, doc]
        first = jnp.where(begin <= row, begin, first)
    return first


def block_mask(starts, q_begin, k_begin, bq, bk):
    row = q_begin + lax.broadcasted_iota(jnp.int32, (bq, 1), 0)
    first = low_key(starts, row)
    col = k_begin + lax.broadcasted_iota(jnp.int32, (1, bk), 1)
    return (col >= first) & (col <= row)


def attend_kernel(starts, q_ref, kv_ref, ov_ref, att_ref, inv_ref):
    block = pl.program_id(0)
    bq = q_ref.shape[0]
    q_begin = block * bq
    q = q_ref[...]
    zero = jnp.zeros((bq, HD), BF16)
    q2 = jnp.concatenate(
        [
            jnp.concatenate([q[:, :HD], zero], axis=1),
            jnp.concatenate([q[:, HD:], zero], axis=1),
        ],
        axis=0,
    )

    def step(j, acc):
        k_begin = pl.multiple_of(j * bq, bq)
        keys = kv_ref[pl.ds(k_begin, bq), :]
        s = lax.dot_general(q2, keys, (((1,), (1,)), ((), ())), preferred_element_type=F32)
        mask = block_mask(starts, q_begin, k_begin, bq, bq)
        p = jnp.exp2(s * (LOG2E * HD**-0.5))
        p = jnp.where(jnp.concatenate([mask, mask], axis=0), p, 0.0).astype(BF16)
        return acc + jnp.dot(p, ov_ref[pl.ds(k_begin, bq), :], preferred_element_type=F32)

    low = low_key(starts, q_begin) // bq
    acc = lax.fori_loop(low, block + 1, step, jnp.zeros((2 * bq, LANES), F32))
    inv = 1.0 / acc[:, :1]
    out = acc[:, HD:] * inv
    att_ref[...] = jnp.concatenate([out[:bq], out[bq:]], axis=1).astype(BF16)
    inv_ref[...] = jnp.concatenate(
        [jnp.broadcast_to(inv[:bq], (bq, HD)), jnp.broadcast_to(inv[bq:], (bq, HD))], axis=1
    )


def attend_back_kernel(starts, q_ref, kv_ref, att_ref, inv_ref, da_ref, dq_ref, dkv_ref):
    block = pl.program_id(0)
    bq = q_ref.shape[0]
    q_begin = block * bq

    @pl.when(block == 0)
    def _():
        dkv_ref[...] = jnp.zeros_like(dkv_ref)

    q = q_ref[...]
    da = da_ref[...]
    zero = jnp.zeros((bq, HD), BF16)
    q2 = jnp.concatenate(
        [
            jnp.concatenate([q[:, :HD], zero], axis=1),
            jnp.concatenate([q[:, HD:], zero], axis=1),
        ],
        axis=0,
    )
    da2 = jnp.concatenate(
        [
            jnp.concatenate([zero, da[:, :HD]], axis=1),
            jnp.concatenate([zero, da[:, HD:]], axis=1),
        ],
        axis=0,
    )
    prod = da.astype(F32) * att_ref[...].astype(F32)
    delta = jnp.concatenate(
        [
            jnp.sum(prod[:, :HD], axis=1, keepdims=True),
            jnp.sum(prod[:, HD:], axis=1, keepdims=True),
        ],
        axis=0,
    )
    inv_all = inv_ref[...]
    inv = jnp.concatenate([inv_all[:, :1], inv_all[:, HD : HD + 1]], axis=0)

    def step(j, dq):
        k_begin = pl.multiple_of(j * bq, bq)
        keys = kv_ref[pl.ds(k_begin, bq), :]
        s = lax.dot_general(q2, keys, (((1,), (1,)), ((), ())), preferred_element_type=F32)
        mask = block_mask(starts, q_begin, k_begin, bq, bq)
        p = jnp.exp2(s * (LOG2E * HD**-0.5)) * inv
        p = jnp.where(jnp.concatenate([mask, mask], axis=0), p, 0.0)
        dp = lax.dot_general(da2, keys, (((1,), (1,)), ((), ())), preferred_element_type=F32)
        ds = (p * (dp - delta)).astype(BF16)
        back = (((0,), (0,)), ((), ()))
        dkv_ref[pl.ds(k_begin, bq), :] += lax.dot_general(
            ds, q2, back, preferred_element_type=F32
        ) + lax.dot_general(p.astype(BF16), da2, back, preferred_element_type=F32)
        return dq + jnp.dot(ds, keys, preferred_element_type=F32)

    low = low_key(starts, q_begin) // bq
    dq = lax.fori_loop(low, block + 1, step, jnp.zeros((2 * bq, LANES), F32))
    dq_ref[...] = jnp.concatenate([dq[:bq, :HD], dq[bq:, :HD]], axis=1)


def attend(starts, q, kv, ov):
    stream = q.shape[0]
    bq = ROWS_BLOCK
    rows = pl.BlockSpec((bq, LANES), lambda i: (i, 0))
    whole = pl.BlockSpec((stream, LANES), lambda i: (0, 0))
    return pl.pallas_call(
        attend_kernel,
        grid=(stream // bq,),
        in_specs=[pl.BlockSpec(memory_space=pltpu.SMEM), rows, whole, whole],
        out_specs=[rows, rows],
        out_shape=[
            jax.ShapeDtypeStruct((stream, LANES), BF16),
            jax.ShapeDtypeStruct((stream, LANES), F32),
        ],
        compiler_params=pltpu.CompilerParams(vmem_limit_bytes=32 * 2**20),
        cost_estimate=pl.CostEstimate(
            flops=4 * stream * 1024 * LANES, bytes_accessed=6 * stream * LANES * 2, transcendentals=0
        ),
    )(starts, q, kv, ov)


def attend_back(starts, q, kv, att, inv, da):
    stream = q.shape[0]
    bq = ROWS_BLOCK
    rows = pl.BlockSpec((bq, LANES), lambda i: (i, 0))
    whole = pl.BlockSpec((stream, LANES), lambda i: (0, 0))
    return pl.pallas_call(
        attend_back_kernel,
        grid=(stream // bq,),
        in_specs=[pl.BlockSpec(memory_space=pltpu.SMEM), rows, whole, rows, rows, rows],
        out_specs=[rows, whole],
        out_shape=[
            jax.ShapeDtypeStruct((stream, LANES), F32),
            jax.ShapeDtypeStruct((stream, LANES), F32),
        ],
        compiler_params=pltpu.CompilerParams(vmem_limit_bytes=32 * 2**20),
        cost_estimate=pl.CostEstimate(
            flops=10 * stream * 1024 * LANES, bytes_accessed=8 * stream * LANES * 2, transcendentals=0
        ),
    )(starts, q, kv, att, inv, da)


def head_prepare(q_raw, k_raw, q_gain, k_gain, position):
    stream = q_raw.shape[0]
    q, k = prepare(
        q_raw.reshape(stream, 2, HD), k_raw.reshape(stream, 1, HD), q_gain, k_gain, position
    )
    return q.reshape(stream, LANES), k.reshape(stream, HD)


MESH_ID = pl.DeviceIdType.MESH


def meet_neighbours(ctx, wa, n_ctx):
    barrier = pltpu.get_barrier_semaphore()

    def greet(where):
        pl.semaphore_signal(barrier, inc=1, device_id=where, device_id_type=MESH_ID)

    greet({"wa": wa ^ 1})
    greet({"wa": wa ^ 2})
    pl.when(ctx > 0)(lambda: greet({"ctx": ctx - 1}))
    pl.when(ctx < n_ctx - 1)(lambda: greet({"ctx": ctx + 1}))
    ends = (ctx == 0).astype(jnp.int32) + (ctx == n_ctx - 1).astype(jnp.int32)
    pl.semaphore_wait(barrier, 4 - ends)


def piece_row(zc, wac, h, half, n_ctx, n_wa, by_position):
    if by_position:
        span = zc if h == 0 else 2 * n_ctx - 1 - zc
        return pl.multiple_of((span * n_wa + wac) * half, half)
    return pl.multiple_of(((zc * n_wa + wac) * 2 + h) * half, half)


def gather_kernel(n_ctx, n_wa, by_position, own_ref, out_ref, own_sem, send_sem, recv_sem):
    ctx = lax.axis_index("ctx")
    wa = lax.axis_index("wa")
    half = own_ref.shape[0] // 2
    meet_neighbours(ctx, wa, n_ctx)
    sends = []

    def place(zc, wac, h):
        return out_ref.at[pl.ds(piece_row(zc, wac, h, half, n_ctx, n_wa, by_position), half)]

    def copy(src, zc, wac, h, where):
        return pltpu.make_async_remote_copy(
            src_ref=src,
            dst_ref=place(zc, wac, h),
            send_sem=send_sem.at[len(sends)],
            recv_sem=recv_sem.at[(zc * n_wa + wac) * 2 + h],
            device_id=where,
            device_id_type=MESH_ID,
        )

    def send(cond, src, zc, wac, h, where):
        made = copy(src, zc, wac, h, where)
        if cond is None:
            made.start()
        else:
            pl.when(cond)(made.start)
        sends.append((cond, made))

    def arrived(cond, zc, wac, h):
        made = pltpu.make_async_remote_copy(
            src_ref=place(zc, wac, h),
            dst_ref=place(zc, wac, h),
            send_sem=send_sem.at[0],
            recv_sem=recv_sem.at[(zc * n_wa + wac) * 2 + h],
            device_id={"wa": wa ^ 1},
            device_id_type=MESH_ID,
        )
        if cond is None:
            made.wait_recv()
        else:
            pl.when(cond)(made.wait_recv)

    def inside(zc):
        return (zc >= 0) & (zc < n_ctx)

    own_copies = []
    for h in range(2):
        own = own_ref.at[pl.ds(h * half, half)]
        for way in (-1, 1):
            send(inside(ctx + way), own, ctx, wa, h, {"ctx": ctx + way})
        send(None, own, ctx, wa, h, {"wa": wa ^ 2})
        send(None, own, ctx, wa, h, {"wa": wa ^ 1})
        made = pltpu.make_async_copy(own, place(ctx, wa, h), own_sem.at[h])
        made.start()
        own_copies.append(made)

    def across(k, h):
        for way in (-1, 1) if k else (1,):
            zc = ctx + way * k
            cond = inside(zc) if k else None
            arrived(cond, zc, wa ^ 2, h)
            send(cond, place(zc, wa ^ 2, h), zc, wa ^ 2, h, {"wa": wa ^ 1})

    for k in range(1, n_ctx):
        for h in range(2):
            for way in (-1, 1):
                zc = ctx + way * k
                cond = inside(zc)
                arrived(cond, zc, wa, h)
                piece = place(zc, wa, h)
                send(cond & inside(ctx - way), piece, zc, wa, h, {"ctx": ctx - way})
                send(cond, piece, zc, wa, h, {"wa": wa ^ 2})
                send(cond, piece, zc, wa, h, {"wa": wa ^ 1})
            across(k - 1, h)
    for h in range(2):
        across(n_ctx - 1, h)
    for zc in range(n_ctx):
        for far in (0, 2):
            for h in range(2):
                arrived(None, zc, wa ^ 1 ^ far, h)
    for cond, made in sends:
        if cond is None:
            made.wait_send()
        else:
            pl.when(cond)(made.wait_send)
    for made in own_copies:
        made.wait()


def gather_tokens(own, n_ctx, n_wa, by_position, call_id):
    rows, width = own.shape
    n = n_ctx * n_wa
    return pl.pallas_call(
        partial(gather_kernel, n_ctx, n_wa, by_position),
        in_specs=[pl.BlockSpec(memory_space=pl.ANY)],
        out_specs=pl.BlockSpec(memory_space=pl.ANY),
        out_shape=jax.ShapeDtypeStruct((rows * n, width), own.dtype),
        scratch_shapes=[
            pltpu.SemaphoreType.DMA((2,)),
            pltpu.SemaphoreType.DMA((8 + 12 * (n_ctx - 1) + 2 * (2 * n_ctx - 1),)),
            pltpu.SemaphoreType.DMA((2 * n,)),
        ],
        compiler_params=pltpu.CompilerParams(collective_id=call_id, has_side_effects=True),
    )(own)


def scatter_kernel(
    n_ctx, n_wa, by_position, part_ref, out_ref, s1, s2, s3, send_sem, recv1, recv2, recv3
):
    ctx = lax.axis_index("ctx")
    wa = lax.axis_index("wa")
    half = out_ref.shape[0] // 2
    slab = 16
    y = wa // 2
    sibling, across = {"wa": wa ^ 1}, {"wa": wa ^ 2}
    meet_neighbours(ctx, wa, n_ctx)
    sends = []

    def begin(cond, act):
        if cond is None:
            act()
        else:
            pl.when(cond)(act)

    def mine(zc, wac, h):
        return part_ref.at[pl.ds(piece_row(zc, wac, h, half, n_ctx, n_wa, by_position), half)]

    def copy(src, dst, sem, where):
        made = pltpu.make_async_remote_copy(
            src_ref=src,
            dst_ref=dst,
            send_sem=send_sem.at[len(sends)],
            recv_sem=sem,
            device_id=where,
            device_id_type=MESH_ID,
        )
        return made

    def send(cond, src, dst, sem, where):
        made = copy(src, dst, sem, where)
        begin(cond, made.start)
        sends.append((cond, made))

    def arrived(cond, dst, sem):
        made = pltpu.make_async_remote_copy(
            src_ref=dst,
            dst_ref=dst,
            send_sem=send_sem.at[0],
            recv_sem=sem,
            device_id=sibling,
            device_id_type=MESH_ID,
        )
        begin(cond, made.wait_recv)

    def add_up(dst, dst_row, srcs):
        def step(i, carry):
            at = pl.multiple_of(i * slab, slab)
            total = srcs[0][pl.ds(at, slab), :].astype(F32)
            for src in srcs[1:]:
                total = total + src[pl.ds(at, slab), :].astype(F32)
            dst[pl.ds(pl.multiple_of(dst_row + at, slab), slab), :] = total.astype(dst.dtype)
            return carry

        lax.fori_loop(0, half // slab, step, 0)

    def inside(zc):
        return (zc >= 0) & (zc < n_ctx)

    def index1(zc, yc, h):
        return (zc * 2 + yc) * 2 + h

    def steps():
        for k in range(n_ctx - 1, -1, -1):
            for way in (-1, 1) if k else (1,):
                for h in range(2):
                    zc = ctx + way * k
                    yield k, way, h, zc, (inside(zc) if k else None)

    for other in (1, 0):
        yc = y ^ 1 if other else y
        for k, way, h, zc, cond in steps():
            at = index1(zc, yc, h)
            send(cond, mine(zc, yc * 2 + ((wa & 1) ^ 1), h), s1.at[at], recv1.at[at], sibling)
    for k, way, h, zc, cond in steps():
        at = index1(zc, y ^ 1, h)
        arrived(cond, s1.at[at], recv1.at[at])
        begin(cond, lambda: add_up(s1.at[at], 0, [s1.at[at], mine(zc, wa ^ 2, h)]))
        send(cond, s1.at[at], s2.at[zc * 2 + h], recv2.at[zc * 2 + h], across)
    for k, way, h, zc, cond in steps():
        at = index1(zc, y, h)
        arrived(cond, s1.at[at], recv1.at[at])
        arrived(cond, s2.at[zc * 2 + h], recv2.at[zc * 2 + h])
        base = [mine(zc, wa, h), s1.at[at], s2.at[zc * 2 + h]]
        here = zc * 2 + h
        low, high = here, (n_ctx + zc) * 2 + h
        if k:
            behind = low if way > 0 else high
            more = cond & inside(ctx - way)
            arrived(more, s3.at[behind], recv3.at[behind])
            begin(more, lambda: add_up(s2.at[here], 0, base + [s3.at[behind]]))
            first = cond & jnp.logical_not(inside(ctx - way))
            begin(first, lambda: add_up(s2.at[here], 0, base))
            send(cond, s2.at[here], s3.at[behind], recv3.at[behind], {"ctx": ctx + way})
        else:
            under, over = ctx > 0, ctx < n_ctx - 1
            arrived(under, s3.at[low], recv3.at[low])
            arrived(over, s3.at[high], recv3.at[high])
            ways = [
                (under & over, [s3.at[low], s3.at[high]]),
                (under & jnp.logical_not(over), [s3.at[low]]),
                (over & jnp.logical_not(under), [s3.at[high]]),
            ]
            for take, extra in ways:
                begin(take, lambda extra=extra: add_up(out_ref, h * half, base + extra))
    for cond, made in sends:
        begin(cond, made.wait_send)


def scatter_tokens(part, n_ctx, n_wa, by_position, call_id):
    n = n_ctx * n_wa
    rows, width = part.shape[0] // n, part.shape[1]
    half = rows // 2
    pieces = 2 * (2 * n_ctx - 1)
    return pl.pallas_call(
        partial(scatter_kernel, n_ctx, n_wa, by_position),
        in_specs=[pl.BlockSpec(memory_space=pltpu.VMEM)],
        out_specs=pl.BlockSpec(memory_space=pltpu.VMEM),
        out_shape=jax.ShapeDtypeStruct((rows, width), F32),
        scratch_shapes=[
            pltpu.VMEM((4 * n_ctx, half, width), BF16),
            pltpu.VMEM((2 * n_ctx, half, width), BF16),
            pltpu.VMEM((4 * n_ctx, half, width), BF16),
            pltpu.SemaphoreType.DMA((4 * pieces,)),
            pltpu.SemaphoreType.DMA((4 * n_ctx,)),
            pltpu.SemaphoreType.DMA((2 * n_ctx,)),
            pltpu.SemaphoreType.DMA((4 * n_ctx,)),
        ],
        compiler_params=pltpu.CompilerParams(
            collective_id=call_id, has_side_effects=True, vmem_limit_bytes=48 * 2**20
        ),
    )(part)


def per_device_heads(
    tokens,
    doc_starts,
    out_grad,
    attn_gain,
    w_query,
    w_key,
    w_value,
    q_gain,
    k_gain,
    w_out,
    ffn_gain,
    w_gate,
    w_up,
    w_down,
):
    n_ctx = lax.axis_size("ctx")
    n_wa = lax.axis_size("wa")
    n = n_ctx * n_wa
    even = lax.axis_index("wa") % 2 == 0
    tok_rows, width = tokens.shape[1:]
    d_rows = w_query.shape[0]
    stream = tok_rows * n
    ff_cols = FF // n
    per = HD // n
    extra = 16
    position = jnp.arange(stream, dtype=jnp.int32)
    swap_dp = [(0, 1), (1, 0)]

    def mm(a, b):
        return jnp.dot(a, b, preferred_element_type=F32)

    def mm_t(a, b):
        return lax.dot_general(a, b, (((1,), (1,)), ((), ())), preferred_element_type=F32)

    def t_mm(a, b):
        return lax.dot_general(a, b, (((0,), (0,)), ((), ())), preferred_element_type=F32)

    def pair(w):
        return jnp.repeat(w.reshape(d_rows, KV, 1, HD), n // KV, axis=2).reshape(d_rows, n, HD)

    def swap(blocks):
        return lax.all_to_all(blocks, AXES, 0, 0, tiled=True)

    gains_own = jnp.concatenate([attn_gain, ffn_gain, q_gain, k_gain])
    gains_row = jnp.pad(gains_own, (0, extra * 2 * LANES - gains_own.shape[0]))
    attn_cols = jnp.concatenate(
        [w_query.reshape(d_rows, n, LANES), pair(w_key), pair(w_value)], axis=2
    ).transpose(1, 0, 2)
    attn_cols = swap(
        jnp.concatenate(
            [
                attn_cols,
                jnp.broadcast_to(gains_row.reshape(1, extra, 2 * LANES), (n, extra, 2 * LANES)),
            ],
            axis=1,
        )
    )
    x_all = gather_tokens(tokens[0], n_ctx, n_wa, True, 1)
    w_qkv = attn_cols[:, :d_rows].reshape(width, 2 * LANES)
    gains = attn_cols[:, d_rows:].reshape(n, -1).astype(F32)
    attn_gain32 = gains[:, :d_rows].reshape(-1)
    ffn_gain32 = gains[:, d_rows : 2 * d_rows].reshape(-1)
    qgain32 = gains[:, 2 * d_rows : 2 * d_rows + per].reshape(-1)
    kgain32 = gains[:, 2 * d_rows + per : 2 * d_rows + 2 * per].reshape(-1)

    w_gate_b, w_up_b, dy_b, _ = lax.optimization_barrier((w_gate, w_up, out_grad[0], x_all))
    ff_blocks = jnp.concatenate(
        [w_gate_b.reshape(d_rows, n, ff_cols), w_up_b.reshape(d_rows, n, ff_cols)], axis=2
    ).transpose(1, 0, 2)
    w_gu = swap(ff_blocks).reshape(width, 2 * ff_cols)
    dy_all = lax.all_gather(dy_b, AXES, axis=0, tiled=True)

    x_own = tokens[0].astype(F32)
    n1_all = rms_norm(x_all.astype(F32), attn_gain32).astype(BF16)
    qkv = mm(n1_all, w_qkv)
    q_raw, k_raw, v_raw = qkv[:, :LANES], qkv[:, LANES : LANES + HD], qkv[:, LANES + HD :]
    v_b = v_raw.astype(BF16)
    (q_rot, k_rot), prep_back = jax.vjp(
        partial(head_prepare, position=position), q_raw, k_raw, qgain32, kgain32
    )
    q_b = q_rot.astype(BF16)
    kv_b = jnp.concatenate([k_rot.astype(BF16), v_b], axis=1)
    ov_b = jnp.concatenate([jnp.ones_like(v_b), v_b], axis=1)
    att, inv = attend(doc_starts, q_b, kv_b, ov_b)
    middle = x_own + scatter_tokens(mm(att, w_out).astype(BF16), n_ctx, n_wa, True, 3)
    n2_own, n2_back = jax.vjp(rms_norm, middle, ffn_gain32)
    n2_all = gather_tokens(n2_own.astype(BF16), n_ctx, n_wa, False, 2)
    gate_up = mm(n2_all, w_gu)
    gate, up = gate_up[:, :ff_cols], gate_up[:, ff_cols:]
    sig = jax.nn.sigmoid(gate)
    silu = gate * sig
    hidden = (silu * up).astype(BF16)
    down_part = mm(hidden, w_down).astype(BF16)
    down = lax.psum_scatter(down_part, AXES, scatter_dimension=0, tiled=True).astype(F32)
    layer_out = middle + down

    d_hidden = mm_t(dy_all, w_down)
    d_gu = jnp.concatenate(
        [d_hidden * up * (sig * (1.0 + gate * (1.0 - sig))), d_hidden * silu], axis=1
    ).astype(BF16)
    gu_grad = t_mm(n2_all, d_gu).astype(BF16)
    gu_rows = swap(gu_grad).reshape(n, d_rows, 2 * ff_cols)
    down_grad = t_mm(hidden, dy_all)
    d_n2 = scatter_tokens(mm_t(d_gu, w_gu).astype(BF16), n_ctx, n_wa, False, 4)
    d_mid_part, _ = n2_back(d_n2)
    d_middle = out_grad[0].astype(F32) + d_mid_part
    db_all = gather_tokens(d_middle.astype(BF16), n_ctx, n_wa, True, 1)
    out_w_grad = t_mm(att, db_all)
    d_att = mm_t(db_all, w_out).astype(BF16)
    dq, dkv = attend_back(doc_starts, q_b, kv_b, att, inv, d_att)
    dkv = dkv + lax.ppermute(dkv, "wa", [(i, i ^ 1) for i in range(n_wa)])
    dq_raw, dk_raw, d_qgain, d_kgain = prep_back((dq * HD**-0.5, dkv[:, :HD] * HD**-0.5))
    d_kgain = jnp.where(even, d_kgain, 0.0)
    d_kv_own = jnp.where(even, dk_raw, dkv[:, HD:])
    w_kv_own = jnp.where(even, w_qkv[:, LANES : LANES + HD], w_qkv[:, LANES + HD :])
    d_qkv = jnp.concatenate([dq_raw, d_kv_own], axis=1).astype(BF16)
    qkv_grad = t_mm(n1_all, d_qkv).astype(BF16)
    head_gains = jnp.concatenate([d_qgain, d_kgain])
    qkv_cols = LANES + HD
    head_row = jnp.pad(head_gains.astype(BF16), (0, extra * qkv_cols - LANES))
    qkv_rows = swap(
        jnp.concatenate(
            [
                qkv_grad.reshape(n, d_rows, qkv_cols),
                jnp.broadcast_to(head_row.reshape(1, extra, qkv_cols), (n, extra, qkv_cols)),
            ],
            axis=1,
        )
    )
    d_n1_part = mm_t(d_qkv, jnp.concatenate([w_qkv[:, :LANES], w_kv_own], axis=1)).astype(BF16)
    d_n1 = scatter_tokens(d_n1_part, n_ctx, n_wa, True, 3)
    _, n1_back = jax.vjp(rms_norm, x_own, attn_gain32)
    d_x_part, _ = n1_back(d_n1)
    input_grad = d_middle + d_x_part

    def both(part):
        part = part.astype(BF16)
        return part.astype(F32) + lax.ppermute(part, "dp", swap_dp).astype(F32)

    def flat(part):
        return part.transpose(1, 0, 2).reshape(d_rows, -1)

    gu_rows = both(gu_rows)
    gate_grad, up_grad = flat(gu_rows[:, :, :ff_cols]), flat(gu_rows[:, :, ff_cols:])
    qkv_rows = both(qkv_rows)
    q_grad = flat(qkv_rows[:, :d_rows, :LANES])
    kv_grad = qkv_rows[:, :d_rows, LANES:].reshape(KV, 2, d_rows, HD)
    k_grad, v_grad = flat(kv_grad[:, 0]), flat(kv_grad[:, 1])
    head_sums = jnp.sum(qkv_rows[:, d_rows:].reshape(n, -1)[:, :LANES], axis=0)
    me = lax.axis_index("ctx") * n_wa + lax.axis_index("wa")

    def row_sum(weight, grad):
        return jnp.sum(weight.astype(F32) * grad, axis=1)

    attn_gain_grad = (
        row_sum(w_query, q_grad) + row_sum(w_key, k_grad) + row_sum(w_value, v_grad)
    ) / attn_gain.astype(F32)
    ffn_gain_grad = (row_sum(w_gate, gate_grad) + row_sum(w_up, up_grad)) / ffn_gain.astype(F32)
    return (
        layer_out.astype(BF16)[None],
        input_grad.astype(BF16)[None],
        attn_gain_grad,
        q_grad,
        k_grad,
        v_grad,
        lax.dynamic_slice_in_dim(head_sums, me * per, per),
        lax.dynamic_slice_in_dim(head_sums, HD + me * per, per),
        both(out_w_grad),
        ffn_gain_grad,
        gate_grad,
        up_grad,
        both(down_grad),
    )


def solution(mesh):
    split = mesh.shape["ctx"] * mesh.shape["wa"]
    by_heads = 2 * split == H
    placed = (
        P("dp", ("ctx", "wa"), None),
        P("dp", None),
        P("dp", ("ctx", "wa"), None),
        P(("ctx", "wa")),
        P(("ctx", "wa"), None),
        P(("ctx", "wa"), None),
        P(("ctx", "wa"), None),
        P(("ctx", "wa")),
        P(("ctx", "wa")),
        P(("ctx", "wa"), None),
        P(("ctx", "wa")),
        P(("ctx", "wa"), None),
        P(("ctx", "wa"), None),
        P(("ctx", "wa"), None),
    )
    return jax.shard_map(
        per_device_heads if by_heads else per_device,
        mesh=mesh,
        in_specs=placed,
        out_specs=(
            P("dp", ("ctx", "wa"), None),
            P("dp", ("ctx", "wa"), None),
            P(("ctx", "wa")),
            P(("ctx", "wa"), None),
            P(("ctx", "wa"), None),
            P(("ctx", "wa"), None),
            P(("ctx", "wa")),
            P(("ctx", "wa")),
            P(("ctx", "wa"), None),
            P(("ctx", "wa")),
            P(("ctx", "wa"), None),
            P(("ctx", "wa"), None),
            P(("ctx", "wa"), None),
        ),
        check_vma=False,
    )
```

```python
from functools import partial

import jax
import jax.numpy as jnp
from jax import lax
from jax.experimental import pallas as pl
from jax.experimental.pallas import tpu as pltpu
from jax.sharding import PartitionSpec as P

H = 32
KV = 8
HD = 64
FF = 8192


EPS = 1e-05
THETA = 1000000.0


def stored_positions(index, tok_rows, n_ctx, n_wa):
    device = index // tok_rows
    local = index % tok_rows
    half_rows = tok_rows // 2
    ctx_part = device // n_wa
    wa_part = device % n_wa
    span_idx = jnp.where(local < half_rows, ctx_part, 2 * n_ctx - 1 - ctx_part)
    return span_idx * (half_rows * n_wa) + wa_part * half_rows + local % half_rows


def segments(position, starts):
    return jnp.sum((starts[None, :] <= position[:, None]).astype(jnp.int32), axis=1) - 1


def rms_norm(values, gain):
    return values * lax.rsqrt(jnp.mean(values * values, axis=-1, keepdims=True) + EPS) * gain


def rotate(values, position):
    half_dim = HD // 2
    frequency = THETA ** (-2.0 * jnp.arange(half_dim, dtype=jnp.float32) / HD)
    angles = position.astype(jnp.float32)[:, None] * frequency[None, :]
    cosine = jnp.cos(angles)[:, None, :]
    sine_part = jnp.sin(angles)[:, None, :]
    first_half = values[..., :half_dim]
    second_half = values[..., half_dim:]
    return jnp.concatenate(
        [
            first_half * cosine - second_half * sine_part,
            second_half * cosine + first_half * sine_part,
        ],
        axis=-1,
    )


def prepare(query_raw, key_raw, query_gain, key_gain, position):
    return (
        rotate(rms_norm(query_raw, query_gain), position),
        rotate(rms_norm(key_raw, key_gain), position),
    )


def per_device(
    tokens,
    doc_starts,
    out_grad,
    attn_gain,
    w_query,
    w_key,
    w_value,
    q_gain,
    k_gain,
    w_out,
    ffn_gain,
    w_gate,
    w_up,
    w_down,
):
    n_ctx = lax.axis_size("ctx")
    n_wa = lax.axis_size("wa")
    tok_rows = tokens.shape[1]
    stream_len = tok_rows * n_ctx * n_wa
    key_width = min(1024, stream_len)
    key_blocks = stream_len // key_width
    groups = H // KV
    scale = HD ** (-0.5)
    first_row = (lax.axis_index("ctx") * n_wa + lax.axis_index("wa")) * tok_rows
    own_pos = stored_positions(
        first_row + jnp.arange(tok_rows, dtype=jnp.int32), tok_rows, n_ctx, n_wa
    )
    starts = doc_starts[0]
    own_seg = segments(own_pos, starts)
    key_pos = stored_positions(jnp.arange(stream_len, dtype=jnp.int32), tok_rows, n_ctx, n_wa)
    key_seg = segments(key_pos, starts)
    residual = tokens[0].astype(jnp.float32)
    attn_set = (
        lax.all_gather(attn_gain, ("ctx", "wa"), axis=0, tiled=True),
        lax.all_gather(w_query, ("ctx", "wa"), axis=0, tiled=True),
        lax.all_gather(w_key, ("ctx", "wa"), axis=0, tiled=True),
        lax.all_gather(w_value, ("ctx", "wa"), axis=0, tiled=True),
        lax.all_gather(q_gain, ("ctx", "wa"), axis=0, tiled=True),
        lax.all_gather(k_gain, ("ctx", "wa"), axis=0, tiled=True),
        lax.all_gather(w_out, ("ctx", "wa"), axis=0, tiled=True),
    )
    g_attn, wq_full, wk_full, wv_full, gq_full, gk_full, wo_full = attn_set
    attn_gain32 = g_attn.astype(jnp.float32)
    qgain32 = gq_full.astype(jnp.float32)
    kgain32 = gk_full.astype(jnp.float32)
    normed_one = rms_norm(residual, attn_gain32).astype(jnp.bfloat16)
    query_raw = jnp.dot(normed_one, wq_full, preferred_element_type=jnp.float32).reshape(
        tok_rows, H, HD
    )
    key_raw = jnp.dot(normed_one, wk_full, preferred_element_type=jnp.float32).reshape(
        tok_rows, KV, HD
    )
    value_b = jnp.dot(normed_one, wv_full, preferred_element_type=jnp.float32).astype(jnp.bfloat16)
    query_rot, key_rot = prepare(query_raw, key_raw, qgain32, kgain32, own_pos)
    query_b = query_rot.astype(jnp.bfloat16).reshape(tok_rows, KV, groups, HD)
    key_b = key_rot.astype(jnp.bfloat16).reshape(tok_rows, KV * HD)
    all_keys, all_values = (
        lax.all_gather(key_b, ("ctx", "wa"), axis=0, tiled=True),
        lax.all_gather(value_b, ("ctx", "wa"), axis=0, tiled=True),
    )

    def key_block(keys_in, values_in, block_idx):
        begin = block_idx * key_width
        key_part = lax.dynamic_slice_in_dim(keys_in, begin, key_width, 0).reshape(key_width, KV, HD)
        value_part = lax.dynamic_slice_in_dim(values_in, begin, key_width, 0).reshape(
            key_width, KV, HD
        )
        pos_part = lax.dynamic_slice_in_dim(key_pos, begin, key_width, 0)
        seg_part = lax.dynamic_slice_in_dim(key_seg, begin, key_width, 0)
        scores = (
            jnp.einsum("rkgd,tkd->kgrt", query_b, key_part, preferred_element_type=jnp.float32)
            * scale
        )
        allowed = (
            (seg_part[None, :] == own_seg[:, None]) & (pos_part[None, :] <= own_pos[:, None])
        )[None, None]
        return (scores, allowed, key_part, value_part)

    def stat_step(block_idx, carry):
        row_max, row_total = carry
        scores, allowed, key_part, value_part = key_block(all_keys, all_values, block_idx)
        masked = jnp.where(allowed, scores, -1e30)
        new_max = jnp.maximum(row_max, jnp.max(masked, axis=-1))
        fresh = jnp.sum(jnp.where(allowed, jnp.exp(masked - new_max[..., None]), 0.0), axis=-1)
        return (new_max, row_total * jnp.exp(row_max - new_max) + fresh)

    stat_init = (
        jnp.full((KV, groups, tok_rows), -1e30, jnp.float32),
        jnp.zeros((KV, groups, tok_rows), jnp.float32),
    )
    row_max, row_total = lax.fori_loop(0, key_blocks, stat_step, stat_init)

    def out_step(block_idx, summed):
        scores, allowed, key_part, value_part = key_block(all_keys, all_values, block_idx)
        probability = (
            jnp.where(allowed, jnp.exp(scores - row_max[..., None]), 0.0) / row_total[..., None]
        )
        return summed + jnp.einsum(
            "kgrt,tkd->rkgd",
            probability.astype(jnp.bfloat16),
            value_part,
            preferred_element_type=jnp.float32,
        )

    attended = lax.fori_loop(
        0, key_blocks, out_step, jnp.zeros((tok_rows, KV, groups, HD), jnp.float32)
    )
    attended_b = attended.reshape(tok_rows, H * HD).astype(jnp.bfloat16)
    middle = residual + jnp.dot(attended_b, wo_full, preferred_element_type=jnp.float32)
    ffn_set = (
        lax.all_gather(ffn_gain, ("ctx", "wa"), axis=0, tiled=True),
        lax.all_gather(w_gate, ("ctx", "wa"), axis=0, tiled=True),
        lax.all_gather(w_up, ("ctx", "wa"), axis=0, tiled=True),
        lax.all_gather(w_down, ("ctx", "wa"), axis=0, tiled=True),
    )
    g_ffn, wg_full, wu_full, wd_full = ffn_set
    ffn_gain32 = g_ffn.astype(jnp.float32)
    normed_two = rms_norm(middle, ffn_gain32).astype(jnp.bfloat16)
    gate_act = jnp.dot(normed_two, wg_full, preferred_element_type=jnp.float32)
    up_act = jnp.dot(normed_two, wu_full, preferred_element_type=jnp.float32)
    sigmoid_gate = jax.nn.sigmoid(gate_act)
    silu_gate = gate_act * sigmoid_gate
    hidden = (silu_gate * up_act).astype(jnp.bfloat16)
    layer_out = (middle + jnp.dot(hidden, wd_full, preferred_element_type=jnp.float32)).astype(
        jnp.bfloat16
    )
    g_ffn, wg_full, wu_full, wd_full = (
        lax.all_gather(ffn_gain, ("ctx", "wa"), axis=0, tiled=True),
        lax.all_gather(w_gate, ("ctx", "wa"), axis=0, tiled=True),
        lax.all_gather(w_up, ("ctx", "wa"), axis=0, tiled=True),
        lax.all_gather(w_down, ("ctx", "wa"), axis=0, tiled=True),
    )
    d_out = out_grad[0].astype(jnp.float32)
    d_out_b = d_out.astype(jnp.bfloat16)
    d_hidden = jnp.einsum("rd,fd->rf", d_out_b, wd_full, preferred_element_type=jnp.float32)
    d_gate = (d_hidden * up_act * (sigmoid_gate * (1.0 + gate_act * (1.0 - sigmoid_gate)))).astype(
        jnp.bfloat16
    )
    d_up = (d_hidden * silu_gate).astype(jnp.bfloat16)
    d_normed_two = jnp.einsum(
        "rf,df->rd", d_gate, wg_full, preferred_element_type=jnp.float32
    ) + jnp.einsum("rf,df->rd", d_up, wu_full, preferred_element_type=jnp.float32)
    norm_out, norm_back = jax.vjp(rms_norm, middle, ffn_gain32)
    d_middle_part, d_ffn_gain = norm_back(d_normed_two)
    d_middle = d_out + d_middle_part
    gate_up = jnp.concatenate([d_gate, d_up], axis=1)
    part_rows = normed_two
    in_grad = lax.psum_scatter(
        jnp.einsum("rc,rf->cf", part_rows, gate_up, preferred_element_type=jnp.float32),
        ("ctx", "wa"),
        scatter_dimension=0,
        tiled=True,
    )
    part_rows = hidden
    down_grad = lax.psum_scatter(
        jnp.einsum("rc,rd->cd", part_rows, d_out_b, preferred_element_type=jnp.float32),
        ("ctx", "wa"),
        scatter_dimension=0,
        tiled=True,
    )
    g_attn, wq_full, wk_full, wv_full, gq_full, gk_full, wo_full = (
        lax.all_gather(attn_gain, ("ctx", "wa"), axis=0, tiled=True),
        lax.all_gather(w_query, ("ctx", "wa"), axis=0, tiled=True),
        lax.all_gather(w_key, ("ctx", "wa"), axis=0, tiled=True),
        lax.all_gather(w_value, ("ctx", "wa"), axis=0, tiled=True),
        lax.all_gather(q_gain, ("ctx", "wa"), axis=0, tiled=True),
        lax.all_gather(k_gain, ("ctx", "wa"), axis=0, tiled=True),
        lax.all_gather(w_out, ("ctx", "wa"), axis=0, tiled=True),
    )
    d_branch = d_middle.astype(jnp.bfloat16)
    wo_grad = jnp.einsum("re,rd->ed", attended_b, d_branch, preferred_element_type=jnp.float32)
    d_attended = jnp.einsum(
        "rd,ed->re", d_branch, wo_full, preferred_element_type=jnp.float32
    ).astype(jnp.bfloat16)
    d_att4 = d_attended.reshape(tok_rows, KV, groups, HD)
    delta = jnp.einsum("rkgd,rkgd->kgr", d_att4.astype(jnp.float32), attended)

    def back_step(d_query, block_idx):
        scores, allowed, key_part, value_part = key_block(all_keys, all_values, block_idx)
        probability = (
            jnp.where(allowed, jnp.exp(scores - row_max[..., None]), 0.0) / row_total[..., None]
        )
        d_prob = jnp.einsum(
            "rkgd,tkd->kgrt", d_att4, value_part, preferred_element_type=jnp.float32
        )
        d_scores = (probability * (d_prob - delta[..., None])).astype(jnp.bfloat16)
        d_query = (
            d_query
            + jnp.einsum("kgrt,tkd->rkgd", d_scores, key_part, preferred_element_type=jnp.float32)
            * scale
        )
        d_key_part = (
            jnp.einsum("kgrt,rkgd->tkd", d_scores, query_b, preferred_element_type=jnp.float32)
            * scale
        )
        d_value_part = jnp.einsum(
            "kgrt,rkgd->tkd",
            probability.astype(jnp.bfloat16),
            d_att4,
            preferred_element_type=jnp.float32,
        )
        return (
            d_query,
            (d_key_part.reshape(key_width, KV * HD), d_value_part.reshape(key_width, KV * HD)),
        )

    d_query, (d_keys, d_values) = lax.scan(
        back_step, jnp.zeros((tok_rows, KV, groups, HD), jnp.float32), jnp.arange(key_blocks)
    )
    d_key_own, d_value_own = (
        lax.psum_scatter(
            d_keys.reshape(stream_len, KV * HD), ("ctx", "wa"), scatter_dimension=0, tiled=True
        ),
        lax.psum_scatter(
            d_values.reshape(stream_len, KV * HD), ("ctx", "wa"), scatter_dimension=0, tiled=True
        ),
    )
    prep_out, prep_back = jax.vjp(
        partial(prepare, position=own_pos), query_raw, key_raw, qgain32, kgain32
    )
    d_query_raw, d_key_raw, d_qgain, d_kgain = prep_back(
        (d_query.reshape(tok_rows, H, HD), d_key_own.reshape(tok_rows, KV, HD))
    )
    dq_b = d_query_raw.reshape(tok_rows, H * HD).astype(jnp.bfloat16)
    dk_b = d_key_raw.reshape(tok_rows, KV * HD).astype(jnp.bfloat16)
    dv_b = d_value_own.astype(jnp.bfloat16)
    d_normed_one = (
        jnp.einsum("re,de->rd", dq_b, wq_full, preferred_element_type=jnp.float32)
        + jnp.einsum("re,de->rd", dk_b, wk_full, preferred_element_type=jnp.float32)
        + jnp.einsum("re,de->rd", dv_b, wv_full, preferred_element_type=jnp.float32)
    )
    first_out, first_back = jax.vjp(rms_norm, residual, attn_gain32)
    d_res_part, d_attn_gain = first_back(d_normed_one)
    input_grad = (d_middle + d_res_part).astype(jnp.bfloat16)
    wq_grad = jnp.einsum("rc,re->ce", normed_one, dq_b, preferred_element_type=jnp.float32)
    wk_grad = jnp.einsum("rc,re->ce", normed_one, dk_b, preferred_element_type=jnp.float32)
    wv_grad = jnp.einsum("rc,re->ce", normed_one, dv_b, preferred_element_type=jnp.float32)
    attn_terms = (d_attn_gain, wq_grad, wk_grad, wv_grad, d_qgain, d_kgain, d_ffn_gain, wo_grad)
    attn_shards = (
        lax.psum_scatter(attn_terms[0], ("ctx", "wa"), scatter_dimension=0, tiled=True),
        lax.psum_scatter(attn_terms[1], ("ctx", "wa"), scatter_dimension=0, tiled=True),
        lax.psum_scatter(attn_terms[2], ("ctx", "wa"), scatter_dimension=0, tiled=True),
        lax.psum_scatter(attn_terms[3], ("ctx", "wa"), scatter_dimension=0, tiled=True),
        lax.psum_scatter(attn_terms[4], ("ctx", "wa"), scatter_dimension=0, tiled=True),
        lax.psum_scatter(attn_terms[5], ("ctx", "wa"), scatter_dimension=0, tiled=True),
        lax.psum_scatter(attn_terms[6], ("ctx", "wa"), scatter_dimension=0, tiled=True),
        lax.psum_scatter(attn_terms[7], ("ctx", "wa"), scatter_dimension=0, tiled=True),
    )
    wo_shard = attn_shards[7]
    summed = (
        lax.psum(attn_shards[0].astype(jnp.bfloat16), "dp").astype(jnp.float32),
        lax.psum(attn_shards[1].astype(jnp.bfloat16), "dp").astype(jnp.float32),
        lax.psum(attn_shards[2].astype(jnp.bfloat16), "dp").astype(jnp.float32),
        lax.psum(attn_shards[3].astype(jnp.bfloat16), "dp").astype(jnp.float32),
        lax.psum(attn_shards[4].astype(jnp.bfloat16), "dp").astype(jnp.float32),
        lax.psum(attn_shards[5].astype(jnp.bfloat16), "dp").astype(jnp.float32),
        lax.psum(wo_shard.astype(jnp.bfloat16), "dp").astype(jnp.float32),
        lax.psum(attn_shards[6].astype(jnp.bfloat16), "dp").astype(jnp.float32),
        lax.psum(in_grad[:, :FF].astype(jnp.bfloat16), "dp").astype(jnp.float32),
        lax.psum(in_grad[:, FF:].astype(jnp.bfloat16), "dp").astype(jnp.float32),
        lax.psum(down_grad.astype(jnp.bfloat16), "dp").astype(jnp.float32),
    )
    return (layer_out[None], input_grad[None]) + tuple(summed)


AXES = ("ctx", "wa")
LANES = 2 * HD
ROWS_BLOCK = 256
LOG2E = 1.4426950408889634
F32 = jnp.float32
BF16 = jnp.bfloat16


def low_key(starts, row):
    first = jnp.int32(0)
    for doc in range(starts.shape[1]):
        begin = starts[0, doc]
        first = jnp.where(begin <= row, begin, first)
    return first


def block_mask(starts, q_begin, k_begin, bq, bk):
    row = q_begin + lax.broadcasted_iota(jnp.int32, (bq, 1), 0)
    first = low_key(starts, row)
    col = k_begin + lax.broadcasted_iota(jnp.int32, (1, bk), 1)
    return (col >= first) & (col <= row)


def attend_kernel(starts, q_ref, kv_ref, ov_ref, att_ref, inv_ref):
    block = pl.program_id(0)
    bq = q_ref.shape[0]
    q_begin = block * bq
    q = q_ref[...]
    zero = jnp.zeros((bq, HD), BF16)
    q2 = jnp.concatenate(
        [
            jnp.concatenate([q[:, :HD], zero], axis=1),
            jnp.concatenate([q[:, HD:], zero], axis=1),
        ],
        axis=0,
    )

    def step(j, acc):
        k_begin = pl.multiple_of(j * bq, bq)
        keys = kv_ref[pl.ds(k_begin, bq), :]
        s = lax.dot_general(q2, keys, (((1,), (1,)), ((), ())), preferred_element_type=F32)
        mask = block_mask(starts, q_begin, k_begin, bq, bq)
        p = jnp.exp2(s * (LOG2E * HD**-0.5))
        p = jnp.where(jnp.concatenate([mask, mask], axis=0), p, 0.0).astype(BF16)
        return acc + jnp.dot(p, ov_ref[pl.ds(k_begin, bq), :], preferred_element_type=F32)

    low = low_key(starts, q_begin) // bq
    acc = lax.fori_loop(low, block + 1, step, jnp.zeros((2 * bq, LANES), F32))
    inv = 1.0 / acc[:, :1]
    out = acc[:, HD:] * inv
    att_ref[...] = jnp.concatenate([out[:bq], out[bq:]], axis=1).astype(BF16)
    inv_ref[...] = jnp.concatenate(
        [jnp.broadcast_to(inv[:bq], (bq, HD)), jnp.broadcast_to(inv[bq:], (bq, HD))], axis=1
    )


def attend_back_kernel(starts, q_ref, kv_ref, att_ref, inv_ref, da_ref, dq_ref, dkv_ref):
    block = pl.program_id(0)
    bq = q_ref.shape[0]
    q_begin = block * bq

    @pl.when(block == 0)
    def _():
        dkv_ref[...] = jnp.zeros_like(dkv_ref)

    q = q_ref[...]
    da = da_ref[...]
    zero = jnp.zeros((bq, HD), BF16)
    q2 = jnp.concatenate(
        [
            jnp.concatenate([q[:, :HD], zero], axis=1),
            jnp.concatenate([q[:, HD:], zero], axis=1),
        ],
        axis=0,
    )
    da2 = jnp.concatenate(
        [
            jnp.concatenate([zero, da[:, :HD]], axis=1),
            jnp.concatenate([zero, da[:, HD:]], axis=1),
        ],
        axis=0,
    )
    prod = da.astype(F32) * att_ref[...].astype(F32)
    delta = jnp.concatenate(
        [
            jnp.sum(prod[:, :HD], axis=1, keepdims=True),
            jnp.sum(prod[:, HD:], axis=1, keepdims=True),
        ],
        axis=0,
    )
    inv_all = inv_ref[...]
    inv = jnp.concatenate([inv_all[:, :1], inv_all[:, HD : HD + 1]], axis=0)

    def step(j, dq):
        k_begin = pl.multiple_of(j * bq, bq)
        keys = kv_ref[pl.ds(k_begin, bq), :]
        s = lax.dot_general(q2, keys, (((1,), (1,)), ((), ())), preferred_element_type=F32)
        mask = block_mask(starts, q_begin, k_begin, bq, bq)
        p = jnp.exp2(s * (LOG2E * HD**-0.5)) * inv
        p = jnp.where(jnp.concatenate([mask, mask], axis=0), p, 0.0)
        dp = lax.dot_general(da2, keys, (((1,), (1,)), ((), ())), preferred_element_type=F32)
        ds = (p * (dp - delta)).astype(BF16)
        back = (((0,), (0,)), ((), ()))
        dkv_ref[pl.ds(k_begin, bq), :] += lax.dot_general(
            ds, q2, back, preferred_element_type=F32
        ) + lax.dot_general(p.astype(BF16), da2, back, preferred_element_type=F32)
        return dq + jnp.dot(ds, keys, preferred_element_type=F32)

    low = low_key(starts, q_begin) // bq
    dq = lax.fori_loop(low, block + 1, step, jnp.zeros((2 * bq, LANES), F32))
    dq_ref[...] = jnp.concatenate([dq[:bq, :HD], dq[bq:, :HD]], axis=1)


def attend(starts, q, kv, ov):
    stream = q.shape[0]
    bq = ROWS_BLOCK
    rows = pl.BlockSpec((bq, LANES), lambda i: (i, 0))
    whole = pl.BlockSpec((stream, LANES), lambda i: (0, 0))
    return pl.pallas_call(
        attend_kernel,
        grid=(stream // bq,),
        in_specs=[pl.BlockSpec(memory_space=pltpu.SMEM), rows, whole, whole],
        out_specs=[rows, rows],
        out_shape=[
            jax.ShapeDtypeStruct((stream, LANES), BF16),
            jax.ShapeDtypeStruct((stream, LANES), F32),
        ],
        compiler_params=pltpu.CompilerParams(vmem_limit_bytes=32 * 2**20),
        cost_estimate=pl.CostEstimate(
            flops=4 * stream * 1024 * LANES, bytes_accessed=6 * stream * LANES * 2, transcendentals=0
        ),
    )(starts, q, kv, ov)


def attend_back(starts, q, kv, att, inv, da):
    stream = q.shape[0]
    bq = ROWS_BLOCK
    rows = pl.BlockSpec((bq, LANES), lambda i: (i, 0))
    whole = pl.BlockSpec((stream, LANES), lambda i: (0, 0))
    return pl.pallas_call(
        attend_back_kernel,
        grid=(stream // bq,),
        in_specs=[pl.BlockSpec(memory_space=pltpu.SMEM), rows, whole, rows, rows, rows],
        out_specs=[rows, whole],
        out_shape=[
            jax.ShapeDtypeStruct((stream, LANES), F32),
            jax.ShapeDtypeStruct((stream, LANES), F32),
        ],
        compiler_params=pltpu.CompilerParams(vmem_limit_bytes=32 * 2**20),
        cost_estimate=pl.CostEstimate(
            flops=10 * stream * 1024 * LANES, bytes_accessed=8 * stream * LANES * 2, transcendentals=0
        ),
    )(starts, q, kv, att, inv, da)


def pack_attn_kernel(query_ref, key_ref, value_ref, gains_ref, out_ref):
    n, rows, _ = out_ref.shape
    d_rows = query_ref.shape[0]
    share = n // KV
    for j in range(n):
        head = j // share * HD
        out_ref[j, :d_rows, :LANES] = query_ref[:, j * LANES : (j + 1) * LANES]
        out_ref[j, :d_rows, LANES:] = jnp.concatenate(
            [key_ref[:, head : head + HD], value_ref[:, head : head + HD]], axis=1
        )
        out_ref[j, d_rows:, :] = gains_ref[...]


def pack_attn(w_query, w_key, w_value, gains, n):
    d_rows = w_query.shape[0]
    return pl.pallas_call(
        pack_attn_kernel,
        out_shape=jax.ShapeDtypeStruct((n, d_rows + gains.shape[0], 2 * LANES), BF16),
    )(w_query, w_key, w_value, gains)


def pack_pair_kernel(gate_ref, up_ref, out_ref):
    cols = gate_ref.shape[1]
    out_ref[0, :, :cols] = gate_ref[...]
    out_ref[0, :, cols:] = up_ref[...]


def pack_pair(w_gate, w_up, n):
    d_rows, cols = w_gate.shape[0], w_gate.shape[1] // n
    part = pl.BlockSpec((d_rows, cols), lambda j: (0, j))
    return pl.pallas_call(
        pack_pair_kernel,
        grid=(n,),
        in_specs=[part, part],
        out_specs=pl.BlockSpec((1, d_rows, 2 * cols), lambda j: (j, 0, 0)),
        out_shape=jax.ShapeDtypeStruct((n, d_rows, 2 * cols), BF16),
    )(w_gate, w_up)


def unpack_pair_kernel(own_ref, other_ref, gate_w, up_w, gate_ref, up_ref, sum_ref):
    first = lax.axis_index("dp") == 0
    own, other = own_ref[0].astype(F32), other_ref[0].astype(F32)
    grads = jnp.concatenate(
        [jnp.where(first, own, other), jnp.where(first, other, own)], axis=0
    )
    cols = gate_ref.shape[1]
    gate, up = grads[:, :cols], grads[:, cols:]
    gate_ref[...] = gate
    up_ref[...] = up
    total = gate * gate_w[...].astype(F32) + up * up_w[...].astype(F32)

    @pl.when(pl.program_id(0) == 0)
    def _():
        sum_ref[...] = jnp.zeros_like(sum_ref)

    sum_ref[...] += jnp.broadcast_to(jnp.sum(total, axis=1, keepdims=True), sum_ref.shape)


def unpack_pair(own, other, w_gate, w_up):
    n, half, both_cols = own.shape
    cols = both_cols // 2
    block = pl.BlockSpec((1, half, both_cols), lambda j: (j, 0, 0))
    part = pl.BlockSpec((2 * half, cols), lambda j: (0, j))
    return pl.pallas_call(
        unpack_pair_kernel,
        grid=(n,),
        in_specs=[block, block, part, part],
        out_specs=[part, part, pl.BlockSpec((2 * half, 128), lambda j: (0, 0))],
        out_shape=[
            jax.ShapeDtypeStruct(w_gate.shape, F32),
            jax.ShapeDtypeStruct(w_up.shape, F32),
            jax.ShapeDtypeStruct((2 * half, 128), F32),
        ],
    )(own, other, w_gate, w_up)


def head_prepare(q_raw, k_raw, q_gain, k_gain, position):
    stream = q_raw.shape[0]
    q, k = prepare(
        q_raw.reshape(stream, 2, HD), k_raw.reshape(stream, 1, HD), q_gain, k_gain, position
    )
    return q.reshape(stream, LANES), k.reshape(stream, HD)


MESH_ID = pl.DeviceIdType.MESH
LINK_COST = pl.CostEstimate(flops=5 * 10**10, bytes_accessed=2**24, transcendentals=0)


def meet_neighbours(ctx, wa, n_ctx):
    barrier = pltpu.get_barrier_semaphore()

    def greet(where):
        pl.semaphore_signal(barrier, inc=1, device_id=where, device_id_type=MESH_ID)

    greet({"dp": lax.axis_index("dp") ^ 1})
    greet({"wa": wa ^ 1})
    greet({"wa": wa ^ 2})
    pl.when(ctx > 0)(lambda: greet({"ctx": ctx - 1}))
    pl.when(ctx < n_ctx - 1)(lambda: greet({"ctx": ctx + 1}))
    ends = (ctx == 0).astype(jnp.int32) + (ctx == n_ctx - 1).astype(jnp.int32)
    pl.semaphore_wait(barrier, 5 - ends)


WHOLE, PLACE, PICK = 0, 1, 2


def pair_shape(kind, src):
    if kind == PLACE:
        return (src.shape[0], 2) + src.shape[1:]
    if kind == PICK:
        return (src.shape[0],) + src.shape[2:]
    return src.shape


def start_pairs(kinds, srcs, dsts, sems):
    dp = lax.axis_index("dp")
    made = []
    for at, (kind, src, dst) in enumerate(zip(kinds, srcs, dsts)):
        if kind == PICK:
            src = src.at[:, dp ^ 1]
        if kind == PLACE:
            dst = dst.at[:, dp]
            keep = pltpu.make_async_copy(src, dst, sems.at[at, 2])
            keep.start()
            made.append((keep, keep.wait))
        send = pltpu.make_async_remote_copy(
            src_ref=src,
            dst_ref=dst,
            send_sem=sems.at[at, 0],
            recv_sem=sems.at[at, 1],
            device_id={"dp": dp ^ 1},
            device_id_type=MESH_ID,
        )
        send.start()
        if kind == PLACE:
            got = pltpu.make_async_remote_copy(
                src_ref=src,
                dst_ref=dsts[at].at[:, dp ^ 1],
                send_sem=sems.at[at, 0],
                recv_sem=sems.at[at, 1],
                device_id={"dp": dp ^ 1},
                device_id_type=MESH_ID,
            )
            made.append((send, send.wait_send))
            made.append((got, got.wait_recv))
        else:
            made.append((send, send.wait))
    return made


def piece_row(zc, wac, h, half, n_ctx, n_wa, by_position):
    if by_position:
        span = zc if h == 0 else 2 * n_ctx - 1 - zc
        return pl.multiple_of((span * n_wa + wac) * half, half)
    return pl.multiple_of(((zc * n_wa + wac) * 2 + h) * half, half)


def gather_kernel(n_ctx, n_wa, by_position, kinds, own_ref, *refs):
    pairs = len(kinds)
    srcs, out_ref, dsts = refs[:pairs], refs[pairs], refs[pairs + 1 : 2 * pairs + 1]
    own_sem, send_sem, recv_sem = refs[2 * pairs + 1 : 2 * pairs + 4]
    ctx = lax.axis_index("ctx")
    wa = lax.axis_index("wa")
    half = own_ref.shape[0] // 2
    meet_neighbours(ctx, wa, n_ctx)
    pair_copies = start_pairs(kinds, srcs, dsts, refs[-1])
    sends = []

    def place(zc, wac, h):
        return out_ref.at[pl.ds(piece_row(zc, wac, h, half, n_ctx, n_wa, by_position), half)]

    def copy(src, zc, wac, h, where):
        return pltpu.make_async_remote_copy(
            src_ref=src,
            dst_ref=place(zc, wac, h),
            send_sem=send_sem.at[len(sends)],
            recv_sem=recv_sem.at[(zc * n_wa + wac) * 2 + h],
            device_id=where,
            device_id_type=MESH_ID,
        )

    def send(cond, src, zc, wac, h, where):
        made = copy(src, zc, wac, h, where)
        if cond is None:
            made.start()
        else:
            pl.when(cond)(made.start)
        sends.append((cond, made))

    def arrived(cond, zc, wac, h):
        made = pltpu.make_async_remote_copy(
            src_ref=place(zc, wac, h),
            dst_ref=place(zc, wac, h),
            send_sem=send_sem.at[0],
            recv_sem=recv_sem.at[(zc * n_wa + wac) * 2 + h],
            device_id={"wa": wa ^ 1},
            device_id_type=MESH_ID,
        )
        if cond is None:
            made.wait_recv()
        else:
            pl.when(cond)(made.wait_recv)

    def inside(zc):
        return (zc >= 0) & (zc < n_ctx)

    own_copies = []
    for h in range(2):
        own = own_ref.at[pl.ds(h * half, half)]
        for way in (-1, 1):
            send(inside(ctx + way), own, ctx, wa, h, {"ctx": ctx + way})
        send(None, own, ctx, wa, h, {"wa": wa ^ 2})
        send(None, own, ctx, wa, h, {"wa": wa ^ 1})
        made = pltpu.make_async_copy(own, place(ctx, wa, h), own_sem.at[h])
        made.start()
        own_copies.append(made)

    def across(k, h):
        for way in (-1, 1) if k else (1,):
            zc = ctx + way * k
            cond = inside(zc) if k else None
            arrived(cond, zc, wa ^ 2, h)
            send(cond, place(zc, wa ^ 2, h), zc, wa ^ 2, h, {"wa": wa ^ 1})

    for k in range(1, n_ctx):
        for h in range(2):
            for way in (-1, 1):
                zc = ctx + way * k
                cond = inside(zc)
                arrived(cond, zc, wa, h)
                piece = place(zc, wa, h)
                send(cond & inside(ctx - way), piece, zc, wa, h, {"ctx": ctx - way})
                send(cond, piece, zc, wa, h, {"wa": wa ^ 2})
                send(cond, piece, zc, wa, h, {"wa": wa ^ 1})
            across(k - 1, h)
    for h in range(2):
        across(n_ctx - 1, h)
    for zc in range(n_ctx):
        for far in (0, 2):
            for h in range(2):
                arrived(None, zc, wa ^ 1 ^ far, h)
    for cond, made in sends:
        if cond is None:
            made.wait_send()
        else:
            pl.when(cond)(made.wait_send)
    for made in own_copies:
        made.wait()
    for _, done in pair_copies:
        done()


def gather_tokens(own, pairs, n_ctx, n_wa, by_position, call_id):
    rows, width = own.shape
    n = n_ctx * n_wa
    kinds = tuple(kind for kind, _ in pairs)
    anywhere = pl.BlockSpec(memory_space=pl.ANY)
    shapes = [jax.ShapeDtypeStruct((rows * n, width), own.dtype)]
    shapes += [jax.ShapeDtypeStruct(pair_shape(*pair), BF16) for pair in pairs]
    return pl.pallas_call(
        partial(gather_kernel, n_ctx, n_wa, by_position, kinds),
        in_specs=[anywhere] * (1 + len(pairs)),
        out_specs=[anywhere] * (1 + len(pairs)),
        out_shape=shapes,
        scratch_shapes=[
            pltpu.SemaphoreType.DMA((2,)),
            pltpu.SemaphoreType.DMA((8 + 12 * (n_ctx - 1) + 2 * (2 * n_ctx - 1),)),
            pltpu.SemaphoreType.DMA((2 * n,)),
            pltpu.SemaphoreType.DMA((max(1, len(pairs)), 3)),
        ],
        compiler_params=pltpu.CompilerParams(collective_id=call_id, has_side_effects=True),
        cost_estimate=LINK_COST,
    )(own, *[array for _, array in pairs])


def scatter_kernel(n_ctx, n_wa, by_position, kinds, part_ref, *refs):
    pairs = len(kinds)
    srcs, out_ref, dsts = refs[:pairs], refs[pairs], refs[pairs + 1 : 2 * pairs + 1]
    s1, s2, s3, send_sem, recv1, recv2, recv3, pair_sem = refs[2 * pairs + 1 :]
    ctx = lax.axis_index("ctx")
    wa = lax.axis_index("wa")
    half = out_ref.shape[0] // 2
    slab = 16
    y = wa // 2
    sibling, across = {"wa": wa ^ 1}, {"wa": wa ^ 2}
    meet_neighbours(ctx, wa, n_ctx)
    pair_copies = start_pairs(kinds, srcs, dsts, pair_sem)
    sends = []

    def begin(cond, act):
        if cond is None:
            act()
        else:
            pl.when(cond)(act)

    def mine(zc, wac, h):
        return part_ref.at[pl.ds(piece_row(zc, wac, h, half, n_ctx, n_wa, by_position), half)]

    def copy(src, dst, sem, where):
        made = pltpu.make_async_remote_copy(
            src_ref=src,
            dst_ref=dst,
            send_sem=send_sem.at[len(sends)],
            recv_sem=sem,
            device_id=where,
            device_id_type=MESH_ID,
        )
        return made

    def send(cond, src, dst, sem, where):
        made = copy(src, dst, sem, where)
        begin(cond, made.start)
        sends.append((cond, made))

    def arrived(cond, dst, sem):
        made = pltpu.make_async_remote_copy(
            src_ref=dst,
            dst_ref=dst,
            send_sem=send_sem.at[0],
            recv_sem=sem,
            device_id=sibling,
            device_id_type=MESH_ID,
        )
        begin(cond, made.wait_recv)

    def add_up(dst, dst_row, srcs):
        def step(i, carry):
            at = pl.multiple_of(i * slab, slab)
            total = srcs[0][pl.ds(at, slab), :].astype(F32)
            for src in srcs[1:]:
                total = total + src[pl.ds(at, slab), :].astype(F32)
            dst[pl.ds(pl.multiple_of(dst_row + at, slab), slab), :] = total.astype(dst.dtype)
            return carry

        lax.fori_loop(0, half // slab, step, 0)

    def inside(zc):
        return (zc >= 0) & (zc < n_ctx)

    def index1(zc, yc, h):
        return (zc * 2 + yc) * 2 + h

    def steps():
        for k in range(n_ctx - 1, -1, -1):
            for way in (-1, 1) if k else (1,):
                for h in range(2):
                    zc = ctx + way * k
                    yield k, way, h, zc, (inside(zc) if k else None)

    for other in (1, 0):
        yc = y ^ 1 if other else y
        for k, way, h, zc, cond in steps():
            at = index1(zc, yc, h)
            send(cond, mine(zc, yc * 2 + ((wa & 1) ^ 1), h), s1.at[at], recv1.at[at], sibling)
    for k, way, h, zc, cond in steps():
        at = index1(zc, y ^ 1, h)
        arrived(cond, s1.at[at], recv1.at[at])
        begin(cond, lambda: add_up(s1.at[at], 0, [s1.at[at], mine(zc, wa ^ 2, h)]))
        send(cond, s1.at[at], s2.at[zc * 2 + h], recv2.at[zc * 2 + h], across)
    for k, way, h, zc, cond in steps():
        at = index1(zc, y, h)
        arrived(cond, s1.at[at], recv1.at[at])
        arrived(cond, s2.at[zc * 2 + h], recv2.at[zc * 2 + h])
        base = [mine(zc, wa, h), s1.at[at], s2.at[zc * 2 + h]]
        here = zc * 2 + h
        low, high = here, (n_ctx + zc) * 2 + h
        if k:
            behind = low if way > 0 else high
            more = cond & inside(ctx - way)
            arrived(more, s3.at[behind], recv3.at[behind])
            begin(more, lambda: add_up(s2.at[here], 0, base + [s3.at[behind]]))
            first = cond & jnp.logical_not(inside(ctx - way))
            begin(first, lambda: add_up(s2.at[here], 0, base))
            send(cond, s2.at[here], s3.at[behind], recv3.at[behind], {"ctx": ctx + way})
        else:
            under, over = ctx > 0, ctx < n_ctx - 1
            arrived(under, s3.at[low], recv3.at[low])
            arrived(over, s3.at[high], recv3.at[high])
            ways = [
                (under & over, [s3.at[low], s3.at[high]]),
                (under & jnp.logical_not(over), [s3.at[low]]),
                (over & jnp.logical_not(under), [s3.at[high]]),
            ]
            for take, extra in ways:
                begin(take, lambda extra=extra: add_up(out_ref, h * half, base + extra))
    for cond, made in sends:
        begin(cond, made.wait_send)
    for _, done in pair_copies:
        done()


def scatter_tokens(part, pairs, n_ctx, n_wa, by_position, call_id):
    n = n_ctx * n_wa
    rows, width = part.shape[0] // n, part.shape[1]
    half = rows // 2
    pieces = 2 * (2 * n_ctx - 1)
    kinds = tuple(kind for kind, _ in pairs)
    anywhere = pl.BlockSpec(memory_space=pl.ANY)
    shapes = [jax.ShapeDtypeStruct((rows, width), F32)]
    shapes += [jax.ShapeDtypeStruct(pair_shape(*pair), BF16) for pair in pairs]
    return pl.pallas_call(
        partial(scatter_kernel, n_ctx, n_wa, by_position, kinds),
        in_specs=[pl.BlockSpec(memory_space=pltpu.VMEM)] + [anywhere] * len(pairs),
        out_specs=[pl.BlockSpec(memory_space=pltpu.VMEM)] + [anywhere] * len(pairs),
        out_shape=shapes,
        scratch_shapes=[
            pltpu.VMEM((4 * n_ctx, half, width), BF16),
            pltpu.VMEM((2 * n_ctx, half, width), BF16),
            pltpu.VMEM((4 * n_ctx, half, width), BF16),
            pltpu.SemaphoreType.DMA((4 * pieces,)),
            pltpu.SemaphoreType.DMA((4 * n_ctx,)),
            pltpu.SemaphoreType.DMA((2 * n_ctx,)),
            pltpu.SemaphoreType.DMA((4 * n_ctx,)),
            pltpu.SemaphoreType.DMA((max(1, len(pairs)), 3)),
        ],
        compiler_params=pltpu.CompilerParams(
            collective_id=call_id, has_side_effects=True, vmem_limit_bytes=48 * 2**20
        ),
        cost_estimate=LINK_COST,
    )(part, *[array for _, array in pairs])


def per_device_heads(
    tokens,
    doc_starts,
    out_grad,
    attn_gain,
    w_query,
    w_key,
    w_value,
    q_gain,
    k_gain,
    w_out,
    ffn_gain,
    w_gate,
    w_up,
    w_down,
):
    n_ctx = lax.axis_size("ctx")
    n_wa = lax.axis_size("wa")
    n = n_ctx * n_wa
    even = lax.axis_index("wa") % 2 == 0
    tok_rows, width = tokens.shape[1:]
    d_rows = w_query.shape[0]
    stream = tok_rows * n
    ff_cols = FF // n
    per = HD // n
    extra = 16
    position = jnp.arange(stream, dtype=jnp.int32)
    swap_dp = [(0, 1), (1, 0)]

    def mm(a, b):
        return jnp.dot(a, b, preferred_element_type=F32)

    def mm_t(a, b):
        return lax.dot_general(a, b, (((1,), (1,)), ((), ())), preferred_element_type=F32)

    def t_mm(a, b):
        return lax.dot_general(a, b, (((0,), (0,)), ((), ())), preferred_element_type=F32)

    def swap(blocks):
        return lax.all_to_all(blocks, AXES, 0, 0, tiled=True)

    def both(part):
        part = part.astype(BF16)
        return part.astype(F32) + lax.ppermute(part, "dp", swap_dp).astype(F32)

    gains_own = jnp.concatenate([attn_gain, ffn_gain, q_gain, k_gain])
    gains_row = jnp.pad(gains_own, (0, extra * 2 * LANES - gains_own.shape[0]))
    attn_cols = pack_attn(w_query, w_key, w_value, gains_row.reshape(extra, 2 * LANES), n)
    half = d_rows // 2
    dp = lax.axis_index("dp")
    ff_blocks = pack_pair(
        lax.dynamic_slice_in_dim(w_gate, dp * half, half),
        lax.dynamic_slice_in_dim(w_up, dp * half, half),
        n,
    )
    attn_cols, tokens_b, ff_blocks = lax.optimization_barrier((attn_cols, tokens[0], ff_blocks))
    attn_cols = swap(attn_cols)
    (x_all,) = gather_tokens(tokens_b, [], n_ctx, n_wa, True, 1)
    w_qkv = attn_cols[:, :d_rows].reshape(width, 2 * LANES)
    gains = attn_cols[:, d_rows:].reshape(n, -1).astype(F32)
    attn_gain32 = gains[:, :d_rows].reshape(-1)
    ffn_gain32 = gains[:, d_rows : 2 * d_rows].reshape(-1)
    qgain32 = gains[:, 2 * d_rows : 2 * d_rows + per].reshape(-1)
    kgain32 = gains[:, 2 * d_rows + per : 2 * d_rows + 2 * per].reshape(-1)

    ff_blocks, dy_b, _ = lax.optimization_barrier((ff_blocks, out_grad[0], x_all))
    ff_half = swap(ff_blocks)
    dy_all = lax.all_gather(dy_b, AXES, axis=0, tiled=True)

    x_own = tokens[0].astype(F32)
    n1_all = rms_norm(x_all.astype(F32), attn_gain32).astype(BF16)
    qkv = mm(n1_all, w_qkv)
    q_raw, k_raw, v_raw = qkv[:, :LANES], qkv[:, LANES : LANES + HD], qkv[:, LANES + HD :]
    v_b = v_raw.astype(BF16)
    (q_rot, k_rot), prep_back = jax.vjp(
        partial(head_prepare, position=position), q_raw, k_raw, qgain32, kgain32
    )
    q_b = q_rot.astype(BF16)
    kv_b = jnp.concatenate([k_rot.astype(BF16), v_b], axis=1)
    ov_b = jnp.concatenate([jnp.ones_like(v_b), v_b], axis=1)
    att, inv = attend(doc_starts, q_b, kv_b, ov_b)
    branch, w_gu = scatter_tokens(
        mm(att, w_out).astype(BF16), [(PLACE, ff_half)], n_ctx, n_wa, True, 3
    )
    w_gu = w_gu.reshape(width, 2 * ff_cols)
    middle = x_own + branch
    n2_own, n2_back = jax.vjp(rms_norm, middle, ffn_gain32)
    (n2_all,) = gather_tokens(n2_own.astype(BF16), [], n_ctx, n_wa, False, 2)
    gate_up = mm(n2_all, w_gu)
    gate, up = gate_up[:, :ff_cols], gate_up[:, ff_cols:]
    sig = jax.nn.sigmoid(gate)
    silu = gate * sig
    hidden = (silu * up).astype(BF16)
    down_part = mm(hidden, w_down).astype(BF16)
    down = lax.psum_scatter(down_part, AXES, scatter_dimension=0, tiled=True).astype(F32)
    layer_out = middle + down

    d_hidden = mm_t(dy_all, w_down)
    d_gu = jnp.concatenate(
        [d_hidden * up * (sig * (1.0 + gate * (1.0 - sig))), d_hidden * silu], axis=1
    ).astype(BF16)
    gu_grad = t_mm(n2_all, d_gu).astype(BF16).reshape(n, 2, half, 2 * ff_cols)
    d_n2, gu_other = scatter_tokens(
        mm_t(d_gu, w_gu).astype(BF16), [(PICK, gu_grad)], n_ctx, n_wa, False, 4
    )
    gu_mine = lax.dynamic_index_in_dim(gu_grad, dp, 1, keepdims=False)
    gu_rows = swap((gu_mine.astype(F32) + gu_other.astype(F32)).astype(BF16))
    down_grad = t_mm(hidden, dy_all).astype(BF16)
    d_mid_part, _ = n2_back(d_n2)
    d_middle = out_grad[0].astype(F32) + d_mid_part
    db_all, down_other = gather_tokens(
        d_middle.astype(BF16), [(WHOLE, down_grad)], n_ctx, n_wa, True, 5
    )
    out_w_grad = t_mm(att, db_all).astype(BF16)
    d_att = mm_t(db_all, w_out).astype(BF16)
    dq, dkv = attend_back(doc_starts, q_b, kv_b, att, inv, d_att)
    dkv = dkv + lax.ppermute(dkv, "wa", [(i, i ^ 1) for i in range(n_wa)])
    dq_raw, dk_raw, d_qgain, d_kgain = prep_back((dq * HD**-0.5, dkv[:, :HD] * HD**-0.5))
    d_kgain = jnp.where(even, d_kgain, 0.0)
    d_kv_own = jnp.where(even, dk_raw, dkv[:, HD:])
    w_kv_own = jnp.where(even, w_qkv[:, LANES : LANES + HD], w_qkv[:, LANES + HD :])
    d_qkv = jnp.concatenate([dq_raw, d_kv_own], axis=1).astype(BF16)
    qkv_grad = t_mm(n1_all, d_qkv).astype(BF16)
    head_gains = jnp.concatenate([d_qgain, d_kgain])
    qkv_cols = LANES + HD
    head_row = jnp.pad(head_gains.astype(BF16), (0, extra * qkv_cols - LANES))
    qkv_rows = swap(
        jnp.concatenate(
            [
                qkv_grad.reshape(n, d_rows, qkv_cols),
                jnp.broadcast_to(head_row.reshape(1, extra, qkv_cols), (n, extra, qkv_cols)),
            ],
            axis=1,
        )
    )
    d_n1_part = mm_t(d_qkv, jnp.concatenate([w_qkv[:, :LANES], w_kv_own], axis=1)).astype(BF16)
    d_n1, gu_others, out_w_other = scatter_tokens(
        d_n1_part, [(WHOLE, gu_rows), (WHOLE, out_w_grad)], n_ctx, n_wa, True, 6
    )
    _, n1_back = jax.vjp(rms_norm, x_own, attn_gain32)
    d_x_part, _ = n1_back(d_n1)
    input_grad = d_middle + d_x_part

    def flat(part):
        return part.transpose(1, 0, 2).reshape(d_rows, -1)

    gate_grad, up_grad, gu_sums = unpack_pair(gu_rows, gu_others, w_gate, w_up)
    qkv_rows = both(qkv_rows)
    q_grad = flat(qkv_rows[:, :d_rows, :LANES])
    kv_grad = qkv_rows[:, :d_rows, LANES:].reshape(KV, 2, d_rows, HD)
    k_grad, v_grad = flat(kv_grad[:, 0]), flat(kv_grad[:, 1])
    head_sums = jnp.sum(qkv_rows[:, d_rows:].reshape(n, -1)[:, :LANES], axis=0)
    me = lax.axis_index("ctx") * n_wa + lax.axis_index("wa")

    def row_sum(weight, grad):
        return jnp.sum(weight.astype(F32) * grad, axis=1)

    attn_gain_grad = (
        row_sum(w_query, q_grad) + row_sum(w_key, k_grad) + row_sum(w_value, v_grad)
    ) / attn_gain.astype(F32)
    ffn_gain_grad = gu_sums[:, 0] / ffn_gain.astype(F32)
    return (
        layer_out.astype(BF16)[None],
        input_grad.astype(BF16)[None],
        attn_gain_grad,
        q_grad,
        k_grad,
        v_grad,
        lax.dynamic_slice_in_dim(head_sums, me * per, per),
        lax.dynamic_slice_in_dim(head_sums, HD + me * per, per),
        out_w_grad.astype(F32) + out_w_other.astype(F32),
        ffn_gain_grad,
        gate_grad,
        up_grad,
        down_grad.astype(F32) + down_other.astype(F32),
    )


def solution(mesh):
    split = mesh.shape["ctx"] * mesh.shape["wa"]
    by_heads = 2 * split == H
    placed = (
        P("dp", ("ctx", "wa"), None),
        P("dp", None),
        P("dp", ("ctx", "wa"), None),
        P(("ctx", "wa")),
        P(("ctx", "wa"), None),
        P(("ctx", "wa"), None),
        P(("ctx", "wa"), None),
        P(("ctx", "wa")),
        P(("ctx", "wa")),
        P(("ctx", "wa"), None),
        P(("ctx", "wa")),
        P(("ctx", "wa"), None),
        P(("ctx", "wa"), None),
        P(("ctx", "wa"), None),
    )
    return jax.shard_map(
        per_device_heads if by_heads else per_device,
        mesh=mesh,
        in_specs=placed,
        out_specs=(
            P("dp", ("ctx", "wa"), None),
            P("dp", ("ctx", "wa"), None),
            P(("ctx", "wa")),
            P(("ctx", "wa"), None),
            P(("ctx", "wa"), None),
            P(("ctx", "wa"), None),
            P(("ctx", "wa")),
            P(("ctx", "wa")),
            P(("ctx", "wa"), None),
            P(("ctx", "wa")),
            P(("ctx", "wa"), None),
            P(("ctx", "wa"), None),
            P(("ctx", "wa"), None),
        ),
        check_vma=False,
    )
```

```python
from functools import partial

import jax
import jax.numpy as jnp
import numpy as np
from jax import lax
from jax.experimental import pallas as pl
from jax.experimental.pallas import tpu as pltpu
from jax.sharding import PartitionSpec as P

H = 32
KV = 8
HD = 64
FF = 8192


EPS = 1e-05
THETA = 1000000.0


def stored_positions(index, tok_rows, n_ctx, n_wa):
    device = index // tok_rows
    local = index % tok_rows
    half_rows = tok_rows // 2
    ctx_part = device // n_wa
    wa_part = device % n_wa
    span_idx = jnp.where(local < half_rows, ctx_part, 2 * n_ctx - 1 - ctx_part)
    return span_idx * (half_rows * n_wa) + wa_part * half_rows + local % half_rows


def segments(position, starts):
    return jnp.sum((starts[None, :] <= position[:, None]).astype(jnp.int32), axis=1) - 1


def rms_norm(values, gain):
    return values * lax.rsqrt(jnp.mean(values * values, axis=-1, keepdims=True) + EPS) * gain


def rotate(values, position):
    half_dim = HD // 2
    frequency = THETA ** (-2.0 * jnp.arange(half_dim, dtype=jnp.float32) / HD)
    angles = position.astype(jnp.float32)[:, None] * frequency[None, :]
    cosine = jnp.cos(angles)[:, None, :]
    sine_part = jnp.sin(angles)[:, None, :]
    first_half = values[..., :half_dim]
    second_half = values[..., half_dim:]
    return jnp.concatenate(
        [
            first_half * cosine - second_half * sine_part,
            second_half * cosine + first_half * sine_part,
        ],
        axis=-1,
    )


def prepare(query_raw, key_raw, query_gain, key_gain, position):
    return (
        rotate(rms_norm(query_raw, query_gain), position),
        rotate(rms_norm(key_raw, key_gain), position),
    )


def per_device(
    tokens,
    doc_starts,
    out_grad,
    attn_gain,
    w_query,
    w_key,
    w_value,
    q_gain,
    k_gain,
    w_out,
    ffn_gain,
    w_gate,
    w_up,
    w_down,
):
    n_ctx = lax.axis_size("ctx")
    n_wa = lax.axis_size("wa")
    tok_rows = tokens.shape[1]
    stream_len = tok_rows * n_ctx * n_wa
    key_width = min(1024, stream_len)
    key_blocks = stream_len // key_width
    groups = H // KV
    scale = HD ** (-0.5)
    first_row = (lax.axis_index("ctx") * n_wa + lax.axis_index("wa")) * tok_rows
    own_pos = stored_positions(
        first_row + jnp.arange(tok_rows, dtype=jnp.int32), tok_rows, n_ctx, n_wa
    )
    starts = doc_starts[0]
    own_seg = segments(own_pos, starts)
    key_pos = stored_positions(jnp.arange(stream_len, dtype=jnp.int32), tok_rows, n_ctx, n_wa)
    key_seg = segments(key_pos, starts)
    residual = tokens[0].astype(jnp.float32)
    attn_set = (
        lax.all_gather(attn_gain, ("ctx", "wa"), axis=0, tiled=True),
        lax.all_gather(w_query, ("ctx", "wa"), axis=0, tiled=True),
        lax.all_gather(w_key, ("ctx", "wa"), axis=0, tiled=True),
        lax.all_gather(w_value, ("ctx", "wa"), axis=0, tiled=True),
        lax.all_gather(q_gain, ("ctx", "wa"), axis=0, tiled=True),
        lax.all_gather(k_gain, ("ctx", "wa"), axis=0, tiled=True),
        lax.all_gather(w_out, ("ctx", "wa"), axis=0, tiled=True),
    )
    g_attn, wq_full, wk_full, wv_full, gq_full, gk_full, wo_full = attn_set
    attn_gain32 = g_attn.astype(jnp.float32)
    qgain32 = gq_full.astype(jnp.float32)
    kgain32 = gk_full.astype(jnp.float32)
    normed_one = rms_norm(residual, attn_gain32).astype(jnp.bfloat16)
    query_raw = jnp.dot(normed_one, wq_full, preferred_element_type=jnp.float32).reshape(
        tok_rows, H, HD
    )
    key_raw = jnp.dot(normed_one, wk_full, preferred_element_type=jnp.float32).reshape(
        tok_rows, KV, HD
    )
    value_b = jnp.dot(normed_one, wv_full, preferred_element_type=jnp.float32).astype(jnp.bfloat16)
    query_rot, key_rot = prepare(query_raw, key_raw, qgain32, kgain32, own_pos)
    query_b = query_rot.astype(jnp.bfloat16).reshape(tok_rows, KV, groups, HD)
    key_b = key_rot.astype(jnp.bfloat16).reshape(tok_rows, KV * HD)
    all_keys, all_values = (
        lax.all_gather(key_b, ("ctx", "wa"), axis=0, tiled=True),
        lax.all_gather(value_b, ("ctx", "wa"), axis=0, tiled=True),
    )

    def key_block(keys_in, values_in, block_idx):
        begin = block_idx * key_width
        key_part = lax.dynamic_slice_in_dim(keys_in, begin, key_width, 0).reshape(key_width, KV, HD)
        value_part = lax.dynamic_slice_in_dim(values_in, begin, key_width, 0).reshape(
            key_width, KV, HD
        )
        pos_part = lax.dynamic_slice_in_dim(key_pos, begin, key_width, 0)
        seg_part = lax.dynamic_slice_in_dim(key_seg, begin, key_width, 0)
        scores = (
            jnp.einsum("rkgd,tkd->kgrt", query_b, key_part, preferred_element_type=jnp.float32)
            * scale
        )
        allowed = (
            (seg_part[None, :] == own_seg[:, None]) & (pos_part[None, :] <= own_pos[:, None])
        )[None, None]
        return (scores, allowed, key_part, value_part)

    def stat_step(block_idx, carry):
        row_max, row_total = carry
        scores, allowed, key_part, value_part = key_block(all_keys, all_values, block_idx)
        masked = jnp.where(allowed, scores, -1e30)
        new_max = jnp.maximum(row_max, jnp.max(masked, axis=-1))
        fresh = jnp.sum(jnp.where(allowed, jnp.exp(masked - new_max[..., None]), 0.0), axis=-1)
        return (new_max, row_total * jnp.exp(row_max - new_max) + fresh)

    stat_init = (
        jnp.full((KV, groups, tok_rows), -1e30, jnp.float32),
        jnp.zeros((KV, groups, tok_rows), jnp.float32),
    )
    row_max, row_total = lax.fori_loop(0, key_blocks, stat_step, stat_init)

    def out_step(block_idx, summed):
        scores, allowed, key_part, value_part = key_block(all_keys, all_values, block_idx)
        probability = (
            jnp.where(allowed, jnp.exp(scores - row_max[..., None]), 0.0) / row_total[..., None]
        )
        return summed + jnp.einsum(
            "kgrt,tkd->rkgd",
            probability.astype(jnp.bfloat16),
            value_part,
            preferred_element_type=jnp.float32,
        )

    attended = lax.fori_loop(
        0, key_blocks, out_step, jnp.zeros((tok_rows, KV, groups, HD), jnp.float32)
    )
    attended_b = attended.reshape(tok_rows, H * HD).astype(jnp.bfloat16)
    middle = residual + jnp.dot(attended_b, wo_full, preferred_element_type=jnp.float32)
    ffn_set = (
        lax.all_gather(ffn_gain, ("ctx", "wa"), axis=0, tiled=True),
        lax.all_gather(w_gate, ("ctx", "wa"), axis=0, tiled=True),
        lax.all_gather(w_up, ("ctx", "wa"), axis=0, tiled=True),
        lax.all_gather(w_down, ("ctx", "wa"), axis=0, tiled=True),
    )
    g_ffn, wg_full, wu_full, wd_full = ffn_set
    ffn_gain32 = g_ffn.astype(jnp.float32)
    normed_two = rms_norm(middle, ffn_gain32).astype(jnp.bfloat16)
    gate_act = jnp.dot(normed_two, wg_full, preferred_element_type=jnp.float32)
    up_act = jnp.dot(normed_two, wu_full, preferred_element_type=jnp.float32)
    sigmoid_gate = jax.nn.sigmoid(gate_act)
    silu_gate = gate_act * sigmoid_gate
    hidden = (silu_gate * up_act).astype(jnp.bfloat16)
    layer_out = (middle + jnp.dot(hidden, wd_full, preferred_element_type=jnp.float32)).astype(
        jnp.bfloat16
    )
    g_ffn, wg_full, wu_full, wd_full = (
        lax.all_gather(ffn_gain, ("ctx", "wa"), axis=0, tiled=True),
        lax.all_gather(w_gate, ("ctx", "wa"), axis=0, tiled=True),
        lax.all_gather(w_up, ("ctx", "wa"), axis=0, tiled=True),
        lax.all_gather(w_down, ("ctx", "wa"), axis=0, tiled=True),
    )
    d_out = out_grad[0].astype(jnp.float32)
    d_out_b = d_out.astype(jnp.bfloat16)
    d_hidden = jnp.einsum("rd,fd->rf", d_out_b, wd_full, preferred_element_type=jnp.float32)
    d_gate = (d_hidden * up_act * (sigmoid_gate * (1.0 + gate_act * (1.0 - sigmoid_gate)))).astype(
        jnp.bfloat16
    )
    d_up = (d_hidden * silu_gate).astype(jnp.bfloat16)
    d_normed_two = jnp.einsum(
        "rf,df->rd", d_gate, wg_full, preferred_element_type=jnp.float32
    ) + jnp.einsum("rf,df->rd", d_up, wu_full, preferred_element_type=jnp.float32)
    norm_out, norm_back = jax.vjp(rms_norm, middle, ffn_gain32)
    d_middle_part, d_ffn_gain = norm_back(d_normed_two)
    d_middle = d_out + d_middle_part
    gate_up = jnp.concatenate([d_gate, d_up], axis=1)
    part_rows = normed_two
    in_grad = lax.psum_scatter(
        jnp.einsum("rc,rf->cf", part_rows, gate_up, preferred_element_type=jnp.float32),
        ("ctx", "wa"),
        scatter_dimension=0,
        tiled=True,
    )
    part_rows = hidden
    down_grad = lax.psum_scatter(
        jnp.einsum("rc,rd->cd", part_rows, d_out_b, preferred_element_type=jnp.float32),
        ("ctx", "wa"),
        scatter_dimension=0,
        tiled=True,
    )
    g_attn, wq_full, wk_full, wv_full, gq_full, gk_full, wo_full = (
        lax.all_gather(attn_gain, ("ctx", "wa"), axis=0, tiled=True),
        lax.all_gather(w_query, ("ctx", "wa"), axis=0, tiled=True),
        lax.all_gather(w_key, ("ctx", "wa"), axis=0, tiled=True),
        lax.all_gather(w_value, ("ctx", "wa"), axis=0, tiled=True),
        lax.all_gather(q_gain, ("ctx", "wa"), axis=0, tiled=True),
        lax.all_gather(k_gain, ("ctx", "wa"), axis=0, tiled=True),
        lax.all_gather(w_out, ("ctx", "wa"), axis=0, tiled=True),
    )
    d_branch = d_middle.astype(jnp.bfloat16)
    wo_grad = jnp.einsum("re,rd->ed", attended_b, d_branch, preferred_element_type=jnp.float32)
    d_attended = jnp.einsum(
        "rd,ed->re", d_branch, wo_full, preferred_element_type=jnp.float32
    ).astype(jnp.bfloat16)
    d_att4 = d_attended.reshape(tok_rows, KV, groups, HD)
    delta = jnp.einsum("rkgd,rkgd->kgr", d_att4.astype(jnp.float32), attended)

    def back_step(d_query, block_idx):
        scores, allowed, key_part, value_part = key_block(all_keys, all_values, block_idx)
        probability = (
            jnp.where(allowed, jnp.exp(scores - row_max[..., None]), 0.0) / row_total[..., None]
        )
        d_prob = jnp.einsum(
            "rkgd,tkd->kgrt", d_att4, value_part, preferred_element_type=jnp.float32
        )
        d_scores = (probability * (d_prob - delta[..., None])).astype(jnp.bfloat16)
        d_query = (
            d_query
            + jnp.einsum("kgrt,tkd->rkgd", d_scores, key_part, preferred_element_type=jnp.float32)
            * scale
        )
        d_key_part = (
            jnp.einsum("kgrt,rkgd->tkd", d_scores, query_b, preferred_element_type=jnp.float32)
            * scale
        )
        d_value_part = jnp.einsum(
            "kgrt,rkgd->tkd",
            probability.astype(jnp.bfloat16),
            d_att4,
            preferred_element_type=jnp.float32,
        )
        return (
            d_query,
            (d_key_part.reshape(key_width, KV * HD), d_value_part.reshape(key_width, KV * HD)),
        )

    d_query, (d_keys, d_values) = lax.scan(
        back_step, jnp.zeros((tok_rows, KV, groups, HD), jnp.float32), jnp.arange(key_blocks)
    )
    d_key_own, d_value_own = (
        lax.psum_scatter(
            d_keys.reshape(stream_len, KV * HD), ("ctx", "wa"), scatter_dimension=0, tiled=True
        ),
        lax.psum_scatter(
            d_values.reshape(stream_len, KV * HD), ("ctx", "wa"), scatter_dimension=0, tiled=True
        ),
    )
    prep_out, prep_back = jax.vjp(
        partial(prepare, position=own_pos), query_raw, key_raw, qgain32, kgain32
    )
    d_query_raw, d_key_raw, d_qgain, d_kgain = prep_back(
        (d_query.reshape(tok_rows, H, HD), d_key_own.reshape(tok_rows, KV, HD))
    )
    dq_b = d_query_raw.reshape(tok_rows, H * HD).astype(jnp.bfloat16)
    dk_b = d_key_raw.reshape(tok_rows, KV * HD).astype(jnp.bfloat16)
    dv_b = d_value_own.astype(jnp.bfloat16)
    d_normed_one = (
        jnp.einsum("re,de->rd", dq_b, wq_full, preferred_element_type=jnp.float32)
        + jnp.einsum("re,de->rd", dk_b, wk_full, preferred_element_type=jnp.float32)
        + jnp.einsum("re,de->rd", dv_b, wv_full, preferred_element_type=jnp.float32)
    )
    first_out, first_back = jax.vjp(rms_norm, residual, attn_gain32)
    d_res_part, d_attn_gain = first_back(d_normed_one)
    input_grad = (d_middle + d_res_part).astype(jnp.bfloat16)
    wq_grad = jnp.einsum("rc,re->ce", normed_one, dq_b, preferred_element_type=jnp.float32)
    wk_grad = jnp.einsum("rc,re->ce", normed_one, dk_b, preferred_element_type=jnp.float32)
    wv_grad = jnp.einsum("rc,re->ce", normed_one, dv_b, preferred_element_type=jnp.float32)
    attn_terms = (d_attn_gain, wq_grad, wk_grad, wv_grad, d_qgain, d_kgain, d_ffn_gain, wo_grad)
    attn_shards = (
        lax.psum_scatter(attn_terms[0], ("ctx", "wa"), scatter_dimension=0, tiled=True),
        lax.psum_scatter(attn_terms[1], ("ctx", "wa"), scatter_dimension=0, tiled=True),
        lax.psum_scatter(attn_terms[2], ("ctx", "wa"), scatter_dimension=0, tiled=True),
        lax.psum_scatter(attn_terms[3], ("ctx", "wa"), scatter_dimension=0, tiled=True),
        lax.psum_scatter(attn_terms[4], ("ctx", "wa"), scatter_dimension=0, tiled=True),
        lax.psum_scatter(attn_terms[5], ("ctx", "wa"), scatter_dimension=0, tiled=True),
        lax.psum_scatter(attn_terms[6], ("ctx", "wa"), scatter_dimension=0, tiled=True),
        lax.psum_scatter(attn_terms[7], ("ctx", "wa"), scatter_dimension=0, tiled=True),
    )
    wo_shard = attn_shards[7]
    summed = (
        lax.psum(attn_shards[0].astype(jnp.bfloat16), "dp").astype(jnp.float32),
        lax.psum(attn_shards[1].astype(jnp.bfloat16), "dp").astype(jnp.float32),
        lax.psum(attn_shards[2].astype(jnp.bfloat16), "dp").astype(jnp.float32),
        lax.psum(attn_shards[3].astype(jnp.bfloat16), "dp").astype(jnp.float32),
        lax.psum(attn_shards[4].astype(jnp.bfloat16), "dp").astype(jnp.float32),
        lax.psum(attn_shards[5].astype(jnp.bfloat16), "dp").astype(jnp.float32),
        lax.psum(wo_shard.astype(jnp.bfloat16), "dp").astype(jnp.float32),
        lax.psum(attn_shards[6].astype(jnp.bfloat16), "dp").astype(jnp.float32),
        lax.psum(in_grad[:, :FF].astype(jnp.bfloat16), "dp").astype(jnp.float32),
        lax.psum(in_grad[:, FF:].astype(jnp.bfloat16), "dp").astype(jnp.float32),
        lax.psum(down_grad.astype(jnp.bfloat16), "dp").astype(jnp.float32),
    )
    return (layer_out[None], input_grad[None]) + tuple(summed)


AXES = ("ctx", "wa")
LANES = 2 * HD
ROWS_BLOCK = 256
FFN_BLOCK = 256
LOG2E = 1.4426950408889634
F32 = jnp.float32
BF16 = jnp.bfloat16


def low_key(starts, row):
    first = jnp.int32(0)
    for doc in range(starts.shape[1]):
        begin = starts[0, doc]
        first = jnp.where(begin <= row, begin, first)
    return first


def block_mask(starts, q_begin, k_begin, bq, bk):
    row = q_begin + lax.broadcasted_iota(jnp.int32, (bq, 1), 0)
    first = low_key(starts, row)
    col = k_begin + lax.broadcasted_iota(jnp.int32, (1, bk), 1)
    return (col >= first) & (col <= row)


def rope_tables(stream):
    frequency = np.float32(THETA) ** (-2.0 * np.arange(HD // 2, dtype=np.float32) / np.float32(HD))
    angles = np.arange(stream, dtype=np.float32)[:, None] * frequency.astype(np.float32)[None, :]
    cosine = np.cos(angles.astype(np.float64)).astype(np.float32)
    sine = np.sin(angles.astype(np.float64)).astype(np.float32)
    return np.tile(cosine, (1, 4)), np.tile(np.concatenate([-sine, sine], axis=1), (1, 2))


def lane_ids():
    return lax.broadcasted_iota(jnp.int32, (1, LANES), 1)


def head_mean(values):
    low = jnp.sum(values[:, :HD], axis=1, keepdims=True)
    high = jnp.sum(values[:, HD:], axis=1, keepdims=True)
    return jnp.where(lane_ids() < HD, low, high) * (1.0 / HD)


def swap_halves(values):
    first = lane_ids() % HD < HD // 2
    return jnp.where(
        first, pltpu.roll(values, LANES - HD // 2, 1), pltpu.roll(values, HD // 2, 1)
    )


def norm_rope(raw, gain, cosine, sine):
    scaled = raw * lax.rsqrt(head_mean(raw * raw) + EPS) * gain
    return scaled * cosine + swap_halves(scaled) * sine


def norm_rope_back(grad, raw, gain, cosine, sine):
    inverse = lax.rsqrt(head_mean(raw * raw) + EPS)
    unit = raw * inverse
    d_scaled = grad * cosine + swap_halves(grad * sine)
    d_unit = d_scaled * gain
    return inverse * (d_unit - unit * head_mean(d_unit * unit)), d_scaled * unit


def stack_heads(rows, at_low):
    lanes = lane_ids()
    zero = jnp.zeros_like(rows)
    low, high = jnp.where(lanes < HD, rows, zero), jnp.where(lanes < HD, zero, rows)
    turned = pltpu.roll(high if at_low else low, HD, 1)
    return jnp.concatenate([low, turned] if at_low else [turned, high], axis=0)


def dot(a, b):
    return jnp.dot(a, b, preferred_element_type=F32)


def dot_t(a, b):
    return lax.dot_general(a, b, (((1,), (1,)), ((), ())), preferred_element_type=F32)


def t_dot(a, b):
    return lax.dot_general(a, b, (((0,), (0,)), ((), ())), preferred_element_type=F32)


def attend_kernel(
    starts, x_ref, gain_ref, w_ref, head_gain_ref, cos_ref, sin_ref, w_out_ref,
    normed_ref, raw_ref, q_ref, kv_ref, att_ref, inv_ref, part_ref, ov_ref,
):
    block = pl.program_id(0)
    bq = x_ref.shape[0]
    q_begin = pl.multiple_of(block * bq, bq)
    x = x_ref[...].astype(F32)
    inverse = lax.rsqrt(jnp.mean(x * x, axis=1, keepdims=True) + EPS)
    normed = (x * inverse * gain_ref[...]).astype(BF16)
    normed_ref[...] = normed
    raw = dot(normed, w_ref[...])
    raw_ref[...] = raw
    cosine, sine = cos_ref[...], sin_ref[...]
    q = norm_rope(raw[:, :LANES], head_gain_ref[:, :LANES], cosine, sine)
    q_ref[...] = q.astype(BF16)
    kv_raw = raw[:, LANES:]
    is_key = lane_ids() < HD
    turned = norm_rope(kv_raw, head_gain_ref[:, LANES:], cosine, sine)
    kv_ref[pl.ds(q_begin, bq), :] = jnp.where(is_key, turned, kv_raw).astype(BF16)
    ov_ref[pl.ds(q_begin, bq), :] = jnp.where(is_key, 1.0, kv_raw).astype(BF16)
    q2 = stack_heads(q, True).astype(BF16)

    def step(j, acc):
        k_begin = pl.multiple_of(j * bq, bq)
        s = dot_t(q2, kv_ref[pl.ds(k_begin, bq), :])
        mask = block_mask(starts, q_begin, k_begin, bq, bq)
        p = jnp.exp2(s * (LOG2E * HD**-0.5))
        p = jnp.where(jnp.concatenate([mask, mask], axis=0), p, 0.0).astype(BF16)
        return acc + dot(p, ov_ref[pl.ds(k_begin, bq), :])

    low = low_key(starts, q_begin) // bq
    acc = lax.fori_loop(low, block + 1, step, jnp.zeros((2 * bq, LANES), F32))
    inv = 1.0 / acc[:, :1]
    out = acc * inv
    att = jnp.where(is_key, pltpu.roll(out[:bq], HD, 1), out[bq:]).astype(BF16)
    att_ref[...] = att
    inv_ref[...] = jnp.where(is_key, inv[:bq], inv[bq:])
    part_ref[...] = dot(att, w_out_ref[...]).astype(BF16)


def attend(starts, x_all, gain, w_qkv, head_gain, cosine, sine, w_out):
    stream, width = x_all.shape
    bq = ROWS_BLOCK

    def rows(cols):
        return pl.BlockSpec((bq, cols), lambda i: (i, 0))

    def whole(shape):
        return pl.BlockSpec(shape, lambda i: (0, 0), pipeline_mode=pl.Buffered(1))

    return pl.pallas_call(
        attend_kernel,
        grid=(stream // bq,),
        in_specs=[
            pl.BlockSpec(memory_space=pltpu.SMEM),
            rows(width),
            whole((1, width)),
            whole(w_qkv.shape),
            whole((1, 2 * LANES)),
            rows(LANES),
            rows(LANES),
            whole(w_out.shape),
        ],
        out_specs=[
            rows(width),
            rows(2 * LANES),
            rows(LANES),
            pl.BlockSpec((stream, LANES), lambda i: (0, 0)),
            rows(LANES),
            rows(LANES),
            rows(width),
        ],
        out_shape=[
            jax.ShapeDtypeStruct((stream, width), BF16),
            jax.ShapeDtypeStruct((stream, 2 * LANES), F32),
            jax.ShapeDtypeStruct((stream, LANES), BF16),
            jax.ShapeDtypeStruct((stream, LANES), BF16),
            jax.ShapeDtypeStruct((stream, LANES), BF16),
            jax.ShapeDtypeStruct((stream, LANES), F32),
            jax.ShapeDtypeStruct((stream, width), BF16),
        ],
        scratch_shapes=[pltpu.VMEM((stream, LANES), BF16)],
        compiler_params=pltpu.CompilerParams(vmem_limit_bytes=48 * 2**20),
        cost_estimate=pl.CostEstimate(flops=2 * 10**10, bytes_accessed=2**25, transcendentals=0),
    )(starts, x_all, gain, w_qkv, head_gain, cosine, sine, w_out)


def attend_back_kernel(
    starts, db_ref, w_out_ref, q_ref, kv_ref, att_ref, inv_ref, raw_ref, head_gain_ref, cos_ref, sin_ref,
    d_ref, w_grad_ref, gain_ref, dkv_ref, w_acc_ref,
):
    block = pl.program_id(0)
    bq = db_ref.shape[0]
    q_begin = pl.multiple_of(block * bq, bq)

    @pl.when(block == 0)
    def _():
        dkv_ref[...] = jnp.zeros_like(dkv_ref)
        w_acc_ref[...] = jnp.zeros_like(w_acc_ref)
        gain_ref[...] = jnp.zeros_like(gain_ref)

    db = db_ref[...]
    att = att_ref[...]
    da = dot_t(db, w_out_ref[...])
    w_acc_ref[...] += t_dot(att, db)
    q2 = stack_heads(q_ref[...].astype(F32), True).astype(BF16)
    da2 = stack_heads(da, False).astype(BF16)
    prod = da.astype(BF16).astype(F32) * att.astype(F32)
    delta = jnp.concatenate(
        [
            jnp.sum(prod[:, :HD], axis=1, keepdims=True),
            jnp.sum(prod[:, HD:], axis=1, keepdims=True),
        ],
        axis=0,
    )
    inv_all = inv_ref[...]
    inv = jnp.concatenate([inv_all[:, :1], inv_all[:, HD : HD + 1]], axis=0)

    def step(j, dq):
        k_begin = pl.multiple_of(j * bq, bq)
        keys = kv_ref[pl.ds(k_begin, bq), :]
        s = dot_t(q2, keys)
        mask = block_mask(starts, q_begin, k_begin, bq, bq)
        p = jnp.exp2(s * (LOG2E * HD**-0.5)) * inv
        p = jnp.where(jnp.concatenate([mask, mask], axis=0), p, 0.0)
        ds = (p * (dot_t(da2, keys) - delta)).astype(BF16)
        dkv_ref[pl.ds(k_begin, bq), :] += t_dot(ds, q2) * HD**-0.5 + t_dot(p.astype(BF16), da2)
        return dq + dot(ds, keys)

    low = low_key(starts, q_begin) // bq
    dq = lax.fori_loop(low, block + 1, step, jnp.zeros((2 * bq, LANES), F32))
    is_key = lane_ids() < HD
    dq = jnp.where(is_key, dq[:bq], pltpu.roll(dq[bq:], HD, 1)) * HD**-0.5
    here = pl.ds(q_begin, bq)
    d_raw, d_gain = norm_rope_back(
        dq, raw_ref[here, :LANES], head_gain_ref[:, :LANES], cos_ref[here, :], sin_ref[here, :]
    )
    d_ref[here, :LANES] = d_raw.astype(BF16)
    gain_ref[0:1, :] += jnp.sum(d_gain, axis=0, keepdims=True)

    @pl.when(block == pl.num_programs(0) - 1)
    def _():
        def finish(j, carry):
            rows = pl.ds(pl.multiple_of(j * bq, bq), bq)
            dkv = dkv_ref[rows, :]
            d_raw, d_gain = norm_rope_back(
                dkv, raw_ref[rows, LANES:], head_gain_ref[:, LANES:], cos_ref[rows, :], sin_ref[rows, :]
            )
            d_ref[rows, LANES:] = jnp.where(is_key, d_raw, dkv).astype(BF16)
            gain_ref[1:2, :] += jnp.sum(d_gain, axis=0, keepdims=True)
            return carry

        lax.fori_loop(0, pl.num_programs(0), finish, 0)
        w_grad_ref[...] = w_acc_ref[...].astype(BF16)


def attend_back(starts, db_all, w_out, q, kv, att, inv, raw, head_gain, cosine, sine):
    stream, width = db_all.shape
    bq = ROWS_BLOCK

    def rows(cols):
        return pl.BlockSpec((bq, cols), lambda i: (i, 0))

    def whole(shape):
        return pl.BlockSpec(shape, lambda i: (0, 0), pipeline_mode=pl.Buffered(1))

    def kept(shape):
        return pl.BlockSpec(shape, lambda i: (0, 0))

    return pl.pallas_call(
        attend_back_kernel,
        grid=(stream // bq,),
        in_specs=[
            pl.BlockSpec(memory_space=pltpu.SMEM),
            rows(width),
            whole(w_out.shape),
            rows(LANES),
            whole((stream, LANES)),
            rows(LANES),
            rows(LANES),
            whole((stream, 2 * LANES)),
            whole((1, 2 * LANES)),
            whole((stream, LANES)),
            whole((stream, LANES)),
        ],
        out_specs=[kept((stream, 2 * LANES)), kept(w_out.shape), kept((8, LANES))],
        out_shape=[
            jax.ShapeDtypeStruct((stream, 2 * LANES), BF16),
            jax.ShapeDtypeStruct(w_out.shape, BF16),
            jax.ShapeDtypeStruct((8, LANES), F32),
        ],
        scratch_shapes=[pltpu.VMEM((stream, LANES), F32), pltpu.VMEM(w_out.shape, F32)],
        compiler_params=pltpu.CompilerParams(vmem_limit_bytes=48 * 2**20),
        cost_estimate=pl.CostEstimate(flops=3 * 10**10, bytes_accessed=2**25, transcendentals=0),
    )(starts, db_all, w_out, q, kv, att, inv, raw, head_gain, cosine, sine)


def ffn_kernel(
    n2_ref, dy_ref, own_ref, other_ref, w_down_ref,
    down_ref, d_n2_ref, gu_grad_ref, down_grad_ref, gu_acc, down_acc, w_gu_ref,
):
    block = pl.program_id(0)
    first = lax.axis_index("dp") == 0

    @pl.when(block == 0)
    def _():
        half = own_ref.shape[1]
        own_row = jnp.where(first, 0, half)

        def put(j, carry):
            for begin, ref in ((own_row, own_ref), (half - own_row, other_ref)):
                at = pl.multiple_of(2 * half * j + begin, half)
                w_gu_ref[pl.ds(at, half), :] = ref[j]
            return carry

        lax.fori_loop(0, own_ref.shape[0], put, 0)
        gu_acc[...] = jnp.zeros_like(gu_acc)
        down_acc[...] = jnp.zeros_like(down_acc)

    cols = w_down_ref.shape[0]
    n2, dy = n2_ref[...], dy_ref[...]
    gate_up = dot(n2, w_gu_ref[...])
    gate, up = gate_up[:, :cols], gate_up[:, cols:]
    sig = jax.nn.sigmoid(gate)
    silu = gate * sig
    hidden = (silu * up).astype(BF16)
    down_ref[...] = dot(hidden, w_down_ref[...]).astype(BF16)
    d_hidden = dot_t(dy, w_down_ref[...])
    d_gu = jnp.concatenate(
        [
            (d_hidden * up * (sig * (1.0 + gate * (1.0 - sig)))).astype(BF16),
            (d_hidden * silu).astype(BF16),
        ],
        axis=1,
    )
    d_n2_ref[...] = dot_t(d_gu, w_gu_ref[...]).astype(BF16)
    gu_acc[...] += t_dot(n2, d_gu)
    down_acc[...] += t_dot(hidden, dy)

    @pl.when(block == pl.num_programs(0) - 1)
    def _():
        gu_grad_ref[...] = gu_acc[...].astype(BF16)
        down_grad_ref[...] = down_acc[...].astype(BF16)


def ffn(n2_all, dy_all, own, other, w_down):
    stream, width = n2_all.shape
    gu_shape = (width, own.shape[2])
    bt = FFN_BLOCK
    rows = pl.BlockSpec((bt, width), lambda i: (i, 0))

    def whole(shape):
        return pl.BlockSpec(shape, lambda i: (0,) * len(shape), pipeline_mode=pl.Buffered(1))

    return pl.pallas_call(
        ffn_kernel,
        grid=(stream // bt,),
        in_specs=[rows, rows, whole(own.shape), whole(own.shape), whole(w_down.shape)],
        out_specs=[rows, rows, whole(gu_shape), whole(w_down.shape)],
        out_shape=[
            jax.ShapeDtypeStruct((stream, width), BF16),
            jax.ShapeDtypeStruct((stream, width), BF16),
            jax.ShapeDtypeStruct(gu_shape, BF16),
            jax.ShapeDtypeStruct(w_down.shape, BF16),
        ],
        scratch_shapes=[
            pltpu.VMEM(gu_shape, F32),
            pltpu.VMEM(w_down.shape, F32),
            pltpu.VMEM(gu_shape, BF16),
        ],
        compiler_params=pltpu.CompilerParams(vmem_limit_bytes=58 * 2**20),
        cost_estimate=pl.CostEstimate(
            flops=18 * stream * width * w_down.shape[0], bytes_accessed=2**25, transcendentals=0
        ),
    )(n2_all, dy_all, own, other, w_down)


def unpack_attn_kernel(
    own_ref, other_ref, wq_ref, wk_ref, wv_ref, q_ref, k_ref, v_ref, sum_ref, gains_ref
):
    n, half = own_ref.shape[0], wq_ref.shape[0] // 2
    first = lax.axis_index("dp") == 0
    low = jnp.where(first, 0, half)
    high = half - low
    share = n // KV
    gains_ref[...] = jnp.sum(own_ref[:, half : half + 8, :].astype(F32), axis=0)
    for begin, ref in ((low, own_ref), (high, other_ref)):
        rows = pl.ds(pl.multiple_of(begin, half), half)
        total = jnp.zeros((half, 1), F32)
        for j in range(n):
            cols = slice(j * LANES, (j + 1) * LANES)
            q = ref[j, :half, :LANES].astype(F32)
            q_ref[rows, cols] = q
            total += jnp.sum(q * wq_ref[rows, cols].astype(F32), axis=1, keepdims=True)
        for pair in range(KV // 2):
            cols = slice(pair * LANES, (pair + 1) * LANES)
            heads = []
            for head in (2 * pair, 2 * pair + 1):
                kv = ref[head * share, :half, LANES:].astype(F32)
                for more in range(1, share):
                    kv = kv + ref[head * share + more, :half, LANES:].astype(F32)
                heads.append(kv)
            k = jnp.concatenate([heads[0][:, :HD], heads[1][:, :HD]], axis=1)
            v = jnp.concatenate([heads[0][:, HD:], heads[1][:, HD:]], axis=1)
            k_ref[rows, cols] = k
            v_ref[rows, cols] = v
            both = k * wk_ref[rows, cols].astype(F32) + v * wv_ref[rows, cols].astype(F32)
            total += jnp.sum(both, axis=1, keepdims=True)
        sum_ref[rows, :] = jnp.broadcast_to(total, (half, LANES))


def unpack_attn(own, other, w_query, w_key, w_value):
    d_rows = w_query.shape[0]
    return pl.pallas_call(
        unpack_attn_kernel,
        out_shape=[
            jax.ShapeDtypeStruct(w_query.shape, F32),
            jax.ShapeDtypeStruct(w_key.shape, F32),
            jax.ShapeDtypeStruct(w_value.shape, F32),
            jax.ShapeDtypeStruct((d_rows, LANES), F32),
            jax.ShapeDtypeStruct((8, 2 * LANES), F32),
        ],
        compiler_params=pltpu.CompilerParams(vmem_limit_bytes=32 * 2**20),
    )(own, other, w_query, w_key, w_value)


def pack_attn_kernel(query_ref, key_ref, value_ref, gains_ref, out_ref):
    n, rows, _ = out_ref.shape
    d_rows = query_ref.shape[0]
    share = n // KV
    for j in range(n):
        head = j // share * HD
        out_ref[j, :d_rows, :LANES] = query_ref[:, j * LANES : (j + 1) * LANES]
        out_ref[j, :d_rows, LANES:] = jnp.concatenate(
            [key_ref[:, head : head + HD], value_ref[:, head : head + HD]], axis=1
        )
        out_ref[j, d_rows:, :] = gains_ref[...]


def pack_attn(w_query, w_key, w_value, gains, n):
    d_rows = w_query.shape[0]
    return pl.pallas_call(
        pack_attn_kernel,
        out_shape=jax.ShapeDtypeStruct((n, d_rows + gains.shape[0], 2 * LANES), BF16),
    )(w_query, w_key, w_value, gains)


def pack_pair_kernel(dp_ref, gate_ref, up_ref, out_ref):
    count, _, both = out_ref.shape
    cols = both // 2
    for j in range(count):
        out_ref[j, :, :cols] = gate_ref[:, j * cols : (j + 1) * cols]
        out_ref[j, :, cols:] = up_ref[:, j * cols : (j + 1) * cols]


def pack_pair(w_gate, w_up, n):
    half, cols = w_gate.shape[0] // 2, w_gate.shape[1] // n
    count = 4
    part = pl.BlockSpec((half, count * cols), lambda j, dp: (dp[0], j))
    return pl.pallas_call(
        pack_pair_kernel,
        grid_spec=pltpu.PrefetchScalarGridSpec(
            num_scalar_prefetch=1,
            grid=(n // count,),
            in_specs=[part, part],
            out_specs=pl.BlockSpec((count, half, 2 * cols), lambda j, dp: (j, 0, 0)),
        ),
        out_shape=jax.ShapeDtypeStruct((n, half, 2 * cols), BF16),
        compiler_params=pltpu.CompilerParams(vmem_limit_bytes=32 * 2**20),
    )(lax.axis_index("dp").reshape(1), w_gate, w_up)


def unpack_pair_kernel(own_ref, other_ref, gate_w, up_w, gate_ref, up_ref, sum_ref):
    count, half, both = own_ref.shape
    cols = both // 2
    first = lax.axis_index("dp") == 0

    @pl.when(pl.program_id(0) == 0)
    def _():
        sum_ref[...] = jnp.zeros_like(sum_ref)

    own_row = pl.multiple_of(jnp.where(first, 0, half), half)
    for begin, ref in ((own_row, own_ref), (half - own_row, other_ref)):
        rows = pl.ds(pl.multiple_of(begin, half), half)
        total = jnp.zeros((half, 128), F32)
        for j in range(count):
            for at in range(0, cols, 128):
                here = slice(j * cols + at, j * cols + at + 128)
                gate = ref[j, :, at : at + 128].astype(F32)
                up = ref[j, :, cols + at : cols + at + 128].astype(F32)
                gate_ref[rows, here] = gate
                up_ref[rows, here] = up
                total += gate * gate_w[rows, here].astype(F32) + up * up_w[rows, here].astype(F32)
        sum_ref[rows, :] += total


def unpack_pair(own, other, w_gate, w_up):
    n, half, both = own.shape
    count = 4
    block = pl.BlockSpec((count, half, both), lambda j: (j, 0, 0))
    part = pl.BlockSpec((2 * half, count * both // 2), lambda j: (0, j))
    return pl.pallas_call(
        unpack_pair_kernel,
        grid=(n // count,),
        in_specs=[block, block, part, part],
        out_specs=[part, part, pl.BlockSpec((2 * half, 128), lambda j: (0, 0))],
        out_shape=[
            jax.ShapeDtypeStruct(w_gate.shape, F32),
            jax.ShapeDtypeStruct(w_up.shape, F32),
            jax.ShapeDtypeStruct((2 * half, 128), F32),
        ],
        compiler_params=pltpu.CompilerParams(vmem_limit_bytes=32 * 2**20),
    )(own, other, w_gate, w_up)


MESH_ID = pl.DeviceIdType.MESH
LINK_COST = pl.CostEstimate(flops=5 * 10**10, bytes_accessed=2**24, transcendentals=0)


def meet_neighbours(ctx, wa, n_ctx, n_wa, everyone):
    barrier = pltpu.get_barrier_semaphore()

    def greet(where):
        pl.semaphore_signal(barrier, inc=1, device_id=where, device_id_type=MESH_ID)

    greet({"dp": lax.axis_index("dp") ^ 1})
    if everyone:
        n = n_ctx * n_wa

        def step(i, carry):
            other = lax.rem(ctx * n_wa + wa + i, n)
            greet({"ctx": other // n_wa, "wa": lax.rem(other, n_wa)})
            return carry

        lax.fori_loop(1, n, step, 0)
        pl.semaphore_wait(barrier, n)
        return
    greet({"wa": wa ^ 1})
    greet({"wa": wa ^ 2})
    pl.when(ctx > 0)(lambda: greet({"ctx": ctx - 1}))
    pl.when(ctx < n_ctx - 1)(lambda: greet({"ctx": ctx + 1}))
    ends = (ctx == 0).astype(jnp.int32) + (ctx == n_ctx - 1).astype(jnp.int32)
    pl.semaphore_wait(barrier, 5 - ends)


WHOLE, PICK, SPREAD = 0, 1, 2


def pair_shape(kind, src):
    if kind == PICK:
        return (src.shape[0],) + src.shape[2:]
    return src.shape


def start_spread(src, dst, n_wa, sems):
    n = src.shape[0]
    me = lax.axis_index("ctx") * n_wa + lax.axis_index("wa")
    keep = pltpu.make_async_copy(src.at[me], dst.at[me], sems.at[0, 0])
    keep.start()

    def made(step, arriving):
        other = lax.rem(me + step, n)
        return pltpu.make_async_remote_copy(
            src_ref=src.at[other],
            dst_ref=dst.at[other if arriving else me],
            send_sem=sems.at[0, step],
            recv_sem=sems.at[1, other if arriving else me],
            device_id={"ctx": other // n_wa, "wa": lax.rem(other, n_wa)},
            device_id_type=MESH_ID,
        )

    def loop(act):
        def step(i, carry):
            act(i)
            return carry

        lax.fori_loop(1, n, step, 0)

    def finish():
        keep.wait()
        loop(lambda i: made(i, True).wait_recv())
        loop(lambda i: made(i, False).wait_send())

    loop(lambda i: made(i, False).start())
    return finish


def start_pairs(kinds, srcs, dsts, n_wa, sems, spread_sems):
    dp = lax.axis_index("dp")
    waits = []
    for at, (kind, src, dst) in enumerate(zip(kinds, srcs, dsts)):
        if kind == SPREAD:
            waits.append(start_spread(src, dst, n_wa, spread_sems))
            continue
        if kind == PICK:
            src = src.at[:, dp ^ 1]
        send = pltpu.make_async_remote_copy(
            src_ref=src,
            dst_ref=dst,
            send_sem=sems.at[at, 0],
            recv_sem=sems.at[at, 1],
            device_id={"dp": dp ^ 1},
            device_id_type=MESH_ID,
        )
        send.start()
        waits.append(send.wait)
    return waits


def piece_row(zc, wac, h, half, n_ctx, n_wa, by_position):
    if by_position:
        span = zc if h == 0 else 2 * n_ctx - 1 - zc
        return pl.multiple_of((span * n_wa + wac) * half, half)
    return pl.multiple_of(((zc * n_wa + wac) * 2 + h) * half, half)


def gather_kernel(n_ctx, n_wa, by_position, kinds, own_ref, *refs):
    pairs = len(kinds)
    srcs, out_ref, dsts = refs[:pairs], refs[pairs], refs[pairs + 1 : 2 * pairs + 1]
    own_sem, send_sem, recv_sem, pair_sem, spread_sem = refs[2 * pairs + 1 :]
    ctx = lax.axis_index("ctx")
    wa = lax.axis_index("wa")
    half = own_ref.shape[0] // 2
    meet_neighbours(ctx, wa, n_ctx, n_wa, SPREAD in kinds)
    sends = []

    def place(zc, wac, h):
        return out_ref.at[pl.ds(piece_row(zc, wac, h, half, n_ctx, n_wa, by_position), half)]

    def copy(src, zc, wac, h, where):
        return pltpu.make_async_remote_copy(
            src_ref=src,
            dst_ref=place(zc, wac, h),
            send_sem=send_sem.at[len(sends)],
            recv_sem=recv_sem.at[(zc * n_wa + wac) * 2 + h],
            device_id=where,
            device_id_type=MESH_ID,
        )

    def send(cond, src, zc, wac, h, where):
        made = copy(src, zc, wac, h, where)
        if cond is None:
            made.start()
        else:
            pl.when(cond)(made.start)
        sends.append((cond, made))

    def arrived(cond, zc, wac, h):
        made = pltpu.make_async_remote_copy(
            src_ref=place(zc, wac, h),
            dst_ref=place(zc, wac, h),
            send_sem=send_sem.at[0],
            recv_sem=recv_sem.at[(zc * n_wa + wac) * 2 + h],
            device_id={"wa": wa ^ 1},
            device_id_type=MESH_ID,
        )
        if cond is None:
            made.wait_recv()
        else:
            pl.when(cond)(made.wait_recv)

    def inside(zc):
        return (zc >= 0) & (zc < n_ctx)

    own_copies = []
    for h in range(2):
        own = own_ref.at[pl.ds(h * half, half)]
        for way in (-1, 1):
            send(inside(ctx + way), own, ctx, wa, h, {"ctx": ctx + way})
        send(None, own, ctx, wa, h, {"wa": wa ^ 2})
        send(None, own, ctx, wa, h, {"wa": wa ^ 1})
        made = pltpu.make_async_copy(own, place(ctx, wa, h), own_sem.at[h])
        made.start()
        own_copies.append(made)
    pair_waits = start_pairs(kinds, srcs, dsts, n_wa, pair_sem, spread_sem)

    def across(k, h):
        for way in (-1, 1) if k else (1,):
            zc = ctx + way * k
            cond = inside(zc) if k else None
            arrived(cond, zc, wa ^ 2, h)
            send(cond, place(zc, wa ^ 2, h), zc, wa ^ 2, h, {"wa": wa ^ 1})

    for k in range(1, n_ctx):
        for h in range(2):
            for way in (-1, 1):
                zc = ctx + way * k
                cond = inside(zc)
                arrived(cond, zc, wa, h)
                piece = place(zc, wa, h)
                send(cond & inside(ctx - way), piece, zc, wa, h, {"ctx": ctx - way})
                send(cond, piece, zc, wa, h, {"wa": wa ^ 2})
                send(cond, piece, zc, wa, h, {"wa": wa ^ 1})
            across(k - 1, h)
    for h in range(2):
        across(n_ctx - 1, h)
    for zc in range(n_ctx):
        for far in (0, 2):
            for h in range(2):
                arrived(None, zc, wa ^ 1 ^ far, h)
    for cond, made in sends:
        if cond is None:
            made.wait_send()
        else:
            pl.when(cond)(made.wait_send)
    for made in own_copies:
        made.wait()
    for wait in pair_waits:
        wait()


def gather_tokens(own, pairs, n_ctx, n_wa, by_position, call_id):
    rows, width = own.shape
    n = n_ctx * n_wa
    kinds = tuple(kind for kind, _ in pairs)
    anywhere = pl.BlockSpec(memory_space=pl.ANY)
    shapes = [jax.ShapeDtypeStruct((rows * n, width), own.dtype)]
    shapes += [jax.ShapeDtypeStruct(pair_shape(*pair), BF16) for pair in pairs]
    return pl.pallas_call(
        partial(gather_kernel, n_ctx, n_wa, by_position, kinds),
        in_specs=[anywhere] * (1 + len(pairs)),
        out_specs=[anywhere] * (1 + len(pairs)),
        out_shape=shapes,
        scratch_shapes=[
            pltpu.SemaphoreType.DMA((2,)),
            pltpu.SemaphoreType.DMA((8 + 12 * (n_ctx - 1) + 2 * (2 * n_ctx - 1),)),
            pltpu.SemaphoreType.DMA((2 * n,)),
            pltpu.SemaphoreType.DMA((max(1, len(pairs)), 2)),
            pltpu.SemaphoreType.DMA((2, n)),
        ],
        compiler_params=pltpu.CompilerParams(collective_id=call_id, has_side_effects=True),
        cost_estimate=LINK_COST,
    )(own, *[array for _, array in pairs])


def scatter_kernel(n_ctx, n_wa, by_position, kinds, part_ref, *refs):
    pairs = len(kinds)
    srcs, out_ref, dsts = refs[:pairs], refs[pairs], refs[pairs + 1 : 2 * pairs + 1]
    s1, s2, s3, send_sem, recv1, recv2, recv3, pair_sem, spread_sem = refs[2 * pairs + 1 :]
    ctx = lax.axis_index("ctx")
    wa = lax.axis_index("wa")
    half = out_ref.shape[0] // 2
    slab = 16
    y = wa // 2
    sibling, across = {"wa": wa ^ 1}, {"wa": wa ^ 2}
    meet_neighbours(ctx, wa, n_ctx, n_wa, SPREAD in kinds)
    pair_waits = start_pairs(kinds, srcs, dsts, n_wa, pair_sem, spread_sem)
    sends = []

    def begin(cond, act):
        if cond is None:
            act()
        else:
            pl.when(cond)(act)

    def mine(zc, wac, h):
        return part_ref.at[pl.ds(piece_row(zc, wac, h, half, n_ctx, n_wa, by_position), half)]

    def copy(src, dst, sem, where):
        made = pltpu.make_async_remote_copy(
            src_ref=src,
            dst_ref=dst,
            send_sem=send_sem.at[len(sends)],
            recv_sem=sem,
            device_id=where,
            device_id_type=MESH_ID,
        )
        return made

    def send(cond, src, dst, sem, where):
        made = copy(src, dst, sem, where)
        begin(cond, made.start)
        sends.append((cond, made))

    def arrived(cond, dst, sem):
        made = pltpu.make_async_remote_copy(
            src_ref=dst,
            dst_ref=dst,
            send_sem=send_sem.at[0],
            recv_sem=sem,
            device_id=sibling,
            device_id_type=MESH_ID,
        )
        begin(cond, made.wait_recv)

    def add_up(dst, dst_row, srcs):
        def step(i, carry):
            at = pl.multiple_of(i * slab, slab)
            total = srcs[0][pl.ds(at, slab), :].astype(F32)
            for src in srcs[1:]:
                total = total + src[pl.ds(at, slab), :].astype(F32)
            dst[pl.ds(pl.multiple_of(dst_row + at, slab), slab), :] = total.astype(dst.dtype)
            return carry

        lax.fori_loop(0, half // slab, step, 0)

    def inside(zc):
        return (zc >= 0) & (zc < n_ctx)

    def index1(zc, yc, h):
        return (zc * 2 + yc) * 2 + h

    def steps():
        for k in range(n_ctx - 1, -1, -1):
            for way in (-1, 1) if k else (1,):
                for h in range(2):
                    zc = ctx + way * k
                    yield k, way, h, zc, (inside(zc) if k else None)

    for other in (1, 0):
        yc = y ^ 1 if other else y
        for k, way, h, zc, cond in steps():
            at = index1(zc, yc, h)
            send(cond, mine(zc, yc * 2 + ((wa & 1) ^ 1), h), s1.at[at], recv1.at[at], sibling)
    for k, way, h, zc, cond in steps():
        at = index1(zc, y ^ 1, h)
        arrived(cond, s1.at[at], recv1.at[at])
        begin(cond, lambda: add_up(s1.at[at], 0, [s1.at[at], mine(zc, wa ^ 2, h)]))
        send(cond, s1.at[at], s2.at[zc * 2 + h], recv2.at[zc * 2 + h], across)
    for k, way, h, zc, cond in steps():
        at = index1(zc, y, h)
        arrived(cond, s1.at[at], recv1.at[at])
        arrived(cond, s2.at[zc * 2 + h], recv2.at[zc * 2 + h])
        base = [mine(zc, wa, h), s1.at[at], s2.at[zc * 2 + h]]
        here = zc * 2 + h
        low, high = here, (n_ctx + zc) * 2 + h
        if k:
            behind = low if way > 0 else high
            more = cond & inside(ctx - way)
            arrived(more, s3.at[behind], recv3.at[behind])
            begin(more, lambda: add_up(s2.at[here], 0, base + [s3.at[behind]]))
            first = cond & jnp.logical_not(inside(ctx - way))
            begin(first, lambda: add_up(s2.at[here], 0, base))
            send(cond, s2.at[here], s3.at[behind], recv3.at[behind], {"ctx": ctx + way})
        else:
            under, over = ctx > 0, ctx < n_ctx - 1
            arrived(under, s3.at[low], recv3.at[low])
            arrived(over, s3.at[high], recv3.at[high])
            ways = [
                (under & over, [s3.at[low], s3.at[high]]),
                (under & jnp.logical_not(over), [s3.at[low]]),
                (over & jnp.logical_not(under), [s3.at[high]]),
            ]
            for take, extra in ways:
                begin(take, lambda extra=extra: add_up(out_ref, h * half, base + extra))
    for cond, made in sends:
        begin(cond, made.wait_send)
    for wait in pair_waits:
        wait()


def scatter_tokens(part, pairs, n_ctx, n_wa, by_position, call_id):
    n = n_ctx * n_wa
    rows, width = part.shape[0] // n, part.shape[1]
    half = rows // 2
    pieces = 2 * (2 * n_ctx - 1)
    kinds = tuple(kind for kind, _ in pairs)
    anywhere = pl.BlockSpec(memory_space=pl.ANY)
    shapes = [jax.ShapeDtypeStruct((rows, width), F32)]
    shapes += [jax.ShapeDtypeStruct(pair_shape(*pair), BF16) for pair in pairs]
    return pl.pallas_call(
        partial(scatter_kernel, n_ctx, n_wa, by_position, kinds),
        in_specs=[pl.BlockSpec(memory_space=pltpu.VMEM)] + [anywhere] * len(pairs),
        out_specs=[pl.BlockSpec(memory_space=pltpu.VMEM)] + [anywhere] * len(pairs),
        out_shape=shapes,
        scratch_shapes=[
            pltpu.VMEM((4 * n_ctx, half, width), BF16),
            pltpu.VMEM((2 * n_ctx, half, width), BF16),
            pltpu.VMEM((4 * n_ctx, half, width), BF16),
            pltpu.SemaphoreType.DMA((4 * pieces,)),
            pltpu.SemaphoreType.DMA((4 * n_ctx,)),
            pltpu.SemaphoreType.DMA((2 * n_ctx,)),
            pltpu.SemaphoreType.DMA((4 * n_ctx,)),
            pltpu.SemaphoreType.DMA((max(1, len(pairs)), 2)),
            pltpu.SemaphoreType.DMA((2, n)),
        ],
        compiler_params=pltpu.CompilerParams(
            collective_id=call_id, has_side_effects=True, vmem_limit_bytes=48 * 2**20
        ),
        cost_estimate=LINK_COST,
    )(part, *[array for _, array in pairs])


def per_device_heads(
    tokens,
    doc_starts,
    out_grad,
    attn_gain,
    w_query,
    w_key,
    w_value,
    q_gain,
    k_gain,
    w_out,
    ffn_gain,
    w_gate,
    w_up,
    w_down,
):
    n_ctx = lax.axis_size("ctx")
    n_wa = lax.axis_size("wa")
    n = n_ctx * n_wa
    tok_rows, width = tokens.shape[1:]
    d_rows = w_query.shape[0]
    stream = tok_rows * n
    ff_cols = FF // n
    per = HD // n
    extra = 16
    swap_dp = [(0, 1), (1, 0)]

    def mm_t(a, b):
        return lax.dot_general(a, b, (((1,), (1,)), ((), ())), preferred_element_type=F32)

    def t_mm(a, b):
        return lax.dot_general(a, b, (((0,), (0,)), ((), ())), preferred_element_type=F32)

    def swap(blocks):
        return lax.all_to_all(blocks, AXES, 0, 0, tiled=True)

    half = d_rows // 2
    dp = lax.axis_index("dp")
    gains_own = jnp.concatenate([attn_gain, ffn_gain, q_gain, k_gain])
    gains_row = jnp.pad(gains_own, (0, extra * 2 * LANES - gains_own.shape[0]))
    attn_cols = pack_attn(w_query, w_key, w_value, gains_row.reshape(extra, 2 * LANES), n)
    x_all, attn_cols = gather_tokens(tokens[0], [(SPREAD, attn_cols)], n_ctx, n_wa, True, 1)
    w_qkv = attn_cols[:, :d_rows].reshape(width, 2 * LANES)
    gains = attn_cols[:, d_rows:].reshape(n, -1).astype(F32)
    attn_gain32 = gains[:, :d_rows].reshape(-1)
    ffn_gain32 = gains[:, d_rows : 2 * d_rows].reshape(-1)
    qgain32 = gains[:, 2 * d_rows : 2 * d_rows + per].reshape(-1)
    kgain32 = gains[:, 2 * d_rows + per : 2 * d_rows + 2 * per].reshape(-1)

    w_gate_b, dy_b, x_all = lax.optimization_barrier((w_gate, out_grad[0], x_all))
    ff_blocks = pack_pair(w_gate_b, w_up, n)
    ff_half = swap(ff_blocks)
    dy_all = lax.all_gather(dy_b, AXES, axis=0, tiled=True)

    x_own = tokens[0].astype(F32)
    cosine, sine = rope_tables(stream)
    head_gain = jnp.concatenate([qgain32, qgain32, kgain32, kgain32]).reshape(1, 2 * LANES)
    n1_all, raw, q_b, kv_b, att, inv, branch_part = attend(
        doc_starts, x_all, attn_gain32.reshape(1, width), w_qkv, head_gain, cosine, sine, w_out
    )
    (branch,) = scatter_tokens(branch_part, [], n_ctx, n_wa, True, 3)
    middle = x_own + branch
    n2_own, n2_back = jax.vjp(rms_norm, middle, ffn_gain32)
    n2_all, ff_other = gather_tokens(
        n2_own.astype(BF16), [(WHOLE, ff_half)], n_ctx, n_wa, False, 2
    )
    down_part, d_n2_part, gu_grad, down_grad = ffn(n2_all, dy_all, ff_half, ff_other, w_down)
    down = lax.psum_scatter(down_part, AXES, scatter_dimension=0, tiled=True).astype(F32)
    layer_out = middle + down
    gu_grad = gu_grad.reshape(n, 2, half, 2 * ff_cols)
    d_n2, gu_other = scatter_tokens(d_n2_part, [(PICK, gu_grad)], n_ctx, n_wa, False, 4)
    gu_mine = lax.dynamic_index_in_dim(gu_grad, dp, 1, keepdims=False)
    gu_sum = (gu_mine.astype(F32) + gu_other.astype(F32)).astype(BF16)
    d_mid_part, _ = n2_back(d_n2)
    d_middle = out_grad[0].astype(F32) + d_mid_part
    db_all, down_other = gather_tokens(
        d_middle.astype(BF16), [(WHOLE, down_grad)], n_ctx, n_wa, True, 5
    )
    gu_sum, db_all = lax.optimization_barrier((gu_sum, db_all))
    gu_rows = swap(gu_sum)
    d_qkv, out_w_grad, head_grad = attend_back(
        doc_starts, db_all, w_out, q_b, kv_b, att, inv, raw, head_gain, cosine, sine
    )
    out_w_other = lax.ppermute(out_w_grad, "dp", swap_dp)
    qkv_grad = t_mm(n1_all, d_qkv).astype(BF16).reshape(n, 2, half, 2 * LANES)
    head_grad = head_grad + lax.ppermute(head_grad, "dp", swap_dp)
    head_row = jnp.concatenate([head_grad, jnp.zeros_like(head_grad)], axis=1).astype(BF16)
    head_row = jnp.concatenate([head_row, jnp.zeros_like(head_row)], axis=0)
    qkv_other = lax.ppermute(
        lax.dynamic_index_in_dim(qkv_grad, 1 - dp, 1, keepdims=False), "dp", swap_dp
    )
    qkv_mine = lax.dynamic_index_in_dim(qkv_grad, dp, 1, keepdims=False)
    qkv_sum = (qkv_mine.astype(F32) + qkv_other.astype(F32)).astype(BF16)
    d_n1_part = mm_t(d_qkv, w_qkv).astype(BF16)
    gu_rows, d_n1_part, qkv_sum = lax.optimization_barrier((gu_rows, d_n1_part, qkv_sum))
    qkv_out = jnp.concatenate(
        [qkv_sum, jnp.broadcast_to(head_row[None], (n,) + head_row.shape)], axis=1
    )
    d_n1, gu_others, qkv_rows = scatter_tokens(
        d_n1_part, [(WHOLE, gu_rows), (SPREAD, qkv_out)], n_ctx, n_wa, True, 6
    )
    out_w_other, d_n1 = lax.optimization_barrier((out_w_other, d_n1))
    _, n1_back = jax.vjp(rms_norm, x_own, attn_gain32)
    d_x_part, _ = n1_back(d_n1)
    input_grad = d_middle + d_x_part

    gate_grad, up_grad, gu_sums = unpack_pair(gu_rows, gu_others, w_gate, w_up)
    qkv_others = lax.ppermute(qkv_rows, "dp", swap_dp)
    q_grad, k_grad, v_grad, attn_sums, head_sums = unpack_attn(
        qkv_rows, qkv_others, w_query, w_key, w_value
    )
    me = lax.axis_index("ctx") * n_wa + lax.axis_index("wa")
    q_gain_grad = head_sums[0, :HD] + head_sums[0, HD:LANES]
    k_gain_grad = head_sums[1, :HD]
    attn_gain_grad = attn_sums[:, 0] / attn_gain.astype(F32)
    ffn_gain_grad = jnp.sum(gu_sums, axis=1) / ffn_gain.astype(F32)
    return (
        layer_out.astype(BF16)[None],
        input_grad.astype(BF16)[None],
        attn_gain_grad,
        q_grad,
        k_grad,
        v_grad,
        lax.dynamic_slice_in_dim(q_gain_grad, me * per, per),
        lax.dynamic_slice_in_dim(k_gain_grad, me * per, per),
        out_w_grad.astype(F32) + out_w_other.astype(F32),
        ffn_gain_grad,
        gate_grad,
        up_grad,
        down_grad.astype(F32) + down_other.astype(F32),
    )


def solution(mesh):
    split = mesh.shape["ctx"] * mesh.shape["wa"]
    by_heads = 2 * split == H
    placed = (
        P("dp", ("ctx", "wa"), None),
        P("dp", None),
        P("dp", ("ctx", "wa"), None),
        P(("ctx", "wa")),
        P(("ctx", "wa"), None),
        P(("ctx", "wa"), None),
        P(("ctx", "wa"), None),
        P(("ctx", "wa")),
        P(("ctx", "wa")),
        P(("ctx", "wa"), None),
        P(("ctx", "wa")),
        P(("ctx", "wa"), None),
        P(("ctx", "wa"), None),
        P(("ctx", "wa"), None),
    )
    return jax.shard_map(
        per_device_heads if by_heads else per_device,
        mesh=mesh,
        in_specs=placed,
        out_specs=(
            P("dp", ("ctx", "wa"), None),
            P("dp", ("ctx", "wa"), None),
            P(("ctx", "wa")),
            P(("ctx", "wa"), None),
            P(("ctx", "wa"), None),
            P(("ctx", "wa"), None),
            P(("ctx", "wa")),
            P(("ctx", "wa")),
            P(("ctx", "wa"), None),
            P(("ctx", "wa")),
            P(("ctx", "wa"), None),
            P(("ctx", "wa"), None),
            P(("ctx", "wa"), None),
        ),
        check_vma=False,
    )
```

```python
from functools import partial

import jax
import jax.numpy as jnp
import numpy as np
from jax import lax
from jax.experimental import pallas as pl
from jax.experimental.pallas import tpu as pltpu
from jax.sharding import PartitionSpec as P

H = 32
KV = 8
HD = 64
FF = 8192


EPS = 1e-05
THETA = 1000000.0


def stored_positions(index, tok_rows, n_ctx, n_wa):
    device = index // tok_rows
    local = index % tok_rows
    half_rows = tok_rows // 2
    ctx_part = device // n_wa
    wa_part = device % n_wa
    span_idx = jnp.where(local < half_rows, ctx_part, 2 * n_ctx - 1 - ctx_part)
    return span_idx * (half_rows * n_wa) + wa_part * half_rows + local % half_rows


def segments(position, starts):
    return jnp.sum((starts[None, :] <= position[:, None]).astype(jnp.int32), axis=1) - 1


def rms_norm(values, gain):
    return values * lax.rsqrt(jnp.mean(values * values, axis=-1, keepdims=True) + EPS) * gain


def rotate(values, position):
    half_dim = HD // 2
    frequency = THETA ** (-2.0 * jnp.arange(half_dim, dtype=jnp.float32) / HD)
    angles = position.astype(jnp.float32)[:, None] * frequency[None, :]
    cosine = jnp.cos(angles)[:, None, :]
    sine_part = jnp.sin(angles)[:, None, :]
    first_half = values[..., :half_dim]
    second_half = values[..., half_dim:]
    return jnp.concatenate(
        [
            first_half * cosine - second_half * sine_part,
            second_half * cosine + first_half * sine_part,
        ],
        axis=-1,
    )


def prepare(query_raw, key_raw, query_gain, key_gain, position):
    return (
        rotate(rms_norm(query_raw, query_gain), position),
        rotate(rms_norm(key_raw, key_gain), position),
    )


def per_device(
    tokens,
    doc_starts,
    out_grad,
    attn_gain,
    w_query,
    w_key,
    w_value,
    q_gain,
    k_gain,
    w_out,
    ffn_gain,
    w_gate,
    w_up,
    w_down,
):
    n_ctx = lax.axis_size("ctx")
    n_wa = lax.axis_size("wa")
    tok_rows = tokens.shape[1]
    stream_len = tok_rows * n_ctx * n_wa
    key_width = min(1024, stream_len)
    key_blocks = stream_len // key_width
    groups = H // KV
    scale = HD ** (-0.5)
    first_row = (lax.axis_index("ctx") * n_wa + lax.axis_index("wa")) * tok_rows
    own_pos = stored_positions(
        first_row + jnp.arange(tok_rows, dtype=jnp.int32), tok_rows, n_ctx, n_wa
    )
    starts = doc_starts[0]
    own_seg = segments(own_pos, starts)
    key_pos = stored_positions(jnp.arange(stream_len, dtype=jnp.int32), tok_rows, n_ctx, n_wa)
    key_seg = segments(key_pos, starts)
    residual = tokens[0].astype(jnp.float32)
    attn_set = (
        lax.all_gather(attn_gain, ("ctx", "wa"), axis=0, tiled=True),
        lax.all_gather(w_query, ("ctx", "wa"), axis=0, tiled=True),
        lax.all_gather(w_key, ("ctx", "wa"), axis=0, tiled=True),
        lax.all_gather(w_value, ("ctx", "wa"), axis=0, tiled=True),
        lax.all_gather(q_gain, ("ctx", "wa"), axis=0, tiled=True),
        lax.all_gather(k_gain, ("ctx", "wa"), axis=0, tiled=True),
        lax.all_gather(w_out, ("ctx", "wa"), axis=0, tiled=True),
    )
    g_attn, wq_full, wk_full, wv_full, gq_full, gk_full, wo_full = attn_set
    attn_gain32 = g_attn.astype(jnp.float32)
    qgain32 = gq_full.astype(jnp.float32)
    kgain32 = gk_full.astype(jnp.float32)
    normed_one = rms_norm(residual, attn_gain32).astype(jnp.bfloat16)
    query_raw = jnp.dot(normed_one, wq_full, preferred_element_type=jnp.float32).reshape(
        tok_rows, H, HD
    )
    key_raw = jnp.dot(normed_one, wk_full, preferred_element_type=jnp.float32).reshape(
        tok_rows, KV, HD
    )
    value_b = jnp.dot(normed_one, wv_full, preferred_element_type=jnp.float32).astype(jnp.bfloat16)
    query_rot, key_rot = prepare(query_raw, key_raw, qgain32, kgain32, own_pos)
    query_b = query_rot.astype(jnp.bfloat16).reshape(tok_rows, KV, groups, HD)
    key_b = key_rot.astype(jnp.bfloat16).reshape(tok_rows, KV * HD)
    all_keys, all_values = (
        lax.all_gather(key_b, ("ctx", "wa"), axis=0, tiled=True),
        lax.all_gather(value_b, ("ctx", "wa"), axis=0, tiled=True),
    )

    def key_block(keys_in, values_in, block_idx):
        begin = block_idx * key_width
        key_part = lax.dynamic_slice_in_dim(keys_in, begin, key_width, 0).reshape(key_width, KV, HD)
        value_part = lax.dynamic_slice_in_dim(values_in, begin, key_width, 0).reshape(
            key_width, KV, HD
        )
        pos_part = lax.dynamic_slice_in_dim(key_pos, begin, key_width, 0)
        seg_part = lax.dynamic_slice_in_dim(key_seg, begin, key_width, 0)
        scores = (
            jnp.einsum("rkgd,tkd->kgrt", query_b, key_part, preferred_element_type=jnp.float32)
            * scale
        )
        allowed = (
            (seg_part[None, :] == own_seg[:, None]) & (pos_part[None, :] <= own_pos[:, None])
        )[None, None]
        return (scores, allowed, key_part, value_part)

    def stat_step(block_idx, carry):
        row_max, row_total = carry
        scores, allowed, key_part, value_part = key_block(all_keys, all_values, block_idx)
        masked = jnp.where(allowed, scores, -1e30)
        new_max = jnp.maximum(row_max, jnp.max(masked, axis=-1))
        fresh = jnp.sum(jnp.where(allowed, jnp.exp(masked - new_max[..., None]), 0.0), axis=-1)
        return (new_max, row_total * jnp.exp(row_max - new_max) + fresh)

    stat_init = (
        jnp.full((KV, groups, tok_rows), -1e30, jnp.float32),
        jnp.zeros((KV, groups, tok_rows), jnp.float32),
    )
    row_max, row_total = lax.fori_loop(0, key_blocks, stat_step, stat_init)

    def out_step(block_idx, summed):
        scores, allowed, key_part, value_part = key_block(all_keys, all_values, block_idx)
        probability = (
            jnp.where(allowed, jnp.exp(scores - row_max[..., None]), 0.0) / row_total[..., None]
        )
        return summed + jnp.einsum(
            "kgrt,tkd->rkgd",
            probability.astype(jnp.bfloat16),
            value_part,
            preferred_element_type=jnp.float32,
        )

    attended = lax.fori_loop(
        0, key_blocks, out_step, jnp.zeros((tok_rows, KV, groups, HD), jnp.float32)
    )
    attended_b = attended.reshape(tok_rows, H * HD).astype(jnp.bfloat16)
    middle = residual + jnp.dot(attended_b, wo_full, preferred_element_type=jnp.float32)
    ffn_set = (
        lax.all_gather(ffn_gain, ("ctx", "wa"), axis=0, tiled=True),
        lax.all_gather(w_gate, ("ctx", "wa"), axis=0, tiled=True),
        lax.all_gather(w_up, ("ctx", "wa"), axis=0, tiled=True),
        lax.all_gather(w_down, ("ctx", "wa"), axis=0, tiled=True),
    )
    g_ffn, wg_full, wu_full, wd_full = ffn_set
    ffn_gain32 = g_ffn.astype(jnp.float32)
    normed_two = rms_norm(middle, ffn_gain32).astype(jnp.bfloat16)
    gate_act = jnp.dot(normed_two, wg_full, preferred_element_type=jnp.float32)
    up_act = jnp.dot(normed_two, wu_full, preferred_element_type=jnp.float32)
    sigmoid_gate = jax.nn.sigmoid(gate_act)
    silu_gate = gate_act * sigmoid_gate
    hidden = (silu_gate * up_act).astype(jnp.bfloat16)
    layer_out = (middle + jnp.dot(hidden, wd_full, preferred_element_type=jnp.float32)).astype(
        jnp.bfloat16
    )
    g_ffn, wg_full, wu_full, wd_full = (
        lax.all_gather(ffn_gain, ("ctx", "wa"), axis=0, tiled=True),
        lax.all_gather(w_gate, ("ctx", "wa"), axis=0, tiled=True),
        lax.all_gather(w_up, ("ctx", "wa"), axis=0, tiled=True),
        lax.all_gather(w_down, ("ctx", "wa"), axis=0, tiled=True),
    )
    d_out = out_grad[0].astype(jnp.float32)
    d_out_b = d_out.astype(jnp.bfloat16)
    d_hidden = jnp.einsum("rd,fd->rf", d_out_b, wd_full, preferred_element_type=jnp.float32)
    d_gate = (d_hidden * up_act * (sigmoid_gate * (1.0 + gate_act * (1.0 - sigmoid_gate)))).astype(
        jnp.bfloat16
    )
    d_up = (d_hidden * silu_gate).astype(jnp.bfloat16)
    d_normed_two = jnp.einsum(
        "rf,df->rd", d_gate, wg_full, preferred_element_type=jnp.float32
    ) + jnp.einsum("rf,df->rd", d_up, wu_full, preferred_element_type=jnp.float32)
    norm_out, norm_back = jax.vjp(rms_norm, middle, ffn_gain32)
    d_middle_part, d_ffn_gain = norm_back(d_normed_two)
    d_middle = d_out + d_middle_part
    gate_up = jnp.concatenate([d_gate, d_up], axis=1)
    part_rows = normed_two
    in_grad = lax.psum_scatter(
        jnp.einsum("rc,rf->cf", part_rows, gate_up, preferred_element_type=jnp.float32),
        ("ctx", "wa"),
        scatter_dimension=0,
        tiled=True,
    )
    part_rows = hidden
    down_grad = lax.psum_scatter(
        jnp.einsum("rc,rd->cd", part_rows, d_out_b, preferred_element_type=jnp.float32),
        ("ctx", "wa"),
        scatter_dimension=0,
        tiled=True,
    )
    g_attn, wq_full, wk_full, wv_full, gq_full, gk_full, wo_full = (
        lax.all_gather(attn_gain, ("ctx", "wa"), axis=0, tiled=True),
        lax.all_gather(w_query, ("ctx", "wa"), axis=0, tiled=True),
        lax.all_gather(w_key, ("ctx", "wa"), axis=0, tiled=True),
        lax.all_gather(w_value, ("ctx", "wa"), axis=0, tiled=True),
        lax.all_gather(q_gain, ("ctx", "wa"), axis=0, tiled=True),
        lax.all_gather(k_gain, ("ctx", "wa"), axis=0, tiled=True),
        lax.all_gather(w_out, ("ctx", "wa"), axis=0, tiled=True),
    )
    d_branch = d_middle.astype(jnp.bfloat16)
    wo_grad = jnp.einsum("re,rd->ed", attended_b, d_branch, preferred_element_type=jnp.float32)
    d_attended = jnp.einsum(
        "rd,ed->re", d_branch, wo_full, preferred_element_type=jnp.float32
    ).astype(jnp.bfloat16)
    d_att4 = d_attended.reshape(tok_rows, KV, groups, HD)
    delta = jnp.einsum("rkgd,rkgd->kgr", d_att4.astype(jnp.float32), attended)

    def back_step(d_query, block_idx):
        scores, allowed, key_part, value_part = key_block(all_keys, all_values, block_idx)
        probability = (
            jnp.where(allowed, jnp.exp(scores - row_max[..., None]), 0.0) / row_total[..., None]
        )
        d_prob = jnp.einsum(
            "rkgd,tkd->kgrt", d_att4, value_part, preferred_element_type=jnp.float32
        )
        d_scores = (probability * (d_prob - delta[..., None])).astype(jnp.bfloat16)
        d_query = (
            d_query
            + jnp.einsum("kgrt,tkd->rkgd", d_scores, key_part, preferred_element_type=jnp.float32)
            * scale
        )
        d_key_part = (
            jnp.einsum("kgrt,rkgd->tkd", d_scores, query_b, preferred_element_type=jnp.float32)
            * scale
        )
        d_value_part = jnp.einsum(
            "kgrt,rkgd->tkd",
            probability.astype(jnp.bfloat16),
            d_att4,
            preferred_element_type=jnp.float32,
        )
        return (
            d_query,
            (d_key_part.reshape(key_width, KV * HD), d_value_part.reshape(key_width, KV * HD)),
        )

    d_query, (d_keys, d_values) = lax.scan(
        back_step, jnp.zeros((tok_rows, KV, groups, HD), jnp.float32), jnp.arange(key_blocks)
    )
    d_key_own, d_value_own = (
        lax.psum_scatter(
            d_keys.reshape(stream_len, KV * HD), ("ctx", "wa"), scatter_dimension=0, tiled=True
        ),
        lax.psum_scatter(
            d_values.reshape(stream_len, KV * HD), ("ctx", "wa"), scatter_dimension=0, tiled=True
        ),
    )
    prep_out, prep_back = jax.vjp(
        partial(prepare, position=own_pos), query_raw, key_raw, qgain32, kgain32
    )
    d_query_raw, d_key_raw, d_qgain, d_kgain = prep_back(
        (d_query.reshape(tok_rows, H, HD), d_key_own.reshape(tok_rows, KV, HD))
    )
    dq_b = d_query_raw.reshape(tok_rows, H * HD).astype(jnp.bfloat16)
    dk_b = d_key_raw.reshape(tok_rows, KV * HD).astype(jnp.bfloat16)
    dv_b = d_value_own.astype(jnp.bfloat16)
    d_normed_one = (
        jnp.einsum("re,de->rd", dq_b, wq_full, preferred_element_type=jnp.float32)
        + jnp.einsum("re,de->rd", dk_b, wk_full, preferred_element_type=jnp.float32)
        + jnp.einsum("re,de->rd", dv_b, wv_full, preferred_element_type=jnp.float32)
    )
    first_out, first_back = jax.vjp(rms_norm, residual, attn_gain32)
    d_res_part, d_attn_gain = first_back(d_normed_one)
    input_grad = (d_middle + d_res_part).astype(jnp.bfloat16)
    wq_grad = jnp.einsum("rc,re->ce", normed_one, dq_b, preferred_element_type=jnp.float32)
    wk_grad = jnp.einsum("rc,re->ce", normed_one, dk_b, preferred_element_type=jnp.float32)
    wv_grad = jnp.einsum("rc,re->ce", normed_one, dv_b, preferred_element_type=jnp.float32)
    attn_terms = (d_attn_gain, wq_grad, wk_grad, wv_grad, d_qgain, d_kgain, d_ffn_gain, wo_grad)
    attn_shards = (
        lax.psum_scatter(attn_terms[0], ("ctx", "wa"), scatter_dimension=0, tiled=True),
        lax.psum_scatter(attn_terms[1], ("ctx", "wa"), scatter_dimension=0, tiled=True),
        lax.psum_scatter(attn_terms[2], ("ctx", "wa"), scatter_dimension=0, tiled=True),
        lax.psum_scatter(attn_terms[3], ("ctx", "wa"), scatter_dimension=0, tiled=True),
        lax.psum_scatter(attn_terms[4], ("ctx", "wa"), scatter_dimension=0, tiled=True),
        lax.psum_scatter(attn_terms[5], ("ctx", "wa"), scatter_dimension=0, tiled=True),
        lax.psum_scatter(attn_terms[6], ("ctx", "wa"), scatter_dimension=0, tiled=True),
        lax.psum_scatter(attn_terms[7], ("ctx", "wa"), scatter_dimension=0, tiled=True),
    )
    wo_shard = attn_shards[7]
    summed = (
        lax.psum(attn_shards[0].astype(jnp.bfloat16), "dp").astype(jnp.float32),
        lax.psum(attn_shards[1].astype(jnp.bfloat16), "dp").astype(jnp.float32),
        lax.psum(attn_shards[2].astype(jnp.bfloat16), "dp").astype(jnp.float32),
        lax.psum(attn_shards[3].astype(jnp.bfloat16), "dp").astype(jnp.float32),
        lax.psum(attn_shards[4].astype(jnp.bfloat16), "dp").astype(jnp.float32),
        lax.psum(attn_shards[5].astype(jnp.bfloat16), "dp").astype(jnp.float32),
        lax.psum(wo_shard.astype(jnp.bfloat16), "dp").astype(jnp.float32),
        lax.psum(attn_shards[6].astype(jnp.bfloat16), "dp").astype(jnp.float32),
        lax.psum(in_grad[:, :FF].astype(jnp.bfloat16), "dp").astype(jnp.float32),
        lax.psum(in_grad[:, FF:].astype(jnp.bfloat16), "dp").astype(jnp.float32),
        lax.psum(down_grad.astype(jnp.bfloat16), "dp").astype(jnp.float32),
    )
    return (layer_out[None], input_grad[None]) + tuple(summed)


AXES = ("ctx", "wa")
LANES = 2 * HD
ROWS_BLOCK = 256
FFN_BLOCK = 256
ROOM = 60 * 2**20
LOG2E = 1.4426950408889634
F32 = jnp.float32
BF16 = jnp.bfloat16


def low_key(starts, row):
    first = jnp.int32(0)
    for doc in range(starts.shape[1]):
        begin = starts[0, doc]
        first = jnp.where(begin <= row, begin, first)
    return first


def block_mask(starts, q_begin, k_begin, bq, bk):
    row = q_begin + lax.broadcasted_iota(jnp.int32, (bq, 1), 0)
    first = low_key(starts, row)
    col = k_begin + lax.broadcasted_iota(jnp.int32, (1, bk), 1)
    return (col >= first) & (col <= row)


def rope_tables(stream):
    frequency = np.float32(THETA) ** (-2.0 * np.arange(HD // 2, dtype=np.float32) / np.float32(HD))
    angles = np.arange(stream, dtype=np.float32)[:, None] * frequency.astype(np.float32)[None, :]
    cosine = np.cos(angles.astype(np.float64)).astype(np.float32)
    sine = np.sin(angles.astype(np.float64)).astype(np.float32)
    return np.tile(cosine, (1, 4)), np.tile(np.concatenate([-sine, sine], axis=1), (1, 2))


def lane_ids():
    return lax.broadcasted_iota(jnp.int32, (1, LANES), 1)


def head_mean(values):
    low = jnp.sum(values[:, :HD], axis=1, keepdims=True)
    high = jnp.sum(values[:, HD:], axis=1, keepdims=True)
    return jnp.where(lane_ids() < HD, low, high) * (1.0 / HD)


def swap_halves(values):
    first = lane_ids() % HD < HD // 2
    return jnp.where(
        first, pltpu.roll(values, LANES - HD // 2, 1), pltpu.roll(values, HD // 2, 1)
    )


def norm_rope(raw, gain, cosine, sine):
    scaled = raw * lax.rsqrt(head_mean(raw * raw) + EPS) * gain
    return scaled * cosine + swap_halves(scaled) * sine


def norm_rope_back(grad, raw, gain, cosine, sine):
    inverse = lax.rsqrt(head_mean(raw * raw) + EPS)
    unit = raw * inverse
    d_scaled = grad * cosine + swap_halves(grad * sine)
    d_unit = d_scaled * gain
    return inverse * (d_unit - unit * head_mean(d_unit * unit)), d_scaled * unit


def stack_heads(rows, at_low):
    lanes = lane_ids()
    zero = jnp.zeros_like(rows)
    low, high = jnp.where(lanes < HD, rows, zero), jnp.where(lanes < HD, zero, rows)
    turned = pltpu.roll(high if at_low else low, HD, 1)
    return jnp.concatenate([low, turned] if at_low else [turned, high], axis=0)


def dot(a, b):
    return jnp.dot(a, b, preferred_element_type=F32)


def dot_t(a, b):
    return lax.dot_general(a, b, (((1,), (1,)), ((), ())), preferred_element_type=F32)


def t_dot(a, b):
    return lax.dot_general(a, b, (((0,), (0,)), ((), ())), preferred_element_type=F32)


def join_halves(half, own_ref, other_ref, whole_ref):
    own_row = jnp.where(lax.axis_index("dp") == 0, 0, half)

    def put(j, carry):
        for begin, ref in ((own_row, own_ref), (half - own_row, other_ref)):
            at = pl.multiple_of(2 * half * j + begin, half)
            whole_ref[pl.ds(at, half), :] = ref[j, :half, :]
        return carry

    lax.fori_loop(0, own_ref.shape[0], put, 0)


def attend_kernel(
    starts, x_ref, gain_ref, own_ref, other_ref, head_gain_ref, cos_ref, sin_ref,
    normed_ref, raw_ref, q_ref, kv_ref, att_ref, inv_ref, w_ref, ov_ref,
):
    block = pl.program_id(0)

    @pl.when(block == 0)
    def _():
        join_halves(w_ref.shape[0] // own_ref.shape[0] // 2, own_ref, other_ref, w_ref)

    bq = x_ref.shape[0]
    q_begin = pl.multiple_of(block * bq, bq)
    x = x_ref[...].astype(F32)
    inverse = lax.rsqrt(jnp.mean(x * x, axis=1, keepdims=True) + EPS)
    normed = (x * inverse * gain_ref[...]).astype(BF16)
    normed_ref[...] = normed
    raw = dot(normed, w_ref[...])
    raw_ref[...] = raw
    cosine, sine = cos_ref[...], sin_ref[...]
    q = norm_rope(raw[:, :LANES], head_gain_ref[:, :LANES], cosine, sine)
    q_ref[...] = q.astype(BF16)
    kv_raw = raw[:, LANES:]
    is_key = lane_ids() < HD
    turned = norm_rope(kv_raw, head_gain_ref[:, LANES:], cosine, sine)
    kv_ref[pl.ds(q_begin, bq), :] = jnp.where(is_key, turned, kv_raw).astype(BF16)
    ov_ref[pl.ds(q_begin, bq), :] = jnp.where(is_key, 1.0, kv_raw).astype(BF16)
    q2 = stack_heads(q, True).astype(BF16)

    def step(j, acc):
        k_begin = pl.multiple_of(j * bq, bq)
        s = dot_t(q2, kv_ref[pl.ds(k_begin, bq), :])
        mask = block_mask(starts, q_begin, k_begin, bq, bq)
        p = jnp.exp2(s * (LOG2E * HD**-0.5))
        p = jnp.where(jnp.concatenate([mask, mask], axis=0), p, 0.0).astype(BF16)
        return acc + dot(p, ov_ref[pl.ds(k_begin, bq), :])

    low = low_key(starts, q_begin) // bq
    acc = lax.fori_loop(low, block + 1, step, jnp.zeros((2 * bq, LANES), F32))
    inv = 1.0 / acc[:, :1]
    out = acc * inv
    att = jnp.where(is_key, pltpu.roll(out[:bq], HD, 1), out[bq:]).astype(BF16)
    att_ref[...] = att
    inv_ref[...] = jnp.where(is_key, inv[:bq], inv[bq:])


def attend(starts, x_all, gain, own, other, head_gain, cosine, sine):
    stream, width = x_all.shape
    bq = ROWS_BLOCK

    def rows(cols):
        return pl.BlockSpec((bq, cols), lambda i: (i, 0))

    def whole(shape):
        return pl.BlockSpec(shape, lambda i: (0,) * len(shape), pipeline_mode=pl.Buffered(1))

    return pl.pallas_call(
        attend_kernel,
        grid=(stream // bq,),
        in_specs=[
            pl.BlockSpec(memory_space=pltpu.SMEM),
            rows(width),
            whole((1, width)),
            whole(own.shape),
            whole(own.shape),
            whole((1, 2 * LANES)),
            rows(LANES),
            rows(LANES),
        ],
        out_specs=[
            rows(width),
            rows(2 * LANES),
            rows(LANES),
            pl.BlockSpec((stream, LANES), lambda i: (0, 0)),
            rows(LANES),
            rows(LANES),
            whole((width, 2 * LANES)),
        ],
        out_shape=[
            jax.ShapeDtypeStruct((stream, width), BF16),
            jax.ShapeDtypeStruct((stream, 2 * LANES), F32),
            jax.ShapeDtypeStruct((stream, LANES), BF16),
            jax.ShapeDtypeStruct((stream, LANES), BF16),
            jax.ShapeDtypeStruct((stream, LANES), BF16),
            jax.ShapeDtypeStruct((stream, LANES), F32),
            jax.ShapeDtypeStruct((width, 2 * LANES), BF16),
        ],
        scratch_shapes=[pltpu.VMEM((stream, LANES), BF16)],
        compiler_params=pltpu.CompilerParams(vmem_limit_bytes=ROOM),
        cost_estimate=pl.CostEstimate(flops=2 * 10**10, bytes_accessed=2**25, transcendentals=0),
    )(starts, x_all, gain, own, other, head_gain, cosine, sine)


def attend_back_kernel(
    starts, db_ref, w_out_ref, q_ref, kv_ref, att_ref, inv_ref, raw_ref, head_gain_ref, cos_ref, sin_ref,
    d_ref, w_grad_ref, gain_ref, dkv_ref, w_acc_ref,
):
    block = pl.program_id(0)
    bq = db_ref.shape[0]
    q_begin = pl.multiple_of(block * bq, bq)

    @pl.when(block == 0)
    def _():
        dkv_ref[...] = jnp.zeros_like(dkv_ref)
        w_acc_ref[...] = jnp.zeros_like(w_acc_ref)
        gain_ref[...] = jnp.zeros_like(gain_ref)

    db = db_ref[...]
    att = att_ref[...]
    da = dot_t(db, w_out_ref[...])
    w_acc_ref[...] += t_dot(att, db)
    q2 = stack_heads(q_ref[...].astype(F32), True).astype(BF16)
    da2 = stack_heads(da, False).astype(BF16)
    prod = da.astype(BF16).astype(F32) * att.astype(F32)
    delta = jnp.concatenate(
        [
            jnp.sum(prod[:, :HD], axis=1, keepdims=True),
            jnp.sum(prod[:, HD:], axis=1, keepdims=True),
        ],
        axis=0,
    )
    inv_all = inv_ref[...]
    inv = jnp.concatenate([inv_all[:, :1], inv_all[:, HD : HD + 1]], axis=0)

    def step(j, dq):
        k_begin = pl.multiple_of(j * bq, bq)
        keys = kv_ref[pl.ds(k_begin, bq), :]
        s = dot_t(q2, keys)
        mask = block_mask(starts, q_begin, k_begin, bq, bq)
        p = jnp.exp2(s * (LOG2E * HD**-0.5)) * inv
        p = jnp.where(jnp.concatenate([mask, mask], axis=0), p, 0.0)
        ds = (p * (dot_t(da2, keys) - delta)).astype(BF16)
        dkv_ref[pl.ds(k_begin, bq), :] += t_dot(ds, q2) * HD**-0.5 + t_dot(p.astype(BF16), da2)
        return dq + dot(ds, keys)

    low = low_key(starts, q_begin) // bq
    dq = lax.fori_loop(low, block + 1, step, jnp.zeros((2 * bq, LANES), F32))
    is_key = lane_ids() < HD
    dq = jnp.where(is_key, dq[:bq], pltpu.roll(dq[bq:], HD, 1)) * HD**-0.5
    here = pl.ds(q_begin, bq)
    d_raw, d_gain = norm_rope_back(
        dq, raw_ref[here, :LANES], head_gain_ref[:, :LANES], cos_ref[here, :], sin_ref[here, :]
    )
    d_ref[here, :LANES] = d_raw.astype(BF16)
    gain_ref[0:1, :] += jnp.sum(d_gain, axis=0, keepdims=True)

    @pl.when(block == pl.num_programs(0) - 1)
    def _():
        def finish(j, carry):
            rows = pl.ds(pl.multiple_of(j * bq, bq), bq)
            dkv = dkv_ref[rows, :]
            d_raw, d_gain = norm_rope_back(
                dkv, raw_ref[rows, LANES:], head_gain_ref[:, LANES:], cos_ref[rows, :], sin_ref[rows, :]
            )
            d_ref[rows, LANES:] = jnp.where(is_key, d_raw, dkv).astype(BF16)
            gain_ref[1:2, :] += jnp.sum(d_gain, axis=0, keepdims=True)
            return carry

        lax.fori_loop(0, pl.num_programs(0), finish, 0)
        w_grad_ref[...] = w_acc_ref[...].astype(BF16)


def attend_back(starts, db_all, w_out, q, kv, att, inv, raw, head_gain, cosine, sine):
    stream, width = db_all.shape
    bq = ROWS_BLOCK

    def rows(cols):
        return pl.BlockSpec((bq, cols), lambda i: (i, 0))

    def whole(shape):
        return pl.BlockSpec(shape, lambda i: (0, 0), pipeline_mode=pl.Buffered(1))

    def kept(shape):
        return pl.BlockSpec(shape, lambda i: (0, 0))

    return pl.pallas_call(
        attend_back_kernel,
        grid=(stream // bq,),
        in_specs=[
            pl.BlockSpec(memory_space=pltpu.SMEM),
            rows(width),
            whole(w_out.shape),
            rows(LANES),
            whole((stream, LANES)),
            rows(LANES),
            rows(LANES),
            whole((stream, 2 * LANES)),
            whole((1, 2 * LANES)),
            whole((stream, LANES)),
            whole((stream, LANES)),
        ],
        out_specs=[kept((stream, 2 * LANES)), kept(w_out.shape), kept((8, LANES))],
        out_shape=[
            jax.ShapeDtypeStruct((stream, 2 * LANES), BF16),
            jax.ShapeDtypeStruct(w_out.shape, BF16),
            jax.ShapeDtypeStruct((8, LANES), F32),
        ],
        scratch_shapes=[pltpu.VMEM((stream, LANES), F32), pltpu.VMEM(w_out.shape, F32)],
        compiler_params=pltpu.CompilerParams(vmem_limit_bytes=ROOM),
        cost_estimate=pl.CostEstimate(flops=3 * 10**10, bytes_accessed=2**25, transcendentals=0),
    )(starts, db_all, w_out, q, kv, att, inv, raw, head_gain, cosine, sine)


def ffn_kernel(
    n2_ref, dy_ref, own_ref, other_ref, w_down_ref,
    down_ref, d_n2_ref, gu_grad_ref, down_grad_ref, gu_acc, down_acc, w_gu_ref,
):
    block = pl.program_id(0)

    @pl.when(block == 0)
    def _():
        join_halves(own_ref.shape[1], own_ref, other_ref, w_gu_ref)
        gu_acc[...] = jnp.zeros_like(gu_acc)
        down_acc[...] = jnp.zeros_like(down_acc)

    cols = w_down_ref.shape[0]
    n2, dy = n2_ref[...], dy_ref[...]
    gate_up = dot(n2, w_gu_ref[...])
    gate, up = gate_up[:, :cols], gate_up[:, cols:]
    sig = jax.nn.sigmoid(gate)
    silu = gate * sig
    hidden = (silu * up).astype(BF16)
    down_ref[...] = dot(hidden, w_down_ref[...]).astype(BF16)
    d_hidden = dot_t(dy, w_down_ref[...])
    d_gu = jnp.concatenate(
        [
            (d_hidden * up * (sig * (1.0 + gate * (1.0 - sig)))).astype(BF16),
            (d_hidden * silu).astype(BF16),
        ],
        axis=1,
    )
    d_n2_ref[...] = dot_t(d_gu, w_gu_ref[...]).astype(BF16)
    gu_acc[...] += t_dot(n2, d_gu)
    down_acc[...] += t_dot(hidden, dy)

    @pl.when(block == pl.num_programs(0) - 1)
    def _():
        gu_grad_ref[...] = gu_acc[...].astype(BF16)
        down_grad_ref[...] = down_acc[...].astype(BF16)


def ffn(n2_all, dy_all, own, other, w_down):
    stream, width = n2_all.shape
    gu_shape = (width, own.shape[2])
    bt = FFN_BLOCK
    rows = pl.BlockSpec((bt, width), lambda i: (i, 0))

    def whole(shape):
        return pl.BlockSpec(shape, lambda i: (0,) * len(shape), pipeline_mode=pl.Buffered(1))

    return pl.pallas_call(
        ffn_kernel,
        grid=(stream // bt,),
        in_specs=[rows, rows, whole(own.shape), whole(own.shape), whole(w_down.shape)],
        out_specs=[rows, rows, whole(gu_shape), whole(w_down.shape)],
        out_shape=[
            jax.ShapeDtypeStruct((stream, width), BF16),
            jax.ShapeDtypeStruct((stream, width), BF16),
            jax.ShapeDtypeStruct(gu_shape, BF16),
            jax.ShapeDtypeStruct(w_down.shape, BF16),
        ],
        scratch_shapes=[
            pltpu.VMEM(gu_shape, F32),
            pltpu.VMEM(w_down.shape, F32),
            pltpu.VMEM(gu_shape, BF16),
        ],
        compiler_params=pltpu.CompilerParams(vmem_limit_bytes=ROOM),
        cost_estimate=pl.CostEstimate(
            flops=18 * stream * width * w_down.shape[0], bytes_accessed=2**25, transcendentals=0
        ),
    )(n2_all, dy_all, own, other, w_down)


def unpack_attn_kernel(
    own_ref, other_ref, wq_ref, wk_ref, wv_ref, q_ref, k_ref, v_ref, sum_ref, gains_ref
):
    n, half = own_ref.shape[0], wq_ref.shape[0] // 2
    first = lax.axis_index("dp") == 0
    low = jnp.where(first, 0, half)
    high = half - low
    share = n // KV
    gains_ref[...] = jnp.sum(own_ref[:, half : half + 8, :].astype(F32), axis=0)
    for begin, ref in ((low, own_ref), (high, other_ref)):
        rows = pl.ds(pl.multiple_of(begin, half), half)
        total = jnp.zeros((half, LANES), F32)
        for j in range(n):
            cols = slice(j * LANES, (j + 1) * LANES)
            q = ref[j, :half, :LANES].astype(F32)
            q_ref[rows, cols] = q
            total += q * wq_ref[rows, cols].astype(F32)
        for pair in range(KV // 2):
            cols = slice(pair * LANES, (pair + 1) * LANES)
            heads = []
            for head in (2 * pair, 2 * pair + 1):
                kv = ref[head * share, :half, LANES:].astype(F32)
                for more in range(1, share):
                    kv = kv + ref[head * share + more, :half, LANES:].astype(F32)
                heads.append(kv)
            k = jnp.concatenate([heads[0][:, :HD], heads[1][:, :HD]], axis=1)
            v = jnp.concatenate([heads[0][:, HD:], heads[1][:, HD:]], axis=1)
            k_ref[rows, cols] = k
            v_ref[rows, cols] = v
            total += k * wk_ref[rows, cols].astype(F32) + v * wv_ref[rows, cols].astype(F32)
        sum_ref[rows, :] = total


def unpack_attn(own, other, w_query, w_key, w_value):
    d_rows = w_query.shape[0]
    return pl.pallas_call(
        unpack_attn_kernel,
        out_shape=[
            jax.ShapeDtypeStruct(w_query.shape, F32),
            jax.ShapeDtypeStruct(w_key.shape, F32),
            jax.ShapeDtypeStruct(w_value.shape, F32),
            jax.ShapeDtypeStruct((d_rows, LANES), F32),
            jax.ShapeDtypeStruct((8, 2 * LANES), F32),
        ],
        compiler_params=pltpu.CompilerParams(vmem_limit_bytes=32 * 2**20),
    )(own, other, w_query, w_key, w_value)


def pack_attn_kernel(query_ref, key_ref, value_ref, gains_ref, out_ref):
    n = out_ref.shape[0]
    half = query_ref.shape[0] // 2
    share = n // KV
    rows = pl.ds(pl.multiple_of(lax.axis_index("dp") * half, half), half)
    keys, values = key_ref[rows, :], value_ref[rows, :]
    for j in range(n):
        head = j // share * HD
        out_ref[j, :half, :LANES] = query_ref[rows, j * LANES : (j + 1) * LANES]
        out_ref[j, :half, LANES:] = jnp.concatenate(
            [keys[:, head : head + HD], values[:, head : head + HD]], axis=1
        )
        out_ref[j, half:, :] = gains_ref[...]


def pack_attn(w_query, w_key, w_value, gains, n):
    half = w_query.shape[0] // 2
    return pl.pallas_call(
        pack_attn_kernel,
        out_shape=jax.ShapeDtypeStruct((n, half + gains.shape[0], 2 * LANES), BF16),
    )(w_query, w_key, w_value, gains)


def pack_pair_kernel(dp_ref, gate_ref, up_ref, out_ref):
    count, _, both = out_ref.shape
    cols = both // 2
    for j in range(count):
        out_ref[j, :, :cols] = gate_ref[:, j * cols : (j + 1) * cols]
        out_ref[j, :, cols:] = up_ref[:, j * cols : (j + 1) * cols]


def pack_pair(w_gate, w_up, n):
    half, cols = w_gate.shape[0] // 2, w_gate.shape[1] // n
    count = 4
    part = pl.BlockSpec((half, count * cols), lambda j, dp: (dp[0], j))
    return pl.pallas_call(
        pack_pair_kernel,
        grid_spec=pltpu.PrefetchScalarGridSpec(
            num_scalar_prefetch=1,
            grid=(n // count,),
            in_specs=[part, part],
            out_specs=pl.BlockSpec((count, half, 2 * cols), lambda j, dp: (j, 0, 0)),
        ),
        out_shape=jax.ShapeDtypeStruct((n, half, 2 * cols), BF16),
        compiler_params=pltpu.CompilerParams(vmem_limit_bytes=ROOM),
    )(lax.axis_index("dp").reshape(1), w_gate, w_up)


def unpack_pair_kernel(own_ref, other_ref, gate_w, up_w, gate_ref, up_ref, sum_ref):
    count, half, both = own_ref.shape
    cols = both // 2
    first = lax.axis_index("dp") == 0

    @pl.when(pl.program_id(0) == 0)
    def _():
        sum_ref[...] = jnp.zeros_like(sum_ref)

    own_row = pl.multiple_of(jnp.where(first, 0, half), half)
    for begin, ref in ((own_row, own_ref), (half - own_row, other_ref)):
        rows = pl.ds(pl.multiple_of(begin, half), half)
        total = jnp.zeros((half, 128), F32)
        for j in range(count):
            for at in range(0, cols, 128):
                here = slice(j * cols + at, j * cols + at + 128)
                gate = ref[j, :, at : at + 128].astype(F32)
                up = ref[j, :, cols + at : cols + at + 128].astype(F32)
                gate_ref[rows, here] = gate
                up_ref[rows, here] = up
                total += gate * gate_w[rows, here].astype(F32) + up * up_w[rows, here].astype(F32)
        sum_ref[rows, :] += total


def unpack_pair(own, other, w_gate, w_up):
    n, half, both = own.shape
    count = 4
    block = pl.BlockSpec((count, half, both), lambda j: (j, 0, 0))
    part = pl.BlockSpec((2 * half, count * both // 2), lambda j: (0, j))
    return pl.pallas_call(
        unpack_pair_kernel,
        grid=(n // count,),
        in_specs=[block, block, part, part],
        out_specs=[part, part, pl.BlockSpec((2 * half, 128), lambda j: (0, 0))],
        out_shape=[
            jax.ShapeDtypeStruct(w_gate.shape, F32),
            jax.ShapeDtypeStruct(w_up.shape, F32),
            jax.ShapeDtypeStruct((2 * half, 128), F32),
        ],
        compiler_params=pltpu.CompilerParams(vmem_limit_bytes=32 * 2**20),
    )(own, other, w_gate, w_up)


MESH_ID = pl.DeviceIdType.MESH
LINK_COST = pl.CostEstimate(flops=5 * 10**10, bytes_accessed=2**24, transcendentals=0)


def meet_neighbours(ctx, wa, n_ctx, n_wa, everyone):
    barrier = pltpu.get_barrier_semaphore()

    def greet(where):
        pl.semaphore_signal(barrier, inc=1, device_id=where, device_id_type=MESH_ID)

    greet({"dp": lax.axis_index("dp") ^ 1})
    if everyone:
        n = n_ctx * n_wa

        def step(i, carry):
            other = lax.rem(ctx * n_wa + wa + i, n)
            greet({"ctx": other // n_wa, "wa": lax.rem(other, n_wa)})
            return carry

        lax.fori_loop(1, n, step, 0)
        pl.semaphore_wait(barrier, n)
        return
    greet({"wa": wa ^ 1})
    greet({"wa": wa ^ 2})
    pl.when(ctx > 0)(lambda: greet({"ctx": ctx - 1}))
    pl.when(ctx < n_ctx - 1)(lambda: greet({"ctx": ctx + 1}))
    ends = (ctx == 0).astype(jnp.int32) + (ctx == n_ctx - 1).astype(jnp.int32)
    pl.semaphore_wait(barrier, 5 - ends)


WHOLE, PICK, SPREAD = 0, 1, 2


def pair_outs(kind):
    return 2 if kind == SPREAD else 1


def pair_shape(kind, src):
    if kind == PICK:
        return (src.shape[0],) + src.shape[2:]
    return src.shape


def start_spread(src, dst, n_wa, sems):
    n = src.shape[0]
    me = lax.axis_index("ctx") * n_wa + lax.axis_index("wa")
    keep = pltpu.make_async_copy(src.at[me], dst.at[me], sems.at[0, 0])
    keep.start()

    def made(step, arriving):
        other = lax.rem(me + step, n)
        return pltpu.make_async_remote_copy(
            src_ref=src.at[other],
            dst_ref=dst.at[other if arriving else me],
            send_sem=sems.at[0, step],
            recv_sem=sems.at[1, other if arriving else me],
            device_id={"ctx": other // n_wa, "wa": lax.rem(other, n_wa)},
            device_id_type=MESH_ID,
        )

    def loop(act):
        def step(i, carry):
            act(i)
            return carry

        lax.fori_loop(1, n, step, 0)

    def finish():
        keep.wait()
        loop(lambda i: made(i, True).wait_recv())
        loop(lambda i: made(i, False).wait_send())

    loop(lambda i: made(i, False).start())
    return finish


def start_pairs(kinds, srcs, dsts, n_wa, sems, spread_sems):
    dp = lax.axis_index("dp")
    dsts = list(dsts)
    midway = []

    def exchange(at, src, dst):
        send = pltpu.make_async_remote_copy(
            src_ref=src,
            dst_ref=dst,
            send_sem=sems.at[at, 0],
            recv_sem=sems.at[at, 1],
            device_id={"dp": dp ^ 1},
            device_id_type=MESH_ID,
        )
        send.start()
        return send.wait

    for at, (kind, src) in enumerate(zip(kinds, srcs)):
        dst = dsts.pop(0)
        if kind == SPREAD:
            finish, other = start_spread(src, dst, n_wa, spread_sems), dsts.pop(0)

            def pass_on(at=at, finish=finish, dst=dst, other=other):
                finish()
                return exchange(at, dst, other)

            midway.append(pass_on)
            continue
        if kind == PICK:
            src = src.at[:, dp ^ 1]
        wait = exchange(at, src, dst)
        midway.append(lambda wait=wait: wait)
    return midway


def piece_row(zc, wac, h, half, n_ctx, n_wa, by_position):
    if by_position:
        span = zc if h == 0 else 2 * n_ctx - 1 - zc
        return pl.multiple_of((span * n_wa + wac) * half, half)
    return pl.multiple_of(((zc * n_wa + wac) * 2 + h) * half, half)


def gather_kernel(n_ctx, n_wa, by_position, kinds, own_ref, *refs):
    pairs = len(kinds)
    outs = sum(pair_outs(kind) for kind in kinds)
    srcs, out_ref, dsts = refs[:pairs], refs[pairs], refs[pairs + 1 : pairs + outs + 1]
    own_sem, send_sem, recv_sem, pair_sem, spread_sem = refs[pairs + outs + 1 :]
    ctx = lax.axis_index("ctx")
    wa = lax.axis_index("wa")
    half = own_ref.shape[0] // 2
    meet_neighbours(ctx, wa, n_ctx, n_wa, SPREAD in kinds)
    sends = []

    def place(zc, wac, h):
        return out_ref.at[pl.ds(piece_row(zc, wac, h, half, n_ctx, n_wa, by_position), half)]

    def copy(src, zc, wac, h, where):
        return pltpu.make_async_remote_copy(
            src_ref=src,
            dst_ref=place(zc, wac, h),
            send_sem=send_sem.at[len(sends)],
            recv_sem=recv_sem.at[(zc * n_wa + wac) * 2 + h],
            device_id=where,
            device_id_type=MESH_ID,
        )

    def send(cond, src, zc, wac, h, where):
        made = copy(src, zc, wac, h, where)
        if cond is None:
            made.start()
        else:
            pl.when(cond)(made.start)
        sends.append((cond, made))

    def arrived(cond, zc, wac, h):
        made = pltpu.make_async_remote_copy(
            src_ref=place(zc, wac, h),
            dst_ref=place(zc, wac, h),
            send_sem=send_sem.at[0],
            recv_sem=recv_sem.at[(zc * n_wa + wac) * 2 + h],
            device_id={"wa": wa ^ 1},
            device_id_type=MESH_ID,
        )
        if cond is None:
            made.wait_recv()
        else:
            pl.when(cond)(made.wait_recv)

    def inside(zc):
        return (zc >= 0) & (zc < n_ctx)

    own_copies = []
    for h in range(2):
        own = own_ref.at[pl.ds(h * half, half)]
        for way in (-1, 1):
            send(inside(ctx + way), own, ctx, wa, h, {"ctx": ctx + way})
        send(None, own, ctx, wa, h, {"wa": wa ^ 2})
        send(None, own, ctx, wa, h, {"wa": wa ^ 1})
        made = pltpu.make_async_copy(own, place(ctx, wa, h), own_sem.at[h])
        made.start()
        own_copies.append(made)
    pair_waits = start_pairs(kinds, srcs, dsts, n_wa, pair_sem, spread_sem)

    def across(k, h):
        for way in (-1, 1) if k else (1,):
            zc = ctx + way * k
            cond = inside(zc) if k else None
            arrived(cond, zc, wa ^ 2, h)
            send(cond, place(zc, wa ^ 2, h), zc, wa ^ 2, h, {"wa": wa ^ 1})

    for k in range(1, n_ctx):
        for h in range(2):
            for way in (-1, 1):
                zc = ctx + way * k
                cond = inside(zc)
                arrived(cond, zc, wa, h)
                piece = place(zc, wa, h)
                send(cond & inside(ctx - way), piece, zc, wa, h, {"ctx": ctx - way})
                send(cond, piece, zc, wa, h, {"wa": wa ^ 2})
                send(cond, piece, zc, wa, h, {"wa": wa ^ 1})
            across(k - 1, h)
        if k == 1:
            pair_waits = [wait() for wait in pair_waits]
    for h in range(2):
        across(n_ctx - 1, h)
    for zc in range(n_ctx):
        for far in (0, 2):
            for h in range(2):
                arrived(None, zc, wa ^ 1 ^ far, h)
    for cond, made in sends:
        if cond is None:
            made.wait_send()
        else:
            pl.when(cond)(made.wait_send)
    for made in own_copies:
        made.wait()
    for wait in pair_waits:
        wait()


def gather_tokens(own, pairs, n_ctx, n_wa, by_position, call_id):
    rows, width = own.shape
    n = n_ctx * n_wa
    kinds = tuple(kind for kind, _ in pairs)
    anywhere = pl.BlockSpec(memory_space=pl.ANY)
    shapes = [jax.ShapeDtypeStruct((rows * n, width), own.dtype)]
    shapes += [
        jax.ShapeDtypeStruct(pair_shape(*pair), BF16)
        for pair in pairs
        for _ in range(pair_outs(pair[0]))
    ]
    return pl.pallas_call(
        partial(gather_kernel, n_ctx, n_wa, by_position, kinds),
        in_specs=[anywhere] * (1 + len(pairs)),
        out_specs=[anywhere] * len(shapes),
        out_shape=shapes,
        scratch_shapes=[
            pltpu.SemaphoreType.DMA((2,)),
            pltpu.SemaphoreType.DMA((8 + 12 * (n_ctx - 1) + 2 * (2 * n_ctx - 1),)),
            pltpu.SemaphoreType.DMA((2 * n,)),
            pltpu.SemaphoreType.DMA((max(1, len(pairs)), 2)),
            pltpu.SemaphoreType.DMA((2, n)),
        ],
        compiler_params=pltpu.CompilerParams(collective_id=call_id, has_side_effects=True),
        cost_estimate=LINK_COST,
    )(own, *[array for _, array in pairs])


def scatter_kernel(n_ctx, n_wa, by_position, product, turned, kinds, *refs):
    left_ref, right_ref = refs[0], refs[1]
    refs = refs[2:] if product else refs[1:]
    pairs = len(kinds)
    outs = sum(pair_outs(kind) for kind in kinds)
    srcs, out_ref, dsts = refs[:pairs], refs[pairs], refs[pairs + 1 : pairs + outs + 1]
    refs = refs[pairs + outs + 1 :]
    part_ref = refs[0] if product else left_ref
    s1, s2, s3, send_sem, recv1, recv2, recv3, pair_sem, spread_sem = refs[1 if product else 0 :]
    ctx = lax.axis_index("ctx")
    wa = lax.axis_index("wa")
    half = out_ref.shape[0] // 2
    slab = 16
    y = wa // 2
    sibling, across = {"wa": wa ^ 1}, {"wa": wa ^ 2}
    meet_neighbours(ctx, wa, n_ctx, n_wa, SPREAD in kinds)
    pair_waits = start_pairs(kinds, srcs, dsts, n_wa, pair_sem, spread_sem)
    sends = []

    def begin(cond, act):
        if cond is None:
            act()
        else:
            pl.when(cond)(act)

    def mine(zc, wac, h):
        return part_ref.at[pl.ds(piece_row(zc, wac, h, half, n_ctx, n_wa, by_position), half)]

    def send(src, dst, sem, where):
        made = pltpu.make_async_remote_copy(
            src_ref=src,
            dst_ref=dst,
            send_sem=send_sem.at[len(sends)],
            recv_sem=sem,
            device_id=where,
            device_id_type=MESH_ID,
        )
        made.start()
        sends.append(made)

    def arrived(cond, dst, sem):
        made = pltpu.make_async_remote_copy(
            src_ref=dst,
            dst_ref=dst,
            send_sem=send_sem.at[0],
            recv_sem=sem,
            device_id=sibling,
            device_id_type=MESH_ID,
        )
        begin(cond, made.wait_recv)

    def add_up(dst, dst_row, srcs):
        def step(i, carry):
            at = pl.multiple_of(i * slab, slab)
            total = srcs[0][pl.ds(at, slab), :].astype(F32)
            for src in srcs[1:]:
                total = total + src[pl.ds(at, slab), :].astype(F32)
            dst[pl.ds(pl.multiple_of(dst_row + at, slab), slab), :] = total.astype(dst.dtype)
            return carry

        lax.fori_loop(0, half // slab, step, 0)

    def inside(zc):
        return (zc >= 0) & (zc < n_ctx)

    def index1(zc, yc, h):
        return (zc * 2 + yc) * 2 + h

    def target(i):
        mirrored = 2 * ctx >= n_ctx
        near = jnp.where(mirrored, n_ctx - 1 - ctx, ctx)
        later = i - (n_ctx - 1 - 2 * near)
        step = jnp.maximum(later, 0) // 2
        paired = jnp.where(lax.rem(jnp.maximum(later, 0), 2) == 0, 2 * near - step, step)
        zc = jnp.where(later < 0, n_ctx - 1 - i, paired)
        return jnp.where(mirrored, n_ctx - 1 - zc, zc)

    def multiply(zc):
        count = n_wa * half

        def step(h, carry):
            if by_position:
                begin_row = jnp.where(h == 0, zc, 2 * n_ctx - 1 - zc) * count
            else:
                begin_row = (zc * 2 + h) * count
            rows = pl.ds(pl.multiple_of(begin_row, count), count)
            left = left_ref[rows, :]
            product = dot_t(left, right_ref[...]) if turned else dot(left, right_ref[...])
            part_ref[rows, :] = product.astype(BF16)
            return carry

        lax.fori_loop(0, 2, step, 0)

    def cross(zc):
        for h in range(2):
            at = index1(zc, y ^ 1, h)
            arrived(None, s1.at[at], recv1.at[at])
            add_up(s1.at[at], 0, [s1.at[at], mine(zc, wa ^ 2, h)])
            send(s1.at[at], s2.at[zc * 2 + h], recv2.at[zc * 2 + h], across)

    targets = [target(i) for i in range(n_ctx)]
    for i, zc in enumerate(targets):
        if product:
            multiply(zc)
        for yc in (y ^ 1, y):
            for h in range(2):
                at = index1(zc, yc, h)
                send(mine(zc, yc * 2 + ((wa & 1) ^ 1), h), s1.at[at], recv1.at[at], sibling)
        if i:
            cross(targets[i - 1])
    cross(targets[-1])
    pair_waits = [wait() for wait in pair_waits]
    for i, zc in enumerate(targets):
        for h in range(2):
            at = index1(zc, y, h)
            here = zc * 2 + h
            arrived(None, s1.at[at], recv1.at[at])
            arrived(None, s2.at[here], recv2.at[here])
            base = [mine(zc, wa, h), s1.at[at], s2.at[here]]
            low, high = here, (n_ctx + zc) * 2 + h
            if i < n_ctx - 1:
                way = jnp.where(zc > ctx, 1, -1)
                behind = jnp.where(zc > ctx, low, high)
                more = inside(ctx - way)
                arrived(more, s3.at[behind], recv3.at[behind])
                pl.when(more)(lambda: add_up(s2.at[here], 0, base + [s3.at[behind]]))
                pl.when(jnp.logical_not(more))(lambda: add_up(s2.at[here], 0, base))
                send(s2.at[here], s3.at[behind], recv3.at[behind], {"ctx": ctx + way})
            else:
                under, over = ctx > 0, ctx < n_ctx - 1
                arrived(under, s3.at[low], recv3.at[low])
                arrived(over, s3.at[high], recv3.at[high])
                ways = [
                    (under & over, [s3.at[low], s3.at[high]]),
                    (under & jnp.logical_not(over), [s3.at[low]]),
                    (over & jnp.logical_not(under), [s3.at[high]]),
                ]
                for take, extra in ways:
                    begin(take, lambda extra=extra: add_up(out_ref, h * half, base + extra))
    for made in sends:
        made.wait_send()
    for wait in pair_waits:
        wait()


def scatter_tokens(left, right, turned, pairs, n_ctx, n_wa, by_position, call_id):
    n = n_ctx * n_wa
    rows = left.shape[0] // n
    product = right is not None
    operands = [left, right] if product else [left]
    width = (right.shape[0] if turned else right.shape[1]) if product else left.shape[1]
    half = rows // 2
    kinds = tuple(kind for kind, _ in pairs)
    anywhere = pl.BlockSpec(memory_space=pl.ANY)
    vmem = pl.BlockSpec(memory_space=pltpu.VMEM)
    shapes = [
        jax.ShapeDtypeStruct(pair_shape(*pair), BF16)
        for pair in pairs
        for _ in range(pair_outs(pair[0]))
    ]
    return pl.pallas_call(
        partial(scatter_kernel, n_ctx, n_wa, by_position, product, turned, kinds),
        in_specs=[vmem] * len(operands) + [anywhere] * len(pairs),
        out_specs=[vmem] + [anywhere] * len(shapes),
        out_shape=[jax.ShapeDtypeStruct((rows, width), F32)] + shapes,
        scratch_shapes=[pltpu.VMEM((rows * n, width), BF16)] * product
        + [
            pltpu.VMEM((4 * n_ctx, half, width), BF16),
            pltpu.VMEM((2 * n_ctx, half, width), BF16),
            pltpu.VMEM((4 * n_ctx, half, width), BF16),
            pltpu.SemaphoreType.DMA((8 * n_ctx,)),
            pltpu.SemaphoreType.DMA((4 * n_ctx,)),
            pltpu.SemaphoreType.DMA((2 * n_ctx,)),
            pltpu.SemaphoreType.DMA((4 * n_ctx,)),
            pltpu.SemaphoreType.DMA((max(1, len(pairs)), 2)),
            pltpu.SemaphoreType.DMA((2, n)),
        ],
        compiler_params=pltpu.CompilerParams(
            collective_id=call_id, has_side_effects=True, vmem_limit_bytes=ROOM
        ),
        cost_estimate=LINK_COST,
    )(*operands, *[array for _, array in pairs])


def per_device_heads(
    tokens,
    doc_starts,
    out_grad,
    attn_gain,
    w_query,
    w_key,
    w_value,
    q_gain,
    k_gain,
    w_out,
    ffn_gain,
    w_gate,
    w_up,
    w_down,
):
    n_ctx = lax.axis_size("ctx")
    n_wa = lax.axis_size("wa")
    n = n_ctx * n_wa
    tok_rows, width = tokens.shape[1:]
    d_rows = w_query.shape[0]
    stream = tok_rows * n
    ff_cols = FF // n
    per = HD // n
    extra = 16
    swap_dp = [(0, 1), (1, 0)]

    def t_mm(a, b):
        return lax.dot_general(a, b, (((0,), (0,)), ((), ())), preferred_element_type=F32)

    def swap(blocks):
        return lax.all_to_all(blocks, AXES, 0, 0, tiled=True)

    half = d_rows // 2
    dp = lax.axis_index("dp")
    gains_own = jnp.concatenate([attn_gain, ffn_gain, q_gain, k_gain])
    gains_row = jnp.pad(gains_own, (0, extra * 2 * LANES - gains_own.shape[0]))
    attn_cols = pack_attn(w_query, w_key, w_value, gains_row.reshape(extra, 2 * LANES), n)
    x_all, attn_half, attn_other = gather_tokens(
        tokens[0], [(SPREAD, attn_cols)], n_ctx, n_wa, True, 1
    )
    gains = attn_half[:, half:].reshape(n, -1).astype(F32)
    attn_gain32 = gains[:, :d_rows].reshape(-1)
    ffn_gain32 = gains[:, d_rows : 2 * d_rows].reshape(-1)
    qgain32 = gains[:, 2 * d_rows : 2 * d_rows + per].reshape(-1)
    kgain32 = gains[:, 2 * d_rows + per : 2 * d_rows + 2 * per].reshape(-1)

    w_gate_b, dy_b, x_all = lax.optimization_barrier((w_gate, out_grad[0], x_all))
    ff_blocks = pack_pair(w_gate_b, w_up, n)
    ff_half = swap(ff_blocks)
    dy_all = lax.all_gather(dy_b, AXES, axis=0, tiled=True)

    x_own = tokens[0].astype(F32)
    cosine, sine = rope_tables(stream)
    head_gain = jnp.concatenate([qgain32, qgain32, kgain32, kgain32]).reshape(1, 2 * LANES)
    n1_all, raw, q_b, kv_b, att, inv, w_qkv = attend(
        doc_starts, x_all, attn_gain32.reshape(1, width), attn_half, attn_other, head_gain, cosine, sine
    )
    (branch,) = scatter_tokens(att, w_out, False, [], n_ctx, n_wa, True, 3)
    middle = x_own + branch
    n2_own, n2_back = jax.vjp(rms_norm, middle, ffn_gain32)
    n2_all, ff_other = gather_tokens(
        n2_own.astype(BF16), [(WHOLE, ff_half)], n_ctx, n_wa, False, 2
    )
    down_part, d_n2_part, gu_grad, down_grad = ffn(n2_all, dy_all, ff_half, ff_other, w_down)
    gu_grad = gu_grad.reshape(n, 2, half, 2 * ff_cols)
    d_n2, gu_other = scatter_tokens(d_n2_part, None, False, [(PICK, gu_grad)], n_ctx, n_wa, False, 4)
    gu_mine = lax.dynamic_index_in_dim(gu_grad, dp, 1, keepdims=False)
    gu_sum = (gu_mine.astype(F32) + gu_other.astype(F32)).astype(BF16)
    down_part, d_n2 = lax.optimization_barrier((down_part, d_n2))
    down = lax.psum_scatter(down_part, AXES, scatter_dimension=0, tiled=True).astype(F32)
    layer_out = middle + down
    d_mid_part, _ = n2_back(d_n2)
    d_middle = out_grad[0].astype(F32) + d_mid_part
    db_all, down_other = gather_tokens(
        d_middle.astype(BF16), [(WHOLE, down_grad)], n_ctx, n_wa, True, 5
    )
    gu_sum, db_all = lax.optimization_barrier((gu_sum, db_all))
    gu_rows = swap(gu_sum)
    d_qkv, out_w_grad, head_grad = attend_back(
        doc_starts, db_all, w_out, q_b, kv_b, att, inv, raw, head_gain, cosine, sine
    )
    out_w_other = lax.ppermute(out_w_grad, "dp", swap_dp)
    qkv_grad = t_mm(n1_all, d_qkv).astype(BF16).reshape(n, 2, half, 2 * LANES)
    qkv_other = lax.ppermute(
        lax.dynamic_index_in_dim(qkv_grad, 1 - dp, 1, keepdims=False), "dp", swap_dp
    )
    head_grad = head_grad + lax.ppermute(head_grad, "dp", swap_dp)
    qkv_other, head_grad, gu_rows = lax.optimization_barrier((qkv_other, head_grad, gu_rows))
    gu_others = lax.ppermute(gu_rows, "dp", swap_dp)
    qkv_mine = lax.dynamic_index_in_dim(qkv_grad, dp, 1, keepdims=False)
    qkv_sum = (qkv_mine.astype(F32) + qkv_other.astype(F32)).astype(BF16)
    head_row = jnp.pad(head_grad.astype(BF16), ((0, 8), (0, LANES)))
    qkv_out = jnp.concatenate(
        [qkv_sum, jnp.broadcast_to(head_row[None], (n,) + head_row.shape)], axis=1
    )
    d_n1, qkv_rows, qkv_others = scatter_tokens(
        d_qkv, w_qkv, True, [(SPREAD, qkv_out)], n_ctx, n_wa, True, 6
    )
    out_w_other, gu_others, d_n1 = lax.optimization_barrier((out_w_other, gu_others, d_n1))
    _, n1_back = jax.vjp(rms_norm, x_own, attn_gain32)
    d_x_part, _ = n1_back(d_n1)
    input_grad = d_middle + d_x_part

    gate_grad, up_grad, gu_sums = unpack_pair(gu_rows, gu_others, w_gate, w_up)
    q_grad, k_grad, v_grad, attn_sums, head_sums = unpack_attn(
        qkv_rows, qkv_others, w_query, w_key, w_value
    )
    me = lax.axis_index("ctx") * n_wa + lax.axis_index("wa")
    q_gain_grad = head_sums[0, :HD] + head_sums[0, HD:LANES]
    k_gain_grad = head_sums[1, :HD]
    attn_gain_grad = jnp.sum(attn_sums, axis=1) / attn_gain.astype(F32)
    ffn_gain_grad = jnp.sum(gu_sums, axis=1) / ffn_gain.astype(F32)
    return (
        layer_out.astype(BF16)[None],
        input_grad.astype(BF16)[None],
        attn_gain_grad,
        q_grad,
        k_grad,
        v_grad,
        lax.dynamic_slice_in_dim(q_gain_grad, me * per, per),
        lax.dynamic_slice_in_dim(k_gain_grad, me * per, per),
        out_w_grad.astype(F32) + out_w_other.astype(F32),
        ffn_gain_grad,
        gate_grad,
        up_grad,
        down_grad.astype(F32) + down_other.astype(F32),
    )


def solution(mesh):
    split = mesh.shape["ctx"] * mesh.shape["wa"]
    by_heads = 2 * split == H
    placed = (
        P("dp", ("ctx", "wa"), None),
        P("dp", None),
        P("dp", ("ctx", "wa"), None),
        P(("ctx", "wa")),
        P(("ctx", "wa"), None),
        P(("ctx", "wa"), None),
        P(("ctx", "wa"), None),
        P(("ctx", "wa")),
        P(("ctx", "wa")),
        P(("ctx", "wa"), None),
        P(("ctx", "wa")),
        P(("ctx", "wa"), None),
        P(("ctx", "wa"), None),
        P(("ctx", "wa"), None),
    )
    return jax.shard_map(
        per_device_heads if by_heads else per_device,
        mesh=mesh,
        in_specs=placed,
        out_specs=(
            P("dp", ("ctx", "wa"), None),
            P("dp", ("ctx", "wa"), None),
            P(("ctx", "wa")),
            P(("ctx", "wa"), None),
            P(("ctx", "wa"), None),
            P(("ctx", "wa"), None),
            P(("ctx", "wa")),
            P(("ctx", "wa")),
            P(("ctx", "wa"), None),
            P(("ctx", "wa")),
            P(("ctx", "wa"), None),
            P(("ctx", "wa"), None),
            P(("ctx", "wa"), None),
        ),
        check_vma=False,
    )
```

```python
from functools import partial

import jax
import jax.numpy as jnp
import numpy as np
from jax import lax
from jax.experimental import pallas as pl
from jax.experimental.pallas import tpu as pltpu
from jax.sharding import PartitionSpec as P

H = 32
KV = 8
HD = 64
FF = 8192


EPS = 1e-05
THETA = 1000000.0


def stored_positions(index, tok_rows, n_ctx, n_wa):
    device = index // tok_rows
    local = index % tok_rows
    half_rows = tok_rows // 2
    ctx_part = device // n_wa
    wa_part = device % n_wa
    span_idx = jnp.where(local < half_rows, ctx_part, 2 * n_ctx - 1 - ctx_part)
    return span_idx * (half_rows * n_wa) + wa_part * half_rows + local % half_rows


def segments(position, starts):
    return jnp.sum((starts[None, :] <= position[:, None]).astype(jnp.int32), axis=1) - 1


def rms_norm(values, gain):
    return values * lax.rsqrt(jnp.mean(values * values, axis=-1, keepdims=True) + EPS) * gain


def rotate(values, position):
    half_dim = HD // 2
    frequency = THETA ** (-2.0 * jnp.arange(half_dim, dtype=jnp.float32) / HD)
    angles = position.astype(jnp.float32)[:, None] * frequency[None, :]
    cosine = jnp.cos(angles)[:, None, :]
    sine_part = jnp.sin(angles)[:, None, :]
    first_half = values[..., :half_dim]
    second_half = values[..., half_dim:]
    return jnp.concatenate(
        [
            first_half * cosine - second_half * sine_part,
            second_half * cosine + first_half * sine_part,
        ],
        axis=-1,
    )


def prepare(query_raw, key_raw, query_gain, key_gain, position):
    return (
        rotate(rms_norm(query_raw, query_gain), position),
        rotate(rms_norm(key_raw, key_gain), position),
    )


def per_device(
    tokens,
    doc_starts,
    out_grad,
    attn_gain,
    w_query,
    w_key,
    w_value,
    q_gain,
    k_gain,
    w_out,
    ffn_gain,
    w_gate,
    w_up,
    w_down,
):
    n_ctx = lax.axis_size("ctx")
    n_wa = lax.axis_size("wa")
    tok_rows = tokens.shape[1]
    stream_len = tok_rows * n_ctx * n_wa
    key_width = min(1024, stream_len)
    key_blocks = stream_len // key_width
    groups = H // KV
    scale = HD ** (-0.5)
    first_row = (lax.axis_index("ctx") * n_wa + lax.axis_index("wa")) * tok_rows
    own_pos = stored_positions(
        first_row + jnp.arange(tok_rows, dtype=jnp.int32), tok_rows, n_ctx, n_wa
    )
    starts = doc_starts[0]
    own_seg = segments(own_pos, starts)
    key_pos = stored_positions(jnp.arange(stream_len, dtype=jnp.int32), tok_rows, n_ctx, n_wa)
    key_seg = segments(key_pos, starts)
    residual = tokens[0].astype(jnp.float32)
    attn_set = (
        lax.all_gather(attn_gain, ("ctx", "wa"), axis=0, tiled=True),
        lax.all_gather(w_query, ("ctx", "wa"), axis=0, tiled=True),
        lax.all_gather(w_key, ("ctx", "wa"), axis=0, tiled=True),
        lax.all_gather(w_value, ("ctx", "wa"), axis=0, tiled=True),
        lax.all_gather(q_gain, ("ctx", "wa"), axis=0, tiled=True),
        lax.all_gather(k_gain, ("ctx", "wa"), axis=0, tiled=True),
        lax.all_gather(w_out, ("ctx", "wa"), axis=0, tiled=True),
    )
    g_attn, wq_full, wk_full, wv_full, gq_full, gk_full, wo_full = attn_set
    attn_gain32 = g_attn.astype(jnp.float32)
    qgain32 = gq_full.astype(jnp.float32)
    kgain32 = gk_full.astype(jnp.float32)
    normed_one = rms_norm(residual, attn_gain32).astype(jnp.bfloat16)
    query_raw = jnp.dot(normed_one, wq_full, preferred_element_type=jnp.float32).reshape(
        tok_rows, H, HD
    )
    key_raw = jnp.dot(normed_one, wk_full, preferred_element_type=jnp.float32).reshape(
        tok_rows, KV, HD
    )
    value_b = jnp.dot(normed_one, wv_full, preferred_element_type=jnp.float32).astype(jnp.bfloat16)
    query_rot, key_rot = prepare(query_raw, key_raw, qgain32, kgain32, own_pos)
    query_b = query_rot.astype(jnp.bfloat16).reshape(tok_rows, KV, groups, HD)
    key_b = key_rot.astype(jnp.bfloat16).reshape(tok_rows, KV * HD)
    all_keys, all_values = (
        lax.all_gather(key_b, ("ctx", "wa"), axis=0, tiled=True),
        lax.all_gather(value_b, ("ctx", "wa"), axis=0, tiled=True),
    )

    def key_block(keys_in, values_in, block_idx):
        begin = block_idx * key_width
        key_part = lax.dynamic_slice_in_dim(keys_in, begin, key_width, 0).reshape(key_width, KV, HD)
        value_part = lax.dynamic_slice_in_dim(values_in, begin, key_width, 0).reshape(
            key_width, KV, HD
        )
        pos_part = lax.dynamic_slice_in_dim(key_pos, begin, key_width, 0)
        seg_part = lax.dynamic_slice_in_dim(key_seg, begin, key_width, 0)
        scores = (
            jnp.einsum("rkgd,tkd->kgrt", query_b, key_part, preferred_element_type=jnp.float32)
            * scale
        )
        allowed = (
            (seg_part[None, :] == own_seg[:, None]) & (pos_part[None, :] <= own_pos[:, None])
        )[None, None]
        return (scores, allowed, key_part, value_part)

    def stat_step(block_idx, carry):
        row_max, row_total = carry
        scores, allowed, key_part, value_part = key_block(all_keys, all_values, block_idx)
        masked = jnp.where(allowed, scores, -1e30)
        new_max = jnp.maximum(row_max, jnp.max(masked, axis=-1))
        fresh = jnp.sum(jnp.where(allowed, jnp.exp(masked - new_max[..., None]), 0.0), axis=-1)
        return (new_max, row_total * jnp.exp(row_max - new_max) + fresh)

    stat_init = (
        jnp.full((KV, groups, tok_rows), -1e30, jnp.float32),
        jnp.zeros((KV, groups, tok_rows), jnp.float32),
    )
    row_max, row_total = lax.fori_loop(0, key_blocks, stat_step, stat_init)

    def out_step(block_idx, summed):
        scores, allowed, key_part, value_part = key_block(all_keys, all_values, block_idx)
        probability = (
            jnp.where(allowed, jnp.exp(scores - row_max[..., None]), 0.0) / row_total[..., None]
        )
        return summed + jnp.einsum(
            "kgrt,tkd->rkgd",
            probability.astype(jnp.bfloat16),
            value_part,
            preferred_element_type=jnp.float32,
        )

    attended = lax.fori_loop(
        0, key_blocks, out_step, jnp.zeros((tok_rows, KV, groups, HD), jnp.float32)
    )
    attended_b = attended.reshape(tok_rows, H * HD).astype(jnp.bfloat16)
    middle = residual + jnp.dot(attended_b, wo_full, preferred_element_type=jnp.float32)
    ffn_set = (
        lax.all_gather(ffn_gain, ("ctx", "wa"), axis=0, tiled=True),
        lax.all_gather(w_gate, ("ctx", "wa"), axis=0, tiled=True),
        lax.all_gather(w_up, ("ctx", "wa"), axis=0, tiled=True),
        lax.all_gather(w_down, ("ctx", "wa"), axis=0, tiled=True),
    )
    g_ffn, wg_full, wu_full, wd_full = ffn_set
    ffn_gain32 = g_ffn.astype(jnp.float32)
    normed_two = rms_norm(middle, ffn_gain32).astype(jnp.bfloat16)
    gate_act = jnp.dot(normed_two, wg_full, preferred_element_type=jnp.float32)
    up_act = jnp.dot(normed_two, wu_full, preferred_element_type=jnp.float32)
    sigmoid_gate = jax.nn.sigmoid(gate_act)
    silu_gate = gate_act * sigmoid_gate
    hidden = (silu_gate * up_act).astype(jnp.bfloat16)
    layer_out = (middle + jnp.dot(hidden, wd_full, preferred_element_type=jnp.float32)).astype(
        jnp.bfloat16
    )
    g_ffn, wg_full, wu_full, wd_full = (
        lax.all_gather(ffn_gain, ("ctx", "wa"), axis=0, tiled=True),
        lax.all_gather(w_gate, ("ctx", "wa"), axis=0, tiled=True),
        lax.all_gather(w_up, ("ctx", "wa"), axis=0, tiled=True),
        lax.all_gather(w_down, ("ctx", "wa"), axis=0, tiled=True),
    )
    d_out = out_grad[0].astype(jnp.float32)
    d_out_b = d_out.astype(jnp.bfloat16)
    d_hidden = jnp.einsum("rd,fd->rf", d_out_b, wd_full, preferred_element_type=jnp.float32)
    d_gate = (d_hidden * up_act * (sigmoid_gate * (1.0 + gate_act * (1.0 - sigmoid_gate)))).astype(
        jnp.bfloat16
    )
    d_up = (d_hidden * silu_gate).astype(jnp.bfloat16)
    d_normed_two = jnp.einsum(
        "rf,df->rd", d_gate, wg_full, preferred_element_type=jnp.float32
    ) + jnp.einsum("rf,df->rd", d_up, wu_full, preferred_element_type=jnp.float32)
    norm_out, norm_back = jax.vjp(rms_norm, middle, ffn_gain32)
    d_middle_part, d_ffn_gain = norm_back(d_normed_two)
    d_middle = d_out + d_middle_part
    gate_up = jnp.concatenate([d_gate, d_up], axis=1)
    part_rows = normed_two
    in_grad = lax.psum_scatter(
        jnp.einsum("rc,rf->cf", part_rows, gate_up, preferred_element_type=jnp.float32),
        ("ctx", "wa"),
        scatter_dimension=0,
        tiled=True,
    )
    part_rows = hidden
    down_grad = lax.psum_scatter(
        jnp.einsum("rc,rd->cd", part_rows, d_out_b, preferred_element_type=jnp.float32),
        ("ctx", "wa"),
        scatter_dimension=0,
        tiled=True,
    )
    g_attn, wq_full, wk_full, wv_full, gq_full, gk_full, wo_full = (
        lax.all_gather(attn_gain, ("ctx", "wa"), axis=0, tiled=True),
        lax.all_gather(w_query, ("ctx", "wa"), axis=0, tiled=True),
        lax.all_gather(w_key, ("ctx", "wa"), axis=0, tiled=True),
        lax.all_gather(w_value, ("ctx", "wa"), axis=0, tiled=True),
        lax.all_gather(q_gain, ("ctx", "wa"), axis=0, tiled=True),
        lax.all_gather(k_gain, ("ctx", "wa"), axis=0, tiled=True),
        lax.all_gather(w_out, ("ctx", "wa"), axis=0, tiled=True),
    )
    d_branch = d_middle.astype(jnp.bfloat16)
    wo_grad = jnp.einsum("re,rd->ed", attended_b, d_branch, preferred_element_type=jnp.float32)
    d_attended = jnp.einsum(
        "rd,ed->re", d_branch, wo_full, preferred_element_type=jnp.float32
    ).astype(jnp.bfloat16)
    d_att4 = d_attended.reshape(tok_rows, KV, groups, HD)
    delta = jnp.einsum("rkgd,rkgd->kgr", d_att4.astype(jnp.float32), attended)

    def back_step(d_query, block_idx):
        scores, allowed, key_part, value_part = key_block(all_keys, all_values, block_idx)
        probability = (
            jnp.where(allowed, jnp.exp(scores - row_max[..., None]), 0.0) / row_total[..., None]
        )
        d_prob = jnp.einsum(
            "rkgd,tkd->kgrt", d_att4, value_part, preferred_element_type=jnp.float32
        )
        d_scores = (probability * (d_prob - delta[..., None])).astype(jnp.bfloat16)
        d_query = (
            d_query
            + jnp.einsum("kgrt,tkd->rkgd", d_scores, key_part, preferred_element_type=jnp.float32)
            * scale
        )
        d_key_part = (
            jnp.einsum("kgrt,rkgd->tkd", d_scores, query_b, preferred_element_type=jnp.float32)
            * scale
        )
        d_value_part = jnp.einsum(
            "kgrt,rkgd->tkd",
            probability.astype(jnp.bfloat16),
            d_att4,
            preferred_element_type=jnp.float32,
        )
        return (
            d_query,
            (d_key_part.reshape(key_width, KV * HD), d_value_part.reshape(key_width, KV * HD)),
        )

    d_query, (d_keys, d_values) = lax.scan(
        back_step, jnp.zeros((tok_rows, KV, groups, HD), jnp.float32), jnp.arange(key_blocks)
    )
    d_key_own, d_value_own = (
        lax.psum_scatter(
            d_keys.reshape(stream_len, KV * HD), ("ctx", "wa"), scatter_dimension=0, tiled=True
        ),
        lax.psum_scatter(
            d_values.reshape(stream_len, KV * HD), ("ctx", "wa"), scatter_dimension=0, tiled=True
        ),
    )
    prep_out, prep_back = jax.vjp(
        partial(prepare, position=own_pos), query_raw, key_raw, qgain32, kgain32
    )
    d_query_raw, d_key_raw, d_qgain, d_kgain = prep_back(
        (d_query.reshape(tok_rows, H, HD), d_key_own.reshape(tok_rows, KV, HD))
    )
    dq_b = d_query_raw.reshape(tok_rows, H * HD).astype(jnp.bfloat16)
    dk_b = d_key_raw.reshape(tok_rows, KV * HD).astype(jnp.bfloat16)
    dv_b = d_value_own.astype(jnp.bfloat16)
    d_normed_one = (
        jnp.einsum("re,de->rd", dq_b, wq_full, preferred_element_type=jnp.float32)
        + jnp.einsum("re,de->rd", dk_b, wk_full, preferred_element_type=jnp.float32)
        + jnp.einsum("re,de->rd", dv_b, wv_full, preferred_element_type=jnp.float32)
    )
    first_out, first_back = jax.vjp(rms_norm, residual, attn_gain32)
    d_res_part, d_attn_gain = first_back(d_normed_one)
    input_grad = (d_middle + d_res_part).astype(jnp.bfloat16)
    wq_grad = jnp.einsum("rc,re->ce", normed_one, dq_b, preferred_element_type=jnp.float32)
    wk_grad = jnp.einsum("rc,re->ce", normed_one, dk_b, preferred_element_type=jnp.float32)
    wv_grad = jnp.einsum("rc,re->ce", normed_one, dv_b, preferred_element_type=jnp.float32)
    attn_terms = (d_attn_gain, wq_grad, wk_grad, wv_grad, d_qgain, d_kgain, d_ffn_gain, wo_grad)
    attn_shards = (
        lax.psum_scatter(attn_terms[0], ("ctx", "wa"), scatter_dimension=0, tiled=True),
        lax.psum_scatter(attn_terms[1], ("ctx", "wa"), scatter_dimension=0, tiled=True),
        lax.psum_scatter(attn_terms[2], ("ctx", "wa"), scatter_dimension=0, tiled=True),
        lax.psum_scatter(attn_terms[3], ("ctx", "wa"), scatter_dimension=0, tiled=True),
        lax.psum_scatter(attn_terms[4], ("ctx", "wa"), scatter_dimension=0, tiled=True),
        lax.psum_scatter(attn_terms[5], ("ctx", "wa"), scatter_dimension=0, tiled=True),
        lax.psum_scatter(attn_terms[6], ("ctx", "wa"), scatter_dimension=0, tiled=True),
        lax.psum_scatter(attn_terms[7], ("ctx", "wa"), scatter_dimension=0, tiled=True),
    )
    wo_shard = attn_shards[7]
    summed = (
        lax.psum(attn_shards[0].astype(jnp.bfloat16), "dp").astype(jnp.float32),
        lax.psum(attn_shards[1].astype(jnp.bfloat16), "dp").astype(jnp.float32),
        lax.psum(attn_shards[2].astype(jnp.bfloat16), "dp").astype(jnp.float32),
        lax.psum(attn_shards[3].astype(jnp.bfloat16), "dp").astype(jnp.float32),
        lax.psum(attn_shards[4].astype(jnp.bfloat16), "dp").astype(jnp.float32),
        lax.psum(attn_shards[5].astype(jnp.bfloat16), "dp").astype(jnp.float32),
        lax.psum(wo_shard.astype(jnp.bfloat16), "dp").astype(jnp.float32),
        lax.psum(attn_shards[6].astype(jnp.bfloat16), "dp").astype(jnp.float32),
        lax.psum(in_grad[:, :FF].astype(jnp.bfloat16), "dp").astype(jnp.float32),
        lax.psum(in_grad[:, FF:].astype(jnp.bfloat16), "dp").astype(jnp.float32),
        lax.psum(down_grad.astype(jnp.bfloat16), "dp").astype(jnp.float32),
    )
    return (layer_out[None], input_grad[None]) + tuple(summed)


AXES = ("ctx", "wa")
LANES = 2 * HD
ROWS_BLOCK = 256
FFN_BLOCK = 256
ROOM = 60 * 2**20
SIDE_ROWS = 256
LOG2E = 1.4426950408889634
F32 = jnp.float32
BF16 = jnp.bfloat16


def low_key(starts, row):
    first = jnp.int32(0)
    for doc in range(starts.shape[1]):
        begin = starts[0, doc]
        first = jnp.where(begin <= row, begin, first)
    return first


def block_mask(starts, q_begin, k_begin, bq, bk):
    row = q_begin + lax.broadcasted_iota(jnp.int32, (bq, 1), 0)
    first = low_key(starts, row)
    col = k_begin + lax.broadcasted_iota(jnp.int32, (1, bk), 1)
    return (col >= first) & (col <= row)


def rope_tables(stream):
    frequency = np.float32(THETA) ** (-2.0 * np.arange(HD // 2, dtype=np.float32) / np.float32(HD))
    angles = np.arange(stream, dtype=np.float32)[:, None] * frequency.astype(np.float32)[None, :]
    cosine = np.cos(angles.astype(np.float64)).astype(np.float32)
    sine = np.sin(angles.astype(np.float64)).astype(np.float32)
    return np.tile(cosine, (1, 4)), np.tile(np.concatenate([-sine, sine], axis=1), (1, 2))


def lane_ids():
    return lax.broadcasted_iota(jnp.int32, (1, LANES), 1)


def head_mean(values):
    low = jnp.sum(values[:, :HD], axis=1, keepdims=True)
    high = jnp.sum(values[:, HD:], axis=1, keepdims=True)
    return jnp.where(lane_ids() < HD, low, high) * (1.0 / HD)


def swap_halves(values):
    first = lane_ids() % HD < HD // 2
    return jnp.where(
        first, pltpu.roll(values, LANES - HD // 2, 1), pltpu.roll(values, HD // 2, 1)
    )


def norm_rope(raw, gain, cosine, sine):
    scaled = raw * lax.rsqrt(head_mean(raw * raw) + EPS) * gain
    return scaled * cosine + swap_halves(scaled) * sine


def norm_rope_back(grad, raw, gain, cosine, sine):
    inverse = lax.rsqrt(head_mean(raw * raw) + EPS)
    unit = raw * inverse
    d_scaled = grad * cosine + swap_halves(grad * sine)
    d_unit = d_scaled * gain
    return inverse * (d_unit - unit * head_mean(d_unit * unit)), d_scaled * unit


def stack_heads(rows, at_low):
    lanes = lane_ids()
    zero = jnp.zeros_like(rows)
    low, high = jnp.where(lanes < HD, rows, zero), jnp.where(lanes < HD, zero, rows)
    turned = pltpu.roll(high if at_low else low, HD, 1)
    return jnp.concatenate([low, turned] if at_low else [turned, high], axis=0)


def dot(a, b):
    return jnp.dot(a, b, preferred_element_type=F32)


def dot_t(a, b):
    return lax.dot_general(a, b, (((1,), (1,)), ((), ())), preferred_element_type=F32)


def t_dot(a, b):
    return lax.dot_general(a, b, (((0,), (0,)), ((), ())), preferred_element_type=F32)


def join_halves(half, own_ref, other_ref, whole_ref):
    own_row = jnp.where(lax.axis_index("dp") == 0, 0, half)

    def put(j, carry):
        for begin, ref in ((own_row, own_ref), (half - own_row, other_ref)):
            at = pl.multiple_of(2 * half * j + begin, half)
            whole_ref[pl.ds(at, half), :] = ref[j, :half, :]
        return carry

    lax.fori_loop(0, own_ref.shape[0], put, 0)


def attend_kernel(
    starts, x_ref, gain_ref, own_ref, other_ref, head_gain_ref, cos_ref, sin_ref,
    normed_ref, raw_ref, q_ref, kv_ref, att_ref, inv_ref, w_ref, ov_ref,
):
    block = pl.program_id(0)

    @pl.when(block == 0)
    def _():
        join_halves(w_ref.shape[0] // own_ref.shape[0] // 2, own_ref, other_ref, w_ref)

    bq = x_ref.shape[0]
    q_begin = pl.multiple_of(block * bq, bq)
    x = x_ref[...].astype(F32)
    inverse = lax.rsqrt(jnp.mean(x * x, axis=1, keepdims=True) + EPS)
    normed = (x * inverse * gain_ref[...]).astype(BF16)
    normed_ref[...] = normed
    raw = dot(normed, w_ref[...])
    raw_ref[...] = raw
    cosine, sine = cos_ref[...], sin_ref[...]
    q = norm_rope(raw[:, :LANES], head_gain_ref[:, :LANES], cosine, sine)
    q_ref[...] = q.astype(BF16)
    kv_raw = raw[:, LANES:]
    is_key = lane_ids() < HD
    turned = norm_rope(kv_raw, head_gain_ref[:, LANES:], cosine, sine)
    kv_ref[pl.ds(q_begin, bq), :] = jnp.where(is_key, turned, kv_raw).astype(BF16)
    ov_ref[pl.ds(q_begin, bq), :] = jnp.where(is_key, 1.0, kv_raw).astype(BF16)
    q2 = stack_heads(q, True).astype(BF16)

    def step(j, acc):
        k_begin = pl.multiple_of(j * bq, bq)
        s = dot_t(q2, kv_ref[pl.ds(k_begin, bq), :])
        mask = block_mask(starts, q_begin, k_begin, bq, bq)
        p = jnp.exp2(s * (LOG2E * HD**-0.5))
        p = jnp.where(jnp.concatenate([mask, mask], axis=0), p, 0.0).astype(BF16)
        return acc + dot(p, ov_ref[pl.ds(k_begin, bq), :])

    low = low_key(starts, q_begin) // bq
    acc = lax.fori_loop(low, block + 1, step, jnp.zeros((2 * bq, LANES), F32))
    inv = 1.0 / acc[:, :1]
    out = acc * inv
    att = jnp.where(is_key, pltpu.roll(out[:bq], HD, 1), out[bq:]).astype(BF16)
    att_ref[...] = att
    inv_ref[...] = jnp.where(is_key, inv[:bq], inv[bq:])


def attend(starts, x_all, gain, own, other, head_gain, cosine, sine):
    stream, width = x_all.shape
    bq = ROWS_BLOCK

    def rows(cols):
        return pl.BlockSpec((bq, cols), lambda i: (i, 0))

    def whole(shape):
        return pl.BlockSpec(shape, lambda i: (0,) * len(shape), pipeline_mode=pl.Buffered(1))

    return pl.pallas_call(
        attend_kernel,
        grid=(stream // bq,),
        in_specs=[
            pl.BlockSpec(memory_space=pltpu.SMEM),
            rows(width),
            whole((1, width)),
            whole(own.shape),
            whole(own.shape),
            whole((1, 2 * LANES)),
            rows(LANES),
            rows(LANES),
        ],
        out_specs=[
            rows(width),
            rows(2 * LANES),
            rows(LANES),
            pl.BlockSpec((stream, LANES), lambda i: (0, 0)),
            rows(LANES),
            rows(LANES),
            whole((width, 2 * LANES)),
        ],
        out_shape=[
            jax.ShapeDtypeStruct((stream, width), BF16),
            jax.ShapeDtypeStruct((stream, 2 * LANES), F32),
            jax.ShapeDtypeStruct((stream, LANES), BF16),
            jax.ShapeDtypeStruct((stream, LANES), BF16),
            jax.ShapeDtypeStruct((stream, LANES), BF16),
            jax.ShapeDtypeStruct((stream, LANES), F32),
            jax.ShapeDtypeStruct((width, 2 * LANES), BF16),
        ],
        scratch_shapes=[pltpu.VMEM((stream, LANES), BF16)],
        compiler_params=pltpu.CompilerParams(vmem_limit_bytes=ROOM),
        cost_estimate=pl.CostEstimate(flops=2 * 10**10, bytes_accessed=2**25, transcendentals=0),
    )(starts, x_all, gain, own, other, head_gain, cosine, sine)


def attend_back_kernel(
    starts, db_ref, w_out_ref, q_ref, kv_ref, att_ref, inv_ref, raw_ref, head_gain_ref, cos_ref, sin_ref,
    d_ref, w_grad_ref, gain_ref, dkv_ref, w_acc_ref,
):
    block = pl.program_id(0)
    bq = db_ref.shape[0]
    q_begin = pl.multiple_of(block * bq, bq)

    @pl.when(block == 0)
    def _():
        dkv_ref[...] = jnp.zeros_like(dkv_ref)
        w_acc_ref[...] = jnp.zeros_like(w_acc_ref)
        gain_ref[...] = jnp.zeros_like(gain_ref)

    db = db_ref[...]
    att = att_ref[...]
    da = dot_t(db, w_out_ref[...])
    w_acc_ref[...] += t_dot(att, db)
    q2 = stack_heads(q_ref[...].astype(F32), True).astype(BF16)
    da2 = stack_heads(da, False).astype(BF16)
    prod = da.astype(BF16).astype(F32) * att.astype(F32)
    delta = jnp.concatenate(
        [
            jnp.sum(prod[:, :HD], axis=1, keepdims=True),
            jnp.sum(prod[:, HD:], axis=1, keepdims=True),
        ],
        axis=0,
    )
    inv_all = inv_ref[...]
    inv = jnp.concatenate([inv_all[:, :1], inv_all[:, HD : HD + 1]], axis=0)

    def step(j, dq):
        k_begin = pl.multiple_of(j * bq, bq)
        keys = kv_ref[pl.ds(k_begin, bq), :]
        s = dot_t(q2, keys)
        mask = block_mask(starts, q_begin, k_begin, bq, bq)
        p = jnp.exp2(s * (LOG2E * HD**-0.5)) * inv
        p = jnp.where(jnp.concatenate([mask, mask], axis=0), p, 0.0)
        ds = (p * (dot_t(da2, keys) - delta)).astype(BF16)
        dkv_ref[pl.ds(k_begin, bq), :] += t_dot(ds, q2) * HD**-0.5 + t_dot(p.astype(BF16), da2)
        return dq + dot(ds, keys)

    low = low_key(starts, q_begin) // bq
    dq = lax.fori_loop(low, block + 1, step, jnp.zeros((2 * bq, LANES), F32))
    is_key = lane_ids() < HD
    dq = jnp.where(is_key, dq[:bq], pltpu.roll(dq[bq:], HD, 1)) * HD**-0.5
    here = pl.ds(q_begin, bq)
    d_raw, d_gain = norm_rope_back(
        dq, raw_ref[here, :LANES], head_gain_ref[:, :LANES], cos_ref[here, :], sin_ref[here, :]
    )
    d_ref[here, :LANES] = d_raw.astype(BF16)
    gain_ref[0:1, :] += jnp.sum(d_gain, axis=0, keepdims=True)

    @pl.when(block == pl.num_programs(0) - 1)
    def _():
        def finish(j, carry):
            rows = pl.ds(pl.multiple_of(j * bq, bq), bq)
            dkv = dkv_ref[rows, :]
            d_raw, d_gain = norm_rope_back(
                dkv, raw_ref[rows, LANES:], head_gain_ref[:, LANES:], cos_ref[rows, :], sin_ref[rows, :]
            )
            d_ref[rows, LANES:] = jnp.where(is_key, d_raw, dkv).astype(BF16)
            gain_ref[1:2, :] += jnp.sum(d_gain, axis=0, keepdims=True)
            return carry

        lax.fori_loop(0, pl.num_programs(0), finish, 0)
        w_grad_ref[...] = w_acc_ref[...].astype(BF16)


def attend_back(starts, db_all, w_out, q, kv, att, inv, raw, head_gain, cosine, sine):
    stream, width = db_all.shape
    bq = ROWS_BLOCK

    def rows(cols):
        return pl.BlockSpec((bq, cols), lambda i: (i, 0))

    def whole(shape):
        return pl.BlockSpec(shape, lambda i: (0, 0), pipeline_mode=pl.Buffered(1))

    def kept(shape):
        return pl.BlockSpec(shape, lambda i: (0, 0))

    return pl.pallas_call(
        attend_back_kernel,
        grid=(stream // bq,),
        in_specs=[
            pl.BlockSpec(memory_space=pltpu.SMEM),
            rows(width),
            whole(w_out.shape),
            rows(LANES),
            whole((stream, LANES)),
            rows(LANES),
            rows(LANES),
            whole((stream, 2 * LANES)),
            whole((1, 2 * LANES)),
            whole((stream, LANES)),
            whole((stream, LANES)),
        ],
        out_specs=[kept((stream, 2 * LANES)), kept(w_out.shape), kept((8, LANES))],
        out_shape=[
            jax.ShapeDtypeStruct((stream, 2 * LANES), BF16),
            jax.ShapeDtypeStruct(w_out.shape, BF16),
            jax.ShapeDtypeStruct((8, LANES), F32),
        ],
        scratch_shapes=[pltpu.VMEM((stream, LANES), F32), pltpu.VMEM(w_out.shape, F32)],
        compiler_params=pltpu.CompilerParams(vmem_limit_bytes=ROOM),
        cost_estimate=pl.CostEstimate(flops=3 * 10**10, bytes_accessed=2**25, transcendentals=0),
    )(starts, db_all, w_out, q, kv, att, inv, raw, head_gain, cosine, sine)


def ffn_kernel(
    n2_ref, dy_ref, own_ref, other_ref, w_down_ref, hidden_ref, d_gu_ref, gu_grad_ref, w_gu_ref, gu_acc
):
    block = pl.program_id(0)

    @pl.when(block == 0)
    def _():
        join_halves(own_ref.shape[1], own_ref, other_ref, w_gu_ref)
        gu_acc[...] = jnp.zeros_like(gu_acc)

    cols = hidden_ref.shape[1]
    n2 = n2_ref[...]
    gate_up = dot(n2, w_gu_ref[...])
    d_hidden = dot_t(dy_ref[...], w_down_ref[...])
    gate, up = gate_up[:, :cols], gate_up[:, cols:]
    sig = jax.nn.sigmoid(gate)
    silu = gate * sig
    hidden_ref[...] = (silu * up).astype(BF16)
    d_gu = jnp.concatenate(
        [
            (d_hidden * up * (sig * (1.0 + gate * (1.0 - sig)))).astype(BF16),
            (d_hidden * silu).astype(BF16),
        ],
        axis=1,
    )
    d_gu_ref[...] = d_gu
    gu_acc[...] += t_dot(n2, d_gu)

    @pl.when(block == pl.num_programs(0) - 1)
    def _():
        gu_grad_ref[...] = gu_acc[...].astype(BF16)


def ffn(n2_all, dy_all, own, other, w_down):
    stream, width = n2_all.shape
    both = own.shape[2]
    bt = FFN_BLOCK

    def rows(cols):
        return pl.BlockSpec((bt, cols), lambda i: (i, 0))

    def whole(shape):
        return pl.BlockSpec(shape, lambda i: (0,) * len(shape), pipeline_mode=pl.Buffered(1))

    return pl.pallas_call(
        ffn_kernel,
        grid=(stream // bt,),
        in_specs=[rows(width), rows(width), whole(own.shape), whole(own.shape), whole(w_down.shape)],
        out_specs=[rows(both // 2), rows(both), whole((width, both)), whole((width, both))],
        out_shape=[
            jax.ShapeDtypeStruct((stream, both // 2), BF16),
            jax.ShapeDtypeStruct((stream, both), BF16),
            jax.ShapeDtypeStruct((width, both), BF16),
            jax.ShapeDtypeStruct((width, both), BF16),
        ],
        scratch_shapes=[pltpu.VMEM((width, both), F32)],
        compiler_params=pltpu.CompilerParams(vmem_limit_bytes=ROOM),
        cost_estimate=pl.CostEstimate(
            flops=5 * stream * width * both, bytes_accessed=2**25, transcendentals=0
        ),
    )(n2_all, dy_all, own, other, w_down)


def unpack_attn_kernel(
    own_ref, other_ref, wq_ref, wk_ref, wv_ref, q_ref, k_ref, v_ref, sum_ref, gains_ref
):
    n, half = own_ref.shape[0], wq_ref.shape[0] // 2
    first = lax.axis_index("dp") == 0
    low = jnp.where(first, 0, half)
    high = half - low
    share = n // KV
    gains_ref[...] = jnp.sum(own_ref[:, half : half + 8, :].astype(F32), axis=0)
    for begin, ref in ((low, own_ref), (high, other_ref)):
        rows = pl.ds(pl.multiple_of(begin, half), half)
        total = jnp.zeros((half, LANES), F32)
        for j in range(n):
            cols = slice(j * LANES, (j + 1) * LANES)
            q = ref[j, :half, :LANES].astype(F32)
            q_ref[rows, cols] = q
            total += q * wq_ref[rows, cols].astype(F32)
        for pair in range(KV // 2):
            cols = slice(pair * LANES, (pair + 1) * LANES)
            heads = []
            for head in (2 * pair, 2 * pair + 1):
                kv = ref[head * share, :half, LANES:].astype(F32)
                for more in range(1, share):
                    kv = kv + ref[head * share + more, :half, LANES:].astype(F32)
                heads.append(kv)
            k = jnp.concatenate([heads[0][:, :HD], heads[1][:, :HD]], axis=1)
            v = jnp.concatenate([heads[0][:, HD:], heads[1][:, HD:]], axis=1)
            k_ref[rows, cols] = k
            v_ref[rows, cols] = v
            total += k * wk_ref[rows, cols].astype(F32) + v * wv_ref[rows, cols].astype(F32)
        sum_ref[rows, :] = total


def unpack_attn(own, other, w_query, w_key, w_value):
    d_rows = w_query.shape[0]
    return pl.pallas_call(
        unpack_attn_kernel,
        out_shape=[
            jax.ShapeDtypeStruct(w_query.shape, F32),
            jax.ShapeDtypeStruct(w_key.shape, F32),
            jax.ShapeDtypeStruct(w_value.shape, F32),
            jax.ShapeDtypeStruct((d_rows, LANES), F32),
            jax.ShapeDtypeStruct((8, 2 * LANES), F32),
        ],
        compiler_params=pltpu.CompilerParams(vmem_limit_bytes=32 * 2**20),
    )(own, other, w_query, w_key, w_value)


def pack_attn_kernel(query_ref, key_ref, value_ref, gains_ref, out_ref):
    n = out_ref.shape[0]
    half = query_ref.shape[0] // 2
    share = n // KV
    rows = pl.ds(pl.multiple_of(lax.axis_index("dp") * half, half), half)
    keys, values = key_ref[rows, :], value_ref[rows, :]
    for j in range(n):
        head = j // share * HD
        out_ref[j, :half, :LANES] = query_ref[rows, j * LANES : (j + 1) * LANES]
        out_ref[j, :half, LANES:] = jnp.concatenate(
            [keys[:, head : head + HD], values[:, head : head + HD]], axis=1
        )
        out_ref[j, half:, :] = gains_ref[...]


def pack_attn(w_query, w_key, w_value, gains, n):
    half = w_query.shape[0] // 2
    return pl.pallas_call(
        pack_attn_kernel,
        out_shape=jax.ShapeDtypeStruct((n, half + gains.shape[0], 2 * LANES), BF16),
    )(w_query, w_key, w_value, gains)


def unpack_pair_kernel(own_ref, other_ref, gate_w, up_w, gate_ref, up_ref, sum_ref):
    count, half, both = own_ref.shape
    cols = both // 2
    first = lax.axis_index("dp") == 0

    @pl.when(pl.program_id(0) == 0)
    def _():
        sum_ref[...] = jnp.zeros_like(sum_ref)

    own_row = pl.multiple_of(jnp.where(first, 0, half), half)
    for begin, ref in ((own_row, own_ref), (half - own_row, other_ref)):
        rows = pl.ds(pl.multiple_of(begin, half), half)
        total = jnp.zeros((half, 128), F32)
        for j in range(count):
            for at in range(0, cols, 128):
                here = slice(j * cols + at, j * cols + at + 128)
                gate = ref[j, :, at : at + 128].astype(F32)
                up = ref[j, :, cols + at : cols + at + 128].astype(F32)
                gate_ref[rows, here] = gate
                up_ref[rows, here] = up
                total += gate * gate_w[rows, here].astype(F32) + up * up_w[rows, here].astype(F32)
        sum_ref[rows, :] += total


def unpack_pair(own, other, w_gate, w_up):
    n, half, both = own.shape
    count = 4
    block = pl.BlockSpec((count, half, both), lambda j: (j, 0, 0))
    part = pl.BlockSpec((2 * half, count * both // 2), lambda j: (0, j))
    return pl.pallas_call(
        unpack_pair_kernel,
        grid=(n // count,),
        in_specs=[block, block, part, part],
        out_specs=[part, part, pl.BlockSpec((2 * half, 128), lambda j: (0, 0))],
        out_shape=[
            jax.ShapeDtypeStruct(w_gate.shape, F32),
            jax.ShapeDtypeStruct(w_up.shape, F32),
            jax.ShapeDtypeStruct((2 * half, 128), F32),
        ],
        compiler_params=pltpu.CompilerParams(vmem_limit_bytes=32 * 2**20),
    )(own, other, w_gate, w_up)


MESH_ID = pl.DeviceIdType.MESH
LINK_COST = pl.CostEstimate(flops=5 * 10**10, bytes_accessed=2**24, transcendentals=0)


def meet_neighbours(ctx, wa, n_ctx, n_wa, everyone):
    barrier = pltpu.get_barrier_semaphore()

    def greet(where):
        pl.semaphore_signal(barrier, inc=1, device_id=where, device_id_type=MESH_ID)

    greet({"dp": lax.axis_index("dp") ^ 1})
    if everyone:
        n = n_ctx * n_wa

        def step(i, carry):
            other = lax.rem(ctx * n_wa + wa + i, n)
            greet({"ctx": other // n_wa, "wa": lax.rem(other, n_wa)})
            return carry

        lax.fori_loop(1, n, step, 0)
        pl.semaphore_wait(barrier, n)
        return
    greet({"wa": wa ^ 1})
    greet({"wa": wa ^ 2})
    pl.when(ctx > 0)(lambda: greet({"ctx": ctx - 1}))
    pl.when(ctx < n_ctx - 1)(lambda: greet({"ctx": ctx + 1}))
    ends = (ctx == 0).astype(jnp.int32) + (ctx == n_ctx - 1).astype(jnp.int32)
    pl.semaphore_wait(barrier, 5 - ends)


WHOLE, PICK, SPREAD = 0, 1, 2


def pair_outs(kind):
    return 2 if kind == SPREAD else 1


def pair_shape(kind, src):
    if kind == PICK:
        return (src.shape[0],) + src.shape[2:]
    return src.shape


def start_spread(src, dst, n_wa, sems):
    n = src.shape[0]
    me = lax.axis_index("ctx") * n_wa + lax.axis_index("wa")
    keep = pltpu.make_async_copy(src.at[me], dst.at[me], sems.at[0, 0])
    keep.start()

    def made(step, arriving):
        other = lax.rem(me + step, n)
        return pltpu.make_async_remote_copy(
            src_ref=src.at[other],
            dst_ref=dst.at[other if arriving else me],
            send_sem=sems.at[0, step],
            recv_sem=sems.at[1, other if arriving else me],
            device_id={"ctx": other // n_wa, "wa": lax.rem(other, n_wa)},
            device_id_type=MESH_ID,
        )

    def loop(act):
        def step(i, carry):
            act(i)
            return carry

        lax.fori_loop(1, n, step, 0)

    def finish():
        keep.wait()
        loop(lambda i: made(i, True).wait_recv())
        loop(lambda i: made(i, False).wait_send())

    loop(lambda i: made(i, False).start())
    return finish


def start_pairs(kinds, srcs, dsts, n_wa, sems, spread_sems):
    dp = lax.axis_index("dp")
    dsts = list(dsts)
    midway = []

    def exchange(at, src, dst):
        send = pltpu.make_async_remote_copy(
            src_ref=src,
            dst_ref=dst,
            send_sem=sems.at[at, 0],
            recv_sem=sems.at[at, 1],
            device_id={"dp": dp ^ 1},
            device_id_type=MESH_ID,
        )
        send.start()
        return send.wait

    for at, (kind, src) in enumerate(zip(kinds, srcs)):
        dst = dsts.pop(0)
        if kind == SPREAD:
            finish, other = start_spread(src, dst, n_wa, spread_sems), dsts.pop(0)

            def pass_on(at=at, finish=finish, dst=dst, other=other):
                finish()
                return exchange(at, dst, other)

            midway.append(pass_on)
            continue
        if kind == PICK:
            src = src.at[:, dp ^ 1]
        wait = exchange(at, src, dst)
        midway.append(lambda wait=wait: wait)
    return midway


def piece_row(zc, wac, h, half, n_ctx, n_wa, by_position):
    if by_position:
        span = zc if h == 0 else 2 * n_ctx - 1 - zc
        return pl.multiple_of((span * n_wa + wac) * half, half)
    return pl.multiple_of(((zc * n_wa + wac) * 2 + h) * half, half)


def unit_rows(values):
    return lax.rsqrt(jnp.mean(values * values, axis=1, keepdims=True) + EPS)


def norm_back(grad, values, gain):
    inverse = unit_rows(values)
    d_unit = grad * gain
    unit = values * inverse
    return inverse * (d_unit - unit * jnp.mean(d_unit * unit, axis=1, keepdims=True))


def after_attention(total, x, gain):
    middle = x.astype(F32) + total
    return middle, middle * unit_rows(middle) * gain


def after_ffn_back(total, middle, gain, d_out):
    d_middle = d_out.astype(F32) + norm_back(total, middle, gain)
    return d_middle, d_middle


def after_attention_back(total, x, gain, d_middle):
    return (d_middle + norm_back(total, x.astype(F32), gain),)


class PackColumns:
    def __init__(self, w_gate, w_up, n):
        self.operands = [w_gate, w_up]
        half, cols = w_gate.shape[0] // 2, w_gate.shape[1] // n
        self.outs = [jax.ShapeDtypeStruct((n, half, 2 * cols), BF16)]
        self.scratch = [
            pltpu.VMEM((half, w_gate.shape[1]), BF16),
            pltpu.VMEM((half, w_gate.shape[1]), BF16),
            pltpu.VMEM((n, half, 2 * cols), BF16),
            pltpu.SemaphoreType.DMA((3,)),
        ]

    def bind(self, ins, outs, scratch):
        self.rows_v, (self.packed, sem) = scratch[:2], scratch[2:]
        half = self.packed.shape[1]
        rows = pl.ds(pl.multiple_of(lax.axis_index("dp") * half, half), half)
        self.loads = [
            pltpu.make_async_copy(ins[at].at[rows], self.rows_v[at], sem.at[at]) for at in range(2)
        ]
        for load in self.loads:
            load.start()
        self.store = pltpu.make_async_copy(self.packed, outs[0], sem.at[2])
        self.at = 0

    def step(self):
        self.at += 1
        if self.at != 2:
            return
        for load in self.loads:
            load.wait()
        n, _, both = self.packed.shape
        cols = both // 2
        for j in range(n):
            for at in range(2):
                self.packed[j, :, at * cols : (at + 1) * cols] = self.rows_v[at][
                    :, j * cols : (j + 1) * cols
                ]
        self.store.start()

    def finish(self):
        self.store.wait()


class PairSum:
    def __init__(self, halves, other):
        self.operands = [halves, other]
        self.outs = [jax.ShapeDtypeStruct(other.shape, BF16)]
        self.scratch = [pltpu.VMEM(other.shape, BF16)] * 2 + [pltpu.SemaphoreType.DMA((3,))]

    def bind(self, ins, outs, scratch):
        self.mine_v, self.other_v, self.sem = scratch
        mine = ins[0].at[:, lax.axis_index("dp")]
        self.loads = [
            pltpu.make_async_copy(mine, self.mine_v, self.sem.at[0]),
            pltpu.make_async_copy(ins[1], self.other_v, self.sem.at[1]),
        ]
        for load in self.loads:
            load.start()
        self.store = pltpu.make_async_copy(self.mine_v, outs[0], self.sem.at[2])
        self.at = 0

    def step(self):
        self.at += 1
        if self.at != 2:
            return
        for load in self.loads:
            load.wait()

        def add(j, carry):
            total = self.mine_v[j].astype(F32) + self.other_v[j].astype(F32)
            self.mine_v[j] = total.astype(BF16)
            return carry

        lax.fori_loop(0, self.mine_v.shape[0], add, 0)
        self.store.start()

    def finish(self):
        self.store.wait()


class DownProducts:
    def __init__(self, dy, w_down, hidden):
        self.operands = [dy, w_down, hidden]
        self.steps = dy.shape[0] // SIDE_ROWS
        self.outs = [
            jax.ShapeDtypeStruct(dy.shape, BF16),
            jax.ShapeDtypeStruct(w_down.shape, BF16),
        ]
        self.scratch = [
            pltpu.VMEM((2, SIDE_ROWS, dy.shape[1]), BF16),
            pltpu.VMEM((2, SIDE_ROWS, dy.shape[1]), BF16),
            pltpu.VMEM(w_down.shape, BF16),
            pltpu.VMEM(hidden.shape, BF16),
            pltpu.VMEM(w_down.shape, F32),
            pltpu.VMEM(w_down.shape, BF16),
            pltpu.SemaphoreType.DMA((7,)),
        ]

    def bind(self, ins, outs, scratch):
        self.dy, (self.out, self.grad) = ins[0], outs
        self.dy_v, self.stage, self.w_v, self.hidden_v, self.acc, self.grad_v, self.sem = scratch
        self.loads = [
            pltpu.make_async_copy(ins[1], self.w_v, self.sem.at[4]),
            pltpu.make_async_copy(ins[2], self.hidden_v, self.sem.at[5]),
        ]
        for load in self.loads:
            load.start()
        self.load(0).start()
        self.acc[...] = jnp.zeros_like(self.acc)
        self.stored = []
        self.at = 0

    def load(self, g):
        rows = pl.ds(g * SIDE_ROWS, SIDE_ROWS)
        return pltpu.make_async_copy(self.dy.at[rows], self.dy_v.at[g % 2], self.sem.at[g % 2])

    def step(self):
        g = self.at
        if g >= self.steps:
            return
        self.at += 1
        if g == 0:
            for load in self.loads:
                load.wait()
        self.load(g).wait()
        if g + 1 < self.steps:
            self.load(g + 1).start()
        rows = pl.ds(g * SIDE_ROWS, SIDE_ROWS)
        if g >= 2:
            self.stored[g - 2].wait()
        hidden = self.hidden_v[rows, :]
        self.stage[g % 2] = dot(hidden, self.w_v[...]).astype(BF16)
        self.acc[...] += t_dot(hidden, self.dy_v[g % 2])
        store = pltpu.make_async_copy(self.stage.at[g % 2], self.out.at[rows], self.sem.at[2 + g % 2])
        store.start()
        self.stored.append(store)

    def finish(self):
        while self.at < self.steps:
            self.step()
        for store in self.stored[-2:]:
            store.wait()
        self.grad_v[...] = self.acc[...].astype(BF16)
        made = pltpu.make_async_copy(self.grad_v, self.grad, self.sem.at[6])
        made.start()
        made.wait()


def split_side(side, at, refs):
    count = len(side.operands) if side else 0
    return refs[at : at + count], refs[:at] + refs[at + count :]


def gather_kernel(n_ctx, n_wa, by_position, kinds, side, own_ref, *refs):
    pairs = len(kinds)
    outs = sum(pair_outs(kind) for kind in kinds)
    side_in, refs = split_side(side, pairs, refs)
    srcs, out_ref, dsts = refs[:pairs], refs[pairs], refs[pairs + 1 : pairs + outs + 1]
    refs = refs[pairs + outs + 1 :]
    side_out, refs = refs[: len(side.outs) if side else 0], refs[len(side.outs) if side else 0 :]
    own_sem, send_sem, recv_sem, pair_sem, spread_sem = refs[:5]
    ctx = lax.axis_index("ctx")
    wa = lax.axis_index("wa")
    half = own_ref.shape[0] // 2
    meet_neighbours(ctx, wa, n_ctx, n_wa, SPREAD in kinds)
    sends = []

    def place(zc, wac, h):
        return out_ref.at[pl.ds(piece_row(zc, wac, h, half, n_ctx, n_wa, by_position), half)]

    def copy(src, zc, wac, h, where):
        return pltpu.make_async_remote_copy(
            src_ref=src,
            dst_ref=place(zc, wac, h),
            send_sem=send_sem.at[len(sends)],
            recv_sem=recv_sem.at[(zc * n_wa + wac) * 2 + h],
            device_id=where,
            device_id_type=MESH_ID,
        )

    def send(cond, src, zc, wac, h, where):
        made = copy(src, zc, wac, h, where)
        if cond is None:
            made.start()
        else:
            pl.when(cond)(made.start)
        sends.append((cond, made))

    def arrived(cond, zc, wac, h):
        made = pltpu.make_async_remote_copy(
            src_ref=place(zc, wac, h),
            dst_ref=place(zc, wac, h),
            send_sem=send_sem.at[0],
            recv_sem=recv_sem.at[(zc * n_wa + wac) * 2 + h],
            device_id={"wa": wa ^ 1},
            device_id_type=MESH_ID,
        )
        if cond is None:
            made.wait_recv()
        else:
            pl.when(cond)(made.wait_recv)

    def inside(zc):
        return (zc >= 0) & (zc < n_ctx)

    own_copies = []
    for h in range(2):
        own = own_ref.at[pl.ds(h * half, half)]
        for way in (-1, 1):
            send(inside(ctx + way), own, ctx, wa, h, {"ctx": ctx + way})
        send(None, own, ctx, wa, h, {"wa": wa ^ 2})
        send(None, own, ctx, wa, h, {"wa": wa ^ 1})
        made = pltpu.make_async_copy(own, place(ctx, wa, h), own_sem.at[h])
        made.start()
        own_copies.append(made)
    pair_waits = start_pairs(kinds, srcs, dsts, n_wa, pair_sem, spread_sem)
    if side:
        side.bind(side_in, side_out, refs[5:])
        side.step()

    def across(k, h):
        for way in (-1, 1) if k else (1,):
            zc = ctx + way * k
            cond = inside(zc) if k else None
            arrived(cond, zc, wa ^ 2, h)
            send(cond, place(zc, wa ^ 2, h), zc, wa ^ 2, h, {"wa": wa ^ 1})

    for k in range(1, n_ctx):
        for h in range(2):
            for way in (-1, 1):
                zc = ctx + way * k
                cond = inside(zc)
                arrived(cond, zc, wa, h)
                piece = place(zc, wa, h)
                send(cond & inside(ctx - way), piece, zc, wa, h, {"ctx": ctx - way})
                send(cond, piece, zc, wa, h, {"wa": wa ^ 2})
                send(cond, piece, zc, wa, h, {"wa": wa ^ 1})
            across(k - 1, h)
            if side:
                side.step()
        if k == 1:
            pair_waits = [wait() for wait in pair_waits]
    for h in range(2):
        across(n_ctx - 1, h)
    for zc in range(n_ctx):
        for far in (0, 2):
            for h in range(2):
                arrived(None, zc, wa ^ 1 ^ far, h)
    for cond, made in sends:
        if cond is None:
            made.wait_send()
        else:
            pl.when(cond)(made.wait_send)
    for made in own_copies:
        made.wait()
    if side:
        side.finish()
    for wait in pair_waits:
        wait()


def gather_tokens(own, pairs, n_ctx, n_wa, by_position, call_id, side=None):
    more = side.operands if side else []
    rows, width = own.shape
    n = n_ctx * n_wa
    kinds = tuple(kind for kind, _ in pairs)
    anywhere = pl.BlockSpec(memory_space=pl.ANY)
    shapes = [jax.ShapeDtypeStruct((rows * n, width), own.dtype)]
    shapes += [
        jax.ShapeDtypeStruct(pair_shape(*pair), BF16)
        for pair in pairs
        for _ in range(pair_outs(pair[0]))
    ]
    shapes += side.outs if side else []
    return pl.pallas_call(
        partial(gather_kernel, n_ctx, n_wa, by_position, kinds, side),
        in_specs=[anywhere] * (1 + len(pairs) + len(more)),
        out_specs=[anywhere] * len(shapes),
        out_shape=shapes,
        scratch_shapes=[
            pltpu.SemaphoreType.DMA((2,)),
            pltpu.SemaphoreType.DMA((8 + 12 * (n_ctx - 1) + 2 * (2 * n_ctx - 1),)),
            pltpu.SemaphoreType.DMA((2 * n,)),
            pltpu.SemaphoreType.DMA((max(1, len(pairs)), 2)),
            pltpu.SemaphoreType.DMA((2, n)),
        ]
        + (side.scratch if side else []),
        compiler_params=pltpu.CompilerParams(
            collective_id=call_id, has_side_effects=True, vmem_limit_bytes=ROOM if side else None
        ),
        cost_estimate=LINK_COST,
    )(own, *[array for _, array in pairs], *more)


def scatter_kernel(
    n_ctx, n_wa, by_position, turned, kinds, side, finish, count, left_ref, right_ref, *refs
):
    row_ins, refs = refs[:count], refs[count:]
    row_count = 1 if finish is after_attention_back else 2
    pairs = len(kinds)
    outs = sum(pair_outs(kind) for kind in kinds)
    side_in, refs = split_side(side, pairs, refs)
    srcs, refs = refs[:pairs], refs[pairs:]
    row_outs, refs = refs[:row_count], refs[row_count:]
    dsts, refs = refs[:outs], refs[outs:]
    side_out, refs = refs[: len(side.outs) if side else 0], refs[len(side.outs) if side else 0 :]
    part_ref, s1, s2, s3, out_ref, send_sem, recv1, recv2, recv3, pair_sem, spread_sem = refs[:11]
    ctx = lax.axis_index("ctx")
    wa = lax.axis_index("wa")
    half = out_ref.shape[0] // 2
    slab = 16
    y = wa // 2
    sibling, across = {"wa": wa ^ 1}, {"wa": wa ^ 2}
    meet_neighbours(ctx, wa, n_ctx, n_wa, SPREAD in kinds)
    pair_waits = start_pairs(kinds, srcs, dsts, n_wa, pair_sem, spread_sem)
    if side:
        side.bind(side_in, side_out, refs[11:])
    sends = []

    def begin(cond, act):
        if cond is None:
            act()
        else:
            pl.when(cond)(act)

    def mine(zc, wac, h):
        return part_ref.at[pl.ds(piece_row(zc, wac, h, half, n_ctx, n_wa, by_position), half)]

    def send(src, dst, sem, where):
        made = pltpu.make_async_remote_copy(
            src_ref=src,
            dst_ref=dst,
            send_sem=send_sem.at[len(sends)],
            recv_sem=sem,
            device_id=where,
            device_id_type=MESH_ID,
        )
        made.start()
        sends.append(made)

    def arrived(cond, dst, sem):
        made = pltpu.make_async_remote_copy(
            src_ref=dst,
            dst_ref=dst,
            send_sem=send_sem.at[0],
            recv_sem=sem,
            device_id=sibling,
            device_id_type=MESH_ID,
        )
        begin(cond, made.wait_recv)

    def add_up(dst, dst_row, srcs):
        def step(i, carry):
            at = pl.multiple_of(i * slab, slab)
            total = srcs[0][pl.ds(at, slab), :].astype(F32)
            for src in srcs[1:]:
                total = total + src[pl.ds(at, slab), :].astype(F32)
            dst[pl.ds(pl.multiple_of(dst_row + at, slab), slab), :] = total.astype(dst.dtype)
            return carry

        lax.fori_loop(0, half // slab, step, 0)

    def inside(zc):
        return (zc >= 0) & (zc < n_ctx)

    def index1(zc, yc, h):
        return (zc * 2 + yc) * 2 + h

    def target(i):
        mirrored = 2 * ctx >= n_ctx
        near = jnp.where(mirrored, n_ctx - 1 - ctx, ctx)
        later = i - (n_ctx - 1 - 2 * near)
        step = jnp.maximum(later, 0) // 2
        paired = jnp.where(lax.rem(jnp.maximum(later, 0), 2) == 0, 2 * near - step, step)
        zc = jnp.where(later < 0, n_ctx - 1 - i, paired)
        return jnp.where(mirrored, n_ctx - 1 - zc, zc)

    def multiply(zc, yc):
        def rows_of(begin_row, count):
            rows = pl.ds(pl.multiple_of(begin_row, count), count)
            left = left_ref[rows, :]
            product = dot_t(left, right_ref[...]) if turned else dot(left, right_ref[...])
            part_ref[rows, :] = product.astype(BF16)

        if not by_position:
            rows_of((zc * n_wa + yc * 2) * 2 * half, 4 * half)
            return

        def step(h, carry):
            span = jnp.where(h == 0, zc, 2 * n_ctx - 1 - zc)
            rows_of((span * n_wa + yc * 2) * half, 2 * half)
            return carry

        lax.fori_loop(0, 2, step, 0)

    def cross(zc):
        for h in range(2):
            at = index1(zc, y ^ 1, h)
            arrived(None, s1.at[at], recv1.at[at])
            add_up(s1.at[at], 0, [s1.at[at], mine(zc, wa ^ 2, h)])
            send(s1.at[at], s2.at[zc * 2 + h], recv2.at[zc * 2 + h], across)

    targets = [target(i) for i in range(n_ctx)]
    for i, zc in enumerate(targets):
        for yc in (y ^ 1, y):
            multiply(zc, yc)
            for h in range(2):
                at = index1(zc, yc, h)
                send(mine(zc, yc * 2 + ((wa & 1) ^ 1), h), s1.at[at], recv1.at[at], sibling)
        cross(zc)
        if side:
            side.step()
    pair_waits = [wait() for wait in pair_waits]
    for i, zc in enumerate(targets):
        if side and i:
            side.step()
        for h in range(2):
            at = index1(zc, y, h)
            here = zc * 2 + h
            arrived(None, s1.at[at], recv1.at[at])
            arrived(None, s2.at[here], recv2.at[here])
            base = [mine(zc, wa, h), s1.at[at], s2.at[here]]
            low, high = here, (n_ctx + zc) * 2 + h
            if i < n_ctx - 1:
                way = jnp.where(zc > ctx, 1, -1)
                behind = jnp.where(zc > ctx, low, high)
                more = inside(ctx - way)
                arrived(more, s3.at[behind], recv3.at[behind])
                pl.when(more)(lambda: add_up(s2.at[here], 0, base + [s3.at[behind]]))
                pl.when(jnp.logical_not(more))(lambda: add_up(s2.at[here], 0, base))
                send(s2.at[here], s3.at[behind], recv3.at[behind], {"ctx": ctx + way})
            else:
                under, over = ctx > 0, ctx < n_ctx - 1
                arrived(under, s3.at[low], recv3.at[low])
                arrived(over, s3.at[high], recv3.at[high])
                ways = [
                    (under & over, [s3.at[low], s3.at[high]]),
                    (under & jnp.logical_not(over), [s3.at[low]]),
                    (over & jnp.logical_not(under), [s3.at[high]]),
                ]
                for take, extra in ways:
                    begin(take, lambda extra=extra: add_up(out_ref, h * half, base + extra))
    for ref, values in zip(row_outs, finish(out_ref[...], *[ref[...] for ref in row_ins])):
        ref[...] = values.astype(ref.dtype)
    if side:
        side.finish()
    for made in sends:
        made.wait_send()
    for wait in pair_waits:
        wait()


def scatter_tokens(
    left, right, turned, finish, rows_in, pairs, n_ctx, n_wa, by_position, call_id, side=None
):
    n = n_ctx * n_wa
    rows = left.shape[0] // n
    width = right.shape[0] if turned else right.shape[1]
    more = side.operands if side else []
    row_types = [BF16] if finish is after_attention_back else [F32, BF16]
    half = rows // 2
    kinds = tuple(kind for kind, _ in pairs)
    anywhere = pl.BlockSpec(memory_space=pl.ANY)
    vmem = pl.BlockSpec(memory_space=pltpu.VMEM)
    shapes = [
        jax.ShapeDtypeStruct(pair_shape(*pair), BF16)
        for pair in pairs
        for _ in range(pair_outs(pair[0]))
    ]
    shapes += side.outs if side else []
    return pl.pallas_call(
        partial(
            scatter_kernel, n_ctx, n_wa, by_position, turned, kinds, side, finish, len(rows_in)
        ),
        in_specs=[vmem] * (2 + len(rows_in)) + [anywhere] * (len(pairs) + len(more)),
        out_specs=[vmem] * len(row_types) + [anywhere] * len(shapes),
        out_shape=[jax.ShapeDtypeStruct((rows, width), dtype) for dtype in row_types] + shapes,
        scratch_shapes=[
            pltpu.VMEM((rows * n, width), BF16),
            pltpu.VMEM((4 * n_ctx, half, width), BF16),
            pltpu.VMEM((2 * n_ctx, half, width), BF16),
            pltpu.VMEM((4 * n_ctx, half, width), BF16),
            pltpu.VMEM((rows, width), F32),
            pltpu.SemaphoreType.DMA((8 * n_ctx,)),
            pltpu.SemaphoreType.DMA((4 * n_ctx,)),
            pltpu.SemaphoreType.DMA((2 * n_ctx,)),
            pltpu.SemaphoreType.DMA((4 * n_ctx,)),
            pltpu.SemaphoreType.DMA((max(1, len(pairs)), 2)),
            pltpu.SemaphoreType.DMA((2, n)),
        ]
        + (side.scratch if side else []),
        compiler_params=pltpu.CompilerParams(
            collective_id=call_id, has_side_effects=True, vmem_limit_bytes=ROOM
        ),
        cost_estimate=LINK_COST,
    )(left, right, *rows_in, *[array for _, array in pairs], *more)


def per_device_heads(
    tokens,
    doc_starts,
    out_grad,
    attn_gain,
    w_query,
    w_key,
    w_value,
    q_gain,
    k_gain,
    w_out,
    ffn_gain,
    w_gate,
    w_up,
    w_down,
):
    n_ctx = lax.axis_size("ctx")
    n_wa = lax.axis_size("wa")
    n = n_ctx * n_wa
    tok_rows, width = tokens.shape[1:]
    d_rows = w_query.shape[0]
    stream = tok_rows * n
    ff_cols = FF // n
    per = HD // n
    extra = 16
    swap_dp = [(0, 1), (1, 0)]

    def t_mm(a, b):
        return lax.dot_general(a, b, (((0,), (0,)), ((), ())), preferred_element_type=F32)

    def swap(blocks):
        return lax.all_to_all(blocks, AXES, 0, 0, tiled=True)

    half = d_rows // 2
    dp = lax.axis_index("dp")
    gains_own = jnp.concatenate([attn_gain, ffn_gain, q_gain, k_gain])
    gains_row = jnp.pad(gains_own, (0, extra * 2 * LANES - gains_own.shape[0]))
    attn_cols = pack_attn(w_query, w_key, w_value, gains_row.reshape(extra, 2 * LANES), n)
    x_all, attn_half, attn_other, ff_blocks = gather_tokens(
        tokens[0], [(SPREAD, attn_cols)], n_ctx, n_wa, True, 1, PackColumns(w_gate, w_up, n)
    )
    gains = attn_half[:, half:].reshape(n, -1).astype(F32)
    attn_gain32 = gains[:, :d_rows].reshape(-1)
    ffn_gain32 = gains[:, d_rows : 2 * d_rows].reshape(-1)
    qgain32 = gains[:, 2 * d_rows : 2 * d_rows + per].reshape(-1)
    kgain32 = gains[:, 2 * d_rows + per : 2 * d_rows + 2 * per].reshape(-1)

    dy_b, x_all = lax.optimization_barrier((out_grad[0], x_all))
    ff_half = swap(ff_blocks)
    dy_all = lax.all_gather(dy_b, AXES, axis=0, tiled=True)

    attn_gain_row, ffn_gain_row = attn_gain32.reshape(1, width), ffn_gain32.reshape(1, width)
    cosine, sine = rope_tables(stream)
    head_gain = jnp.concatenate([qgain32, qgain32, kgain32, kgain32]).reshape(1, 2 * LANES)
    n1_all, raw, q_b, kv_b, att, inv, w_qkv = attend(
        doc_starts, x_all, attn_gain_row, attn_half, attn_other, head_gain, cosine, sine
    )
    middle, n2_own = scatter_tokens(
        att, w_out, False, after_attention, [tokens[0], ffn_gain_row], [], n_ctx, n_wa, True, 3
    )
    n2_all, ff_other = gather_tokens(n2_own, [(WHOLE, ff_half)], n_ctx, n_wa, False, 2)
    hidden, d_gu, gu_grad, w_gu = ffn(n2_all, dy_all, ff_half, ff_other, w_down)
    gu_grad = gu_grad.reshape(n, 2, half, 2 * ff_cols)
    d_middle, d_branch, gu_other, down_part, down_grad = scatter_tokens(
        d_gu,
        w_gu,
        True,
        after_ffn_back,
        [middle, ffn_gain_row, out_grad[0]],
        [(PICK, gu_grad)],
        n_ctx,
        n_wa,
        False,
        4,
        DownProducts(dy_all, w_down, hidden),
    )
    down = lax.psum_scatter(down_part, AXES, scatter_dimension=0, tiled=True).astype(F32)
    layer_out = middle + down
    db_all, down_other, gu_sum = gather_tokens(
        d_branch, [(WHOLE, down_grad)], n_ctx, n_wa, True, 5, PairSum(gu_grad, gu_other)
    )
    gu_rows = swap(gu_sum)
    d_qkv, out_w_grad, head_grad = attend_back(
        doc_starts, db_all, w_out, q_b, kv_b, att, inv, raw, head_gain, cosine, sine
    )
    out_w_other = lax.ppermute(out_w_grad, "dp", swap_dp)
    qkv_grad = t_mm(n1_all, d_qkv).astype(BF16).reshape(n, 2, half, 2 * LANES)
    qkv_other = lax.ppermute(
        lax.dynamic_index_in_dim(qkv_grad, 1 - dp, 1, keepdims=False), "dp", swap_dp
    )
    head_grad = head_grad + lax.ppermute(head_grad, "dp", swap_dp)
    qkv_other, head_grad, gu_rows = lax.optimization_barrier((qkv_other, head_grad, gu_rows))
    gu_others = lax.ppermute(gu_rows, "dp", swap_dp)
    qkv_mine = lax.dynamic_index_in_dim(qkv_grad, dp, 1, keepdims=False)
    qkv_sum = (qkv_mine.astype(F32) + qkv_other.astype(F32)).astype(BF16)
    head_row = jnp.pad(head_grad.astype(BF16), ((0, 8), (0, LANES)))
    qkv_out = jnp.concatenate(
        [qkv_sum, jnp.broadcast_to(head_row[None], (n,) + head_row.shape)], axis=1
    )
    input_grad, qkv_rows, qkv_others = scatter_tokens(
        d_qkv,
        w_qkv,
        True,
        after_attention_back,
        [tokens[0], attn_gain_row, d_middle],
        [(SPREAD, qkv_out)],
        n_ctx,
        n_wa,
        True,
        6,
    )
    out_w_other, gu_others, input_grad = lax.optimization_barrier((out_w_other, gu_others, input_grad))
    gate_grad, up_grad, gu_sums = unpack_pair(gu_rows, gu_others, w_gate, w_up)
    q_grad, k_grad, v_grad, attn_sums, head_sums = unpack_attn(
        qkv_rows, qkv_others, w_query, w_key, w_value
    )
    me = lax.axis_index("ctx") * n_wa + lax.axis_index("wa")
    q_gain_grad = head_sums[0, :HD] + head_sums[0, HD:LANES]
    k_gain_grad = head_sums[1, :HD]
    attn_gain_grad = jnp.sum(attn_sums, axis=1) / attn_gain.astype(F32)
    ffn_gain_grad = jnp.sum(gu_sums, axis=1) / ffn_gain.astype(F32)
    return (
        layer_out.astype(BF16)[None],
        input_grad[None],
        attn_gain_grad,
        q_grad,
        k_grad,
        v_grad,
        lax.dynamic_slice_in_dim(q_gain_grad, me * per, per),
        lax.dynamic_slice_in_dim(k_gain_grad, me * per, per),
        out_w_grad.astype(F32) + out_w_other.astype(F32),
        ffn_gain_grad,
        gate_grad,
        up_grad,
        down_grad.astype(F32) + down_other.astype(F32),
    )


def solution(mesh):
    split = mesh.shape["ctx"] * mesh.shape["wa"]
    by_heads = 2 * split == H
    placed = (
        P("dp", ("ctx", "wa"), None),
        P("dp", None),
        P("dp", ("ctx", "wa"), None),
        P(("ctx", "wa")),
        P(("ctx", "wa"), None),
        P(("ctx", "wa"), None),
        P(("ctx", "wa"), None),
        P(("ctx", "wa")),
        P(("ctx", "wa")),
        P(("ctx", "wa"), None),
        P(("ctx", "wa")),
        P(("ctx", "wa"), None),
        P(("ctx", "wa"), None),
        P(("ctx", "wa"), None),
    )
    return jax.shard_map(
        per_device_heads if by_heads else per_device,
        mesh=mesh,
        in_specs=placed,
        out_specs=(
            P("dp", ("ctx", "wa"), None),
            P("dp", ("ctx", "wa"), None),
            P(("ctx", "wa")),
            P(("ctx", "wa"), None),
            P(("ctx", "wa"), None),
            P(("ctx", "wa"), None),
            P(("ctx", "wa")),
            P(("ctx", "wa")),
            P(("ctx", "wa"), None),
            P(("ctx", "wa")),
            P(("ctx", "wa"), None),
            P(("ctx", "wa"), None),
            P(("ctx", "wa"), None),
        ),
        check_vma=False,
    )
```

```python
from functools import partial

import jax
import jax.numpy as jnp
import numpy as np
from jax import lax
from jax.experimental import pallas as pl
from jax.experimental.pallas import tpu as pltpu
from jax.sharding import PartitionSpec as P

H = 32
KV = 8
HD = 64
FF = 8192


EPS = 1e-05
THETA = 1000000.0


def stored_positions(index, tok_rows, n_ctx, n_wa):
    device = index // tok_rows
    local = index % tok_rows
    half_rows = tok_rows // 2
    ctx_part = device // n_wa
    wa_part = device % n_wa
    span_idx = jnp.where(local < half_rows, ctx_part, 2 * n_ctx - 1 - ctx_part)
    return span_idx * (half_rows * n_wa) + wa_part * half_rows + local % half_rows


def segments(position, starts):
    return jnp.sum((starts[None, :] <= position[:, None]).astype(jnp.int32), axis=1) - 1


def rms_norm(values, gain):
    return values * lax.rsqrt(jnp.mean(values * values, axis=-1, keepdims=True) + EPS) * gain


def rotate(values, position):
    half_dim = HD // 2
    frequency = THETA ** (-2.0 * jnp.arange(half_dim, dtype=jnp.float32) / HD)
    angles = position.astype(jnp.float32)[:, None] * frequency[None, :]
    cosine = jnp.cos(angles)[:, None, :]
    sine_part = jnp.sin(angles)[:, None, :]
    first_half = values[..., :half_dim]
    second_half = values[..., half_dim:]
    return jnp.concatenate(
        [
            first_half * cosine - second_half * sine_part,
            second_half * cosine + first_half * sine_part,
        ],
        axis=-1,
    )


def prepare(query_raw, key_raw, query_gain, key_gain, position):
    return (
        rotate(rms_norm(query_raw, query_gain), position),
        rotate(rms_norm(key_raw, key_gain), position),
    )


def per_device(
    tokens,
    doc_starts,
    out_grad,
    attn_gain,
    w_query,
    w_key,
    w_value,
    q_gain,
    k_gain,
    w_out,
    ffn_gain,
    w_gate,
    w_up,
    w_down,
):
    n_ctx = lax.axis_size("ctx")
    n_wa = lax.axis_size("wa")
    tok_rows = tokens.shape[1]
    stream_len = tok_rows * n_ctx * n_wa
    key_width = min(1024, stream_len)
    key_blocks = stream_len // key_width
    groups = H // KV
    scale = HD ** (-0.5)
    first_row = (lax.axis_index("ctx") * n_wa + lax.axis_index("wa")) * tok_rows
    own_pos = stored_positions(
        first_row + jnp.arange(tok_rows, dtype=jnp.int32), tok_rows, n_ctx, n_wa
    )
    starts = doc_starts[0]
    own_seg = segments(own_pos, starts)
    key_pos = stored_positions(jnp.arange(stream_len, dtype=jnp.int32), tok_rows, n_ctx, n_wa)
    key_seg = segments(key_pos, starts)
    residual = tokens[0].astype(jnp.float32)
    attn_set = (
        lax.all_gather(attn_gain, ("ctx", "wa"), axis=0, tiled=True),
        lax.all_gather(w_query, ("ctx", "wa"), axis=0, tiled=True),
        lax.all_gather(w_key, ("ctx", "wa"), axis=0, tiled=True),
        lax.all_gather(w_value, ("ctx", "wa"), axis=0, tiled=True),
        lax.all_gather(q_gain, ("ctx", "wa"), axis=0, tiled=True),
        lax.all_gather(k_gain, ("ctx", "wa"), axis=0, tiled=True),
        lax.all_gather(w_out, ("ctx", "wa"), axis=0, tiled=True),
    )
    g_attn, wq_full, wk_full, wv_full, gq_full, gk_full, wo_full = attn_set
    attn_gain32 = g_attn.astype(jnp.float32)
    qgain32 = gq_full.astype(jnp.float32)
    kgain32 = gk_full.astype(jnp.float32)
    normed_one = rms_norm(residual, attn_gain32).astype(jnp.bfloat16)
    query_raw = jnp.dot(normed_one, wq_full, preferred_element_type=jnp.float32).reshape(
        tok_rows, H, HD
    )
    key_raw = jnp.dot(normed_one, wk_full, preferred_element_type=jnp.float32).reshape(
        tok_rows, KV, HD
    )
    value_b = jnp.dot(normed_one, wv_full, preferred_element_type=jnp.float32).astype(jnp.bfloat16)
    query_rot, key_rot = prepare(query_raw, key_raw, qgain32, kgain32, own_pos)
    query_b = query_rot.astype(jnp.bfloat16).reshape(tok_rows, KV, groups, HD)
    key_b = key_rot.astype(jnp.bfloat16).reshape(tok_rows, KV * HD)
    all_keys, all_values = (
        lax.all_gather(key_b, ("ctx", "wa"), axis=0, tiled=True),
        lax.all_gather(value_b, ("ctx", "wa"), axis=0, tiled=True),
    )

    def key_block(keys_in, values_in, block_idx):
        begin = block_idx * key_width
        key_part = lax.dynamic_slice_in_dim(keys_in, begin, key_width, 0).reshape(key_width, KV, HD)
        value_part = lax.dynamic_slice_in_dim(values_in, begin, key_width, 0).reshape(
            key_width, KV, HD
        )
        pos_part = lax.dynamic_slice_in_dim(key_pos, begin, key_width, 0)
        seg_part = lax.dynamic_slice_in_dim(key_seg, begin, key_width, 0)
        scores = (
            jnp.einsum("rkgd,tkd->kgrt", query_b, key_part, preferred_element_type=jnp.float32)
            * scale
        )
        allowed = (
            (seg_part[None, :] == own_seg[:, None]) & (pos_part[None, :] <= own_pos[:, None])
        )[None, None]
        return (scores, allowed, key_part, value_part)

    def stat_step(block_idx, carry):
        row_max, row_total = carry
        scores, allowed, key_part, value_part = key_block(all_keys, all_values, block_idx)
        masked = jnp.where(allowed, scores, -1e30)
        new_max = jnp.maximum(row_max, jnp.max(masked, axis=-1))
        fresh = jnp.sum(jnp.where(allowed, jnp.exp(masked - new_max[..., None]), 0.0), axis=-1)
        return (new_max, row_total * jnp.exp(row_max - new_max) + fresh)

    stat_init = (
        jnp.full((KV, groups, tok_rows), -1e30, jnp.float32),
        jnp.zeros((KV, groups, tok_rows), jnp.float32),
    )
    row_max, row_total = lax.fori_loop(0, key_blocks, stat_step, stat_init)

    def out_step(block_idx, summed):
        scores, allowed, key_part, value_part = key_block(all_keys, all_values, block_idx)
        probability = (
            jnp.where(allowed, jnp.exp(scores - row_max[..., None]), 0.0) / row_total[..., None]
        )
        return summed + jnp.einsum(
            "kgrt,tkd->rkgd",
            probability.astype(jnp.bfloat16),
            value_part,
            preferred_element_type=jnp.float32,
        )

    attended = lax.fori_loop(
        0, key_blocks, out_step, jnp.zeros((tok_rows, KV, groups, HD), jnp.float32)
    )
    attended_b = attended.reshape(tok_rows, H * HD).astype(jnp.bfloat16)
    middle = residual + jnp.dot(attended_b, wo_full, preferred_element_type=jnp.float32)
    ffn_set = (
        lax.all_gather(ffn_gain, ("ctx", "wa"), axis=0, tiled=True),
        lax.all_gather(w_gate, ("ctx", "wa"), axis=0, tiled=True),
        lax.all_gather(w_up, ("ctx", "wa"), axis=0, tiled=True),
        lax.all_gather(w_down, ("ctx", "wa"), axis=0, tiled=True),
    )
    g_ffn, wg_full, wu_full, wd_full = ffn_set
    ffn_gain32 = g_ffn.astype(jnp.float32)
    normed_two = rms_norm(middle, ffn_gain32).astype(jnp.bfloat16)
    gate_act = jnp.dot(normed_two, wg_full, preferred_element_type=jnp.float32)
    up_act = jnp.dot(normed_two, wu_full, preferred_element_type=jnp.float32)
    sigmoid_gate = jax.nn.sigmoid(gate_act)
    silu_gate = gate_act * sigmoid_gate
    hidden = (silu_gate * up_act).astype(jnp.bfloat16)
    layer_out = (middle + jnp.dot(hidden, wd_full, preferred_element_type=jnp.float32)).astype(
        jnp.bfloat16
    )
    g_ffn, wg_full, wu_full, wd_full = (
        lax.all_gather(ffn_gain, ("ctx", "wa"), axis=0, tiled=True),
        lax.all_gather(w_gate, ("ctx", "wa"), axis=0, tiled=True),
        lax.all_gather(w_up, ("ctx", "wa"), axis=0, tiled=True),
        lax.all_gather(w_down, ("ctx", "wa"), axis=0, tiled=True),
    )
    d_out = out_grad[0].astype(jnp.float32)
    d_out_b = d_out.astype(jnp.bfloat16)
    d_hidden = jnp.einsum("rd,fd->rf", d_out_b, wd_full, preferred_element_type=jnp.float32)
    d_gate = (d_hidden * up_act * (sigmoid_gate * (1.0 + gate_act * (1.0 - sigmoid_gate)))).astype(
        jnp.bfloat16
    )
    d_up = (d_hidden * silu_gate).astype(jnp.bfloat16)
    d_normed_two = jnp.einsum(
        "rf,df->rd", d_gate, wg_full, preferred_element_type=jnp.float32
    ) + jnp.einsum("rf,df->rd", d_up, wu_full, preferred_element_type=jnp.float32)
    norm_out, norm_back = jax.vjp(rms_norm, middle, ffn_gain32)
    d_middle_part, d_ffn_gain = norm_back(d_normed_two)
    d_middle = d_out + d_middle_part
    gate_up = jnp.concatenate([d_gate, d_up], axis=1)
    part_rows = normed_two
    in_grad = lax.psum_scatter(
        jnp.einsum("rc,rf->cf", part_rows, gate_up, preferred_element_type=jnp.float32),
        ("ctx", "wa"),
        scatter_dimension=0,
        tiled=True,
    )
    part_rows = hidden
    down_grad = lax.psum_scatter(
        jnp.einsum("rc,rd->cd", part_rows, d_out_b, preferred_element_type=jnp.float32),
        ("ctx", "wa"),
        scatter_dimension=0,
        tiled=True,
    )
    g_attn, wq_full, wk_full, wv_full, gq_full, gk_full, wo_full = (
        lax.all_gather(attn_gain, ("ctx", "wa"), axis=0, tiled=True),
        lax.all_gather(w_query, ("ctx", "wa"), axis=0, tiled=True),
        lax.all_gather(w_key, ("ctx", "wa"), axis=0, tiled=True),
        lax.all_gather(w_value, ("ctx", "wa"), axis=0, tiled=True),
        lax.all_gather(q_gain, ("ctx", "wa"), axis=0, tiled=True),
        lax.all_gather(k_gain, ("ctx", "wa"), axis=0, tiled=True),
        lax.all_gather(w_out, ("ctx", "wa"), axis=0, tiled=True),
    )
    d_branch = d_middle.astype(jnp.bfloat16)
    wo_grad = jnp.einsum("re,rd->ed", attended_b, d_branch, preferred_element_type=jnp.float32)
    d_attended = jnp.einsum(
        "rd,ed->re", d_branch, wo_full, preferred_element_type=jnp.float32
    ).astype(jnp.bfloat16)
    d_att4 = d_attended.reshape(tok_rows, KV, groups, HD)
    delta = jnp.einsum("rkgd,rkgd->kgr", d_att4.astype(jnp.float32), attended)

    def back_step(d_query, block_idx):
        scores, allowed, key_part, value_part = key_block(all_keys, all_values, block_idx)
        probability = (
            jnp.where(allowed, jnp.exp(scores - row_max[..., None]), 0.0) / row_total[..., None]
        )
        d_prob = jnp.einsum(
            "rkgd,tkd->kgrt", d_att4, value_part, preferred_element_type=jnp.float32
        )
        d_scores = (probability * (d_prob - delta[..., None])).astype(jnp.bfloat16)
        d_query = (
            d_query
            + jnp.einsum("kgrt,tkd->rkgd", d_scores, key_part, preferred_element_type=jnp.float32)
            * scale
        )
        d_key_part = (
            jnp.einsum("kgrt,rkgd->tkd", d_scores, query_b, preferred_element_type=jnp.float32)
            * scale
        )
        d_value_part = jnp.einsum(
            "kgrt,rkgd->tkd",
            probability.astype(jnp.bfloat16),
            d_att4,
            preferred_element_type=jnp.float32,
        )
        return (
            d_query,
            (d_key_part.reshape(key_width, KV * HD), d_value_part.reshape(key_width, KV * HD)),
        )

    d_query, (d_keys, d_values) = lax.scan(
        back_step, jnp.zeros((tok_rows, KV, groups, HD), jnp.float32), jnp.arange(key_blocks)
    )
    d_key_own, d_value_own = (
        lax.psum_scatter(
            d_keys.reshape(stream_len, KV * HD), ("ctx", "wa"), scatter_dimension=0, tiled=True
        ),
        lax.psum_scatter(
            d_values.reshape(stream_len, KV * HD), ("ctx", "wa"), scatter_dimension=0, tiled=True
        ),
    )
    prep_out, prep_back = jax.vjp(
        partial(prepare, position=own_pos), query_raw, key_raw, qgain32, kgain32
    )
    d_query_raw, d_key_raw, d_qgain, d_kgain = prep_back(
        (d_query.reshape(tok_rows, H, HD), d_key_own.reshape(tok_rows, KV, HD))
    )
    dq_b = d_query_raw.reshape(tok_rows, H * HD).astype(jnp.bfloat16)
    dk_b = d_key_raw.reshape(tok_rows, KV * HD).astype(jnp.bfloat16)
    dv_b = d_value_own.astype(jnp.bfloat16)
    d_normed_one = (
        jnp.einsum("re,de->rd", dq_b, wq_full, preferred_element_type=jnp.float32)
        + jnp.einsum("re,de->rd", dk_b, wk_full, preferred_element_type=jnp.float32)
        + jnp.einsum("re,de->rd", dv_b, wv_full, preferred_element_type=jnp.float32)
    )
    first_out, first_back = jax.vjp(rms_norm, residual, attn_gain32)
    d_res_part, d_attn_gain = first_back(d_normed_one)
    input_grad = (d_middle + d_res_part).astype(jnp.bfloat16)
    wq_grad = jnp.einsum("rc,re->ce", normed_one, dq_b, preferred_element_type=jnp.float32)
    wk_grad = jnp.einsum("rc,re->ce", normed_one, dk_b, preferred_element_type=jnp.float32)
    wv_grad = jnp.einsum("rc,re->ce", normed_one, dv_b, preferred_element_type=jnp.float32)
    attn_terms = (d_attn_gain, wq_grad, wk_grad, wv_grad, d_qgain, d_kgain, d_ffn_gain, wo_grad)
    attn_shards = (
        lax.psum_scatter(attn_terms[0], ("ctx", "wa"), scatter_dimension=0, tiled=True),
        lax.psum_scatter(attn_terms[1], ("ctx", "wa"), scatter_dimension=0, tiled=True),
        lax.psum_scatter(attn_terms[2], ("ctx", "wa"), scatter_dimension=0, tiled=True),
        lax.psum_scatter(attn_terms[3], ("ctx", "wa"), scatter_dimension=0, tiled=True),
        lax.psum_scatter(attn_terms[4], ("ctx", "wa"), scatter_dimension=0, tiled=True),
        lax.psum_scatter(attn_terms[5], ("ctx", "wa"), scatter_dimension=0, tiled=True),
        lax.psum_scatter(attn_terms[6], ("ctx", "wa"), scatter_dimension=0, tiled=True),
        lax.psum_scatter(attn_terms[7], ("ctx", "wa"), scatter_dimension=0, tiled=True),
    )
    wo_shard = attn_shards[7]
    summed = (
        lax.psum(attn_shards[0].astype(jnp.bfloat16), "dp").astype(jnp.float32),
        lax.psum(attn_shards[1].astype(jnp.bfloat16), "dp").astype(jnp.float32),
        lax.psum(attn_shards[2].astype(jnp.bfloat16), "dp").astype(jnp.float32),
        lax.psum(attn_shards[3].astype(jnp.bfloat16), "dp").astype(jnp.float32),
        lax.psum(attn_shards[4].astype(jnp.bfloat16), "dp").astype(jnp.float32),
        lax.psum(attn_shards[5].astype(jnp.bfloat16), "dp").astype(jnp.float32),
        lax.psum(wo_shard.astype(jnp.bfloat16), "dp").astype(jnp.float32),
        lax.psum(attn_shards[6].astype(jnp.bfloat16), "dp").astype(jnp.float32),
        lax.psum(in_grad[:, :FF].astype(jnp.bfloat16), "dp").astype(jnp.float32),
        lax.psum(in_grad[:, FF:].astype(jnp.bfloat16), "dp").astype(jnp.float32),
        lax.psum(down_grad.astype(jnp.bfloat16), "dp").astype(jnp.float32),
    )
    return (layer_out[None], input_grad[None]) + tuple(summed)


AXES = ("ctx", "wa")
LANES = 2 * HD
ROWS_BLOCK = 256
FFN_BLOCK = 512
ROOM = 60 * 2**20
SIDE_ROWS = 256
LOG2E = 1.4426950408889634
F32 = jnp.float32
BF16 = jnp.bfloat16


def low_key(starts, row):
    first = jnp.int32(0)
    for doc in range(starts.shape[1]):
        begin = starts[0, doc]
        first = jnp.where(begin <= row, begin, first)
    return first


def block_mask(starts, q_begin, k_begin, bq, bk):
    row = q_begin + lax.broadcasted_iota(jnp.int32, (bq, 1), 0)
    first = low_key(starts, row)
    col = k_begin + lax.broadcasted_iota(jnp.int32, (1, bk), 1)
    return (col >= first) & (col <= row)


def rope_tables(stream):
    frequency = np.float32(THETA) ** (-2.0 * np.arange(HD // 2, dtype=np.float32) / np.float32(HD))
    angles = np.arange(stream, dtype=np.float32)[:, None] * frequency.astype(np.float32)[None, :]
    cosine = np.cos(angles.astype(np.float64)).astype(np.float32)
    sine = np.sin(angles.astype(np.float64)).astype(np.float32)
    return np.tile(cosine, (1, 4)), np.tile(np.concatenate([-sine, sine], axis=1), (1, 2))


def lane_ids():
    return lax.broadcasted_iota(jnp.int32, (1, LANES), 1)


def head_mean(values):
    low = jnp.sum(values[:, :HD], axis=1, keepdims=True)
    high = jnp.sum(values[:, HD:], axis=1, keepdims=True)
    return jnp.where(lane_ids() < HD, low, high) * (1.0 / HD)


def swap_halves(values):
    first = lane_ids() % HD < HD // 2
    return jnp.where(
        first, pltpu.roll(values, LANES - HD // 2, 1), pltpu.roll(values, HD // 2, 1)
    )


def norm_rope(raw, gain, cosine, sine):
    scaled = raw * lax.rsqrt(head_mean(raw * raw) + EPS) * gain
    return scaled * cosine + swap_halves(scaled) * sine


def norm_rope_back(grad, raw, gain, cosine, sine):
    inverse = lax.rsqrt(head_mean(raw * raw) + EPS)
    unit = raw * inverse
    d_scaled = grad * cosine + swap_halves(grad * sine)
    d_unit = d_scaled * gain
    return inverse * (d_unit - unit * head_mean(d_unit * unit)), d_scaled * unit


def stack_heads(rows, at_low):
    lanes = lane_ids()
    zero = jnp.zeros_like(rows)
    low, high = jnp.where(lanes < HD, rows, zero), jnp.where(lanes < HD, zero, rows)
    turned = pltpu.roll(high if at_low else low, HD, 1)
    return jnp.concatenate([low, turned] if at_low else [turned, high], axis=0)


def dot(a, b):
    return jnp.dot(a, b, preferred_element_type=F32)


def dot_t(a, b):
    return lax.dot_general(a, b, (((1,), (1,)), ((), ())), preferred_element_type=F32)


def t_dot(a, b):
    return lax.dot_general(a, b, (((0,), (0,)), ((), ())), preferred_element_type=F32)


def join_halves(half, own_ref, other_ref, whole_ref):
    own_row = jnp.where(lax.axis_index("dp") == 0, 0, half)

    def put(j, carry):
        for begin, ref in ((own_row, own_ref), (half - own_row, other_ref)):
            at = pl.multiple_of(2 * half * j + begin, half)
            whole_ref[pl.ds(at, half), :] = ref[j, :half, :]
        return carry

    lax.fori_loop(0, own_ref.shape[0], put, 0)


def attend_kernel(
    starts, x_ref, gain_ref, own_ref, other_ref, head_gain_ref, cos_ref, sin_ref,
    normed_ref, raw_ref, q_ref, kv_ref, att_ref, inv_ref, w_ref, ov_ref,
):
    block = pl.program_id(0)

    @pl.when(block == 0)
    def _():
        join_halves(w_ref.shape[0] // own_ref.shape[0] // 2, own_ref, other_ref, w_ref)

    bq = x_ref.shape[0]
    q_begin = pl.multiple_of(block * bq, bq)
    x = x_ref[...].astype(F32)
    inverse = lax.rsqrt(jnp.mean(x * x, axis=1, keepdims=True) + EPS)
    normed = (x * inverse * gain_ref[...]).astype(BF16)
    normed_ref[...] = normed
    raw = dot(normed, w_ref[...])
    raw_ref[...] = raw
    cosine, sine = cos_ref[...], sin_ref[...]
    q = norm_rope(raw[:, :LANES], head_gain_ref[:, :LANES], cosine, sine)
    q_ref[...] = q.astype(BF16)
    kv_raw = raw[:, LANES:]
    is_key = lane_ids() < HD
    turned = norm_rope(kv_raw, head_gain_ref[:, LANES:], cosine, sine)
    kv_ref[pl.ds(q_begin, bq), :] = jnp.where(is_key, turned, kv_raw).astype(BF16)
    ov_ref[pl.ds(q_begin, bq), :] = jnp.where(is_key, 1.0, kv_raw).astype(BF16)
    q2 = stack_heads(q, True).astype(BF16)

    def step(j, acc):
        k_begin = pl.multiple_of(j * bq, bq)
        s = dot_t(q2, kv_ref[pl.ds(k_begin, bq), :])
        mask = block_mask(starts, q_begin, k_begin, bq, bq)
        p = jnp.exp2(s * (LOG2E * HD**-0.5))
        p = jnp.where(jnp.concatenate([mask, mask], axis=0), p, 0.0).astype(BF16)
        return acc + dot(p, ov_ref[pl.ds(k_begin, bq), :])

    low = low_key(starts, q_begin) // bq
    acc = lax.fori_loop(low, block + 1, step, jnp.zeros((2 * bq, LANES), F32))
    inv = 1.0 / acc[:, :1]
    out = acc * inv
    att = jnp.where(is_key, pltpu.roll(out[:bq], HD, 1), out[bq:]).astype(BF16)
    att_ref[...] = att
    inv_ref[...] = jnp.where(is_key, inv[:bq], inv[bq:])


def attend(starts, x_all, gain, own, other, head_gain, cosine, sine):
    stream, width = x_all.shape
    bq = ROWS_BLOCK

    def rows(cols):
        return pl.BlockSpec((bq, cols), lambda i: (i, 0))

    def whole(shape):
        return pl.BlockSpec(shape, lambda i: (0,) * len(shape), pipeline_mode=pl.Buffered(1))

    return pl.pallas_call(
        attend_kernel,
        grid=(stream // bq,),
        in_specs=[
            pl.BlockSpec(memory_space=pltpu.SMEM),
            rows(width),
            whole((1, width)),
            whole(own.shape),
            whole(own.shape),
            whole((1, 2 * LANES)),
            rows(LANES),
            rows(LANES),
        ],
        out_specs=[
            rows(width),
            rows(2 * LANES),
            rows(LANES),
            pl.BlockSpec((stream, LANES), lambda i: (0, 0)),
            rows(LANES),
            rows(LANES),
            whole((width, 2 * LANES)),
        ],
        out_shape=[
            jax.ShapeDtypeStruct((stream, width), BF16),
            jax.ShapeDtypeStruct((stream, 2 * LANES), F32),
            jax.ShapeDtypeStruct((stream, LANES), BF16),
            jax.ShapeDtypeStruct((stream, LANES), BF16),
            jax.ShapeDtypeStruct((stream, LANES), BF16),
            jax.ShapeDtypeStruct((stream, LANES), F32),
            jax.ShapeDtypeStruct((width, 2 * LANES), BF16),
        ],
        scratch_shapes=[pltpu.VMEM((stream, LANES), BF16)],
        compiler_params=pltpu.CompilerParams(vmem_limit_bytes=ROOM),
        cost_estimate=pl.CostEstimate(flops=2 * 10**10, bytes_accessed=2**25, transcendentals=0),
    )(starts, x_all, gain, own, other, head_gain, cosine, sine)


def attend_back_kernel(
    starts, db_ref, w_out_ref, q_ref, kv_ref, att_ref, inv_ref, raw_ref, head_gain_ref, cos_ref, sin_ref,
    d_ref, w_grad_ref, gain_ref, dkv_ref, w_acc_ref,
):
    block = pl.program_id(0)
    bq = db_ref.shape[0]
    q_begin = pl.multiple_of(block * bq, bq)

    @pl.when(block == 0)
    def _():
        dkv_ref[...] = jnp.zeros_like(dkv_ref)
        w_acc_ref[...] = jnp.zeros_like(w_acc_ref)
        gain_ref[...] = jnp.zeros_like(gain_ref)

    db = db_ref[...]
    att = att_ref[...]
    da = dot_t(db, w_out_ref[...])
    w_acc_ref[...] += t_dot(att, db)
    q2 = stack_heads(q_ref[...].astype(F32), True).astype(BF16)
    da2 = stack_heads(da, False).astype(BF16)
    prod = da.astype(BF16).astype(F32) * att.astype(F32)
    delta = jnp.concatenate(
        [
            jnp.sum(prod[:, :HD], axis=1, keepdims=True),
            jnp.sum(prod[:, HD:], axis=1, keepdims=True),
        ],
        axis=0,
    )
    inv_all = inv_ref[...]
    inv = jnp.concatenate([inv_all[:, :1], inv_all[:, HD : HD + 1]], axis=0)

    def step(j, dq):
        k_begin = pl.multiple_of(j * bq, bq)
        keys = kv_ref[pl.ds(k_begin, bq), :]
        s = dot_t(q2, keys)
        mask = block_mask(starts, q_begin, k_begin, bq, bq)
        p = jnp.exp2(s * (LOG2E * HD**-0.5)) * inv
        p = jnp.where(jnp.concatenate([mask, mask], axis=0), p, 0.0)
        ds = (p * (dot_t(da2, keys) - delta)).astype(BF16)
        dkv_ref[pl.ds(k_begin, bq), :] += t_dot(ds, q2) * HD**-0.5 + t_dot(p.astype(BF16), da2)
        return dq + dot(ds, keys)

    low = low_key(starts, q_begin) // bq
    dq = lax.fori_loop(low, block + 1, step, jnp.zeros((2 * bq, LANES), F32))
    is_key = lane_ids() < HD
    dq = jnp.where(is_key, dq[:bq], pltpu.roll(dq[bq:], HD, 1)) * HD**-0.5
    here = pl.ds(q_begin, bq)
    d_raw, d_gain = norm_rope_back(
        dq, raw_ref[here, :LANES], head_gain_ref[:, :LANES], cos_ref[here, :], sin_ref[here, :]
    )
    d_ref[here, :LANES] = d_raw.astype(BF16)
    gain_ref[0:1, :] += jnp.sum(d_gain, axis=0, keepdims=True)

    @pl.when(block == pl.num_programs(0) - 1)
    def _():
        def finish(j, carry):
            rows = pl.ds(pl.multiple_of(j * bq, bq), bq)
            dkv = dkv_ref[rows, :]
            d_raw, d_gain = norm_rope_back(
                dkv, raw_ref[rows, LANES:], head_gain_ref[:, LANES:], cos_ref[rows, :], sin_ref[rows, :]
            )
            d_ref[rows, LANES:] = jnp.where(is_key, d_raw, dkv).astype(BF16)
            gain_ref[1:2, :] += jnp.sum(d_gain, axis=0, keepdims=True)
            return carry

        lax.fori_loop(0, pl.num_programs(0), finish, 0)
        w_grad_ref[...] = w_acc_ref[...].astype(BF16)


def attend_back(starts, db_all, w_out, q, kv, att, inv, raw, head_gain, cosine, sine):
    stream, width = db_all.shape
    bq = ROWS_BLOCK

    def rows(cols):
        return pl.BlockSpec((bq, cols), lambda i: (i, 0))

    def whole(shape):
        return pl.BlockSpec(shape, lambda i: (0, 0), pipeline_mode=pl.Buffered(1))

    def kept(shape):
        return pl.BlockSpec(shape, lambda i: (0, 0))

    return pl.pallas_call(
        attend_back_kernel,
        grid=(stream // bq,),
        in_specs=[
            pl.BlockSpec(memory_space=pltpu.SMEM),
            rows(width),
            whole(w_out.shape),
            rows(LANES),
            whole((stream, LANES)),
            rows(LANES),
            rows(LANES),
            whole((stream, 2 * LANES)),
            whole((1, 2 * LANES)),
            whole((stream, LANES)),
            whole((stream, LANES)),
        ],
        out_specs=[kept((stream, 2 * LANES)), kept(w_out.shape), kept((8, LANES))],
        out_shape=[
            jax.ShapeDtypeStruct((stream, 2 * LANES), BF16),
            jax.ShapeDtypeStruct(w_out.shape, BF16),
            jax.ShapeDtypeStruct((8, LANES), F32),
        ],
        scratch_shapes=[pltpu.VMEM((stream, LANES), F32), pltpu.VMEM(w_out.shape, F32)],
        compiler_params=pltpu.CompilerParams(vmem_limit_bytes=ROOM),
        cost_estimate=pl.CostEstimate(flops=3 * 10**10, bytes_accessed=2**25, transcendentals=0),
    )(starts, db_all, w_out, q, kv, att, inv, raw, head_gain, cosine, sine)


def ffn_kernel(
    n2_ref, dy_ref, own_ref, other_ref, w_down_ref, hidden_ref, d_gu_ref, gu_grad_ref, w_gu_ref, gu_acc
):
    block = pl.program_id(0)

    @pl.when(block == 0)
    def _():
        join_halves(own_ref.shape[1], own_ref, other_ref, w_gu_ref)
        gu_acc[...] = jnp.zeros_like(gu_acc)

    cols = hidden_ref.shape[1]
    n2 = n2_ref[...]
    gate_up = dot(n2, w_gu_ref[...])
    d_hidden = dot_t(dy_ref[...], w_down_ref[...])
    gate, up = gate_up[:, :cols], gate_up[:, cols:]
    sig = jax.nn.sigmoid(gate)
    silu = gate * sig
    hidden_ref[...] = (silu * up).astype(BF16)
    d_gu = jnp.concatenate(
        [
            (d_hidden * up * (sig * (1.0 + gate * (1.0 - sig)))).astype(BF16),
            (d_hidden * silu).astype(BF16),
        ],
        axis=1,
    )
    d_gu_ref[...] = d_gu
    gu_acc[...] += t_dot(n2, d_gu)

    @pl.when(block == pl.num_programs(0) - 1)
    def _():
        gu_grad_ref[...] = gu_acc[...].astype(BF16)


def ffn(n2_all, dy_all, own, other, w_down):
    stream, width = n2_all.shape
    both = own.shape[2]
    bt = FFN_BLOCK

    def rows(cols):
        return pl.BlockSpec((bt, cols), lambda i: (i, 0))

    def whole(shape):
        return pl.BlockSpec(shape, lambda i: (0,) * len(shape), pipeline_mode=pl.Buffered(1))

    return pl.pallas_call(
        ffn_kernel,
        grid=(stream // bt,),
        in_specs=[rows(width), rows(width), whole(own.shape), whole(own.shape), whole(w_down.shape)],
        out_specs=[rows(both // 2), rows(both), whole((width, both)), whole((width, both))],
        out_shape=[
            jax.ShapeDtypeStruct((stream, both // 2), BF16),
            jax.ShapeDtypeStruct((stream, both), BF16),
            jax.ShapeDtypeStruct((width, both), BF16),
            jax.ShapeDtypeStruct((width, both), BF16),
        ],
        scratch_shapes=[pltpu.VMEM((width, both), F32)],
        compiler_params=pltpu.CompilerParams(vmem_limit_bytes=ROOM),
        cost_estimate=pl.CostEstimate(
            flops=5 * stream * width * both, bytes_accessed=2**25, transcendentals=0
        ),
    )(n2_all, dy_all, own, other, w_down)


def unpack_attn_kernel(
    own_ref, other_ref, wq_ref, wk_ref, wv_ref, q_ref, k_ref, v_ref, sum_ref, gains_ref
):
    n, half = own_ref.shape[0], wq_ref.shape[0] // 2
    first = lax.axis_index("dp") == 0
    low = jnp.where(first, 0, half)
    high = half - low
    share = n // KV
    gains_ref[...] = jnp.sum(own_ref[:, half:, :].astype(F32), axis=0)
    for begin, ref in ((low, own_ref), (high, other_ref)):
        rows = pl.ds(pl.multiple_of(begin, half), half)
        total = jnp.zeros((half, LANES), F32)
        for j in range(n):
            cols = slice(j * LANES, (j + 1) * LANES)
            q = ref[j, :half, :LANES].astype(F32)
            q_ref[rows, cols] = q
            total += q * wq_ref[rows, cols].astype(F32)
        for pair in range(KV // 2):
            cols = slice(pair * LANES, (pair + 1) * LANES)
            heads = []
            for head in (2 * pair, 2 * pair + 1):
                kv = ref[head * share, :half, LANES:].astype(F32)
                for more in range(1, share):
                    kv = kv + ref[head * share + more, :half, LANES:].astype(F32)
                heads.append(kv)
            k = jnp.concatenate([heads[0][:, :HD], heads[1][:, :HD]], axis=1)
            v = jnp.concatenate([heads[0][:, HD:], heads[1][:, HD:]], axis=1)
            k_ref[rows, cols] = k
            v_ref[rows, cols] = v
            total += k * wk_ref[rows, cols].astype(F32) + v * wv_ref[rows, cols].astype(F32)
        sum_ref[rows, :] = total


def unpack_attn(own, other, w_query, w_key, w_value):
    d_rows = w_query.shape[0]
    return pl.pallas_call(
        unpack_attn_kernel,
        out_shape=[
            jax.ShapeDtypeStruct(w_query.shape, F32),
            jax.ShapeDtypeStruct(w_key.shape, F32),
            jax.ShapeDtypeStruct(w_value.shape, F32),
            jax.ShapeDtypeStruct((d_rows, LANES), F32),
            jax.ShapeDtypeStruct((own.shape[1] - d_rows // 2, 2 * LANES), F32),
        ],
        compiler_params=pltpu.CompilerParams(vmem_limit_bytes=32 * 2**20),
    )(own, other, w_query, w_key, w_value)


def pack_attn_kernel(query_ref, key_ref, value_ref, gains_ref, out_ref):
    n = out_ref.shape[0]
    half = query_ref.shape[0] // 2
    share = n // KV
    rows = pl.ds(pl.multiple_of(lax.axis_index("dp") * half, half), half)
    keys, values = key_ref[rows, :], value_ref[rows, :]
    for j in range(n):
        head = j // share * HD
        out_ref[j, :half, :LANES] = query_ref[rows, j * LANES : (j + 1) * LANES]
        out_ref[j, :half, LANES:] = jnp.concatenate(
            [keys[:, head : head + HD], values[:, head : head + HD]], axis=1
        )
        out_ref[j, half:, :] = gains_ref[...]


def pack_attn(w_query, w_key, w_value, gains, n):
    half = w_query.shape[0] // 2
    return pl.pallas_call(
        pack_attn_kernel,
        out_shape=jax.ShapeDtypeStruct((n, half + gains.shape[0], 2 * LANES), BF16),
    )(w_query, w_key, w_value, gains)


def unpack_pair_kernel(own_ref, other_ref, gate_w, up_w, gate_ref, up_ref, sum_ref):
    count, half, both = own_ref.shape
    cols = both // 2
    first = lax.axis_index("dp") == 0

    @pl.when(pl.program_id(0) == 0)
    def _():
        sum_ref[...] = jnp.zeros_like(sum_ref)

    own_row = pl.multiple_of(jnp.where(first, 0, half), half)
    for begin, ref in ((own_row, own_ref), (half - own_row, other_ref)):
        rows = pl.ds(pl.multiple_of(begin, half), half)
        total = jnp.zeros((half, 128), F32)
        for j in range(count):
            for at in range(0, cols, 128):
                here = slice(j * cols + at, j * cols + at + 128)
                gate = ref[j, :, at : at + 128].astype(F32)
                up = ref[j, :, cols + at : cols + at + 128].astype(F32)
                gate_ref[rows, here] = gate
                up_ref[rows, here] = up
                total += gate * gate_w[rows, here].astype(F32) + up * up_w[rows, here].astype(F32)
        sum_ref[rows, :] += total


def unpack_pair(own, other, w_gate, w_up):
    n, half, both = own.shape
    count = 4
    block = pl.BlockSpec((count, half, both), lambda j: (j, 0, 0))
    part = pl.BlockSpec((2 * half, count * both // 2), lambda j: (0, j))
    return pl.pallas_call(
        unpack_pair_kernel,
        grid=(n // count,),
        in_specs=[block, block, part, part],
        out_specs=[part, part, pl.BlockSpec((2 * half, 128), lambda j: (0, 0))],
        out_shape=[
            jax.ShapeDtypeStruct(w_gate.shape, F32),
            jax.ShapeDtypeStruct(w_up.shape, F32),
            jax.ShapeDtypeStruct((2 * half, 128), F32),
        ],
        compiler_params=pltpu.CompilerParams(vmem_limit_bytes=32 * 2**20),
    )(own, other, w_gate, w_up)


MESH_ID = pl.DeviceIdType.MESH
LINK_COST = pl.CostEstimate(flops=5 * 10**10, bytes_accessed=2**24, transcendentals=0)


def meet_neighbours(ctx, wa, n_ctx, n_wa, everyone):
    barrier = pltpu.get_barrier_semaphore()

    def greet(where):
        pl.semaphore_signal(barrier, inc=1, device_id=where, device_id_type=MESH_ID)

    greet({"dp": lax.axis_index("dp") ^ 1})
    if everyone:
        n = n_ctx * n_wa

        def step(i, carry):
            other = lax.rem(ctx * n_wa + wa + i, n)
            greet({"ctx": other // n_wa, "wa": lax.rem(other, n_wa)})
            return carry

        lax.fori_loop(1, n, step, 0)
        pl.semaphore_wait(barrier, n)
        return
    greet({"wa": wa ^ 1})
    greet({"wa": wa ^ 2})
    pl.when(ctx > 0)(lambda: greet({"ctx": ctx - 1}))
    pl.when(ctx < n_ctx - 1)(lambda: greet({"ctx": ctx + 1}))
    ends = (ctx == 0).astype(jnp.int32) + (ctx == n_ctx - 1).astype(jnp.int32)
    pl.semaphore_wait(barrier, 5 - ends)


WHOLE, PICK, SPREAD = 0, 1, 2


def pair_outs(kind):
    return 2 if kind == SPREAD else 1


def pair_shape(kind, src):
    if kind == PICK:
        return (src.shape[0],) + src.shape[2:]
    return src.shape


def start_spread(src, dst, n_wa, sems):
    n = src.shape[0]
    me = lax.axis_index("ctx") * n_wa + lax.axis_index("wa")
    keep = pltpu.make_async_copy(src.at[me], dst.at[me], sems.at[0, 0])
    keep.start()

    def made(step, arriving):
        other = lax.rem(me + step, n)
        return pltpu.make_async_remote_copy(
            src_ref=src.at[other],
            dst_ref=dst.at[other if arriving else me],
            send_sem=sems.at[0, step],
            recv_sem=sems.at[1, other if arriving else me],
            device_id={"ctx": other // n_wa, "wa": lax.rem(other, n_wa)},
            device_id_type=MESH_ID,
        )

    def loop(act):
        def step(i, carry):
            act(i)
            return carry

        lax.fori_loop(1, n, step, 0)

    def finish():
        keep.wait()
        loop(lambda i: made(i, True).wait_recv())
        loop(lambda i: made(i, False).wait_send())

    loop(lambda i: made(i, False).start())
    return finish


def start_pairs(kinds, srcs, dsts, n_wa, sems, spread_sems):
    dp = lax.axis_index("dp")
    dsts = list(dsts)
    midway = []

    def exchange(at, src, dst):
        send = pltpu.make_async_remote_copy(
            src_ref=src,
            dst_ref=dst,
            send_sem=sems.at[at, 0],
            recv_sem=sems.at[at, 1],
            device_id={"dp": dp ^ 1},
            device_id_type=MESH_ID,
        )
        send.start()
        return send.wait

    for at, (kind, src) in enumerate(zip(kinds, srcs)):
        dst = dsts.pop(0)
        if kind == SPREAD:
            finish, other = start_spread(src, dst, n_wa, spread_sems), dsts.pop(0)

            def pass_on(at=at, finish=finish, dst=dst, other=other):
                finish()
                return exchange(at, dst, other)

            midway.append(pass_on)
            continue
        if kind == PICK:
            src = src.at[:, dp ^ 1]
        wait = exchange(at, src, dst)
        midway.append(lambda wait=wait: wait)
    return midway


def piece_row(zc, wac, h, half, n_ctx, n_wa, by_position):
    if by_position:
        span = zc if h == 0 else 2 * n_ctx - 1 - zc
        return pl.multiple_of((span * n_wa + wac) * half, half)
    return pl.multiple_of(((zc * n_wa + wac) * 2 + h) * half, half)


def unit_rows(values):
    return lax.rsqrt(jnp.mean(values * values, axis=1, keepdims=True) + EPS)


def norm_back(grad, values, gain):
    inverse = unit_rows(values)
    d_unit = grad * gain
    unit = values * inverse
    return inverse * (d_unit - unit * jnp.mean(d_unit * unit, axis=1, keepdims=True))


def after_attention(total, x, gain):
    middle = x.astype(F32) + total
    return middle, middle * unit_rows(middle) * gain


def after_ffn_back(total, middle, gain, d_out):
    d_middle = d_out.astype(F32) + norm_back(total, middle, gain)
    return d_middle, d_middle


def after_attention_back(total, x, gain, d_middle):
    return (d_middle + norm_back(total, x.astype(F32), gain),)


class PackColumns:
    def __init__(self, w_gate, w_up, n):
        self.operands = [w_gate, w_up]
        half, cols = w_gate.shape[0] // 2, w_gate.shape[1] // n
        self.outs = [jax.ShapeDtypeStruct((n, half, 2 * cols), BF16)]
        self.scratch = [
            pltpu.VMEM((half, w_gate.shape[1]), BF16),
            pltpu.VMEM((half, w_gate.shape[1]), BF16),
            pltpu.VMEM((n, half, 2 * cols), BF16),
            pltpu.SemaphoreType.DMA((3,)),
        ]

    def bind(self, ins, outs, scratch):
        self.rows_v, (self.packed, sem) = scratch[:2], scratch[2:]
        half = self.packed.shape[1]
        rows = pl.ds(pl.multiple_of(lax.axis_index("dp") * half, half), half)
        self.loads = [
            pltpu.make_async_copy(ins[at].at[rows], self.rows_v[at], sem.at[at]) for at in range(2)
        ]
        for load in self.loads:
            load.start()
        self.store = pltpu.make_async_copy(self.packed, outs[0], sem.at[2])
        self.at = 0

    def step(self):
        self.at += 1
        if self.at != 2:
            return
        for load in self.loads:
            load.wait()
        n, _, both = self.packed.shape
        cols = both // 2
        for j in range(n):
            for at in range(2):
                self.packed[j, :, at * cols : (at + 1) * cols] = self.rows_v[at][
                    :, j * cols : (j + 1) * cols
                ]
        self.store.start()

    def finish(self):
        self.store.wait()


class PairSum:
    def __init__(self, halves, other):
        self.operands = [halves, other]
        self.outs = [jax.ShapeDtypeStruct(other.shape, BF16)]
        self.scratch = [pltpu.VMEM(other.shape, BF16)] * 2 + [pltpu.SemaphoreType.DMA((3,))]

    def bind(self, ins, outs, scratch):
        self.mine_v, self.other_v, self.sem = scratch
        mine = ins[0].at[:, lax.axis_index("dp")]
        self.loads = [
            pltpu.make_async_copy(mine, self.mine_v, self.sem.at[0]),
            pltpu.make_async_copy(ins[1], self.other_v, self.sem.at[1]),
        ]
        for load in self.loads:
            load.start()
        self.store = pltpu.make_async_copy(self.mine_v, outs[0], self.sem.at[2])
        self.at = 0

    def step(self):
        self.at += 1
        if self.at != 2:
            return
        for load in self.loads:
            load.wait()

        def add(j, carry):
            total = self.mine_v[j].astype(F32) + self.other_v[j].astype(F32)
            self.mine_v[j] = total.astype(BF16)
            return carry

        lax.fori_loop(0, self.mine_v.shape[0], add, 0)
        self.store.start()

    def finish(self):
        self.store.wait()


class DownProducts:
    def __init__(self, dy, w_down, hidden):
        self.operands = [dy, w_down, hidden]
        self.steps = dy.shape[0] // SIDE_ROWS
        self.outs = [
            jax.ShapeDtypeStruct(dy.shape, BF16),
            jax.ShapeDtypeStruct(w_down.shape, BF16),
        ]
        self.scratch = [
            pltpu.VMEM((2, SIDE_ROWS, dy.shape[1]), BF16),
            pltpu.VMEM((2, SIDE_ROWS, dy.shape[1]), BF16),
            pltpu.VMEM(w_down.shape, BF16),
            pltpu.VMEM(hidden.shape, BF16),
            pltpu.VMEM(w_down.shape, F32),
            pltpu.VMEM(w_down.shape, BF16),
            pltpu.SemaphoreType.DMA((7,)),
        ]

    def bind(self, ins, outs, scratch):
        self.dy, (self.out, self.grad) = ins[0], outs
        self.dy_v, self.stage, self.w_v, self.hidden_v, self.acc, self.grad_v, self.sem = scratch
        self.loads = [
            pltpu.make_async_copy(ins[1], self.w_v, self.sem.at[4]),
            pltpu.make_async_copy(ins[2], self.hidden_v, self.sem.at[5]),
        ]
        for load in self.loads:
            load.start()
        self.load(0).start()
        self.acc[...] = jnp.zeros_like(self.acc)
        self.stored = []
        self.at = 0

    def load(self, g):
        rows = pl.ds(g * SIDE_ROWS, SIDE_ROWS)
        return pltpu.make_async_copy(self.dy.at[rows], self.dy_v.at[g % 2], self.sem.at[g % 2])

    def step(self):
        g = self.at
        if g >= self.steps:
            return
        self.at += 1
        if g == 0:
            for load in self.loads:
                load.wait()
        self.load(g).wait()
        if g + 1 < self.steps:
            self.load(g + 1).start()
        rows = pl.ds(g * SIDE_ROWS, SIDE_ROWS)
        if g >= 2:
            self.stored[g - 2].wait()
        hidden = self.hidden_v[rows, :]
        self.stage[g % 2] = dot(hidden, self.w_v[...]).astype(BF16)
        self.acc[...] += t_dot(hidden, self.dy_v[g % 2])
        store = pltpu.make_async_copy(self.stage.at[g % 2], self.out.at[rows], self.sem.at[2 + g % 2])
        store.start()
        self.stored.append(store)

    def finish(self):
        while self.at < self.steps:
            self.step()
        for store in self.stored[-2:]:
            store.wait()
        self.grad_v[...] = self.acc[...].astype(BF16)
        made = pltpu.make_async_copy(self.grad_v, self.grad, self.sem.at[6])
        made.start()
        made.wait()


def split_side(side, at, refs):
    count = len(side.operands) if side else 0
    return refs[at : at + count], refs[:at] + refs[at + count :]


def gather_kernel(n_ctx, n_wa, by_position, kinds, side, own_ref, *refs):
    pairs = len(kinds)
    outs = sum(pair_outs(kind) for kind in kinds)
    side_in, refs = split_side(side, pairs, refs)
    srcs, out_ref, dsts = refs[:pairs], refs[pairs], refs[pairs + 1 : pairs + outs + 1]
    refs = refs[pairs + outs + 1 :]
    side_out, refs = refs[: len(side.outs) if side else 0], refs[len(side.outs) if side else 0 :]
    own_sem, send_sem, recv_sem, pair_sem, spread_sem = refs[:5]
    ctx = lax.axis_index("ctx")
    wa = lax.axis_index("wa")
    half = own_ref.shape[0] // 2
    meet_neighbours(ctx, wa, n_ctx, n_wa, SPREAD in kinds)
    sends = []

    def place(zc, wac, h):
        return out_ref.at[pl.ds(piece_row(zc, wac, h, half, n_ctx, n_wa, by_position), half)]

    def copy(src, zc, wac, h, where):
        return pltpu.make_async_remote_copy(
            src_ref=src,
            dst_ref=place(zc, wac, h),
            send_sem=send_sem.at[len(sends)],
            recv_sem=recv_sem.at[(zc * n_wa + wac) * 2 + h],
            device_id=where,
            device_id_type=MESH_ID,
        )

    def send(cond, src, zc, wac, h, where):
        made = copy(src, zc, wac, h, where)
        if cond is None:
            made.start()
        else:
            pl.when(cond)(made.start)
        sends.append((cond, made))

    def arrived(cond, zc, wac, h):
        made = pltpu.make_async_remote_copy(
            src_ref=place(zc, wac, h),
            dst_ref=place(zc, wac, h),
            send_sem=send_sem.at[0],
            recv_sem=recv_sem.at[(zc * n_wa + wac) * 2 + h],
            device_id={"wa": wa ^ 1},
            device_id_type=MESH_ID,
        )
        if cond is None:
            made.wait_recv()
        else:
            pl.when(cond)(made.wait_recv)

    def inside(zc):
        return (zc >= 0) & (zc < n_ctx)

    own_copies = []
    for h in range(2):
        own = own_ref.at[pl.ds(h * half, half)]
        for way in (-1, 1):
            send(inside(ctx + way), own, ctx, wa, h, {"ctx": ctx + way})
        send(None, own, ctx, wa, h, {"wa": wa ^ 2})
        send(None, own, ctx, wa, h, {"wa": wa ^ 1})
        made = pltpu.make_async_copy(own, place(ctx, wa, h), own_sem.at[h])
        made.start()
        own_copies.append(made)
    pair_waits = start_pairs(kinds, srcs, dsts, n_wa, pair_sem, spread_sem)
    if side:
        side.bind(side_in, side_out, refs[5:])
        side.step()

    def across(k, h):
        for way in (-1, 1) if k else (1,):
            zc = ctx + way * k
            cond = inside(zc) if k else None
            arrived(cond, zc, wa ^ 2, h)
            send(cond, place(zc, wa ^ 2, h), zc, wa ^ 2, h, {"wa": wa ^ 1})

    for k in range(1, n_ctx):
        for h in range(2):
            for way in (-1, 1):
                zc = ctx + way * k
                cond = inside(zc)
                arrived(cond, zc, wa, h)
                piece = place(zc, wa, h)
                send(cond & inside(ctx - way), piece, zc, wa, h, {"ctx": ctx - way})
                send(cond, piece, zc, wa, h, {"wa": wa ^ 2})
                send(cond, piece, zc, wa, h, {"wa": wa ^ 1})
            across(k - 1, h)
            if side:
                side.step()
        if k == 1:
            pair_waits = [wait() for wait in pair_waits]
    for h in range(2):
        across(n_ctx - 1, h)
    for zc in range(n_ctx):
        for far in (0, 2):
            for h in range(2):
                arrived(None, zc, wa ^ 1 ^ far, h)
    for cond, made in sends:
        if cond is None:
            made.wait_send()
        else:
            pl.when(cond)(made.wait_send)
    for made in own_copies:
        made.wait()
    if side:
        side.finish()
    for wait in pair_waits:
        wait()


def gather_tokens(own, pairs, n_ctx, n_wa, by_position, call_id, side=None):
    more = side.operands if side else []
    rows, width = own.shape
    n = n_ctx * n_wa
    kinds = tuple(kind for kind, _ in pairs)
    anywhere = pl.BlockSpec(memory_space=pl.ANY)
    shapes = [jax.ShapeDtypeStruct((rows * n, width), own.dtype)]
    shapes += [
        jax.ShapeDtypeStruct(pair_shape(*pair), BF16)
        for pair in pairs
        for _ in range(pair_outs(pair[0]))
    ]
    shapes += side.outs if side else []
    return pl.pallas_call(
        partial(gather_kernel, n_ctx, n_wa, by_position, kinds, side),
        in_specs=[anywhere] * (1 + len(pairs) + len(more)),
        out_specs=[anywhere] * len(shapes),
        out_shape=shapes,
        scratch_shapes=[
            pltpu.SemaphoreType.DMA((2,)),
            pltpu.SemaphoreType.DMA((8 + 12 * (n_ctx - 1) + 2 * (2 * n_ctx - 1),)),
            pltpu.SemaphoreType.DMA((2 * n,)),
            pltpu.SemaphoreType.DMA((max(1, len(pairs)), 2)),
            pltpu.SemaphoreType.DMA((2, n)),
        ]
        + (side.scratch if side else []),
        compiler_params=pltpu.CompilerParams(
            collective_id=call_id, has_side_effects=True, vmem_limit_bytes=ROOM if side else None
        ),
        cost_estimate=LINK_COST,
    )(own, *[array for _, array in pairs], *more)


def scatter_kernel(
    n_ctx, n_wa, by_position, turned, kinds, side, finish, count, left_ref, right_ref, *refs
):
    row_ins, refs = refs[:count], refs[count:]
    row_count = 1 if finish is after_attention_back else 2
    pairs = len(kinds)
    outs = sum(pair_outs(kind) for kind in kinds)
    side_in, refs = split_side(side, pairs, refs)
    srcs, refs = refs[:pairs], refs[pairs:]
    row_outs, refs = refs[:row_count], refs[row_count:]
    dsts, refs = refs[:outs], refs[outs:]
    side_out, refs = refs[: len(side.outs) if side else 0], refs[len(side.outs) if side else 0 :]
    part_ref, s1, s2, s3, out_ref, send_sem, recv1, recv2, recv3, pair_sem, spread_sem = refs[:11]
    ctx = lax.axis_index("ctx")
    wa = lax.axis_index("wa")
    half = out_ref.shape[0] // 2
    slab = 16
    y = wa // 2
    sibling, across = {"wa": wa ^ 1}, {"wa": wa ^ 2}
    meet_neighbours(ctx, wa, n_ctx, n_wa, SPREAD in kinds)
    pair_waits = start_pairs(kinds, srcs, dsts, n_wa, pair_sem, spread_sem)
    if side:
        side.bind(side_in, side_out, refs[11:])
    sends = []

    def begin(cond, act):
        if cond is None:
            act()
        else:
            pl.when(cond)(act)

    def mine(zc, wac, h):
        return part_ref.at[pl.ds(piece_row(zc, wac, h, half, n_ctx, n_wa, by_position), half)]

    def send(src, dst, sem, where):
        made = pltpu.make_async_remote_copy(
            src_ref=src,
            dst_ref=dst,
            send_sem=send_sem.at[len(sends)],
            recv_sem=sem,
            device_id=where,
            device_id_type=MESH_ID,
        )
        made.start()
        sends.append(made)

    def arrived(cond, dst, sem):
        made = pltpu.make_async_remote_copy(
            src_ref=dst,
            dst_ref=dst,
            send_sem=send_sem.at[0],
            recv_sem=sem,
            device_id=sibling,
            device_id_type=MESH_ID,
        )
        begin(cond, made.wait_recv)

    def add_up(dst, dst_row, srcs):
        def step(i, carry):
            at = pl.multiple_of(i * slab, slab)
            total = srcs[0][pl.ds(at, slab), :].astype(F32)
            for src in srcs[1:]:
                total = total + src[pl.ds(at, slab), :].astype(F32)
            dst[pl.ds(pl.multiple_of(dst_row + at, slab), slab), :] = total.astype(dst.dtype)
            return carry

        lax.fori_loop(0, half // slab, step, 0)

    def inside(zc):
        return (zc >= 0) & (zc < n_ctx)

    def index1(zc, yc, h):
        return (zc * 2 + yc) * 2 + h

    def target(i):
        mirrored = 2 * ctx >= n_ctx
        near = jnp.where(mirrored, n_ctx - 1 - ctx, ctx)
        later = i - (n_ctx - 1 - 2 * near)
        step = jnp.maximum(later, 0) // 2
        paired = jnp.where(lax.rem(jnp.maximum(later, 0), 2) == 0, 2 * near - step, step)
        zc = jnp.where(later < 0, n_ctx - 1 - i, paired)
        return jnp.where(mirrored, n_ctx - 1 - zc, zc)

    def multiply(zc, yc):
        def rows_of(begin_row, count):
            rows = pl.ds(pl.multiple_of(begin_row, count), count)
            left = left_ref[rows, :]
            product = dot_t(left, right_ref[...]) if turned else dot(left, right_ref[...])
            part_ref[rows, :] = product.astype(BF16)

        if not by_position:
            rows_of((zc * n_wa + yc * 2) * 2 * half, 4 * half)
            return

        def step(h, carry):
            span = jnp.where(h == 0, zc, 2 * n_ctx - 1 - zc)
            rows_of((span * n_wa + yc * 2) * half, 2 * half)
            return carry

        lax.fori_loop(0, 2, step, 0)

    def cross(zc):
        for h in range(2):
            at = index1(zc, y ^ 1, h)
            arrived(None, s1.at[at], recv1.at[at])
            add_up(s1.at[at], 0, [s1.at[at], mine(zc, wa ^ 2, h)])
            send(s1.at[at], s2.at[zc * 2 + h], recv2.at[zc * 2 + h], across)

    targets = [target(i) for i in range(n_ctx)]
    for i, zc in enumerate(targets):
        for yc in (y ^ 1, y):
            multiply(zc, yc)
            for h in range(2):
                at = index1(zc, yc, h)
                send(mine(zc, yc * 2 + ((wa & 1) ^ 1), h), s1.at[at], recv1.at[at], sibling)
        cross(zc)
        if side:
            side.step()
    pair_waits = [wait() for wait in pair_waits]
    for i, zc in enumerate(targets):
        if side and i:
            side.step()
        for h in range(2):
            at = index1(zc, y, h)
            here = zc * 2 + h
            arrived(None, s1.at[at], recv1.at[at])
            arrived(None, s2.at[here], recv2.at[here])
            base = [mine(zc, wa, h), s1.at[at], s2.at[here]]
            low, high = here, (n_ctx + zc) * 2 + h
            if i < n_ctx - 1:
                way = jnp.where(zc > ctx, 1, -1)
                behind = jnp.where(zc > ctx, low, high)
                more = inside(ctx - way)
                arrived(more, s3.at[behind], recv3.at[behind])
                pl.when(more)(lambda: add_up(s2.at[here], 0, base + [s3.at[behind]]))
                pl.when(jnp.logical_not(more))(lambda: add_up(s2.at[here], 0, base))
                send(s2.at[here], s3.at[behind], recv3.at[behind], {"ctx": ctx + way})
            else:
                under, over = ctx > 0, ctx < n_ctx - 1
                arrived(under, s3.at[low], recv3.at[low])
                arrived(over, s3.at[high], recv3.at[high])
                ways = [
                    (under & over, [s3.at[low], s3.at[high]]),
                    (under & jnp.logical_not(over), [s3.at[low]]),
                    (over & jnp.logical_not(under), [s3.at[high]]),
                ]
                for take, extra in ways:
                    begin(take, lambda extra=extra: add_up(out_ref, h * half, base + extra))
    for ref, values in zip(row_outs, finish(out_ref[...], *[ref[...] for ref in row_ins])):
        ref[...] = values.astype(ref.dtype)
    if side:
        side.finish()
    for made in sends:
        made.wait_send()
    for wait in pair_waits:
        wait()


def scatter_tokens(
    left, right, turned, finish, rows_in, pairs, n_ctx, n_wa, by_position, call_id, side=None
):
    n = n_ctx * n_wa
    rows = left.shape[0] // n
    width = right.shape[0] if turned else right.shape[1]
    more = side.operands if side else []
    row_types = [BF16] if finish is after_attention_back else [F32, BF16]
    half = rows // 2
    kinds = tuple(kind for kind, _ in pairs)
    anywhere = pl.BlockSpec(memory_space=pl.ANY)
    vmem = pl.BlockSpec(memory_space=pltpu.VMEM)
    shapes = [
        jax.ShapeDtypeStruct(pair_shape(*pair), BF16)
        for pair in pairs
        for _ in range(pair_outs(pair[0]))
    ]
    shapes += side.outs if side else []
    return pl.pallas_call(
        partial(
            scatter_kernel, n_ctx, n_wa, by_position, turned, kinds, side, finish, len(rows_in)
        ),
        in_specs=[vmem] * (2 + len(rows_in)) + [anywhere] * (len(pairs) + len(more)),
        out_specs=[vmem] * len(row_types) + [anywhere] * len(shapes),
        out_shape=[jax.ShapeDtypeStruct((rows, width), dtype) for dtype in row_types] + shapes,
        scratch_shapes=[
            pltpu.VMEM((rows * n, width), BF16),
            pltpu.VMEM((4 * n_ctx, half, width), BF16),
            pltpu.VMEM((2 * n_ctx, half, width), BF16),
            pltpu.VMEM((4 * n_ctx, half, width), BF16),
            pltpu.VMEM((rows, width), F32),
            pltpu.SemaphoreType.DMA((8 * n_ctx,)),
            pltpu.SemaphoreType.DMA((4 * n_ctx,)),
            pltpu.SemaphoreType.DMA((2 * n_ctx,)),
            pltpu.SemaphoreType.DMA((4 * n_ctx,)),
            pltpu.SemaphoreType.DMA((max(1, len(pairs)), 2)),
            pltpu.SemaphoreType.DMA((2, n)),
        ]
        + (side.scratch if side else []),
        compiler_params=pltpu.CompilerParams(
            collective_id=call_id, has_side_effects=True, vmem_limit_bytes=ROOM
        ),
        cost_estimate=LINK_COST,
    )(left, right, *rows_in, *[array for _, array in pairs], *more)


def per_device_heads(
    tokens,
    doc_starts,
    out_grad,
    attn_gain,
    w_query,
    w_key,
    w_value,
    q_gain,
    k_gain,
    w_out,
    ffn_gain,
    w_gate,
    w_up,
    w_down,
):
    n_ctx = lax.axis_size("ctx")
    n_wa = lax.axis_size("wa")
    n = n_ctx * n_wa
    tok_rows, width = tokens.shape[1:]
    d_rows = w_query.shape[0]
    stream = tok_rows * n
    ff_cols = FF // n
    per = HD // n
    extra = 16
    swap_dp = [(0, 1), (1, 0)]

    def t_mm(a, b):
        return lax.dot_general(a, b, (((0,), (0,)), ((), ())), preferred_element_type=F32)

    def swap(blocks):
        return lax.all_to_all(blocks, AXES, 0, 0, tiled=True)

    half = d_rows // 2
    dp = lax.axis_index("dp")
    gains_own = jnp.concatenate([attn_gain, ffn_gain, q_gain, k_gain])
    gains_row = jnp.pad(gains_own, (0, extra * 2 * LANES - gains_own.shape[0]))
    attn_cols = pack_attn(w_query, w_key, w_value, gains_row.reshape(extra, 2 * LANES), n)
    x_all, attn_half, attn_other, ff_blocks = gather_tokens(
        tokens[0], [(SPREAD, attn_cols)], n_ctx, n_wa, True, 1, PackColumns(w_gate, w_up, n)
    )
    gains = attn_half[:, half:].reshape(n, -1).astype(F32)
    attn_gain32 = gains[:, :d_rows].reshape(-1)
    ffn_gain32 = gains[:, d_rows : 2 * d_rows].reshape(-1)
    qgain32 = gains[:, 2 * d_rows : 2 * d_rows + per].reshape(-1)
    kgain32 = gains[:, 2 * d_rows + per : 2 * d_rows + 2 * per].reshape(-1)

    dy_b, x_all = lax.optimization_barrier((out_grad[0], x_all))
    ff_half = swap(ff_blocks)
    dy_all = lax.all_gather(dy_b, AXES, axis=0, tiled=True)

    attn_gain_row, ffn_gain_row = attn_gain32.reshape(1, width), ffn_gain32.reshape(1, width)
    cosine, sine = rope_tables(stream)
    head_gain = jnp.concatenate([qgain32, qgain32, kgain32, kgain32]).reshape(1, 2 * LANES)
    n1_all, raw, q_b, kv_b, att, inv, w_qkv = attend(
        doc_starts, x_all, attn_gain_row, attn_half, attn_other, head_gain, cosine, sine
    )
    middle, n2_own = scatter_tokens(
        att, w_out, False, after_attention, [tokens[0], ffn_gain_row], [], n_ctx, n_wa, True, 3
    )
    n2_all, ff_other = gather_tokens(n2_own, [(WHOLE, ff_half)], n_ctx, n_wa, False, 2)
    hidden, d_gu, gu_grad, w_gu = ffn(n2_all, dy_all, ff_half, ff_other, w_down)
    gu_grad = gu_grad.reshape(n, 2, half, 2 * ff_cols)
    d_middle, d_branch, gu_other, down_part, down_grad = scatter_tokens(
        d_gu,
        w_gu,
        True,
        after_ffn_back,
        [middle, ffn_gain_row, out_grad[0]],
        [(PICK, gu_grad)],
        n_ctx,
        n_wa,
        False,
        4,
        DownProducts(dy_all, w_down, hidden),
    )
    down = lax.psum_scatter(down_part, AXES, scatter_dimension=0, tiled=True).astype(F32)
    layer_out = middle + down
    db_all, down_other, gu_sum = gather_tokens(
        d_branch, [(WHOLE, down_grad)], n_ctx, n_wa, True, 5, PairSum(gu_grad, gu_other)
    )
    gu_rows = swap(gu_sum)
    d_qkv, out_w_grad, head_grad = attend_back(
        doc_starts, db_all, w_out, q_b, kv_b, att, inv, raw, head_gain, cosine, sine
    )
    out_w_other = lax.ppermute(out_w_grad, "dp", swap_dp)
    qkv_grad = t_mm(n1_all, d_qkv).astype(BF16).reshape(n, 2, half, 2 * LANES)
    qkv_other = lax.ppermute(
        lax.dynamic_index_in_dim(qkv_grad, 1 - dp, 1, keepdims=False), "dp", swap_dp
    )
    head_grad = head_grad + lax.ppermute(head_grad, "dp", swap_dp)
    qkv_other, head_grad, gu_rows = lax.optimization_barrier((qkv_other, head_grad, gu_rows))
    gu_others = lax.ppermute(gu_rows, "dp", swap_dp)
    qkv_mine = lax.dynamic_index_in_dim(qkv_grad, dp, 1, keepdims=False)
    qkv_sum = (qkv_mine.astype(F32) + qkv_other.astype(F32)).astype(BF16)
    head_row = jnp.pad(head_grad.astype(BF16), ((0, 8), (0, LANES)))
    qkv_out = jnp.concatenate(
        [qkv_sum, jnp.broadcast_to(head_row[None], (n,) + head_row.shape)], axis=1
    )
    input_grad, qkv_rows, qkv_others = scatter_tokens(
        d_qkv,
        w_qkv,
        True,
        after_attention_back,
        [tokens[0], attn_gain_row, d_middle],
        [(SPREAD, qkv_out)],
        n_ctx,
        n_wa,
        True,
        6,
    )
    out_w_other, gu_others, input_grad = lax.optimization_barrier((out_w_other, gu_others, input_grad))
    gate_grad, up_grad, gu_sums = unpack_pair(gu_rows, gu_others, w_gate, w_up)
    q_grad, k_grad, v_grad, attn_sums, head_sums = unpack_attn(
        qkv_rows, qkv_others, w_query, w_key, w_value
    )
    me = lax.axis_index("ctx") * n_wa + lax.axis_index("wa")
    q_gain_grad = head_sums[0, :HD] + head_sums[0, HD:LANES]
    k_gain_grad = head_sums[1, :HD]
    attn_gain_grad = jnp.sum(attn_sums, axis=1) / attn_gain.astype(F32)
    ffn_gain_grad = jnp.sum(gu_sums, axis=1) / ffn_gain.astype(F32)
    return (
        layer_out.astype(BF16)[None],
        input_grad[None],
        attn_gain_grad,
        q_grad,
        k_grad,
        v_grad,
        lax.dynamic_slice_in_dim(q_gain_grad, me * per, per),
        lax.dynamic_slice_in_dim(k_gain_grad, me * per, per),
        out_w_grad.astype(F32) + out_w_other.astype(F32),
        ffn_gain_grad,
        gate_grad,
        up_grad,
        down_grad.astype(F32) + down_other.astype(F32),
    )


def solution(mesh):
    split = mesh.shape["ctx"] * mesh.shape["wa"]
    by_heads = 2 * split == H
    placed = (
        P("dp", ("ctx", "wa"), None),
        P("dp", None),
        P("dp", ("ctx", "wa"), None),
        P(("ctx", "wa")),
        P(("ctx", "wa"), None),
        P(("ctx", "wa"), None),
        P(("ctx", "wa"), None),
        P(("ctx", "wa")),
        P(("ctx", "wa")),
        P(("ctx", "wa"), None),
        P(("ctx", "wa")),
        P(("ctx", "wa"), None),
        P(("ctx", "wa"), None),
        P(("ctx", "wa"), None),
    )
    return jax.shard_map(
        per_device_heads if by_heads else per_device,
        mesh=mesh,
        in_specs=placed,
        out_specs=(
            P("dp", ("ctx", "wa"), None),
            P("dp", ("ctx", "wa"), None),
            P(("ctx", "wa")),
            P(("ctx", "wa"), None),
            P(("ctx", "wa"), None),
            P(("ctx", "wa"), None),
            P(("ctx", "wa")),
            P(("ctx", "wa")),
            P(("ctx", "wa"), None),
            P(("ctx", "wa")),
            P(("ctx", "wa"), None),
            P(("ctx", "wa"), None),
            P(("ctx", "wa"), None),
        ),
        check_vma=False,
    )
```

```python
from functools import partial

import jax
import jax.numpy as jnp
import numpy as np
from jax import lax
from jax.experimental import pallas as pl
from jax.experimental.pallas import tpu as pltpu
from jax.sharding import PartitionSpec as P

H = 32
KV = 8
HD = 64
FF = 8192


EPS = 1e-05
THETA = 1000000.0


def stored_positions(index, tok_rows, n_ctx, n_wa):
    device = index // tok_rows
    local = index % tok_rows
    half_rows = tok_rows // 2
    ctx_part = device // n_wa
    wa_part = device % n_wa
    span_idx = jnp.where(local < half_rows, ctx_part, 2 * n_ctx - 1 - ctx_part)
    return span_idx * (half_rows * n_wa) + wa_part * half_rows + local % half_rows


def segments(position, starts):
    return jnp.sum((starts[None, :] <= position[:, None]).astype(jnp.int32), axis=1) - 1


def rms_norm(values, gain):
    return values * lax.rsqrt(jnp.mean(values * values, axis=-1, keepdims=True) + EPS) * gain


def rotate(values, position):
    half_dim = HD // 2
    frequency = THETA ** (-2.0 * jnp.arange(half_dim, dtype=jnp.float32) / HD)
    angles = position.astype(jnp.float32)[:, None] * frequency[None, :]
    cosine = jnp.cos(angles)[:, None, :]
    sine_part = jnp.sin(angles)[:, None, :]
    first_half = values[..., :half_dim]
    second_half = values[..., half_dim:]
    return jnp.concatenate(
        [
            first_half * cosine - second_half * sine_part,
            second_half * cosine + first_half * sine_part,
        ],
        axis=-1,
    )


def prepare(query_raw, key_raw, query_gain, key_gain, position):
    return (
        rotate(rms_norm(query_raw, query_gain), position),
        rotate(rms_norm(key_raw, key_gain), position),
    )


def per_device(
    tokens,
    doc_starts,
    out_grad,
    attn_gain,
    w_query,
    w_key,
    w_value,
    q_gain,
    k_gain,
    w_out,
    ffn_gain,
    w_gate,
    w_up,
    w_down,
):
    n_ctx = lax.axis_size("ctx")
    n_wa = lax.axis_size("wa")
    tok_rows = tokens.shape[1]
    stream_len = tok_rows * n_ctx * n_wa
    key_width = min(1024, stream_len)
    key_blocks = stream_len // key_width
    groups = H // KV
    scale = HD ** (-0.5)
    first_row = (lax.axis_index("ctx") * n_wa + lax.axis_index("wa")) * tok_rows
    own_pos = stored_positions(
        first_row + jnp.arange(tok_rows, dtype=jnp.int32), tok_rows, n_ctx, n_wa
    )
    starts = doc_starts[0]
    own_seg = segments(own_pos, starts)
    key_pos = stored_positions(jnp.arange(stream_len, dtype=jnp.int32), tok_rows, n_ctx, n_wa)
    key_seg = segments(key_pos, starts)
    residual = tokens[0].astype(jnp.float32)
    attn_set = (
        lax.all_gather(attn_gain, ("ctx", "wa"), axis=0, tiled=True),
        lax.all_gather(w_query, ("ctx", "wa"), axis=0, tiled=True),
        lax.all_gather(w_key, ("ctx", "wa"), axis=0, tiled=True),
        lax.all_gather(w_value, ("ctx", "wa"), axis=0, tiled=True),
        lax.all_gather(q_gain, ("ctx", "wa"), axis=0, tiled=True),
        lax.all_gather(k_gain, ("ctx", "wa"), axis=0, tiled=True),
        lax.all_gather(w_out, ("ctx", "wa"), axis=0, tiled=True),
    )
    g_attn, wq_full, wk_full, wv_full, gq_full, gk_full, wo_full = attn_set
    attn_gain32 = g_attn.astype(jnp.float32)
    qgain32 = gq_full.astype(jnp.float32)
    kgain32 = gk_full.astype(jnp.float32)
    normed_one = rms_norm(residual, attn_gain32).astype(jnp.bfloat16)
    query_raw = jnp.dot(normed_one, wq_full, preferred_element_type=jnp.float32).reshape(
        tok_rows, H, HD
    )
    key_raw = jnp.dot(normed_one, wk_full, preferred_element_type=jnp.float32).reshape(
        tok_rows, KV, HD
    )
    value_b = jnp.dot(normed_one, wv_full, preferred_element_type=jnp.float32).astype(jnp.bfloat16)
    query_rot, key_rot = prepare(query_raw, key_raw, qgain32, kgain32, own_pos)
    query_b = query_rot.astype(jnp.bfloat16).reshape(tok_rows, KV, groups, HD)
    key_b = key_rot.astype(jnp.bfloat16).reshape(tok_rows, KV * HD)
    all_keys, all_values = (
        lax.all_gather(key_b, ("ctx", "wa"), axis=0, tiled=True),
        lax.all_gather(value_b, ("ctx", "wa"), axis=0, tiled=True),
    )

    def key_block(keys_in, values_in, block_idx):
        begin = block_idx * key_width
        key_part = lax.dynamic_slice_in_dim(keys_in, begin, key_width, 0).reshape(key_width, KV, HD)
        value_part = lax.dynamic_slice_in_dim(values_in, begin, key_width, 0).reshape(
            key_width, KV, HD
        )
        pos_part = lax.dynamic_slice_in_dim(key_pos, begin, key_width, 0)
        seg_part = lax.dynamic_slice_in_dim(key_seg, begin, key_width, 0)
        scores = (
            jnp.einsum("rkgd,tkd->kgrt", query_b, key_part, preferred_element_type=jnp.float32)
            * scale
        )
        allowed = (
            (seg_part[None, :] == own_seg[:, None]) & (pos_part[None, :] <= own_pos[:, None])
        )[None, None]
        return (scores, allowed, key_part, value_part)

    def stat_step(block_idx, carry):
        row_max, row_total = carry
        scores, allowed, key_part, value_part = key_block(all_keys, all_values, block_idx)
        masked = jnp.where(allowed, scores, -1e30)
        new_max = jnp.maximum(row_max, jnp.max(masked, axis=-1))
        fresh = jnp.sum(jnp.where(allowed, jnp.exp(masked - new_max[..., None]), 0.0), axis=-1)
        return (new_max, row_total * jnp.exp(row_max - new_max) + fresh)

    stat_init = (
        jnp.full((KV, groups, tok_rows), -1e30, jnp.float32),
        jnp.zeros((KV, groups, tok_rows), jnp.float32),
    )
    row_max, row_total = lax.fori_loop(0, key_blocks, stat_step, stat_init)

    def out_step(block_idx, summed):
        scores, allowed, key_part, value_part = key_block(all_keys, all_values, block_idx)
        probability = (
            jnp.where(allowed, jnp.exp(scores - row_max[..., None]), 0.0) / row_total[..., None]
        )
        return summed + jnp.einsum(
            "kgrt,tkd->rkgd",
            probability.astype(jnp.bfloat16),
            value_part,
            preferred_element_type=jnp.float32,
        )

    attended = lax.fori_loop(
        0, key_blocks, out_step, jnp.zeros((tok_rows, KV, groups, HD), jnp.float32)
    )
    attended_b = attended.reshape(tok_rows, H * HD).astype(jnp.bfloat16)
    middle = residual + jnp.dot(attended_b, wo_full, preferred_element_type=jnp.float32)
    ffn_set = (
        lax.all_gather(ffn_gain, ("ctx", "wa"), axis=0, tiled=True),
        lax.all_gather(w_gate, ("ctx", "wa"), axis=0, tiled=True),
        lax.all_gather(w_up, ("ctx", "wa"), axis=0, tiled=True),
        lax.all_gather(w_down, ("ctx", "wa"), axis=0, tiled=True),
    )
    g_ffn, wg_full, wu_full, wd_full = ffn_set
    ffn_gain32 = g_ffn.astype(jnp.float32)
    normed_two = rms_norm(middle, ffn_gain32).astype(jnp.bfloat16)
    gate_act = jnp.dot(normed_two, wg_full, preferred_element_type=jnp.float32)
    up_act = jnp.dot(normed_two, wu_full, preferred_element_type=jnp.float32)
    sigmoid_gate = jax.nn.sigmoid(gate_act)
    silu_gate = gate_act * sigmoid_gate
    hidden = (silu_gate * up_act).astype(jnp.bfloat16)
    layer_out = (middle + jnp.dot(hidden, wd_full, preferred_element_type=jnp.float32)).astype(
        jnp.bfloat16
    )
    g_ffn, wg_full, wu_full, wd_full = (
        lax.all_gather(ffn_gain, ("ctx", "wa"), axis=0, tiled=True),
        lax.all_gather(w_gate, ("ctx", "wa"), axis=0, tiled=True),
        lax.all_gather(w_up, ("ctx", "wa"), axis=0, tiled=True),
        lax.all_gather(w_down, ("ctx", "wa"), axis=0, tiled=True),
    )
    d_out = out_grad[0].astype(jnp.float32)
    d_out_b = d_out.astype(jnp.bfloat16)
    d_hidden = jnp.einsum("rd,fd->rf", d_out_b, wd_full, preferred_element_type=jnp.float32)
    d_gate = (d_hidden * up_act * (sigmoid_gate * (1.0 + gate_act * (1.0 - sigmoid_gate)))).astype(
        jnp.bfloat16
    )
    d_up = (d_hidden * silu_gate).astype(jnp.bfloat16)
    d_normed_two = jnp.einsum(
        "rf,df->rd", d_gate, wg_full, preferred_element_type=jnp.float32
    ) + jnp.einsum("rf,df->rd", d_up, wu_full, preferred_element_type=jnp.float32)
    norm_out, norm_back = jax.vjp(rms_norm, middle, ffn_gain32)
    d_middle_part, d_ffn_gain = norm_back(d_normed_two)
    d_middle = d_out + d_middle_part
    gate_up = jnp.concatenate([d_gate, d_up], axis=1)
    part_rows = normed_two
    in_grad = lax.psum_scatter(
        jnp.einsum("rc,rf->cf", part_rows, gate_up, preferred_element_type=jnp.float32),
        ("ctx", "wa"),
        scatter_dimension=0,
        tiled=True,
    )
    part_rows = hidden
    down_grad = lax.psum_scatter(
        jnp.einsum("rc,rd->cd", part_rows, d_out_b, preferred_element_type=jnp.float32),
        ("ctx", "wa"),
        scatter_dimension=0,
        tiled=True,
    )
    g_attn, wq_full, wk_full, wv_full, gq_full, gk_full, wo_full = (
        lax.all_gather(attn_gain, ("ctx", "wa"), axis=0, tiled=True),
        lax.all_gather(w_query, ("ctx", "wa"), axis=0, tiled=True),
        lax.all_gather(w_key, ("ctx", "wa"), axis=0, tiled=True),
        lax.all_gather(w_value, ("ctx", "wa"), axis=0, tiled=True),
        lax.all_gather(q_gain, ("ctx", "wa"), axis=0, tiled=True),
        lax.all_gather(k_gain, ("ctx", "wa"), axis=0, tiled=True),
        lax.all_gather(w_out, ("ctx", "wa"), axis=0, tiled=True),
    )
    d_branch = d_middle.astype(jnp.bfloat16)
    wo_grad = jnp.einsum("re,rd->ed", attended_b, d_branch, preferred_element_type=jnp.float32)
    d_attended = jnp.einsum(
        "rd,ed->re", d_branch, wo_full, preferred_element_type=jnp.float32
    ).astype(jnp.bfloat16)
    d_att4 = d_attended.reshape(tok_rows, KV, groups, HD)
    delta = jnp.einsum("rkgd,rkgd->kgr", d_att4.astype(jnp.float32), attended)

    def back_step(d_query, block_idx):
        scores, allowed, key_part, value_part = key_block(all_keys, all_values, block_idx)
        probability = (
            jnp.where(allowed, jnp.exp(scores - row_max[..., None]), 0.0) / row_total[..., None]
        )
        d_prob = jnp.einsum(
            "rkgd,tkd->kgrt", d_att4, value_part, preferred_element_type=jnp.float32
        )
        d_scores = (probability * (d_prob - delta[..., None])).astype(jnp.bfloat16)
        d_query = (
            d_query
            + jnp.einsum("kgrt,tkd->rkgd", d_scores, key_part, preferred_element_type=jnp.float32)
            * scale
        )
        d_key_part = (
            jnp.einsum("kgrt,rkgd->tkd", d_scores, query_b, preferred_element_type=jnp.float32)
            * scale
        )
        d_value_part = jnp.einsum(
            "kgrt,rkgd->tkd",
            probability.astype(jnp.bfloat16),
            d_att4,
            preferred_element_type=jnp.float32,
        )
        return (
            d_query,
            (d_key_part.reshape(key_width, KV * HD), d_value_part.reshape(key_width, KV * HD)),
        )

    d_query, (d_keys, d_values) = lax.scan(
        back_step, jnp.zeros((tok_rows, KV, groups, HD), jnp.float32), jnp.arange(key_blocks)
    )
    d_key_own, d_value_own = (
        lax.psum_scatter(
            d_keys.reshape(stream_len, KV * HD), ("ctx", "wa"), scatter_dimension=0, tiled=True
        ),
        lax.psum_scatter(
            d_values.reshape(stream_len, KV * HD), ("ctx", "wa"), scatter_dimension=0, tiled=True
        ),
    )
    prep_out, prep_back = jax.vjp(
        partial(prepare, position=own_pos), query_raw, key_raw, qgain32, kgain32
    )
    d_query_raw, d_key_raw, d_qgain, d_kgain = prep_back(
        (d_query.reshape(tok_rows, H, HD), d_key_own.reshape(tok_rows, KV, HD))
    )
    dq_b = d_query_raw.reshape(tok_rows, H * HD).astype(jnp.bfloat16)
    dk_b = d_key_raw.reshape(tok_rows, KV * HD).astype(jnp.bfloat16)
    dv_b = d_value_own.astype(jnp.bfloat16)
    d_normed_one = (
        jnp.einsum("re,de->rd", dq_b, wq_full, preferred_element_type=jnp.float32)
        + jnp.einsum("re,de->rd", dk_b, wk_full, preferred_element_type=jnp.float32)
        + jnp.einsum("re,de->rd", dv_b, wv_full, preferred_element_type=jnp.float32)
    )
    first_out, first_back = jax.vjp(rms_norm, residual, attn_gain32)
    d_res_part, d_attn_gain = first_back(d_normed_one)
    input_grad = (d_middle + d_res_part).astype(jnp.bfloat16)
    wq_grad = jnp.einsum("rc,re->ce", normed_one, dq_b, preferred_element_type=jnp.float32)
    wk_grad = jnp.einsum("rc,re->ce", normed_one, dk_b, preferred_element_type=jnp.float32)
    wv_grad = jnp.einsum("rc,re->ce", normed_one, dv_b, preferred_element_type=jnp.float32)
    attn_terms = (d_attn_gain, wq_grad, wk_grad, wv_grad, d_qgain, d_kgain, d_ffn_gain, wo_grad)
    attn_shards = (
        lax.psum_scatter(attn_terms[0], ("ctx", "wa"), scatter_dimension=0, tiled=True),
        lax.psum_scatter(attn_terms[1], ("ctx", "wa"), scatter_dimension=0, tiled=True),
        lax.psum_scatter(attn_terms[2], ("ctx", "wa"), scatter_dimension=0, tiled=True),
        lax.psum_scatter(attn_terms[3], ("ctx", "wa"), scatter_dimension=0, tiled=True),
        lax.psum_scatter(attn_terms[4], ("ctx", "wa"), scatter_dimension=0, tiled=True),
        lax.psum_scatter(attn_terms[5], ("ctx", "wa"), scatter_dimension=0, tiled=True),
        lax.psum_scatter(attn_terms[6], ("ctx", "wa"), scatter_dimension=0, tiled=True),
        lax.psum_scatter(attn_terms[7], ("ctx", "wa"), scatter_dimension=0, tiled=True),
    )
    wo_shard = attn_shards[7]
    summed = (
        lax.psum(attn_shards[0].astype(jnp.bfloat16), "dp").astype(jnp.float32),
        lax.psum(attn_shards[1].astype(jnp.bfloat16), "dp").astype(jnp.float32),
        lax.psum(attn_shards[2].astype(jnp.bfloat16), "dp").astype(jnp.float32),
        lax.psum(attn_shards[3].astype(jnp.bfloat16), "dp").astype(jnp.float32),
        lax.psum(attn_shards[4].astype(jnp.bfloat16), "dp").astype(jnp.float32),
        lax.psum(attn_shards[5].astype(jnp.bfloat16), "dp").astype(jnp.float32),
        lax.psum(wo_shard.astype(jnp.bfloat16), "dp").astype(jnp.float32),
        lax.psum(attn_shards[6].astype(jnp.bfloat16), "dp").astype(jnp.float32),
        lax.psum(in_grad[:, :FF].astype(jnp.bfloat16), "dp").astype(jnp.float32),
        lax.psum(in_grad[:, FF:].astype(jnp.bfloat16), "dp").astype(jnp.float32),
        lax.psum(down_grad.astype(jnp.bfloat16), "dp").astype(jnp.float32),
    )
    return (layer_out[None], input_grad[None]) + tuple(summed)


AXES = ("ctx", "wa")
LANES = 2 * HD
ROWS_BLOCK = 256
FFN_BLOCK = 512
ROOM = 60 * 2**20
SIDE_ROWS = 256
LOG2E = 1.4426950408889634
F32 = jnp.float32
BF16 = jnp.bfloat16


def low_key(starts, row):
    first = jnp.int32(0)
    for doc in range(starts.shape[1]):
        begin = starts[0, doc]
        first = jnp.where(begin <= row, begin, first)
    return first


def block_mask(starts, q_begin, k_begin, bq, bk):
    row = q_begin + lax.broadcasted_iota(jnp.int32, (bq, 1), 0)
    first = low_key(starts, row)
    col = k_begin + lax.broadcasted_iota(jnp.int32, (1, bk), 1)
    return (col >= first) & (col <= row)


def rope_tables(stream):
    frequency = np.float32(THETA) ** (-2.0 * np.arange(HD // 2, dtype=np.float32) / np.float32(HD))
    angles = np.arange(stream, dtype=np.float32)[:, None] * frequency.astype(np.float32)[None, :]
    cosine = np.cos(angles.astype(np.float64)).astype(np.float32)
    sine = np.sin(angles.astype(np.float64)).astype(np.float32)
    return np.tile(cosine, (1, 4)), np.tile(np.concatenate([-sine, sine], axis=1), (1, 2))


def lane_ids():
    return lax.broadcasted_iota(jnp.int32, (1, LANES), 1)


def head_mean(values):
    low = jnp.sum(values[:, :HD], axis=1, keepdims=True)
    high = jnp.sum(values[:, HD:], axis=1, keepdims=True)
    return jnp.where(lane_ids() < HD, low, high) * (1.0 / HD)


def swap_halves(values):
    first = lane_ids() % HD < HD // 2
    return jnp.where(
        first, pltpu.roll(values, LANES - HD // 2, 1), pltpu.roll(values, HD // 2, 1)
    )


def norm_rope(raw, gain, cosine, sine):
    scaled = raw * lax.rsqrt(head_mean(raw * raw) + EPS) * gain
    return scaled * cosine + swap_halves(scaled) * sine


def norm_rope_back(grad, raw, gain, cosine, sine):
    inverse = lax.rsqrt(head_mean(raw * raw) + EPS)
    unit = raw * inverse
    d_scaled = grad * cosine + swap_halves(grad * sine)
    d_unit = d_scaled * gain
    return inverse * (d_unit - unit * head_mean(d_unit * unit)), d_scaled * unit


def stack_heads(rows, at_low):
    lanes = lane_ids()
    zero = jnp.zeros_like(rows)
    low, high = jnp.where(lanes < HD, rows, zero), jnp.where(lanes < HD, zero, rows)
    turned = pltpu.roll(high if at_low else low, HD, 1)
    return jnp.concatenate([low, turned] if at_low else [turned, high], axis=0)


def dot(a, b):
    return jnp.dot(a, b, preferred_element_type=F32)


def dot_t(a, b):
    return lax.dot_general(a, b, (((1,), (1,)), ((), ())), preferred_element_type=F32)


def t_dot(a, b):
    return lax.dot_general(a, b, (((0,), (0,)), ((), ())), preferred_element_type=F32)


def join_halves(half, own_ref, other_ref, whole_ref):
    own_row = jnp.where(lax.axis_index("dp") == 0, 0, half)

    def put(j, carry):
        for begin, ref in ((own_row, own_ref), (half - own_row, other_ref)):
            at = pl.multiple_of(2 * half * j + begin, half)
            whole_ref[pl.ds(at, half), :] = ref[j, :half, :]
        return carry

    lax.fori_loop(0, own_ref.shape[0], put, 0)


def attend_kernel(
    starts, x_ref, gain_ref, own_ref, other_ref, head_gain_ref, cos_ref, sin_ref,
    normed_ref, raw_ref, q_ref, kv_ref, att_ref, inv_ref, w_ref, ov_ref,
):
    block = pl.program_id(0)

    @pl.when(block == 0)
    def _():
        join_halves(w_ref.shape[0] // own_ref.shape[0] // 2, own_ref, other_ref, w_ref)

    bq = x_ref.shape[0]
    q_begin = pl.multiple_of(block * bq, bq)
    x = x_ref[...].astype(F32)
    inverse = lax.rsqrt(jnp.mean(x * x, axis=1, keepdims=True) + EPS)
    normed = (x * inverse * gain_ref[...]).astype(BF16)
    normed_ref[...] = normed
    raw = dot(normed, w_ref[...])
    raw_ref[...] = raw
    cosine, sine = cos_ref[...], sin_ref[...]
    q = norm_rope(raw[:, :LANES], head_gain_ref[:, :LANES], cosine, sine)
    q_ref[...] = q.astype(BF16)
    kv_raw = raw[:, LANES:]
    is_key = lane_ids() < HD
    turned = norm_rope(kv_raw, head_gain_ref[:, LANES:], cosine, sine)
    kv_ref[pl.ds(q_begin, bq), :] = jnp.where(is_key, turned, kv_raw).astype(BF16)
    ov_ref[pl.ds(q_begin, bq), :] = jnp.where(is_key, 1.0, kv_raw).astype(BF16)
    q2 = stack_heads(q, True).astype(BF16)

    def step(j, acc):
        k_begin = pl.multiple_of(j * bq, bq)
        s = dot_t(q2, kv_ref[pl.ds(k_begin, bq), :])
        mask = block_mask(starts, q_begin, k_begin, bq, bq)
        p = jnp.exp2(s * (LOG2E * HD**-0.5))
        p = jnp.where(jnp.concatenate([mask, mask], axis=0), p, 0.0).astype(BF16)
        return acc + dot(p, ov_ref[pl.ds(k_begin, bq), :])

    low = low_key(starts, q_begin) // bq
    acc = lax.fori_loop(low, block + 1, step, jnp.zeros((2 * bq, LANES), F32))
    inv = 1.0 / acc[:, :1]
    out = acc * inv
    att = jnp.where(is_key, pltpu.roll(out[:bq], HD, 1), out[bq:]).astype(BF16)
    att_ref[...] = att
    inv_ref[...] = jnp.where(is_key, inv[:bq], inv[bq:])


def attend(starts, x_all, gain, own, other, head_gain, cosine, sine):
    stream, width = x_all.shape
    bq = ROWS_BLOCK

    def rows(cols):
        return pl.BlockSpec((bq, cols), lambda i: (i, 0))

    def whole(shape):
        return pl.BlockSpec(shape, lambda i: (0,) * len(shape), pipeline_mode=pl.Buffered(1))

    return pl.pallas_call(
        attend_kernel,
        grid=(stream // bq,),
        in_specs=[
            pl.BlockSpec(memory_space=pltpu.SMEM),
            rows(width),
            whole((1, width)),
            whole(own.shape),
            whole(own.shape),
            whole((1, 2 * LANES)),
            rows(LANES),
            rows(LANES),
        ],
        out_specs=[
            rows(width),
            rows(2 * LANES),
            rows(LANES),
            pl.BlockSpec((stream, LANES), lambda i: (0, 0)),
            rows(LANES),
            rows(LANES),
            whole((width, 2 * LANES)),
        ],
        out_shape=[
            jax.ShapeDtypeStruct((stream, width), BF16),
            jax.ShapeDtypeStruct((stream, 2 * LANES), F32),
            jax.ShapeDtypeStruct((stream, LANES), BF16),
            jax.ShapeDtypeStruct((stream, LANES), BF16),
            jax.ShapeDtypeStruct((stream, LANES), BF16),
            jax.ShapeDtypeStruct((stream, LANES), F32),
            jax.ShapeDtypeStruct((width, 2 * LANES), BF16),
        ],
        scratch_shapes=[pltpu.VMEM((stream, LANES), BF16)],
        compiler_params=pltpu.CompilerParams(vmem_limit_bytes=ROOM),
        cost_estimate=pl.CostEstimate(flops=2 * 10**10, bytes_accessed=2**25, transcendentals=0),
    )(starts, x_all, gain, own, other, head_gain, cosine, sine)


def attend_back_kernel(
    starts, db_ref, w_out_ref, q_ref, kv_ref, att_ref, inv_ref, raw_ref, head_gain_ref, cos_ref, sin_ref,
    d_ref, gain_ref, dkv_ref,
):
    block = pl.program_id(0)
    bq = db_ref.shape[0]
    q_begin = pl.multiple_of(block * bq, bq)

    @pl.when(block == 0)
    def _():
        dkv_ref[...] = jnp.zeros_like(dkv_ref)
        gain_ref[...] = jnp.zeros_like(gain_ref)

    db = db_ref[...]
    att = att_ref[...]
    da = dot_t(db, w_out_ref[...])
    q2 = stack_heads(q_ref[...].astype(F32), True).astype(BF16)
    da2 = stack_heads(da, False).astype(BF16)
    prod = da.astype(BF16).astype(F32) * att.astype(F32)
    delta = jnp.concatenate(
        [
            jnp.sum(prod[:, :HD], axis=1, keepdims=True),
            jnp.sum(prod[:, HD:], axis=1, keepdims=True),
        ],
        axis=0,
    )
    inv_all = inv_ref[...]
    inv = jnp.concatenate([inv_all[:, :1], inv_all[:, HD : HD + 1]], axis=0)

    def step(j, dq):
        k_begin = pl.multiple_of(j * bq, bq)
        keys = kv_ref[pl.ds(k_begin, bq), :]
        s = dot_t(q2, keys)
        mask = block_mask(starts, q_begin, k_begin, bq, bq)
        p = jnp.exp2(s * (LOG2E * HD**-0.5)) * inv
        p = jnp.where(jnp.concatenate([mask, mask], axis=0), p, 0.0)
        ds = (p * (dot_t(da2, keys) - delta)).astype(BF16)
        dkv_ref[pl.ds(k_begin, bq), :] += t_dot(ds, q2) * HD**-0.5 + t_dot(p.astype(BF16), da2)
        return dq + dot(ds, keys)

    low = low_key(starts, q_begin) // bq
    dq = lax.fori_loop(low, block + 1, step, jnp.zeros((2 * bq, LANES), F32))
    is_key = lane_ids() < HD
    dq = jnp.where(is_key, dq[:bq], pltpu.roll(dq[bq:], HD, 1)) * HD**-0.5
    here = pl.ds(q_begin, bq)
    d_raw, d_gain = norm_rope_back(
        dq, raw_ref[here, :LANES], head_gain_ref[:, :LANES], cos_ref[here, :], sin_ref[here, :]
    )
    d_ref[here, :LANES] = d_raw.astype(BF16)
    gain_ref[0:1, :] += jnp.sum(d_gain, axis=0, keepdims=True)

    @pl.when(block == pl.num_programs(0) - 1)
    def _():
        def finish(j, carry):
            rows = pl.ds(pl.multiple_of(j * bq, bq), bq)
            dkv = dkv_ref[rows, :]
            d_raw, d_gain = norm_rope_back(
                dkv, raw_ref[rows, LANES:], head_gain_ref[:, LANES:], cos_ref[rows, :], sin_ref[rows, :]
            )
            d_ref[rows, LANES:] = jnp.where(is_key, d_raw, dkv).astype(BF16)
            gain_ref[1:2, :] += jnp.sum(d_gain, axis=0, keepdims=True)
            return carry

        lax.fori_loop(0, pl.num_programs(0), finish, 0)


def attend_back(starts, db_all, w_out, q, kv, att, inv, raw, head_gain, cosine, sine):
    stream, width = db_all.shape
    bq = ROWS_BLOCK

    def rows(cols):
        return pl.BlockSpec((bq, cols), lambda i: (i, 0))

    def whole(shape):
        return pl.BlockSpec(shape, lambda i: (0, 0), pipeline_mode=pl.Buffered(1))

    def kept(shape):
        return pl.BlockSpec(shape, lambda i: (0, 0))

    return pl.pallas_call(
        attend_back_kernel,
        grid=(stream // bq,),
        in_specs=[
            pl.BlockSpec(memory_space=pltpu.SMEM),
            rows(width),
            whole(w_out.shape),
            rows(LANES),
            whole((stream, LANES)),
            rows(LANES),
            rows(LANES),
            whole((stream, 2 * LANES)),
            whole((1, 2 * LANES)),
            whole((stream, LANES)),
            whole((stream, LANES)),
        ],
        out_specs=[kept((stream, 2 * LANES)), kept((8, LANES))],
        out_shape=[
            jax.ShapeDtypeStruct((stream, 2 * LANES), BF16),
            jax.ShapeDtypeStruct((8, LANES), F32),
        ],
        scratch_shapes=[pltpu.VMEM((stream, LANES), F32)],
        compiler_params=pltpu.CompilerParams(vmem_limit_bytes=ROOM),
        cost_estimate=pl.CostEstimate(flops=3 * 10**10, bytes_accessed=2**25, transcendentals=0),
    )(starts, db_all, w_out, q, kv, att, inv, raw, head_gain, cosine, sine)


def ffn_kernel(
    n2_ref, dy_ref, own_ref, other_ref, w_down_ref, hidden_ref, d_gu_ref, gu_grad_ref, w_gu_ref, gu_acc
):
    block = pl.program_id(0)

    @pl.when(block == 0)
    def _():
        join_halves(own_ref.shape[1], own_ref, other_ref, w_gu_ref)
        gu_acc[...] = jnp.zeros_like(gu_acc)

    cols = hidden_ref.shape[1]
    n2 = n2_ref[...]
    gate_up = dot(n2, w_gu_ref[...])
    d_hidden = dot_t(dy_ref[...], w_down_ref[...])
    gate, up = gate_up[:, :cols], gate_up[:, cols:]
    sig = jax.nn.sigmoid(gate)
    silu = gate * sig
    hidden_ref[...] = (silu * up).astype(BF16)
    d_gu = jnp.concatenate(
        [
            (d_hidden * up * (sig * (1.0 + gate * (1.0 - sig)))).astype(BF16),
            (d_hidden * silu).astype(BF16),
        ],
        axis=1,
    )
    d_gu_ref[...] = d_gu
    gu_acc[...] += t_dot(n2, d_gu)

    @pl.when(block == pl.num_programs(0) - 1)
    def _():
        gu_grad_ref[...] = gu_acc[...].astype(BF16)


def ffn(n2_all, dy_all, own, other, w_down):
    stream, width = n2_all.shape
    both = own.shape[2]
    bt = FFN_BLOCK

    def rows(cols):
        return pl.BlockSpec((bt, cols), lambda i: (i, 0))

    def whole(shape):
        return pl.BlockSpec(shape, lambda i: (0,) * len(shape), pipeline_mode=pl.Buffered(1))

    return pl.pallas_call(
        ffn_kernel,
        grid=(stream // bt,),
        in_specs=[rows(width), rows(width), whole(own.shape), whole(own.shape), whole(w_down.shape)],
        out_specs=[rows(both // 2), rows(both), whole((width, both)), whole((width, both))],
        out_shape=[
            jax.ShapeDtypeStruct((stream, both // 2), BF16),
            jax.ShapeDtypeStruct((stream, both), BF16),
            jax.ShapeDtypeStruct((width, both), BF16),
            jax.ShapeDtypeStruct((width, both), BF16),
        ],
        scratch_shapes=[pltpu.VMEM((width, both), F32)],
        compiler_params=pltpu.CompilerParams(vmem_limit_bytes=ROOM),
        cost_estimate=pl.CostEstimate(
            flops=5 * stream * width * both, bytes_accessed=2**25, transcendentals=0
        ),
    )(n2_all, dy_all, own, other, w_down)


def unpack_attn_kernel(
    own_ref, other_ref, wq_ref, wk_ref, wv_ref, q_ref, k_ref, v_ref, sum_ref, gains_ref
):
    n, half = own_ref.shape[0], wq_ref.shape[0] // 2
    first = lax.axis_index("dp") == 0
    low = jnp.where(first, 0, half)
    high = half - low
    share = n // KV
    gains_ref[...] = jnp.sum(own_ref[:, half:, :].astype(F32), axis=0)
    for begin, ref in ((low, own_ref), (high, other_ref)):
        rows = pl.ds(pl.multiple_of(begin, half), half)
        total = jnp.zeros((half, LANES), F32)
        for j in range(n):
            cols = slice(j * LANES, (j + 1) * LANES)
            q = ref[j, :half, :LANES].astype(F32)
            q_ref[rows, cols] = q
            total += q * wq_ref[rows, cols].astype(F32)
        for pair in range(KV // 2):
            cols = slice(pair * LANES, (pair + 1) * LANES)
            heads = []
            for head in (2 * pair, 2 * pair + 1):
                kv = ref[head * share, :half, LANES:].astype(F32)
                for more in range(1, share):
                    kv = kv + ref[head * share + more, :half, LANES:].astype(F32)
                heads.append(kv)
            k = jnp.concatenate([heads[0][:, :HD], heads[1][:, :HD]], axis=1)
            v = jnp.concatenate([heads[0][:, HD:], heads[1][:, HD:]], axis=1)
            k_ref[rows, cols] = k
            v_ref[rows, cols] = v
            total += k * wk_ref[rows, cols].astype(F32) + v * wv_ref[rows, cols].astype(F32)
        sum_ref[rows, :] = total


def unpack_attn(own, other, w_query, w_key, w_value):
    d_rows = w_query.shape[0]
    return pl.pallas_call(
        unpack_attn_kernel,
        out_shape=[
            jax.ShapeDtypeStruct(w_query.shape, F32),
            jax.ShapeDtypeStruct(w_key.shape, F32),
            jax.ShapeDtypeStruct(w_value.shape, F32),
            jax.ShapeDtypeStruct((d_rows, LANES), F32),
            jax.ShapeDtypeStruct((own.shape[1] - d_rows // 2, 2 * LANES), F32),
        ],
        compiler_params=pltpu.CompilerParams(vmem_limit_bytes=32 * 2**20),
    )(own, other, w_query, w_key, w_value)


def pack_attn_kernel(query_ref, key_ref, value_ref, gains_ref, out_ref):
    n = out_ref.shape[0]
    half = query_ref.shape[0] // 2
    share = n // KV
    rows = pl.ds(pl.multiple_of(lax.axis_index("dp") * half, half), half)
    keys, values = key_ref[rows, :], value_ref[rows, :]
    for j in range(n):
        head = j // share * HD
        out_ref[j, :half, :LANES] = query_ref[rows, j * LANES : (j + 1) * LANES]
        out_ref[j, :half, LANES:] = jnp.concatenate(
            [keys[:, head : head + HD], values[:, head : head + HD]], axis=1
        )
        out_ref[j, half:, :] = gains_ref[...]


def pack_attn(w_query, w_key, w_value, gains, n):
    half = w_query.shape[0] // 2
    return pl.pallas_call(
        pack_attn_kernel,
        out_shape=jax.ShapeDtypeStruct((n, half + gains.shape[0], 2 * LANES), BF16),
    )(w_query, w_key, w_value, gains)


def unpack_pair_kernel(own_ref, other_ref, gate_w, up_w, gate_ref, up_ref, sum_ref):
    count, half, both = own_ref.shape
    cols = both // 2
    first = lax.axis_index("dp") == 0

    @pl.when(pl.program_id(0) == 0)
    def _():
        sum_ref[...] = jnp.zeros_like(sum_ref)

    own_row = pl.multiple_of(jnp.where(first, 0, half), half)
    for begin, ref in ((own_row, own_ref), (half - own_row, other_ref)):
        rows = pl.ds(pl.multiple_of(begin, half), half)
        total = jnp.zeros((half, 128), F32)
        for j in range(count):
            for at in range(0, cols, 128):
                here = slice(j * cols + at, j * cols + at + 128)
                gate = ref[j, :, at : at + 128].astype(F32)
                up = ref[j, :, cols + at : cols + at + 128].astype(F32)
                gate_ref[rows, here] = gate
                up_ref[rows, here] = up
                total += gate * gate_w[rows, here].astype(F32) + up * up_w[rows, here].astype(F32)
        sum_ref[rows, :] += total


def unpack_pair(own, other, w_gate, w_up):
    n, half, both = own.shape
    count = 4
    block = pl.BlockSpec((count, half, both), lambda j: (j, 0, 0))
    part = pl.BlockSpec((2 * half, count * both // 2), lambda j: (0, j))
    return pl.pallas_call(
        unpack_pair_kernel,
        grid=(n // count,),
        in_specs=[block, block, part, part],
        out_specs=[part, part, pl.BlockSpec((2 * half, 128), lambda j: (0, 0))],
        out_shape=[
            jax.ShapeDtypeStruct(w_gate.shape, F32),
            jax.ShapeDtypeStruct(w_up.shape, F32),
            jax.ShapeDtypeStruct((2 * half, 128), F32),
        ],
        compiler_params=pltpu.CompilerParams(vmem_limit_bytes=32 * 2**20),
    )(own, other, w_gate, w_up)


MESH_ID = pl.DeviceIdType.MESH
LINK_COST = pl.CostEstimate(flops=5 * 10**10, bytes_accessed=2**24, transcendentals=0)


def meet_neighbours(ctx, wa, n_ctx, n_wa, everyone):
    barrier = pltpu.get_barrier_semaphore()

    def greet(where):
        pl.semaphore_signal(barrier, inc=1, device_id=where, device_id_type=MESH_ID)

    greet({"dp": lax.axis_index("dp") ^ 1})
    if everyone:
        n = n_ctx * n_wa

        def step(i, carry):
            other = lax.rem(ctx * n_wa + wa + i, n)
            greet({"ctx": other // n_wa, "wa": lax.rem(other, n_wa)})
            return carry

        lax.fori_loop(1, n, step, 0)
        pl.semaphore_wait(barrier, n)
        return
    greet({"wa": wa ^ 1})
    greet({"wa": wa ^ 2})
    pl.when(ctx > 0)(lambda: greet({"ctx": ctx - 1}))
    pl.when(ctx < n_ctx - 1)(lambda: greet({"ctx": ctx + 1}))
    ends = (ctx == 0).astype(jnp.int32) + (ctx == n_ctx - 1).astype(jnp.int32)
    pl.semaphore_wait(barrier, 5 - ends)


WHOLE, PICK, SPREAD = 0, 1, 2


def pair_outs(kind):
    return 2 if kind == SPREAD else 1


def pair_shape(kind, src):
    if kind == PICK:
        return (src.shape[0],) + src.shape[2:]
    return src.shape


def start_spread(src, dst, n_wa, sems):
    n = src.shape[0]
    me = lax.axis_index("ctx") * n_wa + lax.axis_index("wa")
    keep = pltpu.make_async_copy(src.at[me], dst.at[me], sems.at[0, 0])
    keep.start()

    def made(step, arriving):
        other = lax.rem(me + step, n)
        return pltpu.make_async_remote_copy(
            src_ref=src.at[other],
            dst_ref=dst.at[other if arriving else me],
            send_sem=sems.at[0, step],
            recv_sem=sems.at[1, other if arriving else me],
            device_id={"ctx": other // n_wa, "wa": lax.rem(other, n_wa)},
            device_id_type=MESH_ID,
        )

    def loop(act):
        def step(i, carry):
            act(i)
            return carry

        lax.fori_loop(1, n, step, 0)

    def finish():
        keep.wait()
        loop(lambda i: made(i, True).wait_recv())
        loop(lambda i: made(i, False).wait_send())

    loop(lambda i: made(i, False).start())
    return finish


def start_pairs(kinds, srcs, dsts, n_wa, sems, spread_sems):
    dp = lax.axis_index("dp")
    dsts = list(dsts)
    midway = []

    def exchange(at, src, dst):
        send = pltpu.make_async_remote_copy(
            src_ref=src,
            dst_ref=dst,
            send_sem=sems.at[at, 0],
            recv_sem=sems.at[at, 1],
            device_id={"dp": dp ^ 1},
            device_id_type=MESH_ID,
        )
        send.start()
        return send.wait

    for at, (kind, src) in enumerate(zip(kinds, srcs)):
        dst = dsts.pop(0)
        if kind == SPREAD:
            finish, other = start_spread(src, dst, n_wa, spread_sems), dsts.pop(0)

            def pass_on(at=at, finish=finish, dst=dst, other=other):
                finish()
                return exchange(at, dst, other)

            midway.append(pass_on)
            continue
        if kind == PICK:
            src = src.at[:, dp ^ 1]
        wait = exchange(at, src, dst)
        midway.append(lambda wait=wait: wait)
    return midway


def piece_row(zc, wac, h, half, n_ctx, n_wa, by_position):
    if by_position:
        span = zc if h == 0 else 2 * n_ctx - 1 - zc
        return pl.multiple_of((span * n_wa + wac) * half, half)
    return pl.multiple_of(((zc * n_wa + wac) * 2 + h) * half, half)


def unit_rows(values):
    return lax.rsqrt(jnp.mean(values * values, axis=1, keepdims=True) + EPS)


def norm_back(grad, values, gain):
    inverse = unit_rows(values)
    d_unit = grad * gain
    unit = values * inverse
    return inverse * (d_unit - unit * jnp.mean(d_unit * unit, axis=1, keepdims=True))


def after_attention(total, x, gain):
    middle = x.astype(F32) + total
    return middle, middle * unit_rows(middle) * gain


def after_ffn_back(total, middle, gain, d_out):
    d_middle = d_out.astype(F32) + norm_back(total, middle, gain)
    return d_middle, d_middle


def after_attention_back(total, x, gain, d_middle):
    return (d_middle + norm_back(total, x.astype(F32), gain),)


class PackColumns:
    def __init__(self, w_gate, w_up, n):
        self.operands = [w_gate, w_up]
        half, cols = w_gate.shape[0] // 2, w_gate.shape[1] // n
        self.outs = [jax.ShapeDtypeStruct((n, half, 2 * cols), BF16)]
        self.scratch = [
            pltpu.VMEM((half, w_gate.shape[1]), BF16),
            pltpu.VMEM((half, w_gate.shape[1]), BF16),
            pltpu.VMEM((n, half, 2 * cols), BF16),
            pltpu.SemaphoreType.DMA((3,)),
        ]

    def bind(self, ins, outs, scratch):
        self.rows_v, (self.packed, sem) = scratch[:2], scratch[2:]
        half = self.packed.shape[1]
        rows = pl.ds(pl.multiple_of(lax.axis_index("dp") * half, half), half)
        self.loads = [
            pltpu.make_async_copy(ins[at].at[rows], self.rows_v[at], sem.at[at]) for at in range(2)
        ]
        for load in self.loads:
            load.start()
        self.store = pltpu.make_async_copy(self.packed, outs[0], sem.at[2])
        self.at = 0

    def step(self):
        self.at += 1
        if self.at != 2:
            return
        for load in self.loads:
            load.wait()
        n, _, both = self.packed.shape
        cols = both // 2
        for j in range(n):
            for at in range(2):
                self.packed[j, :, at * cols : (at + 1) * cols] = self.rows_v[at][
                    :, j * cols : (j + 1) * cols
                ]
        self.store.start()

    def finish(self):
        self.store.wait()


class PairSum:
    def __init__(self, halves, other):
        self.operands = [halves, other]
        self.outs = [jax.ShapeDtypeStruct(other.shape, BF16)]
        self.scratch = [pltpu.VMEM(other.shape, BF16)] * 2 + [pltpu.SemaphoreType.DMA((3,))]

    def bind(self, ins, outs, scratch):
        self.mine_v, self.other_v, self.sem = scratch
        mine = ins[0].at[:, lax.axis_index("dp")]
        self.loads = [
            pltpu.make_async_copy(mine, self.mine_v, self.sem.at[0]),
            pltpu.make_async_copy(ins[1], self.other_v, self.sem.at[1]),
        ]
        for load in self.loads:
            load.start()
        self.store = pltpu.make_async_copy(self.mine_v, outs[0], self.sem.at[2])
        self.at = 0

    def step(self):
        self.at += 1
        if self.at != 2:
            return
        for load in self.loads:
            load.wait()

        def add(j, carry):
            total = self.mine_v[j].astype(F32) + self.other_v[j].astype(F32)
            self.mine_v[j] = total.astype(BF16)
            return carry

        lax.fori_loop(0, self.mine_v.shape[0], add, 0)
        self.store.start()

    def finish(self):
        self.store.wait()


class DownProducts:
    def __init__(self, dy, w_down, hidden):
        self.operands = [dy, w_down, hidden]
        self.steps = dy.shape[0] // SIDE_ROWS
        self.outs = [
            jax.ShapeDtypeStruct(dy.shape, BF16),
            jax.ShapeDtypeStruct(w_down.shape, BF16),
        ]
        self.scratch = [
            pltpu.VMEM((2, SIDE_ROWS, dy.shape[1]), BF16),
            pltpu.VMEM((2, SIDE_ROWS, dy.shape[1]), BF16),
            pltpu.VMEM(w_down.shape, BF16),
            pltpu.VMEM(hidden.shape, BF16),
            pltpu.VMEM(w_down.shape, F32),
            pltpu.VMEM(w_down.shape, BF16),
            pltpu.SemaphoreType.DMA((7,)),
        ]

    def bind(self, ins, outs, scratch):
        self.dy, (self.out, self.grad) = ins[0], outs
        self.dy_v, self.stage, self.w_v, self.hidden_v, self.acc, self.grad_v, self.sem = scratch
        self.loads = [
            pltpu.make_async_copy(ins[1], self.w_v, self.sem.at[4]),
            pltpu.make_async_copy(ins[2], self.hidden_v, self.sem.at[5]),
        ]
        for load in self.loads:
            load.start()
        self.load(0).start()
        self.acc[...] = jnp.zeros_like(self.acc)
        self.stored = []
        self.at = 0

    def load(self, g):
        rows = pl.ds(g * SIDE_ROWS, SIDE_ROWS)
        return pltpu.make_async_copy(self.dy.at[rows], self.dy_v.at[g % 2], self.sem.at[g % 2])

    def step(self):
        g = self.at
        if g >= self.steps:
            return
        self.at += 1
        if g == 0:
            for load in self.loads:
                load.wait()
        self.load(g).wait()
        if g + 1 < self.steps:
            self.load(g + 1).start()
        rows = pl.ds(g * SIDE_ROWS, SIDE_ROWS)
        if g >= 2:
            self.stored[g - 2].wait()
        hidden = self.hidden_v[rows, :]
        self.stage[g % 2] = dot(hidden, self.w_v[...]).astype(BF16)
        self.acc[...] += t_dot(hidden, self.dy_v[g % 2])
        store = pltpu.make_async_copy(self.stage.at[g % 2], self.out.at[rows], self.sem.at[2 + g % 2])
        store.start()
        self.stored.append(store)

    def finish(self):
        while self.at < self.steps:
            self.step()
        for store in self.stored[-2:]:
            store.wait()
        self.grad_v[...] = self.acc[...].astype(BF16)
        made = pltpu.make_async_copy(self.grad_v, self.grad, self.sem.at[6])
        made.start()
        made.wait()


def split_side(side, at, refs):
    count = len(side.operands) if side else 0
    return refs[at : at + count], refs[:at] + refs[at + count :]


def gather_kernel(n_ctx, n_wa, by_position, kinds, side, own_ref, *refs):
    pairs = len(kinds)
    outs = sum(pair_outs(kind) for kind in kinds)
    side_in, refs = split_side(side, pairs, refs)
    srcs, out_ref, dsts = refs[:pairs], refs[pairs], refs[pairs + 1 : pairs + outs + 1]
    refs = refs[pairs + outs + 1 :]
    side_out, refs = refs[: len(side.outs) if side else 0], refs[len(side.outs) if side else 0 :]
    own_sem, send_sem, recv_sem, pair_sem, spread_sem = refs[:5]
    ctx = lax.axis_index("ctx")
    wa = lax.axis_index("wa")
    half = own_ref.shape[0] // 2
    meet_neighbours(ctx, wa, n_ctx, n_wa, SPREAD in kinds)
    sends = []

    def place(zc, wac, h):
        return out_ref.at[pl.ds(piece_row(zc, wac, h, half, n_ctx, n_wa, by_position), half)]

    def copy(src, zc, wac, h, where):
        return pltpu.make_async_remote_copy(
            src_ref=src,
            dst_ref=place(zc, wac, h),
            send_sem=send_sem.at[len(sends)],
            recv_sem=recv_sem.at[(zc * n_wa + wac) * 2 + h],
            device_id=where,
            device_id_type=MESH_ID,
        )

    def send(cond, src, zc, wac, h, where):
        made = copy(src, zc, wac, h, where)
        if cond is None:
            made.start()
        else:
            pl.when(cond)(made.start)
        sends.append((cond, made))

    def arrived(cond, zc, wac, h):
        made = pltpu.make_async_remote_copy(
            src_ref=place(zc, wac, h),
            dst_ref=place(zc, wac, h),
            send_sem=send_sem.at[0],
            recv_sem=recv_sem.at[(zc * n_wa + wac) * 2 + h],
            device_id={"wa": wa ^ 1},
            device_id_type=MESH_ID,
        )
        if cond is None:
            made.wait_recv()
        else:
            pl.when(cond)(made.wait_recv)

    def inside(zc):
        return (zc >= 0) & (zc < n_ctx)

    own_copies = []
    for h in range(2):
        own = own_ref.at[pl.ds(h * half, half)]
        for way in (-1, 1):
            send(inside(ctx + way), own, ctx, wa, h, {"ctx": ctx + way})
        send(None, own, ctx, wa, h, {"wa": wa ^ 2})
        send(None, own, ctx, wa, h, {"wa": wa ^ 1})
        made = pltpu.make_async_copy(own, place(ctx, wa, h), own_sem.at[h])
        made.start()
        own_copies.append(made)
    pair_waits = start_pairs(kinds, srcs, dsts, n_wa, pair_sem, spread_sem)
    if side:
        side.bind(side_in, side_out, refs[5:])
        side.step()

    def across(k, h):
        for way in (-1, 1) if k else (1,):
            zc = ctx + way * k
            cond = inside(zc) if k else None
            arrived(cond, zc, wa ^ 2, h)
            send(cond, place(zc, wa ^ 2, h), zc, wa ^ 2, h, {"wa": wa ^ 1})

    for k in range(1, n_ctx):
        for h in range(2):
            for way in (-1, 1):
                zc = ctx + way * k
                cond = inside(zc)
                arrived(cond, zc, wa, h)
                piece = place(zc, wa, h)
                send(cond & inside(ctx - way), piece, zc, wa, h, {"ctx": ctx - way})
                send(cond, piece, zc, wa, h, {"wa": wa ^ 2})
                send(cond, piece, zc, wa, h, {"wa": wa ^ 1})
            across(k - 1, h)
            if side:
                side.step()
        if k == 1:
            pair_waits = [wait() for wait in pair_waits]
    for h in range(2):
        across(n_ctx - 1, h)
    for zc in range(n_ctx):
        for far in (0, 2):
            for h in range(2):
                arrived(None, zc, wa ^ 1 ^ far, h)
    for cond, made in sends:
        if cond is None:
            made.wait_send()
        else:
            pl.when(cond)(made.wait_send)
    for made in own_copies:
        made.wait()
    if side:
        side.finish()
    for wait in pair_waits:
        wait()


def gather_tokens(own, pairs, n_ctx, n_wa, by_position, call_id, side=None):
    more = side.operands if side else []
    rows, width = own.shape
    n = n_ctx * n_wa
    kinds = tuple(kind for kind, _ in pairs)
    anywhere = pl.BlockSpec(memory_space=pl.ANY)
    shapes = [jax.ShapeDtypeStruct((rows * n, width), own.dtype)]
    shapes += [
        jax.ShapeDtypeStruct(pair_shape(*pair), BF16)
        for pair in pairs
        for _ in range(pair_outs(pair[0]))
    ]
    shapes += side.outs if side else []
    return pl.pallas_call(
        partial(gather_kernel, n_ctx, n_wa, by_position, kinds, side),
        in_specs=[anywhere] * (1 + len(pairs) + len(more)),
        out_specs=[anywhere] * len(shapes),
        out_shape=shapes,
        scratch_shapes=[
            pltpu.SemaphoreType.DMA((2,)),
            pltpu.SemaphoreType.DMA((8 + 12 * (n_ctx - 1) + 2 * (2 * n_ctx - 1),)),
            pltpu.SemaphoreType.DMA((2 * n,)),
            pltpu.SemaphoreType.DMA((max(1, len(pairs)), 2)),
            pltpu.SemaphoreType.DMA((2, n)),
        ]
        + (side.scratch if side else []),
        compiler_params=pltpu.CompilerParams(
            collective_id=call_id, has_side_effects=True, vmem_limit_bytes=ROOM if side else None
        ),
        cost_estimate=LINK_COST,
    )(own, *[array for _, array in pairs], *more)


def scatter_kernel(
    n_ctx, n_wa, by_position, turned, kinds, side, finish, count, left_ref, right_ref, *refs
):
    row_ins, refs = refs[:count], refs[count:]
    row_count = 1 if finish is after_attention_back else 2
    pairs = len(kinds)
    outs = sum(pair_outs(kind) for kind in kinds)
    side_in, refs = split_side(side, pairs, refs)
    srcs, refs = refs[:pairs], refs[pairs:]
    row_outs, refs = refs[:row_count], refs[row_count:]
    dsts, refs = refs[:outs], refs[outs:]
    side_out, refs = refs[: len(side.outs) if side else 0], refs[len(side.outs) if side else 0 :]
    part_ref, s1, s2, s3, out_ref, send_sem, recv1, recv2, recv3, pair_sem, spread_sem = refs[:11]
    ctx = lax.axis_index("ctx")
    wa = lax.axis_index("wa")
    half = out_ref.shape[0] // 2
    slab = 16
    y = wa // 2
    sibling, across = {"wa": wa ^ 1}, {"wa": wa ^ 2}
    meet_neighbours(ctx, wa, n_ctx, n_wa, SPREAD in kinds)
    pair_waits = start_pairs(kinds, srcs, dsts, n_wa, pair_sem, spread_sem)
    if side:
        side.bind(side_in, side_out, refs[11:])
    sends = []

    def begin(cond, act):
        if cond is None:
            act()
        else:
            pl.when(cond)(act)

    def mine(zc, wac, h):
        return part_ref.at[pl.ds(piece_row(zc, wac, h, half, n_ctx, n_wa, by_position), half)]

    def send(src, dst, sem, where):
        made = pltpu.make_async_remote_copy(
            src_ref=src,
            dst_ref=dst,
            send_sem=send_sem.at[len(sends)],
            recv_sem=sem,
            device_id=where,
            device_id_type=MESH_ID,
        )
        made.start()
        sends.append(made)

    def arrived(cond, dst, sem):
        made = pltpu.make_async_remote_copy(
            src_ref=dst,
            dst_ref=dst,
            send_sem=send_sem.at[0],
            recv_sem=sem,
            device_id=sibling,
            device_id_type=MESH_ID,
        )
        begin(cond, made.wait_recv)

    def add_up(dst, dst_row, srcs):
        def step(i, carry):
            at = pl.multiple_of(i * slab, slab)
            total = srcs[0][pl.ds(at, slab), :].astype(F32)
            for src in srcs[1:]:
                total = total + src[pl.ds(at, slab), :].astype(F32)
            dst[pl.ds(pl.multiple_of(dst_row + at, slab), slab), :] = total.astype(dst.dtype)
            return carry

        lax.fori_loop(0, half // slab, step, 0)

    def inside(zc):
        return (zc >= 0) & (zc < n_ctx)

    def index1(zc, yc, h):
        return (zc * 2 + yc) * 2 + h

    def target(i):
        mirrored = 2 * ctx >= n_ctx
        near = jnp.where(mirrored, n_ctx - 1 - ctx, ctx)
        later = i - (n_ctx - 1 - 2 * near)
        step = jnp.maximum(later, 0) // 2
        paired = jnp.where(lax.rem(jnp.maximum(later, 0), 2) == 0, 2 * near - step, step)
        zc = jnp.where(later < 0, n_ctx - 1 - i, paired)
        return jnp.where(mirrored, n_ctx - 1 - zc, zc)

    def multiply(zc, yc):
        def rows_of(begin_row, count):
            rows = pl.ds(pl.multiple_of(begin_row, count), count)
            left = left_ref[rows, :]
            product = dot_t(left, right_ref[...]) if turned else dot(left, right_ref[...])
            part_ref[rows, :] = product.astype(BF16)

        if not by_position:
            rows_of((zc * n_wa + yc * 2) * 2 * half, 4 * half)
            return

        def step(h, carry):
            span = jnp.where(h == 0, zc, 2 * n_ctx - 1 - zc)
            rows_of((span * n_wa + yc * 2) * half, 2 * half)
            return carry

        lax.fori_loop(0, 2, step, 0)

    def cross(zc):
        for h in range(2):
            at = index1(zc, y ^ 1, h)
            arrived(None, s1.at[at], recv1.at[at])
            add_up(s1.at[at], 0, [s1.at[at], mine(zc, wa ^ 2, h)])
            send(s1.at[at], s2.at[zc * 2 + h], recv2.at[zc * 2 + h], across)

    targets = [target(i) for i in range(n_ctx)]
    for i, zc in enumerate(targets):
        for yc in (y ^ 1, y):
            multiply(zc, yc)
            for h in range(2):
                at = index1(zc, yc, h)
                send(mine(zc, yc * 2 + ((wa & 1) ^ 1), h), s1.at[at], recv1.at[at], sibling)
        cross(zc)
        if side:
            side.step()
    pair_waits = [wait() for wait in pair_waits]
    for i, zc in enumerate(targets):
        if side and i:
            side.step()
        for h in range(2):
            at = index1(zc, y, h)
            here = zc * 2 + h
            arrived(None, s1.at[at], recv1.at[at])
            arrived(None, s2.at[here], recv2.at[here])
            base = [mine(zc, wa, h), s1.at[at], s2.at[here]]
            low, high = here, (n_ctx + zc) * 2 + h
            if i < n_ctx - 1:
                way = jnp.where(zc > ctx, 1, -1)
                behind = jnp.where(zc > ctx, low, high)
                more = inside(ctx - way)
                arrived(more, s3.at[behind], recv3.at[behind])
                pl.when(more)(lambda: add_up(s2.at[here], 0, base + [s3.at[behind]]))
                pl.when(jnp.logical_not(more))(lambda: add_up(s2.at[here], 0, base))
                send(s2.at[here], s3.at[behind], recv3.at[behind], {"ctx": ctx + way})
            else:
                under, over = ctx > 0, ctx < n_ctx - 1
                arrived(under, s3.at[low], recv3.at[low])
                arrived(over, s3.at[high], recv3.at[high])
                ways = [
                    (under & over, [s3.at[low], s3.at[high]]),
                    (under & jnp.logical_not(over), [s3.at[low]]),
                    (over & jnp.logical_not(under), [s3.at[high]]),
                ]
                for take, extra in ways:
                    begin(take, lambda extra=extra: add_up(out_ref, h * half, base + extra))
    for ref, values in zip(row_outs, finish(out_ref[...], *[ref[...] for ref in row_ins])):
        ref[...] = values.astype(ref.dtype)
    if side:
        side.finish()
    for made in sends:
        made.wait_send()
    for wait in pair_waits:
        wait()


def scatter_tokens(
    left, right, turned, finish, rows_in, pairs, n_ctx, n_wa, by_position, call_id, side=None
):
    n = n_ctx * n_wa
    rows = left.shape[0] // n
    width = right.shape[0] if turned else right.shape[1]
    more = side.operands if side else []
    row_types = [BF16] if finish is after_attention_back else [F32, BF16]
    half = rows // 2
    kinds = tuple(kind for kind, _ in pairs)
    anywhere = pl.BlockSpec(memory_space=pl.ANY)
    vmem = pl.BlockSpec(memory_space=pltpu.VMEM)
    shapes = [
        jax.ShapeDtypeStruct(pair_shape(*pair), BF16)
        for pair in pairs
        for _ in range(pair_outs(pair[0]))
    ]
    shapes += side.outs if side else []
    return pl.pallas_call(
        partial(
            scatter_kernel, n_ctx, n_wa, by_position, turned, kinds, side, finish, len(rows_in)
        ),
        in_specs=[vmem] * (2 + len(rows_in)) + [anywhere] * (len(pairs) + len(more)),
        out_specs=[vmem] * len(row_types) + [anywhere] * len(shapes),
        out_shape=[jax.ShapeDtypeStruct((rows, width), dtype) for dtype in row_types] + shapes,
        scratch_shapes=[
            pltpu.VMEM((rows * n, width), BF16),
            pltpu.VMEM((4 * n_ctx, half, width), BF16),
            pltpu.VMEM((2 * n_ctx, half, width), BF16),
            pltpu.VMEM((4 * n_ctx, half, width), BF16),
            pltpu.VMEM((rows, width), F32),
            pltpu.SemaphoreType.DMA((8 * n_ctx,)),
            pltpu.SemaphoreType.DMA((4 * n_ctx,)),
            pltpu.SemaphoreType.DMA((2 * n_ctx,)),
            pltpu.SemaphoreType.DMA((4 * n_ctx,)),
            pltpu.SemaphoreType.DMA((max(1, len(pairs)), 2)),
            pltpu.SemaphoreType.DMA((2, n)),
        ]
        + (side.scratch if side else []),
        compiler_params=pltpu.CompilerParams(
            collective_id=call_id, has_side_effects=True, vmem_limit_bytes=ROOM
        ),
        cost_estimate=LINK_COST,
    )(left, right, *rows_in, *[array for _, array in pairs], *more)


def per_device_heads(
    tokens,
    doc_starts,
    out_grad,
    attn_gain,
    w_query,
    w_key,
    w_value,
    q_gain,
    k_gain,
    w_out,
    ffn_gain,
    w_gate,
    w_up,
    w_down,
):
    n_ctx = lax.axis_size("ctx")
    n_wa = lax.axis_size("wa")
    n = n_ctx * n_wa
    tok_rows, width = tokens.shape[1:]
    d_rows = w_query.shape[0]
    stream = tok_rows * n
    ff_cols = FF // n
    per = HD // n
    extra = 16
    swap_dp = [(0, 1), (1, 0)]

    def t_mm(a, b):
        return lax.dot_general(a, b, (((0,), (0,)), ((), ())), preferred_element_type=F32)

    def swap(blocks):
        return lax.all_to_all(blocks, AXES, 0, 0, tiled=True)

    half = d_rows // 2
    dp = lax.axis_index("dp")
    gains_own = jnp.concatenate([attn_gain, ffn_gain, q_gain, k_gain])
    gains_row = jnp.pad(gains_own, (0, extra * 2 * LANES - gains_own.shape[0]))
    attn_cols = pack_attn(w_query, w_key, w_value, gains_row.reshape(extra, 2 * LANES), n)
    x_all, attn_half, attn_other, ff_blocks = gather_tokens(
        tokens[0], [(SPREAD, attn_cols)], n_ctx, n_wa, True, 1, PackColumns(w_gate, w_up, n)
    )
    gains = attn_half[:, half:].reshape(n, -1).astype(F32)
    attn_gain32 = gains[:, :d_rows].reshape(-1)
    ffn_gain32 = gains[:, d_rows : 2 * d_rows].reshape(-1)
    qgain32 = gains[:, 2 * d_rows : 2 * d_rows + per].reshape(-1)
    kgain32 = gains[:, 2 * d_rows + per : 2 * d_rows + 2 * per].reshape(-1)

    dy_b, x_all = lax.optimization_barrier((out_grad[0], x_all))
    ff_half = swap(ff_blocks)
    dy_all = lax.all_gather(dy_b, AXES, axis=0, tiled=True)

    attn_gain_row, ffn_gain_row = attn_gain32.reshape(1, width), ffn_gain32.reshape(1, width)
    cosine, sine = rope_tables(stream)
    head_gain = jnp.concatenate([qgain32, qgain32, kgain32, kgain32]).reshape(1, 2 * LANES)
    n1_all, raw, q_b, kv_b, att, inv, w_qkv = attend(
        doc_starts, x_all, attn_gain_row, attn_half, attn_other, head_gain, cosine, sine
    )
    middle, n2_own = scatter_tokens(
        att, w_out, False, after_attention, [tokens[0], ffn_gain_row], [], n_ctx, n_wa, True, 3
    )
    n2_all, ff_other = gather_tokens(n2_own, [(WHOLE, ff_half)], n_ctx, n_wa, False, 2)
    hidden, d_gu, gu_grad, w_gu = ffn(n2_all, dy_all, ff_half, ff_other, w_down)
    gu_grad = gu_grad.reshape(n, 2, half, 2 * ff_cols)
    d_middle, d_branch, gu_other, down_part, down_grad = scatter_tokens(
        d_gu,
        w_gu,
        True,
        after_ffn_back,
        [middle, ffn_gain_row, out_grad[0]],
        [(PICK, gu_grad)],
        n_ctx,
        n_wa,
        False,
        4,
        DownProducts(dy_all, w_down, hidden),
    )
    down = lax.psum_scatter(down_part, AXES, scatter_dimension=0, tiled=True).astype(F32)
    layer_out = middle + down
    db_all, down_other, gu_sum = gather_tokens(
        d_branch, [(WHOLE, down_grad)], n_ctx, n_wa, True, 5, PairSum(gu_grad, gu_other)
    )
    gu_rows = swap(gu_sum)
    out_w_grad = t_mm(att, db_all).astype(BF16)
    out_w_other = lax.ppermute(out_w_grad, "dp", swap_dp)
    d_qkv, head_grad = attend_back(
        doc_starts, db_all, w_out, q_b, kv_b, att, inv, raw, head_gain, cosine, sine
    )
    out_w_other, d_qkv = lax.optimization_barrier((out_w_other, d_qkv))
    qkv_grad = t_mm(n1_all, d_qkv).astype(BF16).reshape(n, 2, half, 2 * LANES)
    qkv_other = lax.ppermute(
        lax.dynamic_index_in_dim(qkv_grad, 1 - dp, 1, keepdims=False), "dp", swap_dp
    )
    head_grad = head_grad + lax.ppermute(head_grad, "dp", swap_dp)
    qkv_other, head_grad, gu_rows = lax.optimization_barrier((qkv_other, head_grad, gu_rows))
    gu_others = lax.ppermute(gu_rows, "dp", swap_dp)
    qkv_mine = lax.dynamic_index_in_dim(qkv_grad, dp, 1, keepdims=False)
    qkv_sum = (qkv_mine.astype(F32) + qkv_other.astype(F32)).astype(BF16)
    head_row = jnp.pad(head_grad.astype(BF16), ((0, 8), (0, LANES)))
    qkv_out = jnp.concatenate(
        [qkv_sum, jnp.broadcast_to(head_row[None], (n,) + head_row.shape)], axis=1
    )
    input_grad, qkv_rows, qkv_others = scatter_tokens(
        d_qkv,
        w_qkv,
        True,
        after_attention_back,
        [tokens[0], attn_gain_row, d_middle],
        [(SPREAD, qkv_out)],
        n_ctx,
        n_wa,
        True,
        6,
    )
    gu_others, input_grad = lax.optimization_barrier((gu_others, input_grad))
    gate_grad, up_grad, gu_sums = unpack_pair(gu_rows, gu_others, w_gate, w_up)
    q_grad, k_grad, v_grad, attn_sums, head_sums = unpack_attn(
        qkv_rows, qkv_others, w_query, w_key, w_value
    )
    me = lax.axis_index("ctx") * n_wa + lax.axis_index("wa")
    q_gain_grad = head_sums[0, :HD] + head_sums[0, HD:LANES]
    k_gain_grad = head_sums[1, :HD]
    attn_gain_grad = jnp.sum(attn_sums, axis=1) / attn_gain.astype(F32)
    ffn_gain_grad = jnp.sum(gu_sums, axis=1) / ffn_gain.astype(F32)
    return (
        layer_out.astype(BF16)[None],
        input_grad[None],
        attn_gain_grad,
        q_grad,
        k_grad,
        v_grad,
        lax.dynamic_slice_in_dim(q_gain_grad, me * per, per),
        lax.dynamic_slice_in_dim(k_gain_grad, me * per, per),
        out_w_grad.astype(F32) + out_w_other.astype(F32),
        ffn_gain_grad,
        gate_grad,
        up_grad,
        down_grad.astype(F32) + down_other.astype(F32),
    )


def solution(mesh):
    split = mesh.shape["ctx"] * mesh.shape["wa"]
    by_heads = 2 * split == H
    placed = (
        P("dp", ("ctx", "wa"), None),
        P("dp", None),
        P("dp", ("ctx", "wa"), None),
        P(("ctx", "wa")),
        P(("ctx", "wa"), None),
        P(("ctx", "wa"), None),
        P(("ctx", "wa"), None),
        P(("ctx", "wa")),
        P(("ctx", "wa")),
        P(("ctx", "wa"), None),
        P(("ctx", "wa")),
        P(("ctx", "wa"), None),
        P(("ctx", "wa"), None),
        P(("ctx", "wa"), None),
    )
    return jax.shard_map(
        per_device_heads if by_heads else per_device,
        mesh=mesh,
        in_specs=placed,
        out_specs=(
            P("dp", ("ctx", "wa"), None),
            P("dp", ("ctx", "wa"), None),
            P(("ctx", "wa")),
            P(("ctx", "wa"), None),
            P(("ctx", "wa"), None),
            P(("ctx", "wa"), None),
            P(("ctx", "wa")),
            P(("ctx", "wa")),
            P(("ctx", "wa"), None),
            P(("ctx", "wa")),
            P(("ctx", "wa"), None),
            P(("ctx", "wa"), None),
            P(("ctx", "wa"), None),
        ),
        check_vma=False,
    )
```
